32 devices in a mesh: rep: 8 (over y, x, core), shard: 4 (over z).
Axes of the slice: x: 2, y: 2, z: 4, core: 2. Of those that a mesh axis runs over, the one named last changes fastest.
Arguments:
- tokens: bfloat16 [16384, 1280], P(('rep', 'shard')), may hold values from -6 to 6
- doc_lengths: int32 [8, 8], P('rep'), may hold values from 1 to 1024, 2048 in all within a row
- cotangent: bfloat16 [16384, 1280], P(('rep', 'shard')), may hold values from -6 to 6
- attn_w: float32 [4, 1280, 1280], P(None, 'shard'), may hold values from -0.15625 to 0.15625
- ffn_w: float32 [3, 5120, 1280], P(None, 'shard'), may hold values from -0.15625 to 0.15625
- attn_m: float32 [4, 1280, 1280], P(None, 'shard'), may hold values from -1.75 to 1.75
- attn_v: float32 [4, 1280, 1280], P(None, 'shard'), may hold values from 0.0564 to 0.228
- ffn_m: float32 [3, 5120, 1280], P(None, 'shard'), may hold values from -1.75 to 1.75
- ffn_v: float32 [3, 5120, 1280], P(None, 'shard'), may hold values from 0.0564 to 0.228
- gains_d: float32 [3, 1280], P(None, 'shard'), as said below
- gains_ff: float32 [2, 5120], P(None, 'shard'), may hold values from 0.25 to 1.75
- gd_m: float32 [3, 1280], P(None, 'shard'), may hold values from -6 to 6
- gd_v: float32 [3, 1280], P(None, 'shard'), may hold values from 0.6312 to 2.52
- gf_m: float32 [2, 5120], P(None, 'shard'), may hold values from -6 to 6
- gf_v: float32 [2, 5120], P(None, 'shard'), may hold values from 0.6312 to 2.52
Outputs:
- output: bfloat16 [16384, 1280], P(('rep', 'shard'))
- grad_tokens: float32 [16384, 1280], P(('rep', 'shard'))
- attn_new: float32 [4, 1280, 1280], P(None, 'shard')
- attn_m_new: float32 [4, 1280, 1280], P(None, 'shard')
- attn_v_new: float32 [4, 1280, 1280], P(None, 'shard')
- ffn_new: float32 [3, 5120, 1280], P(None, 'shard')
- ffn_m_new: float32 [3, 5120, 1280], P(None, 'shard')
- ffn_v_new: float32 [3, 5120, 1280], P(None, 'shard')
- gd_new: float32 [3, 1280], P(None, 'shard')
- gd_m_new: float32 [3, 1280], P(None, 'shard')
- gd_v_new: float32 [3, 1280], P(None, 'shard')
- gf_new: float32 [2, 5120], P(None, 'shard')
- gf_m_new: float32 [2, 5120], P(None, 'shard')
- gf_v_new: float32 [2, 5120], P(None, 'shard')
The draws below stay inside these ranges and needn't reach their ends.
Inputs may be any that keep to these rules, and one draw needn't show every extreme that they name: `doc_lengths`: each row sums to 2048; its longest document has exactly 1024 tokens. `gains_d`: row 0 (s_qk) lies between 1 and 2, rows 1 and 2 (alpha_A, alpha_M) between 0.2 and 0.6.
All inputs are finite; a program needn't handle non-finite values.
Results may differ from the reference program's by a relative error of at most 0.025.
The reference program's roundings to bfloat16 on the way count: a program that leaves them out, or rounds other values in their place, can miss the bound.
Values may be sent and summed in bfloat16 or wider, within the bound.
A program may use at most 448 MiB of HBM per device.

```python
import math
import jax
import jax.numpy as jnp
import numpy as np
from jax import lax

D = 1280
FF = 5120
HEADS = 20
HEAD_DIM = 64
TOK_DEV = 512
WINDOW = 1024
DOCS = 8
STEP = 10
SEQ_LEN = 2048
SEQS = 8
TOKENS = 16384
N_REP = 8
N_SHARD = 4


def draw_gains_d(key, part):
    key = jax.random.fold_in(key, 11)
    first = jax.random.uniform(jax.random.fold_in(key, 1), (1, D), jnp.float32, 1.0, 2.0)
    rates = jax.random.uniform(jax.random.fold_in(key, 2), (2, D), jnp.float32, 0.2, 0.6)
    return jnp.concatenate([first, rates], 0)


def steps_of(key, shape, cuts, least, top_value):
    def one(position, shards_of):
        heights = jax.random.uniform(jax.random.fold_in(jax.random.fold_in(key, 6), position), (shards_of,), jnp.float32, least / len(cuts), top_value / len(cuts))
        return jnp.repeat(jnp.exp(heights), shape[position] // shards_of).reshape((-1,) + (1,) * (len(shape) - position - 1))

    loudness = one(*cuts[0])
    for cut in cuts[1:]:
        loudness = loudness * one(*cut)
    return loudness


def profile(number_of, total, most, slope):
    weights = [(1 << 20) // math.isqrt(standing ** slope) + 1 for standing in range(2, number_of + 1)]
    rest, counts = total - most - (number_of - 1), [1] * (number_of - 1)
    while rest > 0:
        free = [i for i in range(number_of - 1) if counts[i] < most]
        pool, left = sum([weights[i] for i in free]), rest
        for i in free:
            more = min(most - counts[i], max(1, left * weights[i] // pool), rest)
            counts[i] = counts[i] + more
            rest = rest - more
    return np.array([most] + counts)


def uneven(rng, number_of, total, most, skew):
    if number_of == 2:
        one = jax.random.randint(rng, (), max(1, total - most), min(most, total - 1) + 1)
        return jnp.stack([one, total - one])
    sizes = jnp.asarray(profile(number_of, total, most, skew), jnp.int32)
    pairs = (number_of - 1) // 2
    donor, taker = sizes[1:1 + 2 * pairs:2], sizes[2:2 + 2 * pairs:2]
    margin = jnp.minimum(donor - 1, most - taker)
    passed = jax.random.randint(jax.random.fold_in(rng, 1), (pairs,), 0, 1 << 20) % (margin + 1)
    sizes = sizes.at[1:1 + 2 * pairs:2].set(donor - passed).at[2:2 + 2 * pairs:2].set(taker + passed)
    return sizes[jax.random.permutation(jax.random.fold_in(rng, 2), number_of)]


def bell_draw(key, shape, spread, reach, pieces=(), kind=jnp.bfloat16):
    loudness = steps_of(key, shape, pieces, -0.22, 0.18) if pieces else 1.0
    entries = jax.random.normal(key, shape, jnp.float32) * spread * loudness
    return jnp.minimum(jnp.maximum(entries, -reach), reach).astype(kind)


def setup_inputs(seed: int = 0) -> dict:
    seeds = jax.random.split(jax.random.key(seed), 16)
    tokens = bell_draw(seeds[0], (TOKENS, D), 1.0, 6.0, ((0, 32),))
    doc_lengths = jax.vmap(lambda own: uneven(own, DOCS, SEQ_LEN, SEQ_LEN // 2, 2))(jax.random.split(seeds[1], SEQS)).reshape((SEQS, DOCS)).astype(jnp.int32)
    cotangent = bell_draw(seeds[2], (TOKENS, D), 1.0, 6.0, ((0, 32),))
    attn_w = bell_draw(seeds[3], (4, D, D), D ** -0.5, 0.15625, ((1, 4),), jnp.float32)
    ffn_w = bell_draw(seeds[4], (3, FF, D), D ** -0.5, 0.15625, ((1, 4),), jnp.float32)
    attn_m = bell_draw(seeds[5], (4, D, D), (0.033 * (TOKENS // D) ** 0.5), 1.75, ((1, 4),), jnp.float32)
    attn_v = jnp.clip(jnp.exp(math.log(0.228) - 1.3968765 * jax.random.uniform(seeds[6], (4, D, D), jnp.float32) ** steps_of(seeds[6], (4, D, D), ((1, 4),), -0.2, 0.2)), 0.0564, 0.228)
    ffn_m = bell_draw(seeds[7], (3, FF, D), (0.033 * (TOKENS // D) ** 0.5), 1.75, ((1, 4),), jnp.float32)
    ffn_v = jnp.clip(jnp.exp(math.log(0.228) - 1.3968765 * jax.random.uniform(seeds[8], (3, FF, D), jnp.float32) ** steps_of(seeds[8], (3, FF, D), ((1, 4),), -0.2, 0.2)), 0.0564, 0.228)
    gains_d = draw_gains_d(jax.random.fold_in(seeds[15], 71), 0)
    gains_ff = jnp.clip(1.0 + 0.15 * jax.random.normal(seeds[10], (2, FF), jnp.float32), 0.25, 1.75)
    gd_m = bell_draw(seeds[11], (3, D), (0.11 * (TOKENS // D) ** 0.5), 6.0, ((1, 4),), jnp.float32)
    gd_v = jnp.clip(jnp.exp(math.log(2.52) - 1.3843914 * jax.random.uniform(seeds[12], (3, D), jnp.float32) ** steps_of(seeds[12], (3, D), ((1, 4),), -0.2, 0.2)), 0.6312, 2.52)
    gf_m = bell_draw(seeds[13], (2, FF), (0.11 * (TOKENS // D) ** 0.5), 6.0, ((1, 4),), jnp.float32)
    gf_v = jnp.clip(jnp.exp(math.log(2.52) - 1.3843914 * jax.random.uniform(seeds[14], (2, FF), jnp.float32) ** steps_of(seeds[14], (2, FF), ((1, 4),), -0.2, 0.2)), 0.6312, 2.52)
    return {"tokens": tokens, "doc_lengths": doc_lengths, "cotangent": cotangent, "attn_w": attn_w, "ffn_w": ffn_w, "attn_m": attn_m, "attn_v": attn_v, "ffn_m": ffn_m, "ffn_v": ffn_v, "gains_d": gains_d, "gains_ff": gains_ff, "gd_m": gd_m, "gd_v": gd_v, "gf_m": gf_m, "gf_v": gf_v}


@jax.custom_vjp
def low(v):
    return lax.optimization_barrier(v.astype(jnp.bfloat16)).astype(jnp.float32)

@jax.custom_vjp
def low_back(v):
    return v

def low_keep(v):
    return (low(v), None)

def low_pass(kept, grad):
    return (grad,)

def back_keep(v):
    return (v, None)

def back_low(kept, grad):
    return (low(grad),)
low.defvjp(low_keep, low_pass)
low_back.defvjp(back_keep, back_low)
SMALL = 1e-06
NEGATIVE = -1e+30
BETA_ONE = 0.9
BETA_TWO = 0.95
RATE = 0.02
GAIN_RATE = 1.0
DECAY = 0.1
TINY = 1e-08
HIGH = lax.Precision.HIGHEST

def rownorm(value):
    return value * lax.rsqrt(lax.optimization_barrier(jnp.sum(value * value, -1, keepdims=True)) + SMALL)

def headnorm(value):
    rows = value.shape[0]
    return rownorm(value.reshape(rows, HEADS, HEAD_DIM)).reshape(rows, HEADS * HEAD_DIM)

def attend(queries, keys, values, query_pos, key_pos, start):
    rows = queries.shape[0]
    cols = keys.shape[0]
    raw = jnp.einsum('qhd,khd->hqk', queries.reshape(rows, HEADS, HEAD_DIM), keys.reshape(cols, HEADS, HEAD_DIM), precision=HIGH)
    scores = low_back(raw * math.sqrt(HEAD_DIM))
    mask = (key_pos[None, :] <= query_pos[:, None]) & (query_pos[:, None] - key_pos[None, :] < WINDOW) & (key_pos[None, :] >= start[:, None])
    scores = jnp.where(mask[None], scores, NEGATIVE)
    peak = lax.optimization_barrier(jnp.max(scores, -1, keepdims=True))
    shifted = jnp.exp(scores - peak)
    probs = low(shifted / lax.optimization_barrier(jnp.sum(shifted, -1, keepdims=True)))
    out = jnp.einsum('hqk,khd->qhd', probs, values.reshape(cols, HEADS, HEAD_DIM), precision=HIGH)
    return out.reshape(rows, HEADS * HEAD_DIM)

def attention(q_low, k_low, v_low, doc_start):
    length = q_low.shape[0]
    blocks = length // TOK_DEV
    padding = jnp.zeros((WINDOW, k_low.shape[1]), k_low.dtype)
    keys = jnp.concatenate([padding, k_low], 0)
    values = jnp.concatenate([padding, v_low], 0)

    def block(index):
        first = index * TOK_DEV
        queries = lax.dynamic_slice_in_dim(q_low, first, TOK_DEV, 0)
        key_rows = lax.dynamic_slice_in_dim(keys, first, WINDOW + TOK_DEV, 0)
        value_rows = lax.dynamic_slice_in_dim(values, first, WINDOW + TOK_DEV, 0)
        start = lax.dynamic_slice_in_dim(doc_start, first, TOK_DEV, 0)
        query_pos = first + jnp.arange(TOK_DEV, dtype=jnp.int32)
        key_pos = first - WINDOW + jnp.arange(WINDOW + TOK_DEV, dtype=jnp.int32)
        return attend(queries, key_rows, value_rows, query_pos, key_pos, start)
    out = lax.map(jax.checkpoint(block), jnp.arange(blocks, dtype=jnp.int32))
    return out.reshape(length, -1)

def layer(inputs, attn_w, ffn_w, gains_d, gains_ff, doc_start):
    weights = low(attn_w)
    ffn = low(ffn_w)
    gain_d = low(gains_d)
    gain_ff = low(gains_ff)
    normed = rownorm(inputs)
    in_low = low(normed)
    proj = jnp.einsum('td,jod->jto', in_low, weights[:3], precision=HIGH)
    q_pre = low_back(proj[0])
    k_pre = low_back(proj[1])
    v_low = low(low_back(proj[2]))
    q_low = low(headnorm(q_pre) * gain_d[0])
    k_low = low(headnorm(k_pre) * gain_d[0])
    attended = low(low_back(attention(q_low, k_low, v_low, doc_start)))
    side = rownorm(low_back(jnp.dot(attended, weights[3], precision=HIGH)))
    middle = rownorm(normed + gain_d[1] * (side - normed))
    mid_low = low(middle)
    both = jnp.einsum('td,jfd->jtf', mid_low, ffn[:2], precision=HIGH)
    upward = low_back(both[0]) * gain_ff[0]
    gate = low_back(both[1]) * (gain_ff[1] * math.sqrt(D))
    hidden = low(jax.nn.silu(gate) * upward)
    branch = rownorm(low_back(jnp.dot(hidden, ffn[2], precision=HIGH)))
    return rownorm(middle + gain_d[2] * (branch - middle))

def adam(weight, grad, first, second, rate, decay):
    first = BETA_ONE * first + (1.0 - BETA_ONE) * grad
    second = BETA_TWO * second + (1.0 - BETA_TWO) * grad * grad
    fix_one = 1.0 - BETA_ONE ** STEP
    fix_two = 1.0 - BETA_TWO ** STEP
    change = first / fix_one / (jnp.sqrt(second / fix_two) + TINY) + decay * weight
    return (weight - rate * change, first, second)

def reference(tokens, doc_lengths, cotangent, attn_w, ffn_w, attn_m, attn_v, ffn_m, ffn_v, gains_d, gains_ff, gd_m, gd_v, gf_m, gf_v):
    seq_len = TOK_DEV * N_SHARD
    seqs = tokens.astype(jnp.float32).reshape(N_REP, seq_len, D)
    backs = cotangent.astype(jnp.float32).reshape(N_REP, seq_len, D)
    params = (attn_w, ffn_w, gains_d, gains_ff)
    zero = tuple((jnp.zeros_like(item) for item in params))

    def one(total, item):
        inputs, back, lengths = item
        starts = jnp.cumsum(lengths) - lengths
        places = jnp.arange(seq_len, dtype=jnp.int32)
        doc_start = lax.optimization_barrier(jnp.max(jnp.where(starts[None, :] <= places[:, None], starts[None, :], 0), axis=1)).astype(jnp.int32)

        def forward(inner, first_w, second_w, third_w, fourth_w):
            return layer(inner, first_w, second_w, third_w, fourth_w, doc_start)
        out, pull = jax.vjp(forward, inputs, *params)
        grads = pull(back)
        total = tuple((acc + new for acc, new in zip(total, grads[1:])))
        return (total, (out.astype(jnp.bfloat16), grads[0]))
    total, (outs, grad_in) = lax.scan(one, zero, (seqs, backs, doc_lengths))
    attn_new, attn_m_new, attn_v_new = adam(attn_w, total[0], attn_m, attn_v, RATE, DECAY)
    ffn_new, ffn_m_new, ffn_v_new = adam(ffn_w, total[1], ffn_m, ffn_v, RATE, DECAY)
    gd_new, gd_m_new, gd_v_new = adam(gains_d, total[2], gd_m, gd_v, GAIN_RATE, 0.0)
    gf_new, gf_m_new, gf_v_new = adam(gains_ff, total[3], gf_m, gf_v, GAIN_RATE, 0.0)
    return (outs.reshape(-1, D), grad_in.reshape(-1, D), rownorm(attn_new), attn_m_new, attn_v_new, rownorm(ffn_new), ffn_m_new, ffn_v_new, gd_new, gd_m_new, gd_v_new, gf_new, gf_m_new, gf_v_new)
```

```python
import math

import jax
import jax.numpy as jnp
from jax import lax
from jax.sharding import PartitionSpec as P

D = 1280
HEADS = 20
HEAD_DIM = 64
WINDOW = 1024
STEP = 10


SMALL = 1e-06
NEGATIVE = -1e30
BETA_ONE = 0.9
BETA_TWO = 0.95
RATE = 0.02
GAIN_RATE = 1.0
DECAY = 0.1
TINY = 1e-08
GROUP = 4
F32 = jnp.float32
BF16 = jnp.bfloat16


def from_behind(block, axis, distance):
    devices = range(lax.axis_size(axis))
    route = [(i - distance, i) for i in devices if i - distance in devices]
    return lax.ppermute(block, axis, route)


def rownorm(value):
    factor = lax.rsqrt(jnp.sum(value * value, -1, keepdims=True) + SMALL)
    return (value * factor, factor)


def norm_back(normed, factor, grad):
    return factor * (grad - normed * jnp.sum(normed * grad, -1, keepdims=True))


def head_norm(value):
    rows = value.shape[0]
    normed, factor = rownorm(value.reshape(rows, HEADS, HEAD_DIM))
    return (normed.reshape(rows, HEADS * HEAD_DIM), factor)


def head_back(normed, factor, grad):
    rows = grad.shape[0]
    split = normed.reshape(rows, HEADS, HEAD_DIM)
    return norm_back(split, factor, grad.reshape(rows, HEADS, HEAD_DIM)).reshape(
        rows, HEADS * HEAD_DIM
    )


def group_scores(queries, keys, mask):
    rows = queries.shape[0]
    cols = keys.shape[0]
    raw = jnp.einsum(
        "qhd,khd->hqk",
        queries.reshape(rows, GROUP, HEAD_DIM),
        keys.reshape(cols, GROUP, HEAD_DIM),
        preferred_element_type=F32,
    )
    return jnp.where(mask[None], raw * math.sqrt(HEAD_DIM), NEGATIVE)


def adam(weight, grad, first, second, rate, decay):
    first = BETA_ONE * first + (1.0 - BETA_ONE) * grad
    second = BETA_TWO * second + (1.0 - BETA_TWO) * grad * grad
    fix_one = 1.0 - BETA_ONE**STEP
    fix_two = 1.0 - BETA_TWO**STEP
    change = first / fix_one / (jnp.sqrt(second / fix_two) + TINY) + decay * weight
    return (weight - rate * change, first, second)


def dot(a, b):
    return jnp.dot(a, b, preferred_element_type=F32)


def dot_nt(a, b):
    return lax.dot_general(a, b, (((1,), (1,)), ((), ())), preferred_element_type=F32)


def dot_tn(a, b):
    return lax.dot_general(a, b, (((0,), (0,)), ((), ())), preferred_element_type=F32)


def gather_rows(shard_rows):
    reps = lax.axis_size("rep")
    piece = shard_rows.shape[0] // reps
    mine = lax.dynamic_slice_in_dim(shard_rows, lax.axis_index("rep") * piece, piece, 0)
    column = lax.all_gather(mine, "shard", axis=0)
    return lax.all_gather(column, "rep", axis=0)


def reduce_rows(grad):
    part = lax.psum_scatter(grad, "rep", scatter_dimension=0)
    part = lax.psum_scatter(part, "shard", scatter_dimension=0)
    return lax.all_gather(part, "rep", axis=0, tiled=True)


def body(
    tokens,
    doc_lengths,
    cotangent,
    attn_w,
    ffn_w,
    attn_m,
    attn_v,
    ffn_m,
    ffn_v,
    gains_d,
    gains_ff,
    gd_m,
    gd_v,
    gf_m,
    gf_v,
):
    shards = lax.axis_size("shard")
    reps = lax.axis_size("rep")
    device_index = lax.axis_index("shard")
    rows = tokens.shape[0]
    reach = WINDOW // rows
    cols = (reach + 1) * rows
    width = GROUP * HEAD_DIM
    groups = HEADS // GROUP
    attn_rows = attn_w.shape[1]
    ffn_rows = ffn_w.shape[1]
    ffn_all = shards * ffn_rows
    piece = ffn_rows // reps

    attn_got = gather_rows(attn_w.reshape(4 * attn_rows, D).astype(BF16))
    attn_low = (
        attn_got.reshape(reps, shards, -1, D)
        .transpose(1, 0, 2, 3)
        .reshape(shards, 4, attn_rows, D)
        .transpose(1, 0, 2, 3)
        .reshape(4, shards * attn_rows, D)
    )
    up_low = gather_rows(ffn_w[0].astype(BF16)).reshape(ffn_all, D)
    gate_low = gather_rows(ffn_w[1].astype(BF16)).reshape(ffn_all, D)
    down_low = gather_rows(ffn_w[2].astype(BF16)).reshape(ffn_all, D)
    small = jnp.concatenate([gains_d.reshape(-1), gains_ff.reshape(-1)]).astype(BF16)
    small = lax.all_gather(small, "shard", axis=0).astype(F32)
    cut = gains_d.size
    gd_all = small[:, :cut].reshape(shards, 3, -1).transpose(1, 0, 2).reshape(3, D)
    gf_all = small[:, cut:].reshape(shards, 2, reps, piece).transpose(1, 2, 0, 3).reshape(2, ffn_all)
    gain_qk = gd_all[0]
    alpha_attn = gd_all[1]
    alpha_ffn = gd_all[2]
    scale_up = gf_all[0]
    scale_gate = gf_all[1] * math.sqrt(D)

    lengths_row = doc_lengths[0]
    starts = jnp.cumsum(lengths_row) - lengths_row
    positions = device_index * rows + jnp.arange(rows, dtype=jnp.int32)
    doc_start = jnp.max(
        jnp.where(starts[None, :] <= positions[:, None], starts[None, :], 0), axis=1
    )
    key_pos = device_index * rows - reach * rows + jnp.arange(cols, dtype=jnp.int32)
    mask = (
        (key_pos[None, :] <= positions[:, None])
        & (positions[:, None] - key_pos[None, :] < WINDOW)
        & (key_pos[None, :] >= doc_start[:, None])
    )
    earlier = [from_behind(tokens, "shard", offset) for offset in range(reach, 0, -1)]
    tokens_all = jnp.concatenate(earlier + [tokens], 0)
    normed_all, factor_all = rownorm(tokens_all.astype(F32))
    low_all = normed_all.astype(BF16)
    normed_in, factor_in = normed_all[-rows:], factor_all[-rows:]
    in_low = low_all[-rows:]
    q_hat, q_factor = head_norm(dot_nt(in_low, attn_low[0]))
    k_hat, k_factor = head_norm(dot_nt(low_all, attn_low[1]))
    value_all = dot_nt(low_all, attn_low[2]).astype(BF16)
    q_low = (q_hat * gain_qk).astype(BF16)
    key_all = (k_hat * gain_qk).astype(BF16)

    def forward_group(group, carry):
        attended, maxima, totals = carry
        first = group * width
        queries = lax.dynamic_slice_in_dim(q_low, first, width, 1)
        keys = lax.dynamic_slice_in_dim(key_all, first, width, 1)
        values = lax.dynamic_slice_in_dim(value_all, first, width, 1)
        scores = group_scores(queries, keys, mask)
        peak = jnp.max(scores, -1, keepdims=True)
        shifted = jnp.exp(scores - peak)
        total = jnp.sum(shifted, -1, keepdims=True)
        probs = (shifted / total).astype(BF16)
        out = jnp.einsum(
            "hqk,khd->qhd",
            probs,
            values.reshape(cols, GROUP, HEAD_DIM),
            preferred_element_type=F32,
        ).reshape(rows, width)
        attended = lax.dynamic_update_slice_in_dim(attended, out, first, 1)
        maxima = lax.dynamic_update_slice_in_dim(maxima, peak, group * GROUP, 0)
        totals = lax.dynamic_update_slice_in_dim(totals, total, group * GROUP, 0)
        return (attended, maxima, totals)

    start_carry = (
        jnp.zeros((rows, D), F32),
        jnp.zeros((HEADS, rows, 1), F32),
        jnp.zeros((HEADS, rows, 1), F32),
    )
    attended, maxima, totals = lax.fori_loop(0, groups, forward_group, start_carry)
    o_low = attended.astype(BF16)
    side, side_factor = rownorm(dot(o_low, attn_low[3]))
    middle, mid_factor = rownorm(normed_in + alpha_attn * (side - normed_in))
    mid_low = middle.astype(BF16)
    up_raw = dot_nt(mid_low, up_low)
    gate_raw = dot_nt(mid_low, gate_low)
    upward = up_raw * scale_up
    gate = gate_raw * scale_gate
    sigma = jax.nn.sigmoid(gate)
    active = gate * sigma
    hidden = (active * upward).astype(BF16)
    branch, branch_factor = rownorm(dot(hidden, down_low))
    final, final_factor = rownorm(middle + alpha_ffn * (branch - middle))
    output = final.astype(BF16)
    grad_pre = norm_back(final, final_factor, cotangent.astype(F32))
    grad_mid = grad_pre * (1.0 - alpha_ffn)
    grad_alpha_ffn = jnp.sum(grad_pre * (branch - middle), 0)
    grad_bpre = norm_back(branch, branch_factor, grad_pre * alpha_ffn).astype(BF16)
    ready = (reps, shards, piece, D)
    down_grad = reduce_rows(dot_tn(hidden, grad_bpre).astype(BF16).reshape(ready))
    grad_hidden = dot_nt(grad_bpre, down_low)
    grad_upward = grad_hidden * active
    grad_gate = grad_hidden * upward * sigma * (1.0 + gate * (1.0 - sigma))
    grad_scale_up = jnp.sum(grad_upward * up_raw, 0)
    grad_scale_gate = jnp.sum(grad_gate * gate_raw, 0) * math.sqrt(D)
    grad_u = (grad_upward * scale_up).astype(BF16)
    grad_g = (grad_gate * scale_gate).astype(BF16)
    up_grad = reduce_rows(dot_tn(grad_u, mid_low).astype(BF16).reshape(ready))
    gate_grad = reduce_rows(dot_tn(grad_g, mid_low).astype(BF16).reshape(ready))
    grad_mid = grad_mid + dot(grad_u, up_low) + dot(grad_g, gate_low)
    grad_mixed = norm_back(middle, mid_factor, grad_mid)
    grad_in = grad_mixed * (1.0 - alpha_attn)
    grad_alpha_attn = jnp.sum(grad_mixed * (side - normed_in), 0)
    grad_spre = norm_back(side, side_factor, grad_mixed * alpha_attn).astype(BF16)
    out_proj_grad = dot_tn(o_low, grad_spre)
    grad_att = dot_nt(grad_spre, attn_low[3]).astype(BF16)

    def backward_group(group, carry):
        grad_q, grad_k, grad_v = carry
        first = group * width
        queries = lax.dynamic_slice_in_dim(q_low, first, width, 1)
        keys = lax.dynamic_slice_in_dim(key_all, first, width, 1)
        values = lax.dynamic_slice_in_dim(value_all, first, width, 1)
        heads_out = lax.dynamic_slice_in_dim(grad_att, first, width, 1).reshape(
            rows, GROUP, HEAD_DIM
        )
        peak = lax.dynamic_slice_in_dim(maxima, group * GROUP, GROUP, 0)
        total = lax.dynamic_slice_in_dim(totals, group * GROUP, GROUP, 0)
        scores = group_scores(queries, keys, mask)
        probs = jnp.exp(scores - peak) / total
        grad_probs = jnp.einsum(
            "qhd,khd->hqk",
            heads_out,
            values.reshape(cols, GROUP, HEAD_DIM),
            preferred_element_type=F32,
        )
        inner = jnp.sum(probs * grad_probs, -1, keepdims=True)
        grad_scores = (probs * (grad_probs - inner)).astype(BF16)
        part_q = jnp.einsum(
            "hqk,khd->qhd",
            grad_scores,
            keys.reshape(cols, GROUP, HEAD_DIM),
            preferred_element_type=F32,
        ).reshape(rows, width) * math.sqrt(HEAD_DIM)
        part_k = jnp.einsum(
            "hqk,qhd->khd",
            grad_scores,
            queries.reshape(rows, GROUP, HEAD_DIM),
            preferred_element_type=F32,
        ).reshape(cols, width) * math.sqrt(HEAD_DIM)
        part_v = jnp.einsum(
            "hqk,qhd->khd",
            probs.astype(BF16),
            heads_out,
            preferred_element_type=F32,
        ).reshape(cols, width)
        grad_q = lax.dynamic_update_slice_in_dim(grad_q, part_q, first, 1)
        grad_k = lax.dynamic_update_slice_in_dim(grad_k, part_k, first, 1)
        grad_v = lax.dynamic_update_slice_in_dim(grad_v, part_v, first, 1)
        return (grad_q, grad_k, grad_v)

    back_carry = (
        jnp.zeros((rows, D), F32),
        jnp.zeros((cols, D), F32),
        jnp.zeros((cols, D), F32),
    )
    grad_query, grad_keys, grad_values = lax.fori_loop(0, groups, backward_group, back_carry)
    grad_gain_qk = jnp.sum(grad_query * q_hat, 0) + jnp.sum(grad_keys * k_hat, 0)
    grad_qpre = head_back(q_hat, q_factor, grad_query * gain_qk).astype(BF16)
    grad_kpre = head_back(k_hat, k_factor, grad_keys * gain_qk).astype(BF16)
    grad_vpre = grad_values.astype(BF16)
    attn_grad = jnp.stack(
        [
            dot_tn(grad_qpre, in_low),
            dot_tn(grad_kpre, low_all),
            dot_tn(grad_vpre, low_all),
            out_proj_grad,
        ]
    ).astype(BF16)
    attn_grad = (
        attn_grad.reshape(4, shards, attn_rows, D)
        .transpose(1, 0, 2, 3)
        .reshape(shards, reps, 4 * attn_rows // reps, D)
        .transpose(1, 0, 2, 3)
    )
    sum_attn = reduce_rows(attn_grad).astype(F32).reshape(4, attn_rows, D)
    back_all = dot(grad_kpre, attn_low[1]) + dot(grad_vpre, attn_low[2])
    grad_in = grad_in + dot(grad_qpre, attn_low[0]) + back_all[reach * rows :]
    for offset in range(1, reach + 1):
        first = (reach - offset) * rows
        part = back_all[first : first + rows].astype(BF16)
        grad_in = grad_in + from_behind(part, "shard", -offset).astype(F32)
    grad_tokens = norm_back(normed_in, factor_in, grad_in)

    grad_gf = jnp.stack([grad_scale_up, grad_scale_gate])
    grad_gf = grad_gf.reshape(2, reps, shards, piece).transpose(0, 2, 1, 3).reshape(2, ffn_all)
    grad_small = jnp.concatenate(
        [grad_gain_qk, grad_alpha_attn, grad_alpha_ffn, grad_gf.reshape(-1)]
    )
    grad_small = lax.psum(grad_small, ("rep", "shard"))
    gd_rows = D // shards
    sum_gd = lax.dynamic_slice_in_dim(
        grad_small[: 3 * D].reshape(3, D), device_index * gd_rows, gd_rows, 1
    )
    sum_gf = lax.dynamic_slice_in_dim(
        grad_small[3 * D :].reshape(2, ffn_all), device_index * ffn_rows, ffn_rows, 1
    )
    sum_ffn = jnp.stack([up_grad, gate_grad, down_grad]).astype(F32)
    attn_new, attn_m_new, attn_v_new = adam(attn_w, sum_attn, attn_m, attn_v, RATE, DECAY)
    ffn_new, ffn_m_new, ffn_v_new = adam(ffn_w, sum_ffn, ffn_m, ffn_v, RATE, DECAY)
    gd_new, gd_m_new, gd_v_new = adam(gains_d, sum_gd, gd_m, gd_v, GAIN_RATE, 0.0)
    gf_new, gf_m_new, gf_v_new = adam(gains_ff, sum_gf, gf_m, gf_v, GAIN_RATE, 0.0)
    attn_unit, attn_scale = rownorm(attn_new)
    ffn_unit, ffn_scale = rownorm(ffn_new)
    return (
        output,
        grad_tokens,
        attn_unit,
        attn_m_new,
        attn_v_new,
        ffn_unit,
        ffn_m_new,
        ffn_v_new,
        gd_new,
        gd_m_new,
        gd_v_new,
        gf_new,
        gf_m_new,
        gf_v_new,
    )

def solution(mesh):
    return jax.shard_map(
        body,
        mesh=mesh,
        in_specs=(
            P(("rep", "shard"), None),
            P("rep", None),
            P(("rep", "shard"), None),
            P(None, "shard", None),
            P(None, "shard", None),
            P(None, "shard", None),
            P(None, "shard", None),
            P(None, "shard", None),
            P(None, "shard", None),
            P(None, "shard"),
            P(None, "shard"),
            P(None, "shard"),
            P(None, "shard"),
            P(None, "shard"),
            P(None, "shard"),
        ),
        out_specs=(
            P(("rep", "shard"), None),
            P(("rep", "shard"), None),
            P(None, "shard", None),
            P(None, "shard", None),
            P(None, "shard", None),
            P(None, "shard", None),
            P(None, "shard", None),
            P(None, "shard", None),
            P(None, "shard"),
            P(None, "shard"),
            P(None, "shard"),
            P(None, "shard"),
            P(None, "shard"),
            P(None, "shard"),
        ),
        check_vma=False,
    )
```

```python
import functools
import math

import jax
import jax.numpy as jnp
from jax import lax
from jax.experimental import pallas as pl
from jax.experimental.pallas import tpu as pltpu
from jax.sharding import PartitionSpec as P

D = 1280
HEADS = 20
HEAD_DIM = 64
WINDOW = 1024
STEP = 10


SMALL = 1e-06
NEGATIVE = -1e30
BETA_ONE = 0.9
BETA_TWO = 0.95
RATE = 0.02
GAIN_RATE = 1.0
DECAY = 0.1
TINY = 1e-08
GROUP = 4
F32 = jnp.float32
BF16 = jnp.bfloat16


def from_behind(block, axis, distance):
    devices = range(lax.axis_size(axis))
    route = [(i - distance, i) for i in devices if i - distance in devices]
    return lax.ppermute(block, axis, route)


def rownorm(value):
    factor = lax.rsqrt(jnp.sum(value * value, -1, keepdims=True) + SMALL)
    return (value * factor, factor)


def norm_back(normed, factor, grad):
    return factor * (grad - normed * jnp.sum(normed * grad, -1, keepdims=True))


def head_norm(value):
    rows = value.shape[0]
    normed, factor = rownorm(value.reshape(rows, HEADS, HEAD_DIM))
    return (normed.reshape(rows, HEADS * HEAD_DIM), factor)


def head_back(normed, factor, grad):
    rows = grad.shape[0]
    split = normed.reshape(rows, HEADS, HEAD_DIM)
    return norm_back(split, factor, grad.reshape(rows, HEADS, HEAD_DIM)).reshape(
        rows, HEADS * HEAD_DIM
    )


def group_scores(queries, keys, mask):
    rows = queries.shape[0]
    cols = keys.shape[0]
    raw = jnp.einsum(
        "qhd,khd->hqk",
        queries.reshape(rows, GROUP, HEAD_DIM),
        keys.reshape(cols, GROUP, HEAD_DIM),
        preferred_element_type=F32,
    )
    return jnp.where(mask[None], raw * math.sqrt(HEAD_DIM), NEGATIVE)


def adam(weight, grad, first, second, rate, decay):
    first = BETA_ONE * first + (1.0 - BETA_ONE) * grad
    second = BETA_TWO * second + (1.0 - BETA_TWO) * grad * grad
    fix_one = 1.0 - BETA_ONE**STEP
    fix_two = 1.0 - BETA_TWO**STEP
    change = first / fix_one / (jnp.sqrt(second / fix_two) + TINY) + decay * weight
    return (weight - rate * change, first, second)


def dot(a, b):
    return jnp.dot(a, b, preferred_element_type=F32)


def dot_nt(a, b):
    return lax.dot_general(a, b, (((1,), (1,)), ((), ())), preferred_element_type=F32)


def dot_tn(a, b):
    return lax.dot_general(a, b, (((0,), (0,)), ((), ())), preferred_element_type=F32)


def gather_rows(shard_rows):
    reps = lax.axis_size("rep")
    piece = shard_rows.shape[0] // reps
    mine = lax.dynamic_slice_in_dim(shard_rows, lax.axis_index("rep") * piece, piece, 0)
    column = lax.all_gather(mine, "shard", axis=0)
    return lax.all_gather(column, "rep", axis=1)


def reduce_rows(grad):
    part = lax.psum_scatter(grad, "rep", scatter_dimension=0)
    part = lax.psum_scatter(part, "shard", scatter_dimension=0)
    return lax.all_gather(part, "rep", axis=0, tiled=True)


MESH = pl.DeviceIdType.MESH
HALF = 80


def place():
    rep = lax.axis_index("rep")
    core, chip = lax.rem(rep, 2), rep // 2
    beside, above = chip + 1 - 2 * lax.rem(chip, 2), chip + 2 - 4 * (chip // 2)
    return core, chip, beside, above, 3 - chip


def greet(shards):
    core, chip, beside, above, across = place()
    line = lax.axis_index("shard")
    barrier = pltpu.get_barrier_semaphore()
    for other in (2 * chip + 1 - core, 2 * beside + core, 2 * above + core, 2 * across + core):
        pl.semaphore_signal(barrier, inc=1, device_id=(other, line), device_id_type=MESH)

    @pl.when(line > 0)
    def _():
        pl.semaphore_signal(barrier, inc=1, device_id=(2 * chip + core, line - 1), device_id_type=MESH)

    @pl.when(line < shards - 1)
    def _():
        pl.semaphore_signal(barrier, inc=1, device_id=(2 * chip + core, line + 1), device_id_type=MESH)

    inner = (line > 0).astype(jnp.int32) + (line < shards - 1).astype(jnp.int32)
    pl.semaphore_wait(barrier, 4 + inner)


def add_into(target, sources, rows):
    def step(i, _):
        part = pl.ds(pl.multiple_of(i * 16, 16), 16)
        value = target[part, :].astype(F32)
        for source in sources:
            value = value + source[part, :].astype(F32)
        target[part, :] = value.astype(BF16)
        return 0

    lax.fori_loop(0, rows // 16, step, 0)


def reduce_kernel(count, shards, rows, *refs):
    grads = refs[:count]
    out = refs[count]
    (acc, own, half, piece, below, own_sem, pair_send, pair_recv, half_send, half_recv,
     piece_send, piece_recv, line_send, line_recv, out_send, out_recv, out_local) = refs[count + 1 :]
    core, chip, beside, above, across = place()
    line = lax.axis_index("shard")
    steps = count * shards
    greet(shards)

    def owner(step):
        i = lax.rem(step, shards)
        back = lax.select(i < shards - 1 - line, shards - 1 - i, i - (shards - 1 - line))
        ahead = lax.select(i < line, i, shards - 1 - (i - line))
        other = lax.select(2 * line < shards, back, ahead)
        return lax.select(i == shards - 1, line, other)

    def remote(src, dst, send, recv, rep, shard):
        return pltpu.make_async_remote_copy(
            src_ref=src, dst_ref=dst, send_sem=send, recv_sem=recv,
            device_id=(rep, shard), device_id_type=MESH,
        )

    def load(step, grad):
        slot = lax.rem(step, 2)
        return pltpu.make_async_copy(grad.at[owner(step), :, core], own.at[slot], own_sem.at[slot])

    def pair(step, grad):
        return remote(
            grad.at[owner(step), :, 1 - core], acc.at[step], pair_send, pair_recv.at[step],
            2 * chip + 1 - core, line,
        )

    def begin(step):
        for m in range(count):
            @pl.when(step // shards == m)
            def _(m=m):
                load(step, grads[m]).start()
                pair(step, grads[m]).start()

    def halves(step):
        return (
            remote(acc.at[step, across, pl.ds(0, HALF)], half.at[step, pl.ds(0, HALF)],
                   half_send, half_recv.at[step, 0], 2 * beside + core, line),
            remote(acc.at[step, across, pl.ds(HALF, rows - HALF)], half.at[step, pl.ds(HALF, rows - HALF)],
                   half_send, half_recv.at[step, 1], 2 * above + core, line),
        )

    def pieces(step):
        return (
            remote(acc.at[step, beside], piece.at[step, 0], piece_send, piece_recv.at[step, 0],
                   2 * beside + core, line),
            remote(acc.at[step, above], piece.at[step, 1], piece_send, piece_recv.at[step, 1],
                   2 * above + core, line),
        )

    def upward(step, target):
        m = step // shards
        return remote(acc.at[step, chip], below.at[m, target], line_send, line_recv.at[m, target],
                      2 * chip + core, line + 1)

    def downward(step, target):
        m = step // shards
        slot = lax.select(target == line - 1, shards, target)
        return remote(acc.at[step, chip], below.at[m, slot], line_send, line_recv.at[m, slot],
                      2 * chip + core, line - 1)

    def wait_line(step, slot):
        m = step // shards
        pltpu.make_async_copy(below.at[m, slot], below.at[m, slot], line_recv.at[m, slot]).wait()
        add_into(acc.at[step, chip], (below.at[m, slot],), rows)

    def first(step):
        slot = lax.rem(step, 2)
        pltpu.make_async_copy(own.at[slot], own.at[slot], own_sem.at[slot]).wait()
        pltpu.make_async_copy(acc.at[step], acc.at[step], pair_recv.at[step]).wait()
        for q in range(4):
            add_into(acc.at[step, q], (own.at[slot, q],), rows)
        for copy in halves(step):
            copy.start()

    def second(step):
        for copy in halves(step):
            copy.wait_recv()
        add_into(acc.at[step, above, pl.ds(0, HALF)], (half.at[step, pl.ds(0, HALF)],), HALF)
        add_into(acc.at[step, beside, pl.ds(HALF, rows - HALF)],
                 (half.at[step, pl.ds(HALF, rows - HALF)],), rows - HALF)
        for copy in pieces(step):
            copy.start()

    def third(step):
        target = owner(step)
        for copy in pieces(step):
            copy.wait_recv()
        add_into(acc.at[step, chip], (piece.at[step, 0], piece.at[step, 1]), rows)

        @pl.when((target >= line) & (line > 0))
        def _():
            wait_line(step, target)

        @pl.when((target < line) & (line < shards - 1))
        def _():
            wait_line(step, target)

        @pl.when((target == line) & (line < shards - 1))
        def _():
            wait_line(step, shards)

        @pl.when(target > line)
        def _():
            upward(step, target).start()

        @pl.when(target < line)
        def _():
            downward(step, target).start()

        @pl.when(target == line)
        def _():
            m = step // shards
            mine = 2 * chip + core
            pltpu.make_async_copy(acc.at[step, chip], out.at[m, mine], out_local).start()
            for n, other in enumerate((2 * beside + core, 2 * above + core, 2 * across + core, 2 * chip + 1 - core)):
                remote(acc.at[step, chip], out.at[m, mine], out_send, out_recv.at[m, n], other, line).start()

    def fourth(step):
        m = step // shards
        for n, origin in enumerate((2 * beside + core, 2 * above + core, 2 * across + core)):
            pltpu.make_async_copy(out.at[m, origin], out.at[m, origin], out_recv.at[m, n]).wait()
            remote(out.at[m, origin], out.at[m, origin], out_send, out_recv.at[m, 4 + n],
                   2 * chip + 1 - core, line).start()

    begin(0)

    def turn(t, _):
        @pl.when(t + 1 < steps)
        def _():
            begin(t + 1)

        @pl.when(t < steps)
        def _():
            first(t)

        @pl.when((t >= 1) & (t < steps + 1))
        def _():
            second(t - 1)

        @pl.when((t >= 2) & (t < steps + 2))
        def _():
            third(t - 2)

        @pl.when((t >= 4) & (lax.rem(t - 4, shards) == shards - 1))
        def _():
            fourth(t - 4)

        return 0

    lax.fori_loop(0, steps + 4, turn, 0)
    for m in range(count):
        for n in range(4):
            pltpu.make_async_copy(out.at[m, 0], out.at[m, 0], out_recv.at[m, 3 + n]).wait()
    pltpu.make_async_copy(out.at[:, 0], out.at[:, 0], out_local).wait()
    pltpu.make_async_copy(out.at[:, pl.ds(0, 7)], out.at[:, pl.ds(0, 7)], out_send).wait()
    pltpu.make_async_copy(acc, acc, pair_send).wait()
    pltpu.make_async_copy(half, half, half_send).wait()
    pltpu.make_async_copy(piece, piece, piece_send).wait()
    pltpu.make_async_copy(
        below.at[:, pl.ds(0, shards - 1)], below.at[:, pl.ds(0, shards - 1)], line_send
    ).wait()


def reduce_all(grads, collective):
    count = len(grads)
    shards, _, _, rows, _ = grads[0].shape
    steps = count * shards
    any_space = pl.BlockSpec(memory_space=pl.ANY)
    dma = pltpu.SemaphoreType.DMA
    return pl.pallas_call(
        functools.partial(reduce_kernel, count, shards, rows),
        out_shape=jax.ShapeDtypeStruct((count, 8, rows, D), BF16),
        in_specs=[any_space] * count,
        out_specs=any_space,
        scratch_shapes=[
            pltpu.VMEM((steps, 4, rows, D), BF16),
            pltpu.VMEM((2, 4, rows, D), BF16),
            pltpu.VMEM((steps, rows, D), BF16),
            pltpu.VMEM((steps, 2, rows, D), BF16),
            pltpu.VMEM((count, shards + 1, rows, D), BF16),
            dma((2,)), dma(()), dma((steps,)), dma(()), dma((steps, 2)),
            dma(()), dma((steps, 2)), dma(()), dma((count, shards + 1)),
            dma(()), dma((count, 7)), dma(()),
        ],
        compiler_params=pltpu.CompilerParams(
            collective_id=collective, has_side_effects=True, vmem_limit_bytes=62 * 2**20
        ),
        cost_estimate=pl.CostEstimate(flops=count * 10**7, bytes_accessed=count * 10**8, transcendentals=0),
    )(*grads)


def body(
    tokens,
    doc_lengths,
    cotangent,
    attn_w,
    ffn_w,
    attn_m,
    attn_v,
    ffn_m,
    ffn_v,
    gains_d,
    gains_ff,
    gd_m,
    gd_v,
    gf_m,
    gf_v,
):
    shards = lax.axis_size("shard")
    reps = lax.axis_size("rep")
    device_index = lax.axis_index("shard")
    rows = tokens.shape[0]
    reach = WINDOW // rows
    cols = (reach + 1) * rows
    width = GROUP * HEAD_DIM
    groups = HEADS // GROUP
    attn_rows = attn_w.shape[1]
    ffn_rows = ffn_w.shape[1]
    ffn_all = shards * ffn_rows
    piece = ffn_rows // reps

    attn_got = gather_rows(attn_w.reshape(4 * attn_rows, D).astype(BF16))
    attn_low = (
        attn_got.reshape(shards, 4, attn_rows, D)
        .transpose(1, 0, 2, 3)
        .reshape(4, shards * attn_rows, D)
    )
    up_low = gather_rows(ffn_w[0].astype(BF16)).reshape(ffn_all, D)
    gate_low = gather_rows(ffn_w[1].astype(BF16)).reshape(ffn_all, D)
    down_low = gather_rows(ffn_w[2].astype(BF16)).reshape(ffn_all, D)
    small = jnp.concatenate([gains_d.reshape(-1), gains_ff.reshape(-1)]).astype(BF16)
    small = lax.all_gather(small, "shard", axis=0).astype(F32)
    cut = gains_d.size
    gd_all = small[:, :cut].reshape(shards, 3, -1).transpose(1, 0, 2).reshape(3, D)
    gf_all = small[:, cut:].reshape(shards, 2, ffn_rows).transpose(1, 0, 2).reshape(2, ffn_all)
    gain_qk = gd_all[0]
    alpha_attn = gd_all[1]
    alpha_ffn = gd_all[2]
    scale_up = gf_all[0]
    scale_gate = gf_all[1] * math.sqrt(D)

    lengths_row = doc_lengths[0]
    starts = jnp.cumsum(lengths_row) - lengths_row
    positions = device_index * rows + jnp.arange(rows, dtype=jnp.int32)
    doc_start = jnp.max(
        jnp.where(starts[None, :] <= positions[:, None], starts[None, :], 0), axis=1
    )
    key_pos = device_index * rows - reach * rows + jnp.arange(cols, dtype=jnp.int32)
    mask = (
        (key_pos[None, :] <= positions[:, None])
        & (positions[:, None] - key_pos[None, :] < WINDOW)
        & (key_pos[None, :] >= doc_start[:, None])
    )
    earlier = [from_behind(tokens, "shard", offset) for offset in range(reach, 0, -1)]
    tokens_all = jnp.concatenate(earlier + [tokens], 0)
    normed_all, factor_all = rownorm(tokens_all.astype(F32))
    low_all = normed_all.astype(BF16)
    normed_in, factor_in = normed_all[-rows:], factor_all[-rows:]
    in_low = low_all[-rows:]
    q_hat, q_factor = head_norm(dot_nt(in_low, attn_low[0]))
    k_hat, k_factor = head_norm(dot_nt(low_all, attn_low[1]))
    value_all = dot_nt(low_all, attn_low[2]).astype(BF16)
    q_low = (q_hat * gain_qk).astype(BF16)
    key_all = (k_hat * gain_qk).astype(BF16)

    def forward_group(group, carry):
        attended, maxima, totals = carry
        first = group * width
        queries = lax.dynamic_slice_in_dim(q_low, first, width, 1)
        keys = lax.dynamic_slice_in_dim(key_all, first, width, 1)
        values = lax.dynamic_slice_in_dim(value_all, first, width, 1)
        scores = group_scores(queries, keys, mask)
        peak = jnp.max(scores, -1, keepdims=True)
        shifted = jnp.exp(scores - peak)
        total = jnp.sum(shifted, -1, keepdims=True)
        probs = (shifted / total).astype(BF16)
        out = jnp.einsum(
            "hqk,khd->qhd",
            probs,
            values.reshape(cols, GROUP, HEAD_DIM),
            preferred_element_type=F32,
        ).reshape(rows, width)
        attended = lax.dynamic_update_slice_in_dim(attended, out, first, 1)
        maxima = lax.dynamic_update_slice_in_dim(maxima, peak, group * GROUP, 0)
        totals = lax.dynamic_update_slice_in_dim(totals, total, group * GROUP, 0)
        return (attended, maxima, totals)

    start_carry = (
        jnp.zeros((rows, D), F32),
        jnp.zeros((HEADS, rows, 1), F32),
        jnp.zeros((HEADS, rows, 1), F32),
    )
    attended, maxima, totals = lax.fori_loop(0, groups, forward_group, start_carry)
    o_low = attended.astype(BF16)
    side, side_factor = rownorm(dot(o_low, attn_low[3]))
    middle, mid_factor = rownorm(normed_in + alpha_attn * (side - normed_in))
    mid_low = middle.astype(BF16)
    up_raw = dot_nt(mid_low, up_low)
    gate_raw = dot_nt(mid_low, gate_low)
    upward = up_raw * scale_up
    gate = gate_raw * scale_gate
    sigma = jax.nn.sigmoid(gate)
    active = gate * sigma
    hidden = (active * upward).astype(BF16)
    branch, branch_factor = rownorm(dot(hidden, down_low))
    final, final_factor = rownorm(middle + alpha_ffn * (branch - middle))
    output = final.astype(BF16)
    grad_pre = norm_back(final, final_factor, cotangent.astype(F32))
    grad_mid = grad_pre * (1.0 - alpha_ffn)
    grad_alpha_ffn = jnp.sum(grad_pre * (branch - middle), 0)
    grad_bpre = norm_back(branch, branch_factor, grad_pre * alpha_ffn).astype(BF16)
    down_grad = dot_tn(hidden, grad_bpre).astype(BF16)
    grad_hidden = dot_nt(grad_bpre, down_low)
    grad_upward = grad_hidden * active
    grad_gate = grad_hidden * upward * sigma * (1.0 + gate * (1.0 - sigma))
    grad_scale_up = jnp.sum(grad_upward * up_raw, 0)
    grad_scale_gate = jnp.sum(grad_gate * gate_raw, 0) * math.sqrt(D)
    grad_u = (grad_upward * scale_up).astype(BF16)
    grad_g = (grad_gate * scale_gate).astype(BF16)
    up_grad = dot_tn(grad_u, mid_low).astype(BF16)
    gate_grad = dot_tn(grad_g, mid_low).astype(BF16)
    grad_mid = grad_mid + dot(grad_u, up_low) + dot(grad_g, gate_low)
    grad_mixed = norm_back(middle, mid_factor, grad_mid)
    grad_in = grad_mixed * (1.0 - alpha_attn)
    grad_alpha_attn = jnp.sum(grad_mixed * (side - normed_in), 0)
    grad_spre = norm_back(side, side_factor, grad_mixed * alpha_attn).astype(BF16)
    out_proj_grad = dot_tn(o_low, grad_spre)
    grad_att = dot_nt(grad_spre, attn_low[3]).astype(BF16)

    def backward_group(group, carry):
        grad_q, grad_k, grad_v = carry
        first = group * width
        queries = lax.dynamic_slice_in_dim(q_low, first, width, 1)
        keys = lax.dynamic_slice_in_dim(key_all, first, width, 1)
        values = lax.dynamic_slice_in_dim(value_all, first, width, 1)
        heads_out = lax.dynamic_slice_in_dim(grad_att, first, width, 1).reshape(
            rows, GROUP, HEAD_DIM
        )
        peak = lax.dynamic_slice_in_dim(maxima, group * GROUP, GROUP, 0)
        total = lax.dynamic_slice_in_dim(totals, group * GROUP, GROUP, 0)
        scores = group_scores(queries, keys, mask)
        probs = jnp.exp(scores - peak) / total
        grad_probs = jnp.einsum(
            "qhd,khd->hqk",
            heads_out,
            values.reshape(cols, GROUP, HEAD_DIM),
            preferred_element_type=F32,
        )
        inner = jnp.sum(probs * grad_probs, -1, keepdims=True)
        grad_scores = (probs * (grad_probs - inner)).astype(BF16)
        part_q = jnp.einsum(
            "hqk,khd->qhd",
            grad_scores,
            keys.reshape(cols, GROUP, HEAD_DIM),
            preferred_element_type=F32,
        ).reshape(rows, width) * math.sqrt(HEAD_DIM)
        part_k = jnp.einsum(
            "hqk,qhd->khd",
            grad_scores,
            queries.reshape(rows, GROUP, HEAD_DIM),
            preferred_element_type=F32,
        ).reshape(cols, width) * math.sqrt(HEAD_DIM)
        part_v = jnp.einsum(
            "hqk,qhd->khd",
            probs.astype(BF16),
            heads_out,
            preferred_element_type=F32,
        ).reshape(cols, width)
        grad_q = lax.dynamic_update_slice_in_dim(grad_q, part_q, first, 1)
        grad_k = lax.dynamic_update_slice_in_dim(grad_k, part_k, first, 1)
        grad_v = lax.dynamic_update_slice_in_dim(grad_v, part_v, first, 1)
        return (grad_q, grad_k, grad_v)

    back_carry = (
        jnp.zeros((rows, D), F32),
        jnp.zeros((cols, D), F32),
        jnp.zeros((cols, D), F32),
    )
    grad_query, grad_keys, grad_values = lax.fori_loop(0, groups, backward_group, back_carry)
    grad_gain_qk = jnp.sum(grad_query * q_hat, 0) + jnp.sum(grad_keys * k_hat, 0)
    grad_qpre = head_back(q_hat, q_factor, grad_query * gain_qk).astype(BF16)
    grad_kpre = head_back(k_hat, k_factor, grad_keys * gain_qk).astype(BF16)
    grad_vpre = grad_values.astype(BF16)
    attn_grad = jnp.stack(
        [
            dot_tn(grad_qpre, in_low),
            dot_tn(grad_kpre, low_all),
            dot_tn(grad_vpre, low_all),
            out_proj_grad,
        ]
    ).astype(BF16)
    back_all = dot(grad_kpre, attn_low[1]) + dot(grad_vpre, attn_low[2])
    grad_in = grad_in + dot(grad_qpre, attn_low[0]) + back_all[reach * rows :]
    for offset in range(1, reach + 1):
        first = (reach - offset) * rows
        part = back_all[first : first + rows].astype(BF16)
        grad_in = grad_in + from_behind(part, "shard", -offset).astype(F32)
    grad_tokens = norm_back(normed_in, factor_in, grad_in)

    grad_gf = jnp.stack([grad_scale_up, grad_scale_gate])
    attn_grad = attn_grad.reshape(4, shards, attn_rows, D).transpose(1, 0, 2, 3)
    gd_rows = D // shards
    if reps == 8 and attn_rows == 320:
        grad_gd = jnp.stack([grad_gain_qk, grad_alpha_attn, grad_alpha_ffn])
        small = jnp.concatenate(
            [
                grad_gd.reshape(3, shards, gd_rows).transpose(1, 0, 2).reshape(shards, -1),
                grad_gf.reshape(2, shards, ffn_rows).transpose(1, 0, 2).reshape(shards, -1),
            ],
            1,
        ).astype(BF16)
        extra = jnp.pad(small, ((0, 0), (0, 8 * 16 * D - small.shape[1])))
        attn_pieces = jnp.concatenate(
            [attn_grad.reshape(shards, 8, piece, D), extra.reshape(shards, 8, 16, D)], 2
        )
        ffn_sums = reduce_all(
            [part.reshape(shards, 4, 2, piece, D) for part in (up_grad, gate_grad, down_grad)], 1
        )
        sum_ffn = ffn_sums.reshape(3, ffn_rows, D).astype(F32)
        attn_sums = reduce_all([attn_pieces.reshape(shards, 4, 2, piece + 16, D)], 2)[0]
        sum_attn = attn_sums[:, :piece].reshape(4, attn_rows, D).astype(F32)
        sum_small = attn_sums[0, piece:].reshape(-1).astype(F32)
        sum_gd = sum_small[: 3 * gd_rows].reshape(3, gd_rows)
        sum_gf = sum_small[3 * gd_rows : 3 * gd_rows + 2 * ffn_rows].reshape(2, ffn_rows)
    else:
        attn_grad = attn_grad.reshape(shards, reps, 4 * attn_rows // reps, D).transpose(1, 0, 2, 3)
        sum_attn = reduce_rows(attn_grad).astype(F32).reshape(4, attn_rows, D)
        ready = (shards, reps, piece, D)
        sum_ffn = jnp.stack(
            [
                reduce_rows(part.reshape(ready).transpose(1, 0, 2, 3))
                for part in (up_grad, gate_grad, down_grad)
            ]
        ).astype(F32).reshape(3, ffn_rows, D)
        grad_small = jnp.concatenate(
            [grad_gain_qk, grad_alpha_attn, grad_alpha_ffn, grad_gf.reshape(-1)]
        )
        grad_small = lax.psum(grad_small, ("rep", "shard"))
        sum_gd = lax.dynamic_slice_in_dim(
            grad_small[: 3 * D].reshape(3, D), device_index * gd_rows, gd_rows, 1
        )
        sum_gf = lax.dynamic_slice_in_dim(
            grad_small[3 * D :].reshape(2, ffn_all), device_index * ffn_rows, ffn_rows, 1
        )
    attn_new, attn_m_new, attn_v_new = adam(attn_w, sum_attn, attn_m, attn_v, RATE, DECAY)
    ffn_new, ffn_m_new, ffn_v_new = adam(ffn_w, sum_ffn, ffn_m, ffn_v, RATE, DECAY)
    gd_new, gd_m_new, gd_v_new = adam(gains_d, sum_gd, gd_m, gd_v, GAIN_RATE, 0.0)
    gf_new, gf_m_new, gf_v_new = adam(gains_ff, sum_gf, gf_m, gf_v, GAIN_RATE, 0.0)
    attn_unit, attn_scale = rownorm(attn_new)
    ffn_unit, ffn_scale = rownorm(ffn_new)
    return (
        output,
        grad_tokens,
        attn_unit,
        attn_m_new,
        attn_v_new,
        ffn_unit,
        ffn_m_new,
        ffn_v_new,
        gd_new,
        gd_m_new,
        gd_v_new,
        gf_new,
        gf_m_new,
        gf_v_new,
    )

def solution(mesh):
    return jax.shard_map(
        body,
        mesh=mesh,
        in_specs=(
            P(("rep", "shard"), None),
            P("rep", None),
            P(("rep", "shard"), None),
            P(None, "shard", None),
            P(None, "shard", None),
            P(None, "shard", None),
            P(None, "shard", None),
            P(None, "shard", None),
            P(None, "shard", None),
            P(None, "shard"),
            P(None, "shard"),
            P(None, "shard"),
            P(None, "shard"),
            P(None, "shard"),
            P(None, "shard"),
        ),
        out_specs=(
            P(("rep", "shard"), None),
            P(("rep", "shard"), None),
            P(None, "shard", None),
            P(None, "shard", None),
            P(None, "shard", None),
            P(None, "shard", None),
            P(None, "shard", None),
            P(None, "shard", None),
            P(None, "shard"),
            P(None, "shard"),
            P(None, "shard"),
            P(None, "shard"),
            P(None, "shard"),
            P(None, "shard"),
        ),
        check_vma=False,
    )
```

```python
import functools
import math

import jax
import jax.numpy as jnp
from jax import lax
from jax.experimental import pallas as pl
from jax.experimental.pallas import tpu as pltpu
from jax.sharding import PartitionSpec as P

D = 1280
HEADS = 20
HEAD_DIM = 64
WINDOW = 1024
STEP = 10


SMALL = 1e-06
NEGATIVE = -1e30
BETA_ONE = 0.9
BETA_TWO = 0.95
RATE = 0.02
GAIN_RATE = 1.0
DECAY = 0.1
TINY = 1e-08
F32 = jnp.float32
BF16 = jnp.bfloat16


def from_behind(block, axis, distance):
    devices = range(lax.axis_size(axis))
    route = [(i - distance, i) for i in devices if i - distance in devices]
    return lax.ppermute(block, axis, route)


def rownorm(value):
    factor = lax.rsqrt(jnp.sum(value * value, -1, keepdims=True) + SMALL)
    return (value * factor, factor)


def norm_back(normed, factor, grad):
    return factor * (grad - normed * jnp.sum(normed * grad, -1, keepdims=True))


def adam(weight, grad, first, second, rate, decay):
    first = BETA_ONE * first + (1.0 - BETA_ONE) * grad
    second = BETA_TWO * second + (1.0 - BETA_TWO) * grad * grad
    fix_one = 1.0 - BETA_ONE**STEP
    fix_two = 1.0 - BETA_TWO**STEP
    change = first / fix_one / (jnp.sqrt(second / fix_two) + TINY) + decay * weight
    return (weight - rate * change, first, second)


def dot(a, b):
    return jnp.dot(a, b, preferred_element_type=F32)


def dot_nt(a, b):
    return lax.dot_general(a, b, (((1,), (1,)), ((), ())), preferred_element_type=F32)


def dot_tn(a, b):
    return lax.dot_general(a, b, (((0,), (0,)), ((), ())), preferred_element_type=F32)


def gather_rows(shard_rows):
    reps = lax.axis_size("rep")
    piece = shard_rows.shape[0] // reps
    mine = lax.dynamic_slice_in_dim(shard_rows, lax.axis_index("rep") * piece, piece, 0)
    column = lax.all_gather(mine, "shard", axis=0)
    return lax.all_gather(column, "rep", axis=1)


def reduce_rows(grad):
    part = lax.psum_scatter(grad, "rep", scatter_dimension=0)
    part = lax.psum_scatter(part, "shard", scatter_dimension=0)
    return lax.all_gather(part, "rep", axis=0, tiled=True)


MESH = pl.DeviceIdType.MESH
HALF = 80


def place():
    rep = lax.axis_index("rep")
    core, chip = lax.rem(rep, 2), rep // 2
    beside, above = chip + 1 - 2 * lax.rem(chip, 2), chip + 2 - 4 * (chip // 2)
    return core, chip, beside, above, 3 - chip


def greet(shards):
    core, chip, beside, above, across = place()
    line = lax.axis_index("shard")
    barrier = pltpu.get_barrier_semaphore()
    for other in (2 * chip + 1 - core, 2 * beside + core, 2 * above + core, 2 * across + core):
        pl.semaphore_signal(barrier, inc=1, device_id=(other, line), device_id_type=MESH)

    @pl.when(line > 0)
    def _():
        pl.semaphore_signal(barrier, inc=1, device_id=(2 * chip + core, line - 1), device_id_type=MESH)

    @pl.when(line < shards - 1)
    def _():
        pl.semaphore_signal(barrier, inc=1, device_id=(2 * chip + core, line + 1), device_id_type=MESH)

    inner = (line > 0).astype(jnp.int32) + (line < shards - 1).astype(jnp.int32)
    pl.semaphore_wait(barrier, 4 + inner)


def add_into(target, sources, rows):
    def step(i, _):
        part = pl.ds(pl.multiple_of(i * 16, 16), 16)
        value = target[part, :].astype(F32)
        for source in sources:
            value = value + source[part, :].astype(F32)
        target[part, :] = value.astype(BF16)
        return 0

    lax.fori_loop(0, rows // 16, step, 0)


def reduce_kernel(count, shards, rows, *refs):
    grads = refs[:count]
    out = refs[count]
    (acc, own, half, piece, below, own_sem, pair_send, pair_recv, half_send, half_recv,
     piece_send, piece_recv, line_send, line_recv, out_send, out_recv, out_local) = refs[count + 1 :]
    core, chip, beside, above, across = place()
    line = lax.axis_index("shard")
    steps = count * shards
    greet(shards)

    def owner(step):
        i = lax.rem(step, shards)
        back = lax.select(i < shards - 1 - line, shards - 1 - i, i - (shards - 1 - line))
        ahead = lax.select(i < line, i, shards - 1 - (i - line))
        other = lax.select(2 * line < shards, back, ahead)
        return lax.select(i == shards - 1, line, other)

    def remote(src, dst, send, recv, rep, shard):
        return pltpu.make_async_remote_copy(
            src_ref=src, dst_ref=dst, send_sem=send, recv_sem=recv,
            device_id=(rep, shard), device_id_type=MESH,
        )

    def load(step, grad):
        slot = lax.rem(step, 2)
        return pltpu.make_async_copy(grad.at[owner(step), :, core], own.at[slot], own_sem.at[slot])

    def pair(step, grad):
        return remote(
            grad.at[owner(step), :, 1 - core], acc.at[step], pair_send, pair_recv.at[step],
            2 * chip + 1 - core, line,
        )

    def begin(step):
        for m in range(count):
            @pl.when(step // shards == m)
            def _(m=m):
                load(step, grads[m]).start()
                pair(step, grads[m]).start()

    def halves(step):
        return (
            remote(acc.at[step, across, pl.ds(0, HALF)], half.at[step, pl.ds(0, HALF)],
                   half_send, half_recv.at[step, 0], 2 * beside + core, line),
            remote(acc.at[step, across, pl.ds(HALF, rows - HALF)], half.at[step, pl.ds(HALF, rows - HALF)],
                   half_send, half_recv.at[step, 1], 2 * above + core, line),
        )

    def pieces(step):
        return (
            remote(acc.at[step, beside], piece.at[step, 0], piece_send, piece_recv.at[step, 0],
                   2 * beside + core, line),
            remote(acc.at[step, above], piece.at[step, 1], piece_send, piece_recv.at[step, 1],
                   2 * above + core, line),
        )

    def upward(step, target):
        m = step // shards
        return remote(acc.at[step, chip], below.at[m, target], line_send, line_recv.at[m, target],
                      2 * chip + core, line + 1)

    def downward(step, target):
        m = step // shards
        slot = lax.select(target == line - 1, shards, target)
        return remote(acc.at[step, chip], below.at[m, slot], line_send, line_recv.at[m, slot],
                      2 * chip + core, line - 1)

    def wait_line(step, slot):
        m = step // shards
        pltpu.make_async_copy(below.at[m, slot], below.at[m, slot], line_recv.at[m, slot]).wait()
        add_into(acc.at[step, chip], (below.at[m, slot],), rows)

    def first(step):
        slot = lax.rem(step, 2)
        pltpu.make_async_copy(own.at[slot], own.at[slot], own_sem.at[slot]).wait()
        pltpu.make_async_copy(acc.at[step], acc.at[step], pair_recv.at[step]).wait()
        for q in range(4):
            add_into(acc.at[step, q], (own.at[slot, q],), rows)
        for copy in halves(step):
            copy.start()

    def second(step):
        for copy in halves(step):
            copy.wait_recv()
        add_into(acc.at[step, above, pl.ds(0, HALF)], (half.at[step, pl.ds(0, HALF)],), HALF)
        add_into(acc.at[step, beside, pl.ds(HALF, rows - HALF)],
                 (half.at[step, pl.ds(HALF, rows - HALF)],), rows - HALF)
        for copy in pieces(step):
            copy.start()

    def third(step):
        target = owner(step)
        for copy in pieces(step):
            copy.wait_recv()
        add_into(acc.at[step, chip], (piece.at[step, 0], piece.at[step, 1]), rows)

        @pl.when((target >= line) & (line > 0))
        def _():
            wait_line(step, target)

        @pl.when((target < line) & (line < shards - 1))
        def _():
            wait_line(step, target)

        @pl.when((target == line) & (line < shards - 1))
        def _():
            wait_line(step, shards)

        @pl.when(target > line)
        def _():
            upward(step, target).start()

        @pl.when(target < line)
        def _():
            downward(step, target).start()

        @pl.when(target == line)
        def _():
            m = step // shards
            mine = 2 * chip + core
            pltpu.make_async_copy(acc.at[step, chip], out.at[m, mine], out_local).start()
            for n, other in enumerate((2 * beside + core, 2 * above + core, 2 * across + core, 2 * chip + 1 - core)):
                remote(acc.at[step, chip], out.at[m, mine], out_send, out_recv.at[m, n], other, line).start()

    def fourth(step):
        m = step // shards
        for n, origin in enumerate((2 * beside + core, 2 * above + core, 2 * across + core)):
            pltpu.make_async_copy(out.at[m, origin], out.at[m, origin], out_recv.at[m, n]).wait()
            remote(out.at[m, origin], out.at[m, origin], out_send, out_recv.at[m, 4 + n],
                   2 * chip + 1 - core, line).start()

    begin(0)

    def turn(t, _):
        @pl.when(t + 1 < steps)
        def _():
            begin(t + 1)

        @pl.when(t < steps)
        def _():
            first(t)

        @pl.when((t >= 1) & (t < steps + 1))
        def _():
            second(t - 1)

        @pl.when((t >= 2) & (t < steps + 2))
        def _():
            third(t - 2)

        @pl.when((t >= 4) & (lax.rem(t - 4, shards) == shards - 1))
        def _():
            fourth(t - 4)

        return 0

    lax.fori_loop(0, steps + 4, turn, 0)
    for m in range(count):
        for n in range(4):
            pltpu.make_async_copy(out.at[m, 0], out.at[m, 0], out_recv.at[m, 3 + n]).wait()
    pltpu.make_async_copy(out.at[:, 0], out.at[:, 0], out_local).wait()
    pltpu.make_async_copy(out.at[:, pl.ds(0, 7)], out.at[:, pl.ds(0, 7)], out_send).wait()
    pltpu.make_async_copy(acc, acc, pair_send).wait()
    pltpu.make_async_copy(half, half, half_send).wait()
    pltpu.make_async_copy(piece, piece, piece_send).wait()
    pltpu.make_async_copy(
        below.at[:, pl.ds(0, shards - 1)], below.at[:, pl.ds(0, shards - 1)], line_send
    ).wait()


def reduce_all(grads, collective):
    count = len(grads)
    shards, _, _, rows, _ = grads[0].shape
    steps = count * shards
    any_space = pl.BlockSpec(memory_space=pl.ANY)
    dma = pltpu.SemaphoreType.DMA
    return pl.pallas_call(
        functools.partial(reduce_kernel, count, shards, rows),
        out_shape=jax.ShapeDtypeStruct((count, 8, rows, D), BF16),
        in_specs=[any_space] * count,
        out_specs=any_space,
        scratch_shapes=[
            pltpu.VMEM((steps, 4, rows, D), BF16),
            pltpu.VMEM((2, 4, rows, D), BF16),
            pltpu.VMEM((steps, rows, D), BF16),
            pltpu.VMEM((steps, 2, rows, D), BF16),
            pltpu.VMEM((count, shards + 1, rows, D), BF16),
            dma((2,)), dma(()), dma((steps,)), dma(()), dma((steps, 2)),
            dma(()), dma((steps, 2)), dma(()), dma((count, shards + 1)),
            dma(()), dma((count, 7)), dma(()),
        ],
        compiler_params=pltpu.CompilerParams(
            collective_id=collective, has_side_effects=True, vmem_limit_bytes=62 * 2**20
        ),
        cost_estimate=pl.CostEstimate(flops=count * 10**7, bytes_accessed=count * 10**8, transcendentals=0),
    )(*grads)


def gather_kernel(shards, attn_ref, ffn_ref, gains_ref, tokens_ref, out, gains_out, before,
                  wide, low, mine, wide_sem, low_sem, mine_sem, line_send, line_recv, plane_send, beside_recv,
                  above_recv, across_recv, pair_send, pair_recv, gains_send, gains_recv, tokens_send,
                  tokens_recv, local_sem):
    core, chip, beside, above, across = place()
    line = lax.axis_index("shard")
    rep = 2 * chip + core
    sibling = 2 * chip + 1 - core
    to_beside, to_above = 2 * beside + core, 2 * above + core
    piece = attn_ref.shape[1]
    others = shards - 1
    steps = 4 * others
    barrier = pltpu.get_barrier_semaphore()
    for other in (sibling, to_beside, to_above):
        pl.semaphore_signal(barrier, inc=1, device_id=(other, line), device_id_type=MESH)
    for n in range(1, shards):
        pl.semaphore_signal(barrier, inc=1, device_id=(rep, lax.rem(line + n, shards)), device_id_type=MESH)
    pl.semaphore_wait(barrier, 3 + others)

    def remote(src, dst, send, recv, rep, shard):
        return pltpu.make_async_remote_copy(
            src_ref=src, dst_ref=dst, send_sem=send, recv_sem=recv,
            device_id=(rep, shard), device_id_type=MESH,
        )

    def arrived(ref, sem):
        pltpu.make_async_copy(ref, ref, sem).wait()

    def source(n):
        low_side = 2 * line < shards
        edge = lax.select(low_side, line, shards - 1 - line)
        near = lax.select(lax.rem(n, 2) == 0, edge - 1 - n // 2, edge + 1 + n // 2)
        found = lax.select(n < 2 * edge, near, n + 1)
        return lax.select(low_side, found, shards - 1 - found)

    def own_send(m):
        @pl.when(line < shards - 1)
        def _():
            remote(mine.at[m], out.at[m, line, rep], line_send, line_recv.at[m, line], rep, line + 1).start()

        @pl.when(line > 0)
        def _():
            remote(mine.at[m], out.at[m, line, rep], line_send, line_recv.at[m, line], rep, line - 1).start()

    def fetch(index, slot):
        @pl.when(index < 8)
        def _():
            pltpu.make_async_copy(attn_ref.at[lax.rem(index, 8)], wide.at[slot], wide_sem.at[slot]).start()

        @pl.when(index >= 8)
        def _():
            pltpu.make_async_copy(
                ffn_ref.at[jnp.maximum(index // 8 - 1, 0), lax.rem(index, 8)], wide.at[slot], wide_sem.at[slot]
            ).start()

    def store(index, slot):
        return pltpu.make_async_copy(low.at[slot], out.at[index // 8, line, lax.rem(index, 8)], low_sem.at[slot])

    def lower(src, dst):
        def step(i, _):
            part = pl.ds(pl.multiple_of(i * 32, 32), 32)
            dst[part, :] = src[part, :].astype(BF16)
            return 0

        lax.fori_loop(0, piece // 32, step, 0)

    for n in range(1, shards):
        other = lax.rem(line + n, shards)
        remote(gains_ref, gains_out.at[line], gains_send, gains_recv.at[line], rep, other).start()
    pltpu.make_async_copy(gains_ref, gains_out.at[line], local_sem).start()
    for m in range(4):
        origin = attn_ref.at[rep] if m == 0 else ffn_ref.at[m - 1, rep]
        pltpu.make_async_copy(origin, wide.at[m], mine_sem.at[m]).start()
    for m in range(4):
        arrived(wide.at[m], mine_sem.at[m])
        lower(wide.at[m], mine.at[m])
        if m == 0:
            own_send(0)

            @pl.when(line < shards - 1)
            def _():
                remote(tokens_ref, before.at[1], tokens_send, tokens_recv.at[1], rep, line + 1).start()

    for n in range(2):
        fetch(n, n)

    def begin(c):
        m, origin = c // others, source(lax.rem(c, others))
        got = out.at[m, origin, rep]
        arrived(got, line_recv.at[m, origin])

        @pl.when((origin < line) & (line < shards - 1))
        def _():
            remote(got, got, line_send, line_recv.at[m, origin], rep, line + 1).start()

        @pl.when((origin > line) & (line > 0))
        def _():
            remote(got, got, line_send, line_recv.at[m, origin], rep, line - 1).start()

        remote(got, got, plane_send, beside_recv.at[m, origin], to_beside, line).start()
        remote(got, got, plane_send, above_recv.at[m, origin], to_above, line).start()
        remote(got, got, pair_send, pair_recv.at[m], sibling, line).start()

    def middle(c):
        m, origin = c // others, source(lax.rem(c, others))
        got = out.at[m, origin, to_beside]
        arrived(got, beside_recv.at[m, origin])
        part = out.at[m, origin, to_beside, pl.ds(0, HALF)]
        remote(part, part, plane_send, across_recv.at[m, origin, 0], to_above, line).start()
        remote(got, got, pair_send, pair_recv.at[m], sibling, line).start()
        got = out.at[m, origin, to_above]
        arrived(got, above_recv.at[m, origin])
        part = out.at[m, origin, to_above, pl.ds(HALF, piece - HALF)]
        remote(part, part, plane_send, across_recv.at[m, origin, 1], to_beside, line).start()
        remote(got, got, pair_send, pair_recv.at[m], sibling, line).start()

    def last(c):
        m, origin = c // others, source(lax.rem(c, others))
        got = out.at[m, origin, 2 * across + core]
        arrived(out.at[m, origin, 2 * across + core, pl.ds(0, HALF)], across_recv.at[m, origin, 0])
        arrived(out.at[m, origin, 2 * across + core, pl.ds(HALF, piece - HALF)], across_recv.at[m, origin, 1])
        remote(got, got, pair_send, pair_recv.at[m], sibling, line).start()

    def local(t):
        for n in range(2):
            index = 2 * t + n
            slot = 2 * lax.rem(t, 2) + n
            arrived(wide.at[slot], wide_sem.at[slot])

            @pl.when(index + 2 < 32)
            def _():
                fetch(index + 2, lax.rem(slot + 2, 4))

            @pl.when(t >= 2)
            def _():
                store(index - 4, slot).wait()

            lower(wide.at[slot], low.at[slot])
            store(index, slot).start()

    def turn(t, _):
        @pl.when((lax.rem(t, others) == 0) & (t // others < 3))
        def _():
            own_send(t // others + 1)

        @pl.when(t < steps)
        def _():
            begin(t)

        @pl.when((t == 1) & (line > 0))
        def _():
            arrived(before.at[1], tokens_recv.at[1])

            @pl.when(line < shards - 1)
            def _():
                remote(before.at[1], before.at[0], tokens_send, tokens_recv.at[0], rep, line + 1).start()

        @pl.when((t >= 1) & (t < steps + 1))
        def _():
            middle(t - 1)

        @pl.when((t >= 2) & (t < steps + 2))
        def _():
            last(t - 2)

        local(t)
        return 0

    lax.fori_loop(0, 16, turn, 0)
    for n in range(4):
        store(28 + n, n).wait()
    for m in range(4):
        arrived(out.at[m, pl.ds(0, others), pl.ds(0, 4)], pair_recv.at[m])
    for n in range(1, shards):
        other = lax.rem(line + n, shards)
        arrived(gains_out.at[other], gains_recv.at[other])
    pltpu.make_async_copy(gains_ref, gains_out.at[line], local_sem).wait()

    @pl.when(line > 1)
    def _():
        arrived(before.at[0], tokens_recv.at[0])

    @pl.when((line == 1) | (line == shards - 2))
    def _():
        arrived(before, tokens_send)

    @pl.when(line == 0)
    def _():
        arrived(before.at[0], tokens_send)

    @pl.when((line == 0) | (line == shards - 1))
    def _():
        arrived(out.at[:, 0, pl.ds(0, 1)], line_send)

    @pl.when((line > 0) & (line < shards - 1))
    def _():
        arrived(out.at[:, 0, pl.ds(0, 5)], line_send)

    arrived(out.at[:, pl.ds(0, others), pl.ds(0, 3)], plane_send)
    arrived(out.at[:, pl.ds(0, others), pl.ds(0, 4)], pair_send)
    arrived(gains_out.at[pl.ds(0, others)], gains_send)


def gather_all(attn_w, ffn_w, gains, tokens, shards, collective):
    piece = attn_w.shape[1]
    any_space = pl.BlockSpec(memory_space=pl.ANY)
    dma = pltpu.SemaphoreType.DMA
    return pl.pallas_call(
        functools.partial(gather_kernel, shards),
        out_shape=(
            jax.ShapeDtypeStruct((4, shards, 8, piece, D), BF16),
            jax.ShapeDtypeStruct((shards,) + gains.shape, BF16),
            jax.ShapeDtypeStruct((2,) + tokens.shape, BF16),
        ),
        in_specs=[any_space] * 4,
        out_specs=(any_space,) * 3,
        scratch_shapes=[
            pltpu.VMEM((4, piece, D), F32),
            pltpu.VMEM((4, piece, D), BF16),
            pltpu.VMEM((4, piece, D), BF16),
            dma((4,)), dma((4,)), dma((4,)), dma(()), dma((4, shards)), dma(()), dma((4, shards)),
            dma((4, shards)), dma((4, shards, 2)), dma(()), dma((4,)), dma(()), dma((shards,)), dma(()),
            dma((2,)), dma(()),
        ],
        compiler_params=pltpu.CompilerParams(
            collective_id=collective, has_side_effects=True, vmem_limit_bytes=40 * 2**20
        ),
        cost_estimate=pl.CostEstimate(flops=10**7, bytes_accessed=2 * 10**8, transcendentals=0),
    )(attn_w, ffn_w, gains, tokens)


QUERY_BLOCK = 256
PAIR = 2 * HEAD_DIM
PAIRS = HEADS // 2


def head_ones():
    row = lax.broadcasted_iota(jnp.int32, (PAIR, PAIR), 0) // HEAD_DIM
    col = lax.broadcasted_iota(jnp.int32, (PAIR, PAIR), 1) // HEAD_DIM
    return (row == col).astype(F32).astype(BF16)


def head_sum(value, ones):
    high = value.astype(BF16)
    rest = (value - high.astype(F32)).astype(BF16)
    return dot(high, ones) + dot(rest, ones)


def of_head(value, head):
    lane = lax.broadcasted_iota(jnp.int32, value.shape, 1) // HEAD_DIM
    return jnp.where(lane == head, value, jnp.zeros_like(value))


def attend_pair(h_ref, wq_ref, wq2_ref, wk_ref, wk2_ref, wv_ref, wv2_ref, gain_ref, bias_ref, qp_ref, kp_ref, v_ref, o_ref, lse_ref,
                key_buf, query_buf, value_buf):
    cols = h_ref.shape[0]
    rows = qp_ref.shape[0]
    span = bias_ref.shape[1]
    ones = head_ones()
    gain = gain_ref[...]
    weights = jnp.concatenate([wk_ref[...], wk2_ref[...], wv_ref[...], wv2_ref[...]], 0)
    query_weights = jnp.concatenate([wq_ref[...], wq2_ref[...]], 0)

    def project(i, _):
        part = pl.ds(pl.multiple_of(i * QUERY_BLOCK, QUERY_BLOCK), QUERY_BLOCK)
        both = dot_nt(h_ref[part, :], weights)
        keys = both[:, :PAIR]
        kp_ref[part, :] = keys
        factor = lax.rsqrt(head_sum(keys * keys, ones) + SMALL)
        key_buf[part, :] = (keys * factor * gain).astype(BF16)
        values = both[:, PAIR:].astype(BF16)
        v_ref[part, :] = values
        value_buf[part, :PAIR] = values
        value_buf[part, PAIR:] = jnp.ones_like(values)
        return 0

    lax.fori_loop(0, cols // QUERY_BLOCK, project, 0)

    def project_queries(i, _):
        part = pl.ds(pl.multiple_of(i * QUERY_BLOCK, QUERY_BLOCK), QUERY_BLOCK)
        own = pl.ds(pl.multiple_of(cols - rows + i * QUERY_BLOCK, QUERY_BLOCK), QUERY_BLOCK)
        queries = dot_nt(h_ref[own, :], query_weights)
        qp_ref[part, :] = queries
        factor = lax.rsqrt(head_sum(queries * queries, ones) + SMALL)
        scaled = (queries * factor * gain).astype(BF16).astype(F32) * math.sqrt(HEAD_DIM)
        query_buf[part, :] = scaled.astype(BF16)
        return 0

    lax.fori_loop(0, rows // QUERY_BLOCK, project_queries, 0)
    for i in range(rows // QUERY_BLOCK):
        part = pl.ds(i * QUERY_BLOCK, QUERY_BLOCK)
        reach = pl.ds(i * QUERY_BLOCK, span)
        sides = []
        for head in range(2):
            scores = dot_nt(of_head(query_buf[part, :], head), key_buf[reach, :])
            probs = jnp.exp(scores + bias_ref[part, :]).astype(BF16)
            both = dot(probs, value_buf[reach, :])
            total = both[:, PAIR:]
            sides.append(both[:, :PAIR] / total)
            lse_ref[head : head + 1, part] = jnp.log(total).T[:1, :]
        lane = lax.broadcasted_iota(jnp.int32, sides[0].shape, 1)
        o_ref[part, :] = jnp.where(lane < HEAD_DIM, sides[0], sides[1]).astype(BF16)


def back_pair(qp_ref, kp_ref, v_ref, o_ref, da_ref, wo_ref, wo2_ref, gain_ref, bias_ref, lse_ref,
              dq_ref, dk_ref, dv_ref, sum_ref, key_buf, key_turned, k_total, v_total, sum_total):
    cols = kp_ref.shape[0]
    rows = qp_ref.shape[0]
    span = bias_ref.shape[1]
    ones = head_ones()
    gain = gain_ref[...]
    weights = jnp.concatenate([wo_ref[...], wo2_ref[...]], 0)

    def keys_of(i, _):
        part = pl.ds(pl.multiple_of(i * QUERY_BLOCK, QUERY_BLOCK), QUERY_BLOCK)
        keys = kp_ref[part, :]
        factor = lax.rsqrt(head_sum(keys * keys, ones) + SMALL)
        low = keys * factor * gain
        key_buf[part, :] = low.astype(BF16)
        key_turned[:, part] = low.T.astype(BF16)
        k_total[part, :] = jnp.zeros_like(keys)
        v_total[part, :] = jnp.zeros_like(keys)
        return 0

    lax.fori_loop(0, cols // QUERY_BLOCK, keys_of, 0)
    for i in range(rows // QUERY_BLOCK):
        part = pl.ds(i * QUERY_BLOCK, QUERY_BLOCK)
        reach = pl.ds(i * QUERY_BLOCK, span)
        queries = qp_ref[part, :]
        factor = lax.rsqrt(head_sum(queries * queries, ones) + SMALL)
        hat = queries * factor
        scaled = ((hat * gain).astype(BF16).astype(F32) * math.sqrt(HEAD_DIM)).astype(BF16)
        back = dot_nt(da_ref[part, :], weights).astype(BF16)
        inner = (back.astype(F32) * o_ref[part, :].astype(F32)).T
        sides = []
        for head in range(2):
            mine = slice(head * HEAD_DIM, (head + 1) * HEAD_DIM)
            query, grad = of_head(scaled, head), of_head(back, head)
            scores = dot_nt(key_buf[reach, :], query)
            probs = jnp.exp(scores + bias_ref[i] - lse_ref[head : head + 1, part])
            v_total[reach, :] += dot(probs.astype(BF16), grad)
            delta = jnp.sum(inner[mine, :], 0, keepdims=True)
            grad_scores = (probs * (dot_nt(v_ref[reach, :], grad) - delta)).astype(BF16)
            k_total[reach, :] += dot(grad_scores, query)
            sides.append(dot(key_turned[mine, reach], grad_scores))
        grad_q = jnp.concatenate(sides, 0).T * math.sqrt(HEAD_DIM)
        sums = jnp.sum(grad_q * hat, 0, keepdims=True)
        if i == 0:
            sum_total[...] = jnp.broadcast_to(sums, sum_total.shape)
        else:
            sum_total[...] += jnp.broadcast_to(sums, sum_total.shape)
        grad_q = grad_q * gain
        dq_ref[part, :] = (factor * (grad_q - hat * head_sum(hat * grad_q, ones))).astype(BF16)

    def finish(i, _):
        part = pl.ds(pl.multiple_of(i * QUERY_BLOCK, QUERY_BLOCK), QUERY_BLOCK)
        keys = kp_ref[part, :]
        factor = lax.rsqrt(head_sum(keys * keys, ones) + SMALL)
        hat = keys * factor
        grad_k = k_total[part, :]
        sum_total[...] += jnp.broadcast_to(jnp.sum(grad_k * hat, 0, keepdims=True), sum_total.shape)
        grad_k = grad_k * gain
        dk_ref[part, :] = (factor * (grad_k - hat * head_sum(hat * grad_k, ones))).astype(BF16)
        dv_ref[part, :] = v_total[part, :].astype(BF16)
        return 0

    lax.fori_loop(0, cols // QUERY_BLOCK, finish, 0)
    sum_ref[...] = sum_total[...]


def head_rows(attn_low, matrix, second):
    heads = attn_low.shape[2]

    def index(p):
        head = 2 * p + second
        return (head // heads, matrix, lax.rem(head, heads), 0, 0)

    return pl.BlockSpec((None, None, None, HEAD_DIM, D), index)


def attention_forward(low_all, attn_low, gain_qk, bias, rows):
    cols = low_all.shape[0]
    span = bias.shape[1]
    side = lambda n: pl.BlockSpec((n, PAIR), lambda p: (0, p))
    whole = lambda *shape: pl.BlockSpec(shape, lambda p: (0,) * len(shape))
    return pl.pallas_call(
        attend_pair,
        grid=(PAIRS,),
        out_shape=(
            jax.ShapeDtypeStruct((rows, D), F32),
            jax.ShapeDtypeStruct((cols, D), F32),
            jax.ShapeDtypeStruct((cols, D), BF16),
            jax.ShapeDtypeStruct((rows, D), BF16),
            jax.ShapeDtypeStruct((PAIRS, 8, rows), F32),
        ),
        in_specs=[whole(cols, D)]
        + [head_rows(attn_low, j, second) for j in range(3) for second in range(2)]
        + [side(1), whole(rows, span)],
        out_specs=(side(rows), side(cols), side(cols), side(rows),
                   pl.BlockSpec((None, 8, rows), lambda p: (p, 0, 0))),
        scratch_shapes=[
            pltpu.VMEM((cols, PAIR), BF16),
            pltpu.VMEM((rows, PAIR), BF16),
            pltpu.VMEM((cols, 2 * PAIR), BF16),
        ],
        compiler_params=pltpu.CompilerParams(vmem_limit_bytes=56 * 2**20),
        cost_estimate=pl.CostEstimate(flops=20 * 10**9, bytes_accessed=30 * 10**6, transcendentals=13 * 10**6),
    )(low_all, *[attn_low] * 6, gain_qk, bias)


def attention_backward(q_pre, k_pre, value_all, o_low, grad_spre, attn_low, gain_qk, bias_turned, lse):
    rows, cols = q_pre.shape[0], k_pre.shape[0]
    side = lambda n: pl.BlockSpec((n, PAIR), lambda p: (0, p))
    whole = lambda *shape: pl.BlockSpec(shape, lambda p: (0,) * len(shape))
    stat = pl.BlockSpec((None, 8, rows), lambda p: (p, 0, 0))
    return pl.pallas_call(
        back_pair,
        grid=(PAIRS,),
        out_shape=(
            jax.ShapeDtypeStruct((rows, D), BF16),
            jax.ShapeDtypeStruct((cols, D), BF16),
            jax.ShapeDtypeStruct((cols, D), BF16),
            jax.ShapeDtypeStruct((8, D), F32),
        ),
        in_specs=[
            side(rows), side(cols), side(cols), side(rows), whole(rows, D),
            head_rows(attn_low, 3, 0), head_rows(attn_low, 3, 1), side(1), whole(*bias_turned.shape), stat,
        ],
        out_specs=(side(rows), side(cols), side(cols), side(8)),
        scratch_shapes=[
            pltpu.VMEM((cols, PAIR), BF16),
            pltpu.VMEM((PAIR, cols), BF16),
            pltpu.VMEM((cols, PAIR), F32),
            pltpu.VMEM((cols, PAIR), F32),
            pltpu.VMEM((8, PAIR), F32),
        ],
        compiler_params=pltpu.CompilerParams(vmem_limit_bytes=56 * 2**20),
        cost_estimate=pl.CostEstimate(flops=30 * 10**9, bytes_accessed=40 * 10**6, transcendentals=13 * 10**6),
    )(q_pre, k_pre, value_all, o_low, grad_spre, attn_low, attn_low, gain_qk, bias_turned, lse)


def body(
    tokens,
    doc_lengths,
    cotangent,
    attn_w,
    ffn_w,
    attn_m,
    attn_v,
    ffn_m,
    ffn_v,
    gains_d,
    gains_ff,
    gd_m,
    gd_v,
    gf_m,
    gf_v,
):
    shards = lax.axis_size("shard")
    reps = lax.axis_size("rep")
    device_index = lax.axis_index("shard")
    rows = tokens.shape[0]
    reach = WINDOW // rows
    cols = (reach + 1) * rows
    attn_rows = attn_w.shape[1]
    ffn_rows = ffn_w.shape[1]
    ffn_all = shards * ffn_rows
    piece = ffn_rows // reps

    cut = gains_d.size
    small = jnp.concatenate([gains_d.reshape(-1), gains_ff.reshape(-1)]).astype(BF16)
    fast = reps == 8 and shards == 4 and attn_rows % HEAD_DIM == 0
    if fast:
        gathered, small, before = gather_all(
            attn_w.reshape(8, piece, D),
            ffn_w.reshape(3, 8, piece, D),
            jnp.pad(small, (0, 16 * D - small.size)).reshape(16, D),
            tokens,
            shards,
            3,
        )
        attn_low = gathered[0].reshape(shards, 4, attn_rows // HEAD_DIM, HEAD_DIM, D)
        up_low, gate_low, down_low = (gathered[m].reshape(ffn_all, D) for m in (1, 2, 3))
        small = small.reshape(shards, -1)[:, : cut + gains_ff.size]
        present = jnp.arange(reach)[:, None, None] >= reach - device_index
        earlier = [jnp.where(present, before, 0).reshape(reach * rows, D)]
    else:
        attn_low = (
            gather_rows(attn_w.reshape(4 * attn_rows, D).astype(BF16))
            .reshape(shards, 4, attn_rows, D)
            .transpose(1, 0, 2, 3)
            .reshape(1, 4, HEADS, HEAD_DIM, D)
        )
        up_low = gather_rows(ffn_w[0].astype(BF16)).reshape(ffn_all, D)
        gate_low = gather_rows(ffn_w[1].astype(BF16)).reshape(ffn_all, D)
        down_low = gather_rows(ffn_w[2].astype(BF16)).reshape(ffn_all, D)
        small = lax.all_gather(small, "shard", axis=0)
        earlier = [from_behind(tokens, "shard", offset) for offset in range(reach, 0, -1)]
    small = small.astype(F32)
    query_low, key_low, value_low, out_low = (attn_low[:, j].reshape(D, D) for j in range(4))
    gd_all = small[:, :cut].reshape(shards, 3, -1).transpose(1, 0, 2).reshape(3, D)
    gf_all = small[:, cut:].reshape(shards, 2, ffn_rows).transpose(1, 0, 2).reshape(2, ffn_all)
    gain_qk = gd_all[0]
    alpha_attn = gd_all[1]
    alpha_ffn = gd_all[2]
    scale_up = gf_all[0]
    scale_gate = gf_all[1] * math.sqrt(D)

    lengths_row = doc_lengths[0]
    starts = jnp.cumsum(lengths_row) - lengths_row
    positions = device_index * rows + jnp.arange(rows, dtype=jnp.int32)
    doc_start = jnp.max(
        jnp.where(starts[None, :] <= positions[:, None], starts[None, :], 0), axis=1
    )
    blocks = rows // QUERY_BLOCK
    span = WINDOW + QUERY_BLOCK
    query = jnp.arange(rows, dtype=jnp.int32).reshape(blocks, QUERY_BLOCK)
    lead = query[:, :1] - reach * rows + jnp.arange(span, dtype=jnp.int32)
    ahead = query[:, :, None] - lead[:, None, :]
    floor = (doc_start - device_index * rows).reshape(blocks, QUERY_BLOCK, 1)
    mask = (ahead >= 0) & (ahead < WINDOW) & (lead[:, None, :] >= floor)
    bias = jnp.where(mask, 0.0, NEGATIVE).astype(F32)
    bias_turned = bias.transpose(0, 2, 1)
    bias = bias.reshape(rows, span)
    tokens_all = jnp.concatenate(earlier + [tokens], 0)
    normed_all, factor_all = rownorm(tokens_all.astype(F32))
    low_all = normed_all.astype(BF16)
    normed_in, factor_in = normed_all[-rows:], factor_all[-rows:]
    in_low = low_all[-rows:]
    q_pre, k_pre, value_all, o_low, lse = attention_forward(
        low_all, attn_low, gain_qk[None], bias, rows
    )
    side, side_factor = rownorm(dot(o_low, out_low))
    middle, mid_factor = rownorm(normed_in + alpha_attn * (side - normed_in))
    mid_low = middle.astype(BF16)
    up_raw = dot_nt(mid_low, up_low)
    gate_raw = dot_nt(mid_low, gate_low)
    upward = up_raw * scale_up
    gate = gate_raw * scale_gate
    sigma = jax.nn.sigmoid(gate)
    active = gate * sigma
    hidden = (active * upward).astype(BF16)
    branch, branch_factor = rownorm(dot(hidden, down_low))
    final, final_factor = rownorm(middle + alpha_ffn * (branch - middle))
    output = final.astype(BF16)
    grad_pre = norm_back(final, final_factor, cotangent.astype(F32))
    grad_mid = grad_pre * (1.0 - alpha_ffn)
    grad_alpha_ffn = jnp.sum(grad_pre * (branch - middle), 0)
    grad_bpre = norm_back(branch, branch_factor, grad_pre * alpha_ffn).astype(BF16)
    down_grad = dot_tn(hidden, grad_bpre).astype(BF16)
    grad_hidden = dot_nt(grad_bpre, down_low)
    grad_upward = grad_hidden * active
    grad_gate = grad_hidden * upward * sigma * (1.0 + gate * (1.0 - sigma))
    grad_scale_up = jnp.sum(grad_upward * up_raw, 0)
    grad_scale_gate = jnp.sum(grad_gate * gate_raw, 0) * math.sqrt(D)
    grad_u = (grad_upward * scale_up).astype(BF16)
    grad_g = (grad_gate * scale_gate).astype(BF16)
    up_grad = dot_tn(grad_u, mid_low).astype(BF16)
    gate_grad = dot_tn(grad_g, mid_low).astype(BF16)
    grad_mid = grad_mid + dot(grad_u, up_low) + dot(grad_g, gate_low)
    grad_mixed = norm_back(middle, mid_factor, grad_mid)
    grad_in = grad_mixed * (1.0 - alpha_attn)
    grad_alpha_attn = jnp.sum(grad_mixed * (side - normed_in), 0)
    grad_spre = norm_back(side, side_factor, grad_mixed * alpha_attn).astype(BF16)
    out_proj_grad = dot_tn(o_low, grad_spre)
    grad_qpre, grad_kpre, grad_vpre, gain_sums = attention_backward(
        q_pre, k_pre, value_all, o_low, grad_spre, attn_low, gain_qk[None], bias_turned, lse
    )
    grad_gain_qk = gain_sums[0]
    attn_grad = jnp.stack(
        [
            dot_tn(grad_qpre, in_low),
            dot_tn(grad_kpre, low_all),
            dot_tn(grad_vpre, low_all),
            out_proj_grad,
        ]
    ).astype(BF16)
    back_all = dot(grad_kpre, key_low) + dot(grad_vpre, value_low)
    grad_in = grad_in + dot(grad_qpre, query_low) + back_all[reach * rows :]
    for offset in range(1, reach + 1):
        first = (reach - offset) * rows
        part = back_all[first : first + rows].astype(BF16)
        grad_in = grad_in + from_behind(part, "shard", -offset).astype(F32)
    grad_tokens = norm_back(normed_in, factor_in, grad_in)

    grad_gf = jnp.stack([grad_scale_up, grad_scale_gate])
    attn_grad = attn_grad.reshape(4, shards, attn_rows, D).transpose(1, 0, 2, 3)
    gd_rows = D // shards
    if fast:
        grad_gd = jnp.stack([grad_gain_qk, grad_alpha_attn, grad_alpha_ffn])
        small = jnp.concatenate(
            [
                grad_gd.reshape(3, shards, gd_rows).transpose(1, 0, 2).reshape(shards, -1),
                grad_gf.reshape(2, shards, ffn_rows).transpose(1, 0, 2).reshape(shards, -1),
            ],
            1,
        ).astype(BF16)
        extra = jnp.pad(small, ((0, 0), (0, 8 * 16 * D - small.shape[1])))
        attn_pieces = jnp.concatenate(
            [attn_grad.reshape(shards, 8, piece, D), extra.reshape(shards, 8, 16, D)], 2
        )
        ffn_sums = reduce_all(
            [part.reshape(shards, 4, 2, piece, D) for part in (up_grad, gate_grad, down_grad)], 1
        )
        sum_ffn = ffn_sums.reshape(3, ffn_rows, D).astype(F32)
        attn_sums = reduce_all([attn_pieces.reshape(shards, 4, 2, piece + 16, D)], 2)[0]
        sum_attn = attn_sums[:, :piece].reshape(4, attn_rows, D).astype(F32)
        sum_small = attn_sums[0, piece:].reshape(-1).astype(F32)
        sum_gd = sum_small[: 3 * gd_rows].reshape(3, gd_rows)
        sum_gf = sum_small[3 * gd_rows : 3 * gd_rows + 2 * ffn_rows].reshape(2, ffn_rows)
    else:
        attn_grad = attn_grad.reshape(shards, reps, 4 * attn_rows // reps, D).transpose(1, 0, 2, 3)
        sum_attn = reduce_rows(attn_grad).astype(F32).reshape(4, attn_rows, D)
        ready = (shards, reps, piece, D)
        sum_ffn = jnp.stack(
            [
                reduce_rows(part.reshape(ready).transpose(1, 0, 2, 3))
                for part in (up_grad, gate_grad, down_grad)
            ]
        ).astype(F32).reshape(3, ffn_rows, D)
        grad_small = jnp.concatenate(
            [grad_gain_qk, grad_alpha_attn, grad_alpha_ffn, grad_gf.reshape(-1)]
        )
        grad_small = lax.psum(grad_small, ("rep", "shard"))
        sum_gd = lax.dynamic_slice_in_dim(
            grad_small[: 3 * D].reshape(3, D), device_index * gd_rows, gd_rows, 1
        )
        sum_gf = lax.dynamic_slice_in_dim(
            grad_small[3 * D :].reshape(2, ffn_all), device_index * ffn_rows, ffn_rows, 1
        )
    attn_new, attn_m_new, attn_v_new = adam(attn_w, sum_attn, attn_m, attn_v, RATE, DECAY)
    ffn_new, ffn_m_new, ffn_v_new = adam(ffn_w, sum_ffn, ffn_m, ffn_v, RATE, DECAY)
    gd_new, gd_m_new, gd_v_new = adam(gains_d, sum_gd, gd_m, gd_v, GAIN_RATE, 0.0)
    gf_new, gf_m_new, gf_v_new = adam(gains_ff, sum_gf, gf_m, gf_v, GAIN_RATE, 0.0)
    attn_unit, attn_scale = rownorm(attn_new)
    ffn_unit, ffn_scale = rownorm(ffn_new)
    return (
        output,
        grad_tokens,
        attn_unit,
        attn_m_new,
        attn_v_new,
        ffn_unit,
        ffn_m_new,
        ffn_v_new,
        gd_new,
        gd_m_new,
        gd_v_new,
        gf_new,
        gf_m_new,
        gf_v_new,
    )

def solution(mesh):
    return jax.shard_map(
        body,
        mesh=mesh,
        in_specs=(
            P(("rep", "shard"), None),
            P("rep", None),
            P(("rep", "shard"), None),
            P(None, "shard", None),
            P(None, "shard", None),
            P(None, "shard", None),
            P(None, "shard", None),
            P(None, "shard", None),
            P(None, "shard", None),
            P(None, "shard"),
            P(None, "shard"),
            P(None, "shard"),
            P(None, "shard"),
            P(None, "shard"),
            P(None, "shard"),
        ),
        out_specs=(
            P(("rep", "shard"), None),
            P(("rep", "shard"), None),
            P(None, "shard", None),
            P(None, "shard", None),
            P(None, "shard", None),
            P(None, "shard", None),
            P(None, "shard", None),
            P(None, "shard", None),
            P(None, "shard"),
            P(None, "shard"),
            P(None, "shard"),
            P(None, "shard"),
            P(None, "shard"),
            P(None, "shard"),
        ),
        check_vma=False,
    )
```

```python
import functools
import math

import jax
import jax.numpy as jnp
from jax import lax
from jax.experimental import pallas as pl
from jax.experimental.pallas import tpu as pltpu
from jax.sharding import PartitionSpec as P

D = 1280
HEADS = 20
HEAD_DIM = 64
WINDOW = 1024
STEP = 10


SMALL = 1e-06
NEGATIVE = -1e30
BETA_ONE = 0.9
BETA_TWO = 0.95
RATE = 0.02
GAIN_RATE = 1.0
DECAY = 0.1
TINY = 1e-08
F32 = jnp.float32
BF16 = jnp.bfloat16


def from_behind(block, axis, distance):
    devices = range(lax.axis_size(axis))
    route = [(i - distance, i) for i in devices if i - distance in devices]
    return lax.ppermute(block, axis, route)


def rownorm(value):
    factor = lax.rsqrt(jnp.sum(value * value, -1, keepdims=True) + SMALL)
    return (value * factor, factor)


def norm_back(normed, factor, grad):
    return factor * (grad - normed * jnp.sum(normed * grad, -1, keepdims=True))


def adam(weight, grad, first, second, rate, decay):
    first = BETA_ONE * first + (1.0 - BETA_ONE) * grad
    second = BETA_TWO * second + (1.0 - BETA_TWO) * grad * grad
    fix_one = 1.0 - BETA_ONE**STEP
    fix_two = 1.0 - BETA_TWO**STEP
    change = first / fix_one / (jnp.sqrt(second / fix_two) + TINY) + decay * weight
    return (weight - rate * change, first, second)


def dot(a, b):
    return jnp.dot(a, b, preferred_element_type=F32)


def dot_nt(a, b):
    return lax.dot_general(a, b, (((1,), (1,)), ((), ())), preferred_element_type=F32)


def dot_tn(a, b):
    return lax.dot_general(a, b, (((0,), (0,)), ((), ())), preferred_element_type=F32)


def gather_rows(shard_rows):
    reps = lax.axis_size("rep")
    piece = shard_rows.shape[0] // reps
    mine = lax.dynamic_slice_in_dim(shard_rows, lax.axis_index("rep") * piece, piece, 0)
    column = lax.all_gather(mine, "shard", axis=0)
    return lax.all_gather(column, "rep", axis=1)


def reduce_rows(grad):
    part = lax.psum_scatter(grad, "rep", scatter_dimension=0)
    part = lax.psum_scatter(part, "shard", scatter_dimension=0)
    return lax.all_gather(part, "rep", axis=0, tiled=True)


MESH = pl.DeviceIdType.MESH
HALF = 80


def place():
    rep = lax.axis_index("rep")
    core, chip = lax.rem(rep, 2), rep // 2
    beside, above = chip + 1 - 2 * lax.rem(chip, 2), chip + 2 - 4 * (chip // 2)
    return core, chip, beside, above, 3 - chip


def greet(shards):
    core, chip, beside, above, across = place()
    line = lax.axis_index("shard")
    barrier = pltpu.get_barrier_semaphore()
    for other in (2 * chip + 1 - core, 2 * beside + core, 2 * above + core, 2 * across + core):
        pl.semaphore_signal(barrier, inc=1, device_id=(other, line), device_id_type=MESH)

    @pl.when(line > 0)
    def _():
        pl.semaphore_signal(barrier, inc=1, device_id=(2 * chip + core, line - 1), device_id_type=MESH)

    @pl.when(line < shards - 1)
    def _():
        pl.semaphore_signal(barrier, inc=1, device_id=(2 * chip + core, line + 1), device_id_type=MESH)

    inner = (line > 0).astype(jnp.int32) + (line < shards - 1).astype(jnp.int32)
    pl.semaphore_wait(barrier, 4 + inner)


def add_into(target, sources, rows):
    def step(i, _):
        part = pl.ds(pl.multiple_of(i * 16, 16), 16)
        value = target[part, :].astype(F32)
        for source in sources:
            value = value + source[part, :].astype(F32)
        target[part, :] = value.astype(BF16)
        return 0

    lax.fori_loop(0, rows // 16, step, 0)


def reduce_kernel(count, shards, rows, *refs):
    grads, out = refs[:2]
    (acc, own, half, piece, below, own_sem, pair_send, pair_recv, half_send, half_recv,
     piece_send, piece_recv, line_send, line_recv, out_send, out_recv, out_local) = refs[2:]
    core, chip, beside, above, across = place()
    line = lax.axis_index("shard")
    steps = count * shards
    greet(shards)

    def owner(step):
        i = lax.rem(step, shards)
        back = lax.select(i < shards - 1 - line, shards - 1 - i, i - (shards - 1 - line))
        ahead = lax.select(i < line, i, shards - 1 - (i - line))
        other = lax.select(2 * line < shards, back, ahead)
        return lax.select(i == shards - 1, line, other)

    def remote(src, dst, send, recv, rep, shard):
        return pltpu.make_async_remote_copy(
            src_ref=src, dst_ref=dst, send_sem=send, recv_sem=recv,
            device_id=(rep, shard), device_id_type=MESH,
        )

    def begin(step):
        m, slot = step // shards, lax.rem(step, 2)
        remote(
            grads.at[m, owner(step), :, 1 - core], acc.at[step], pair_send, pair_recv.at[step],
            2 * chip + 1 - core, line,
        ).start()
        pltpu.make_async_copy(grads.at[m, owner(step), :, core], own.at[slot], own_sem.at[slot]).start()

    def halves(step):
        return (
            remote(acc.at[step, across, pl.ds(0, HALF)], half.at[step, pl.ds(0, HALF)],
                   half_send, half_recv.at[step, 0], 2 * beside + core, line),
            remote(acc.at[step, across, pl.ds(HALF, rows - HALF)], half.at[step, pl.ds(HALF, rows - HALF)],
                   half_send, half_recv.at[step, 1], 2 * above + core, line),
        )

    def pieces(step):
        return (
            remote(acc.at[step, beside], piece.at[step, 0], piece_send, piece_recv.at[step, 0],
                   2 * beside + core, line),
            remote(acc.at[step, above], piece.at[step, 1], piece_send, piece_recv.at[step, 1],
                   2 * above + core, line),
        )

    def upward(step, target):
        m = step // shards
        return remote(acc.at[step, chip], below.at[m, target], line_send, line_recv.at[m, target],
                      2 * chip + core, line + 1)

    def downward(step, target):
        m = step // shards
        slot = lax.select(target == line - 1, shards, target)
        return remote(acc.at[step, chip], below.at[m, slot], line_send, line_recv.at[m, slot],
                      2 * chip + core, line - 1)

    def wait_line(step, slot):
        m = step // shards
        pltpu.make_async_copy(below.at[m, slot], below.at[m, slot], line_recv.at[m, slot]).wait()
        add_into(acc.at[step, chip], (below.at[m, slot],), rows)

    def first(step):
        slot = lax.rem(step, 2)
        pltpu.make_async_copy(own.at[slot], own.at[slot], own_sem.at[slot]).wait()
        pltpu.make_async_copy(acc.at[step], acc.at[step], pair_recv.at[step]).wait()
        for q in range(4):
            add_into(acc.at[step, q], (own.at[slot, q],), rows)
        for copy in halves(step):
            copy.start()

    def second(step):
        for copy in halves(step):
            copy.wait_recv()
        add_into(acc.at[step, above, pl.ds(0, HALF)], (half.at[step, pl.ds(0, HALF)],), HALF)
        add_into(acc.at[step, beside, pl.ds(HALF, rows - HALF)],
                 (half.at[step, pl.ds(HALF, rows - HALF)],), rows - HALF)
        for copy in pieces(step):
            copy.start()

    def third(step):
        target = owner(step)
        for copy in pieces(step):
            copy.wait_recv()
        add_into(acc.at[step, chip], (piece.at[step, 0], piece.at[step, 1]), rows)

        @pl.when((target >= line) & (line > 0))
        def _():
            wait_line(step, target)

        @pl.when((target < line) & (line < shards - 1))
        def _():
            wait_line(step, target)

        @pl.when((target == line) & (line < shards - 1))
        def _():
            wait_line(step, shards)

        @pl.when(target > line)
        def _():
            upward(step, target).start()

        @pl.when(target < line)
        def _():
            downward(step, target).start()

        @pl.when(target == line)
        def _():
            m = step // shards
            mine = 2 * chip + core
            pltpu.make_async_copy(acc.at[step, chip], out.at[m, mine], out_local).start()
            for n, other in enumerate((2 * beside + core, 2 * above + core, 2 * across + core, 2 * chip + 1 - core)):
                remote(acc.at[step, chip], out.at[m, mine], out_send, out_recv.at[m, n], other, line).start()

    def fourth(step):
        m = step // shards
        for n, origin in enumerate((2 * beside + core, 2 * above + core, 2 * across + core)):
            pltpu.make_async_copy(out.at[m, origin], out.at[m, origin], out_recv.at[m, n]).wait()
            remote(out.at[m, origin], out.at[m, origin], out_send, out_recv.at[m, 4 + n],
                   2 * chip + 1 - core, line).start()

    begin(0)

    def turn(t, _):
        @pl.when(t + 1 < steps)
        def _():
            begin(t + 1)

        @pl.when(t < steps)
        def _():
            first(t)

        @pl.when((t >= 1) & (t < steps + 1))
        def _():
            second(t - 1)

        @pl.when((t >= 2) & (t < steps + 2))
        def _():
            third(t - 2)

        @pl.when((t >= 4) & (lax.rem(t - 4, shards) == shards - 1))
        def _():
            fourth(t - 4)

        return 0

    lax.fori_loop(0, steps + 4, turn, 0)
    for m in range(count):
        for n in range(4):
            pltpu.make_async_copy(out.at[m, 0], out.at[m, 0], out_recv.at[m, 3 + n]).wait()
    pltpu.make_async_copy(out.at[:, 0], out.at[:, 0], out_local).wait()
    pltpu.make_async_copy(out.at[:, pl.ds(0, 7)], out.at[:, pl.ds(0, 7)], out_send).wait()
    pltpu.make_async_copy(acc, acc, pair_send).wait()
    pltpu.make_async_copy(half, half, half_send).wait()
    pltpu.make_async_copy(piece, piece, piece_send).wait()
    pltpu.make_async_copy(
        below.at[:, pl.ds(0, shards - 1)], below.at[:, pl.ds(0, shards - 1)], line_send
    ).wait()


def reduce_all(grads, collective):
    count, shards, _, _, rows, _ = grads.shape
    steps = count * shards
    any_space = pl.BlockSpec(memory_space=pl.ANY)
    dma = pltpu.SemaphoreType.DMA
    return pl.pallas_call(
        functools.partial(reduce_kernel, count, shards, rows),
        out_shape=jax.ShapeDtypeStruct((count, 8, rows, D), BF16),
        in_specs=[any_space],
        out_specs=any_space,
        scratch_shapes=[
            pltpu.VMEM((steps, 4, rows, D), BF16),
            pltpu.VMEM((2, 4, rows, D), BF16),
            pltpu.VMEM((steps, rows, D), BF16),
            pltpu.VMEM((steps, 2, rows, D), BF16),
            pltpu.VMEM((count, shards + 1, rows, D), BF16),
            dma((2,)), dma(()), dma((steps,)), dma(()), dma((steps, 2)),
            dma(()), dma((steps, 2)), dma(()), dma((count, shards + 1)),
            dma(()), dma((count, 7)), dma(()),
        ],
        compiler_params=pltpu.CompilerParams(
            collective_id=collective, has_side_effects=True, vmem_limit_bytes=62 * 2**20
        ),
        cost_estimate=pl.CostEstimate(flops=count * 10**7, bytes_accessed=count * 10**8, transcendentals=0),
    )(grads)


def gather_kernel(shards, attn_ref, ffn_ref, gains_ref, tokens_ref, out, gains_out, before,
                  wide, low, mine, wide_sem, low_sem, mine_sem, line_send, line_recv, plane_send, beside_recv,
                  above_recv, across_recv, pair_send, pair_recv, gains_send, gains_recv, tokens_send,
                  tokens_recv, local_sem):
    core, chip, beside, above, across = place()
    line = lax.axis_index("shard")
    rep = 2 * chip + core
    sibling = 2 * chip + 1 - core
    to_beside, to_above = 2 * beside + core, 2 * above + core
    piece = attn_ref.shape[1]
    others = shards - 1
    steps = 4 * others
    barrier = pltpu.get_barrier_semaphore()
    for other in (sibling, to_beside, to_above):
        pl.semaphore_signal(barrier, inc=1, device_id=(other, line), device_id_type=MESH)
    for n in range(1, shards):
        pl.semaphore_signal(barrier, inc=1, device_id=(rep, lax.rem(line + n, shards)), device_id_type=MESH)
    pl.semaphore_wait(barrier, 3 + others)

    def remote(src, dst, send, recv, rep, shard):
        return pltpu.make_async_remote_copy(
            src_ref=src, dst_ref=dst, send_sem=send, recv_sem=recv,
            device_id=(rep, shard), device_id_type=MESH,
        )

    def arrived(ref, sem):
        pltpu.make_async_copy(ref, ref, sem).wait()

    def source(n):
        low_side = 2 * line < shards
        edge = lax.select(low_side, line, shards - 1 - line)
        near = lax.select(lax.rem(n, 2) == 0, edge - 1 - n // 2, edge + 1 + n // 2)
        found = lax.select(n < 2 * edge, near, n + 1)
        return lax.select(low_side, found, shards - 1 - found)

    def own_send(m):
        @pl.when(line < shards - 1)
        def _():
            remote(mine.at[m], out.at[m, line, rep], line_send, line_recv.at[m, line], rep, line + 1).start()

        @pl.when(line > 0)
        def _():
            remote(mine.at[m], out.at[m, line, rep], line_send, line_recv.at[m, line], rep, line - 1).start()

    def fetch(index, slot):
        @pl.when(index < 8)
        def _():
            pltpu.make_async_copy(attn_ref.at[lax.rem(index, 8)], wide.at[slot], wide_sem.at[slot]).start()

        @pl.when(index >= 8)
        def _():
            pltpu.make_async_copy(
                ffn_ref.at[jnp.maximum(index // 8 - 1, 0), lax.rem(index, 8)], wide.at[slot], wide_sem.at[slot]
            ).start()

    def store(index, slot):
        return pltpu.make_async_copy(low.at[slot], out.at[index // 8, line, lax.rem(index, 8)], low_sem.at[slot])

    def lower(src, dst):
        def step(i, _):
            part = pl.ds(pl.multiple_of(i * 32, 32), 32)
            dst[part, :] = src[part, :].astype(BF16)
            return 0

        lax.fori_loop(0, piece // 32, step, 0)

    for n in range(1, shards):
        other = lax.rem(line + n, shards)
        remote(gains_ref, gains_out.at[line], gains_send, gains_recv.at[line], rep, other).start()
    pltpu.make_async_copy(gains_ref, gains_out.at[line], local_sem).start()
    for m in range(4):
        origin = attn_ref.at[rep] if m == 0 else ffn_ref.at[m - 1, rep]
        pltpu.make_async_copy(origin, wide.at[m], mine_sem.at[m]).start()
    for m in range(4):
        arrived(wide.at[m], mine_sem.at[m])
        lower(wide.at[m], mine.at[m])
        if m == 0:
            own_send(0)

            @pl.when(line < shards - 1)
            def _():
                remote(tokens_ref, before.at[1], tokens_send, tokens_recv.at[1], rep, line + 1).start()

    for n in range(2):
        fetch(n, n)

    def begin(c):
        m, origin = c // others, source(lax.rem(c, others))
        got = out.at[m, origin, rep]
        arrived(got, line_recv.at[m, origin])

        @pl.when((origin < line) & (line < shards - 1))
        def _():
            remote(got, got, line_send, line_recv.at[m, origin], rep, line + 1).start()

        @pl.when((origin > line) & (line > 0))
        def _():
            remote(got, got, line_send, line_recv.at[m, origin], rep, line - 1).start()

        remote(got, got, plane_send, beside_recv.at[m, origin], to_beside, line).start()
        remote(got, got, plane_send, above_recv.at[m, origin], to_above, line).start()
        remote(got, got, pair_send, pair_recv.at[m], sibling, line).start()

    def middle(c):
        m, origin = c // others, source(lax.rem(c, others))
        got = out.at[m, origin, to_beside]
        arrived(got, beside_recv.at[m, origin])
        part = out.at[m, origin, to_beside, pl.ds(0, HALF)]
        remote(part, part, plane_send, across_recv.at[m, origin, 0], to_above, line).start()
        remote(got, got, pair_send, pair_recv.at[m], sibling, line).start()
        got = out.at[m, origin, to_above]
        arrived(got, above_recv.at[m, origin])
        part = out.at[m, origin, to_above, pl.ds(HALF, piece - HALF)]
        remote(part, part, plane_send, across_recv.at[m, origin, 1], to_beside, line).start()
        remote(got, got, pair_send, pair_recv.at[m], sibling, line).start()

    def last(c):
        m, origin = c // others, source(lax.rem(c, others))
        got = out.at[m, origin, 2 * across + core]
        arrived(out.at[m, origin, 2 * across + core, pl.ds(0, HALF)], across_recv.at[m, origin, 0])
        arrived(out.at[m, origin, 2 * across + core, pl.ds(HALF, piece - HALF)], across_recv.at[m, origin, 1])
        remote(got, got, pair_send, pair_recv.at[m], sibling, line).start()

    def local(t):
        for n in range(2):
            index = 2 * t + n
            slot = 2 * lax.rem(t, 2) + n
            arrived(wide.at[slot], wide_sem.at[slot])

            @pl.when(index + 2 < 32)
            def _():
                fetch(index + 2, lax.rem(slot + 2, 4))

            @pl.when(t >= 2)
            def _():
                store(index - 4, slot).wait()

            lower(wide.at[slot], low.at[slot])
            store(index, slot).start()

    def turn(t, _):
        @pl.when((lax.rem(t, others) == 0) & (t // others < 3))
        def _():
            own_send(t // others + 1)

        @pl.when(t < steps)
        def _():
            begin(t)

        @pl.when((t == 1) & (line > 0))
        def _():
            arrived(before.at[1], tokens_recv.at[1])

            @pl.when(line < shards - 1)
            def _():
                remote(before.at[1], before.at[0], tokens_send, tokens_recv.at[0], rep, line + 1).start()

        @pl.when((t >= 1) & (t < steps + 1))
        def _():
            middle(t - 1)

        @pl.when((t >= 2) & (t < steps + 2))
        def _():
            last(t - 2)

        local(t)
        return 0

    lax.fori_loop(0, 16, turn, 0)
    for n in range(4):
        store(28 + n, n).wait()
    for m in range(4):
        arrived(out.at[m, pl.ds(0, others), pl.ds(0, 4)], pair_recv.at[m])
    for n in range(1, shards):
        other = lax.rem(line + n, shards)
        arrived(gains_out.at[other], gains_recv.at[other])
    pltpu.make_async_copy(gains_ref, gains_out.at[line], local_sem).wait()

    @pl.when(line > 1)
    def _():
        arrived(before.at[0], tokens_recv.at[0])

    @pl.when((line == 1) | (line == shards - 2))
    def _():
        arrived(before, tokens_send)

    @pl.when(line == 0)
    def _():
        arrived(before.at[0], tokens_send)

    @pl.when((line == 0) | (line == shards - 1))
    def _():
        arrived(out.at[:, 0, pl.ds(0, 1)], line_send)

    @pl.when((line > 0) & (line < shards - 1))
    def _():
        arrived(out.at[:, 0, pl.ds(0, 5)], line_send)

    arrived(out.at[:, pl.ds(0, others), pl.ds(0, 3)], plane_send)
    arrived(out.at[:, pl.ds(0, others), pl.ds(0, 4)], pair_send)
    arrived(gains_out.at[pl.ds(0, others)], gains_send)


def gather_all(attn_w, ffn_w, gains, tokens, shards, collective):
    piece = attn_w.shape[1]
    any_space = pl.BlockSpec(memory_space=pl.ANY)
    dma = pltpu.SemaphoreType.DMA
    return pl.pallas_call(
        functools.partial(gather_kernel, shards),
        out_shape=(
            jax.ShapeDtypeStruct((4, shards, 8, piece, D), BF16),
            jax.ShapeDtypeStruct((shards,) + gains.shape, BF16),
            jax.ShapeDtypeStruct((2,) + tokens.shape, BF16),
        ),
        in_specs=[any_space] * 4,
        out_specs=(any_space,) * 3,
        scratch_shapes=[
            pltpu.VMEM((4, piece, D), F32),
            pltpu.VMEM((4, piece, D), BF16),
            pltpu.VMEM((4, piece, D), BF16),
            dma((4,)), dma((4,)), dma((4,)), dma(()), dma((4, shards)), dma(()), dma((4, shards)),
            dma((4, shards)), dma((4, shards, 2)), dma(()), dma((4,)), dma(()), dma((shards,)), dma(()),
            dma((2,)), dma(()),
        ],
        compiler_params=pltpu.CompilerParams(
            collective_id=collective, has_side_effects=True, vmem_limit_bytes=40 * 2**20
        ),
        cost_estimate=pl.CostEstimate(flops=10**7, bytes_accessed=2 * 10**8, transcendentals=0),
    )(attn_w, ffn_w, gains, tokens)


UNITS = 256


def feed_kernel(blocks, mid_ref, middle_ref, cot_ref, alpha_ref, up_scale_ref, gate_scale_ref, wu_ref, wg_ref, wd_ref,
                out_ref, grad_mid_ref, grad_ref, up_sum_ref, gate_sum_ref, alpha_sum_ref,
                up_buf, gate_buf, hidden_buf, total, back):
    turn = pl.program_id(0)
    up_scale, gate_scale = up_scale_ref[...], gate_scale_ref[...] * math.sqrt(D)

    @pl.when(turn < blocks)
    def _():
        up_raw = dot_nt(mid_ref[...], wu_ref[...])
        gate_raw = dot_nt(mid_ref[...], wg_ref[...])
        up_buf[turn] = up_raw
        gate_buf[turn] = gate_raw
        gate = gate_raw * gate_scale
        hidden = (gate * jax.nn.sigmoid(gate) * (up_raw * up_scale)).astype(BF16)
        hidden_buf[turn] = hidden
        part = dot(hidden, wd_ref[...])

        @pl.when(turn == 0)
        def _():
            total[...] = part

        @pl.when(turn > 0)
        def _():
            total[...] += part

    @pl.when(turn == blocks - 1)
    def _():
        alpha = alpha_ref[...]
        rows = total.shape[0]

        def step(i, sums):
            part = pl.ds(pl.multiple_of(i * 32, 32), 32)
            branch, factor = rownorm(total[part, :])
            middle = middle_ref[part, :]
            final, final_factor = rownorm(middle + alpha * (branch - middle))
            out_ref[part, :] = final.astype(BF16)
            grad = norm_back(final, final_factor, cot_ref[part, :].astype(F32))
            grad_mid_ref[part, :] = grad * (1.0 - alpha)
            back[part, :] = norm_back(branch, factor, grad * alpha).astype(BF16)
            return sums + jnp.sum(grad * (branch - middle), 0, keepdims=True)

        alpha_sum_ref[...] = lax.fori_loop(0, rows // 32, step, jnp.zeros((1, D), F32))

    @pl.when(turn >= blocks)
    def _():
        block = turn - blocks
        grads = back[...]
        grad_hidden = dot_nt(grads, wd_ref[...])
        up_raw, gate_raw = up_buf[block], gate_buf[block]
        gate = gate_raw * gate_scale
        sigma = jax.nn.sigmoid(gate)
        active = gate * sigma
        upward = up_raw * up_scale
        grad_upward = grad_hidden * active
        grad_gate = grad_hidden * upward * (sigma * (1.0 + gate * (1.0 - sigma)))
        up_sum_ref[...] = jnp.sum(grad_upward * up_raw, 0, keepdims=True)
        gate_sum_ref[...] = jnp.sum(grad_gate * gate_raw, 0, keepdims=True) * math.sqrt(D)
        grad_u = (grad_upward * up_scale).astype(BF16)
        grad_g = (grad_gate * gate_scale).astype(BF16)
        grad_ref[0] = dot_tn(grad_u, mid_ref[...]).astype(BF16)
        grad_ref[1] = dot_tn(grad_g, mid_ref[...]).astype(BF16)
        grad_ref[2] = dot_tn(hidden_buf[block], grads).astype(BF16)
        grad_mid_ref[...] += dot(grad_u, wu_ref[...]) + dot(grad_g, wg_ref[...])


def feed_forward(mid_low, middle, cotangent, alpha_ffn, scales, weights, firsts):
    rows = mid_low.shape[0]
    blocks = scales.shape[1] // UNITS
    whole = lambda *shape: pl.BlockSpec(shape, lambda t: (0,) * len(shape))
    weight = lambda m: pl.BlockSpec((None, UNITS, D), lambda t: (m, lax.rem(t, blocks), 0))
    after = lambda t: jnp.maximum(t - blocks, 0)
    units = pl.BlockSpec((1, UNITS), lambda t: (0, after(t)))
    scale = pl.BlockSpec((1, UNITS), lambda t: (0, lax.rem(t, blocks)))
    return pl.pallas_call(
        functools.partial(feed_kernel, blocks),
        grid=(2 * blocks,),
        out_shape=(
            jax.ShapeDtypeStruct((rows, D), BF16),
            jax.ShapeDtypeStruct((rows, D), F32),
            jax.ShapeDtypeStruct((3, blocks * UNITS, D), BF16),
            jax.ShapeDtypeStruct((1, blocks * UNITS), F32),
            jax.ShapeDtypeStruct((1, blocks * UNITS), F32),
            jax.ShapeDtypeStruct((1, D), F32),
        ),
        in_specs=[whole(rows, D), whole(rows, D), whole(rows, D), whole(1, D), scale, scale]
        + [weight(first) for first in firsts],
        out_specs=(
            whole(rows, D), whole(rows, D), pl.BlockSpec((3, UNITS, D), lambda t: (0, after(t), 0)),
            units, units, whole(1, D),
        ),
        scratch_shapes=[
            pltpu.VMEM((blocks, rows, UNITS), F32),
            pltpu.VMEM((blocks, rows, UNITS), F32),
            pltpu.VMEM((blocks, rows, UNITS), BF16),
            pltpu.VMEM((rows, D), F32),
            pltpu.VMEM((rows, D), BF16),
        ],
        compiler_params=pltpu.CompilerParams(vmem_limit_bytes=62 * 2**20),
        cost_estimate=pl.CostEstimate(flops=60 * 10**9, bytes_accessed=120 * 10**6, transcendentals=5 * 10**6),
    )(mid_low, middle, cotangent, alpha_ffn, scales[:1], scales[1:], *weights)


def adam_kernel(w_ref, g_ref, m_ref, v_ref, w_out, m_out, v_out):
    def step(i, _):
        part = pl.ds(pl.multiple_of(i * 16, 16), 16)
        new, first, second = adam(
            w_ref[part, :], g_ref[part, :].astype(F32), m_ref[part, :], v_ref[part, :], RATE, DECAY
        )
        w_out[part, :] = rownorm(new)[0]
        m_out[part, :] = first
        v_out[part, :] = second
        return 0

    lax.fori_loop(0, w_ref.shape[0] // 16, step, 0)


def adam_rows(weight, grad, first, second):
    pieces, piece, _ = weight.shape
    spec = pl.BlockSpec((None, piece, D), lambda p: (p, 0, 0))
    shape = jax.ShapeDtypeStruct(weight.shape, F32)
    return pl.pallas_call(
        adam_kernel,
        grid=(pieces,),
        out_shape=(shape,) * 3,
        in_specs=[spec] * 4,
        out_specs=(spec,) * 3,
        compiler_params=pltpu.CompilerParams(vmem_limit_bytes=32 * 2**20),
        cost_estimate=pl.CostEstimate(flops=20 * weight.size, bytes_accessed=26 * weight.size, transcendentals=0),
    )(weight, grad, first, second)


QUERY_BLOCK = 256
PAIR = 2 * HEAD_DIM
PAIRS = HEADS // 2


def head_ones():
    row = lax.broadcasted_iota(jnp.int32, (PAIR, PAIR), 0) // HEAD_DIM
    col = lax.broadcasted_iota(jnp.int32, (PAIR, PAIR), 1) // HEAD_DIM
    return (row == col).astype(F32).astype(BF16)


def head_sum(value, ones):
    high = value.astype(BF16)
    rest = (value - high.astype(F32)).astype(BF16)
    return dot(high, ones) + dot(rest, ones)


def of_head(value, head):
    lane = lax.broadcasted_iota(jnp.int32, value.shape, 1) // HEAD_DIM
    return jnp.where(lane == head, value, jnp.zeros_like(value))


def attend_pair(h_ref, wq_ref, wq2_ref, wk_ref, wk2_ref, wv_ref, wv2_ref, gain_ref, bias_ref, qp_ref, kp_ref, v_ref, o_ref, lse_ref,
                key_buf, query_buf, value_buf):
    cols = h_ref.shape[0]
    rows = qp_ref.shape[0]
    span = bias_ref.shape[1]
    ones = head_ones()
    gain = gain_ref[...]
    weights = jnp.concatenate([wk_ref[...], wk2_ref[...], wv_ref[...], wv2_ref[...]], 0)
    query_weights = jnp.concatenate([wq_ref[...], wq2_ref[...]], 0)

    def project(i, _):
        part = pl.ds(pl.multiple_of(i * QUERY_BLOCK, QUERY_BLOCK), QUERY_BLOCK)
        both = dot_nt(h_ref[part, :], weights)
        keys = both[:, :PAIR]
        kp_ref[part, :] = keys
        factor = lax.rsqrt(head_sum(keys * keys, ones) + SMALL)
        key_buf[part, :] = (keys * factor * gain).astype(BF16)
        values = both[:, PAIR:].astype(BF16)
        v_ref[part, :] = values
        value_buf[part, :PAIR] = values
        value_buf[part, PAIR:] = jnp.ones_like(values)
        return 0

    lax.fori_loop(0, cols // QUERY_BLOCK, project, 0)

    def project_queries(i, _):
        part = pl.ds(pl.multiple_of(i * QUERY_BLOCK, QUERY_BLOCK), QUERY_BLOCK)
        own = pl.ds(pl.multiple_of(cols - rows + i * QUERY_BLOCK, QUERY_BLOCK), QUERY_BLOCK)
        queries = dot_nt(h_ref[own, :], query_weights)
        qp_ref[part, :] = queries
        factor = lax.rsqrt(head_sum(queries * queries, ones) + SMALL)
        scaled = (queries * factor * gain).astype(BF16).astype(F32) * math.sqrt(HEAD_DIM)
        query_buf[part, :] = scaled.astype(BF16)
        return 0

    lax.fori_loop(0, rows // QUERY_BLOCK, project_queries, 0)
    for i in range(rows // QUERY_BLOCK):
        part = pl.ds(i * QUERY_BLOCK, QUERY_BLOCK)
        reach = pl.ds(i * QUERY_BLOCK, span)
        sides = []
        for head in range(2):
            scores = dot_nt(of_head(query_buf[part, :], head), key_buf[reach, :])
            probs = jnp.exp(scores + bias_ref[part, :]).astype(BF16)
            both = dot(probs, value_buf[reach, :])
            total = both[:, PAIR:]
            sides.append(both[:, :PAIR] / total)
            lse_ref[head : head + 1, part] = jnp.log(total).T[:1, :]
        lane = lax.broadcasted_iota(jnp.int32, sides[0].shape, 1)
        o_ref[part, :] = jnp.where(lane < HEAD_DIM, sides[0], sides[1]).astype(BF16)


def back_pair(qp_ref, kp_ref, v_ref, o_ref, da_ref, wo_ref, wo2_ref, gain_ref, bias_ref, lse_ref,
              dq_ref, dk_ref, dv_ref, sum_ref, key_buf, key_turned, k_total, v_total, sum_total):
    cols = kp_ref.shape[0]
    rows = qp_ref.shape[0]
    span = bias_ref.shape[1]
    ones = head_ones()
    gain = gain_ref[...]
    weights = jnp.concatenate([wo_ref[...], wo2_ref[...]], 0)

    def keys_of(i, _):
        part = pl.ds(pl.multiple_of(i * QUERY_BLOCK, QUERY_BLOCK), QUERY_BLOCK)
        keys = kp_ref[part, :]
        factor = lax.rsqrt(head_sum(keys * keys, ones) + SMALL)
        low = keys * factor * gain
        key_buf[part, :] = low.astype(BF16)
        key_turned[:, part] = low.T.astype(BF16)
        k_total[part, :] = jnp.zeros_like(keys)
        v_total[part, :] = jnp.zeros_like(keys)
        return 0

    lax.fori_loop(0, cols // QUERY_BLOCK, keys_of, 0)
    for i in range(rows // QUERY_BLOCK):
        part = pl.ds(i * QUERY_BLOCK, QUERY_BLOCK)
        reach = pl.ds(i * QUERY_BLOCK, span)
        queries = qp_ref[part, :]
        factor = lax.rsqrt(head_sum(queries * queries, ones) + SMALL)
        hat = queries * factor
        scaled = ((hat * gain).astype(BF16).astype(F32) * math.sqrt(HEAD_DIM)).astype(BF16)
        back = dot_nt(da_ref[part, :], weights).astype(BF16)
        inner = (back.astype(F32) * o_ref[part, :].astype(F32)).T
        sides = []
        for head in range(2):
            mine = slice(head * HEAD_DIM, (head + 1) * HEAD_DIM)
            query, grad = of_head(scaled, head), of_head(back, head)
            scores = dot_nt(key_buf[reach, :], query)
            probs = jnp.exp(scores + bias_ref[i] - lse_ref[head : head + 1, part])
            v_total[reach, :] += dot(probs.astype(BF16), grad)
            delta = jnp.sum(inner[mine, :], 0, keepdims=True)
            grad_scores = (probs * (dot_nt(v_ref[reach, :], grad) - delta)).astype(BF16)
            k_total[reach, :] += dot(grad_scores, query)
            sides.append(dot(key_turned[mine, reach], grad_scores))
        grad_q = jnp.concatenate(sides, 0).T * math.sqrt(HEAD_DIM)
        sums = jnp.sum(grad_q * hat, 0, keepdims=True)
        if i == 0:
            sum_total[...] = jnp.broadcast_to(sums, sum_total.shape)
        else:
            sum_total[...] += jnp.broadcast_to(sums, sum_total.shape)
        grad_q = grad_q * gain
        dq_ref[part, :] = (factor * (grad_q - hat * head_sum(hat * grad_q, ones))).astype(BF16)

    def finish(i, _):
        part = pl.ds(pl.multiple_of(i * QUERY_BLOCK, QUERY_BLOCK), QUERY_BLOCK)
        keys = kp_ref[part, :]
        factor = lax.rsqrt(head_sum(keys * keys, ones) + SMALL)
        hat = keys * factor
        grad_k = k_total[part, :]
        sum_total[...] += jnp.broadcast_to(jnp.sum(grad_k * hat, 0, keepdims=True), sum_total.shape)
        grad_k = grad_k * gain
        dk_ref[part, :] = (factor * (grad_k - hat * head_sum(hat * grad_k, ones))).astype(BF16)
        dv_ref[part, :] = v_total[part, :].astype(BF16)
        return 0

    lax.fori_loop(0, cols // QUERY_BLOCK, finish, 0)
    sum_ref[...] = sum_total[...]


def head_rows(attn_low, matrix, second):
    heads = attn_low.shape[2]

    def index(p):
        head = 2 * p + second
        return (head // heads, matrix, lax.rem(head, heads), 0, 0)

    return pl.BlockSpec((None, None, None, HEAD_DIM, D), index)


def attention_forward(low_all, attn_low, gain_qk, bias, rows):
    cols = low_all.shape[0]
    span = bias.shape[1]
    side = lambda n: pl.BlockSpec((n, PAIR), lambda p: (0, p))
    whole = lambda *shape: pl.BlockSpec(shape, lambda p: (0,) * len(shape))
    return pl.pallas_call(
        attend_pair,
        grid=(PAIRS,),
        out_shape=(
            jax.ShapeDtypeStruct((rows, D), F32),
            jax.ShapeDtypeStruct((cols, D), F32),
            jax.ShapeDtypeStruct((cols, D), BF16),
            jax.ShapeDtypeStruct((rows, D), BF16),
            jax.ShapeDtypeStruct((PAIRS, 8, rows), F32),
        ),
        in_specs=[whole(cols, D)]
        + [head_rows(attn_low, j, second) for j in range(3) for second in range(2)]
        + [side(1), whole(rows, span)],
        out_specs=(side(rows), side(cols), side(cols), side(rows),
                   pl.BlockSpec((None, 8, rows), lambda p: (p, 0, 0))),
        scratch_shapes=[
            pltpu.VMEM((cols, PAIR), BF16),
            pltpu.VMEM((rows, PAIR), BF16),
            pltpu.VMEM((cols, 2 * PAIR), BF16),
        ],
        compiler_params=pltpu.CompilerParams(vmem_limit_bytes=56 * 2**20),
        cost_estimate=pl.CostEstimate(flops=20 * 10**9, bytes_accessed=30 * 10**6, transcendentals=13 * 10**6),
    )(low_all, *[attn_low] * 6, gain_qk, bias)


def attention_backward(q_pre, k_pre, value_all, o_low, grad_spre, attn_low, gain_qk, bias_turned, lse):
    rows, cols = q_pre.shape[0], k_pre.shape[0]
    side = lambda n: pl.BlockSpec((n, PAIR), lambda p: (0, p))
    whole = lambda *shape: pl.BlockSpec(shape, lambda p: (0,) * len(shape))
    stat = pl.BlockSpec((None, 8, rows), lambda p: (p, 0, 0))
    return pl.pallas_call(
        back_pair,
        grid=(PAIRS,),
        out_shape=(
            jax.ShapeDtypeStruct((rows, D), BF16),
            jax.ShapeDtypeStruct((cols, D), BF16),
            jax.ShapeDtypeStruct((cols, D), BF16),
            jax.ShapeDtypeStruct((8, D), F32),
        ),
        in_specs=[
            side(rows), side(cols), side(cols), side(rows), whole(rows, D),
            head_rows(attn_low, 3, 0), head_rows(attn_low, 3, 1), side(1), whole(*bias_turned.shape), stat,
        ],
        out_specs=(side(rows), side(cols), side(cols), side(8)),
        scratch_shapes=[
            pltpu.VMEM((cols, PAIR), BF16),
            pltpu.VMEM((PAIR, cols), BF16),
            pltpu.VMEM((cols, PAIR), F32),
            pltpu.VMEM((cols, PAIR), F32),
            pltpu.VMEM((8, PAIR), F32),
        ],
        compiler_params=pltpu.CompilerParams(vmem_limit_bytes=56 * 2**20),
        cost_estimate=pl.CostEstimate(flops=30 * 10**9, bytes_accessed=40 * 10**6, transcendentals=13 * 10**6),
    )(q_pre, k_pre, value_all, o_low, grad_spre, attn_low, attn_low, gain_qk, bias_turned, lse)


def body(
    tokens,
    doc_lengths,
    cotangent,
    attn_w,
    ffn_w,
    attn_m,
    attn_v,
    ffn_m,
    ffn_v,
    gains_d,
    gains_ff,
    gd_m,
    gd_v,
    gf_m,
    gf_v,
):
    shards = lax.axis_size("shard")
    reps = lax.axis_size("rep")
    device_index = lax.axis_index("shard")
    rows = tokens.shape[0]
    reach = WINDOW // rows
    cols = (reach + 1) * rows
    attn_rows = attn_w.shape[1]
    ffn_rows = ffn_w.shape[1]
    ffn_all = shards * ffn_rows
    piece = ffn_rows // reps

    cut = gains_d.size
    small = jnp.concatenate([gains_d.reshape(-1), gains_ff.reshape(-1)]).astype(BF16)
    fast = reps == 8 and shards == 4 and attn_rows % HEAD_DIM == 0
    if fast:
        gathered, small, before = gather_all(
            attn_w.reshape(8, piece, D),
            ffn_w.reshape(3, 8, piece, D),
            jnp.pad(small, (0, 16 * D - small.size)).reshape(16, D),
            tokens,
            shards,
            3,
        )
        attn_low = gathered[0].reshape(shards, 4, attn_rows // HEAD_DIM, HEAD_DIM, D)
        ffn_low = [gathered.reshape(4, ffn_all, D)] * 3
        firsts = (1, 2, 3)
        small = small.reshape(shards, -1)[:, : cut + gains_ff.size]
        present = jnp.arange(reach)[:, None, None] >= reach - device_index
        earlier = [jnp.where(present, before, 0).reshape(reach * rows, D)]
    else:
        attn_low = (
            gather_rows(attn_w.reshape(4 * attn_rows, D).astype(BF16))
            .reshape(shards, 4, attn_rows, D)
            .transpose(1, 0, 2, 3)
            .reshape(1, 4, HEADS, HEAD_DIM, D)
        )
        ffn_low = [gather_rows(ffn_w[m].astype(BF16)).reshape(1, ffn_all, D) for m in range(3)]
        firsts = (0, 0, 0)
        small = lax.all_gather(small, "shard", axis=0)
        earlier = [from_behind(tokens, "shard", offset) for offset in range(reach, 0, -1)]
    small = small.astype(F32)
    query_low, key_low, value_low, out_low = (attn_low[:, j].reshape(D, D) for j in range(4))
    gd_all = small[:, :cut].reshape(shards, 3, -1).transpose(1, 0, 2).reshape(3, D)
    gf_all = small[:, cut:].reshape(shards, 2, ffn_rows).transpose(1, 0, 2).reshape(2, ffn_all)
    gain_qk = gd_all[0]
    alpha_attn = gd_all[1]
    alpha_ffn = gd_all[2]

    lengths_row = doc_lengths[0]
    starts = jnp.cumsum(lengths_row) - lengths_row
    positions = device_index * rows + jnp.arange(rows, dtype=jnp.int32)
    doc_start = jnp.max(
        jnp.where(starts[None, :] <= positions[:, None], starts[None, :], 0), axis=1
    )
    blocks = rows // QUERY_BLOCK
    span = WINDOW + QUERY_BLOCK
    query = jnp.arange(rows, dtype=jnp.int32).reshape(blocks, QUERY_BLOCK)
    lead = query[:, :1] - reach * rows + jnp.arange(span, dtype=jnp.int32)
    ahead = query[:, :, None] - lead[:, None, :]
    floor = (doc_start - device_index * rows).reshape(blocks, QUERY_BLOCK, 1)
    mask = (ahead >= 0) & (ahead < WINDOW) & (lead[:, None, :] >= floor)
    bias = jnp.where(mask, 0.0, NEGATIVE).astype(F32)
    bias_turned = bias.transpose(0, 2, 1)
    bias = bias.reshape(rows, span)
    tokens_all = jnp.concatenate(earlier + [tokens], 0)
    normed_all, factor_all = rownorm(tokens_all.astype(F32))
    low_all = normed_all.astype(BF16)
    normed_in, factor_in = normed_all[-rows:], factor_all[-rows:]
    in_low = low_all[-rows:]
    q_pre, k_pre, value_all, o_low, lse = attention_forward(
        low_all, attn_low, gain_qk[None], bias, rows
    )
    side, side_factor = rownorm(dot(o_low, out_low))
    middle, mid_factor = rownorm(normed_in + alpha_attn * (side - normed_in))
    mid_low = middle.astype(BF16)
    output, grad_mid, ffn_grads, grad_scale_up, grad_scale_gate, grad_alpha_ffn = feed_forward(
        mid_low, middle, cotangent, alpha_ffn[None], gf_all, ffn_low, firsts
    )
    grad_mixed = norm_back(middle, mid_factor, grad_mid)
    grad_in = grad_mixed * (1.0 - alpha_attn)
    grad_alpha_attn = jnp.sum(grad_mixed * (side - normed_in), 0)
    grad_spre = norm_back(side, side_factor, grad_mixed * alpha_attn).astype(BF16)
    out_proj_grad = dot_tn(o_low, grad_spre)
    grad_qpre, grad_kpre, grad_vpre, gain_sums = attention_backward(
        q_pre, k_pre, value_all, o_low, grad_spre, attn_low, gain_qk[None], bias_turned, lse
    )
    grad_gain_qk = gain_sums[0]
    attn_grad = jnp.stack(
        [
            dot_tn(grad_qpre, in_low),
            dot_tn(grad_kpre, low_all),
            dot_tn(grad_vpre, low_all),
            out_proj_grad,
        ]
    ).astype(BF16)
    back_all = dot(grad_kpre, key_low) + dot(grad_vpre, value_low)
    grad_in = grad_in + dot(grad_qpre, query_low) + back_all[reach * rows :]
    for offset in range(1, reach + 1):
        first = (reach - offset) * rows
        part = back_all[first : first + rows].astype(BF16)
        grad_in = grad_in + from_behind(part, "shard", -offset).astype(F32)
    grad_tokens = norm_back(normed_in, factor_in, grad_in)

    grad_gf = jnp.concatenate([grad_scale_up, grad_scale_gate])
    attn_grad = attn_grad.reshape(4, shards, attn_rows, D).transpose(1, 0, 2, 3)
    gd_rows = D // shards
    if fast:
        grad_gd = jnp.stack([grad_gain_qk, grad_alpha_attn, grad_alpha_ffn[0]])
        small = jnp.concatenate(
            [
                grad_gd.reshape(3, shards, gd_rows).transpose(1, 0, 2).reshape(shards, -1),
                grad_gf.reshape(2, shards, ffn_rows).transpose(1, 0, 2).reshape(shards, -1),
            ],
            1,
        ).astype(BF16)
        extra = jnp.pad(small, ((0, 0), (0, 8 * 16 * D - small.shape[1])))
        attn_pieces = jnp.concatenate(
            [attn_grad.reshape(shards, 8, piece, D), extra.reshape(shards, 8, 16, D)], 2
        )
        sum_ffn = reduce_all(ffn_grads.reshape(3, shards, 4, 2, piece, D), 1).reshape(24, piece, D)
        attn_sums = reduce_all(attn_pieces.reshape(1, shards, 4, 2, piece + 16, D), 2)[0]
        sum_attn = attn_sums
        sum_small = attn_sums[0, piece:].reshape(-1).astype(F32)
        sum_gd = sum_small[: 3 * gd_rows].reshape(3, gd_rows)
        sum_gf = sum_small[3 * gd_rows : 3 * gd_rows + 2 * ffn_rows].reshape(2, ffn_rows)
    else:
        attn_grad = attn_grad.reshape(shards, reps, 4 * attn_rows // reps, D).transpose(1, 0, 2, 3)
        sum_attn = reduce_rows(attn_grad).reshape(4, attn_rows, D)
        ready = (shards, reps, piece, D)
        sum_ffn = jnp.concatenate(
            [reduce_rows(part.reshape(ready).transpose(1, 0, 2, 3)) for part in ffn_grads]
        ).reshape(3, ffn_rows, D)
        grad_small = jnp.concatenate(
            [grad_gain_qk, grad_alpha_attn, grad_alpha_ffn[0], grad_gf.reshape(-1)]
        )
        grad_small = lax.psum(grad_small, ("rep", "shard"))
        sum_gd = lax.dynamic_slice_in_dim(
            grad_small[: 3 * D].reshape(3, D), device_index * gd_rows, gd_rows, 1
        )
        sum_gf = lax.dynamic_slice_in_dim(
            grad_small[3 * D :].reshape(2, ffn_all), device_index * ffn_rows, ffn_rows, 1
        )
    attn_unit, attn_m_new, attn_v_new = (
        new.reshape(attn_w.shape)
        for new in adam_rows(
            *(attn_w.reshape(sum_attn.shape[0], -1, D), sum_attn),
            *(old.reshape(sum_attn.shape[0], -1, D) for old in (attn_m, attn_v)),
        )
    )
    ffn_unit, ffn_m_new, ffn_v_new = (
        new.reshape(ffn_w.shape)
        for new in adam_rows(
            *(ffn_w.reshape(sum_ffn.shape[0], -1, D), sum_ffn),
            *(old.reshape(sum_ffn.shape[0], -1, D) for old in (ffn_m, ffn_v)),
        )
    )
    gd_new, gd_m_new, gd_v_new = adam(gains_d, sum_gd, gd_m, gd_v, GAIN_RATE, 0.0)
    gf_new, gf_m_new, gf_v_new = adam(gains_ff, sum_gf, gf_m, gf_v, GAIN_RATE, 0.0)
    return (
        output,
        grad_tokens,
        attn_unit,
        attn_m_new,
        attn_v_new,
        ffn_unit,
        ffn_m_new,
        ffn_v_new,
        gd_new,
        gd_m_new,
        gd_v_new,
        gf_new,
        gf_m_new,
        gf_v_new,
    )

def solution(mesh):
    return jax.shard_map(
        body,
        mesh=mesh,
        in_specs=(
            P(("rep", "shard"), None),
            P("rep", None),
            P(("rep", "shard"), None),
            P(None, "shard", None),
            P(None, "shard", None),
            P(None, "shard", None),
            P(None, "shard", None),
            P(None, "shard", None),
            P(None, "shard", None),
            P(None, "shard"),
            P(None, "shard"),
            P(None, "shard"),
            P(None, "shard"),
            P(None, "shard"),
            P(None, "shard"),
        ),
        out_specs=(
            P(("rep", "shard"), None),
            P(("rep", "shard"), None),
            P(None, "shard", None),
            P(None, "shard", None),
            P(None, "shard", None),
            P(None, "shard", None),
            P(None, "shard", None),
            P(None, "shard", None),
            P(None, "shard"),
            P(None, "shard"),
            P(None, "shard"),
            P(None, "shard"),
            P(None, "shard"),
            P(None, "shard"),
        ),
        check_vma=False,
    )
```

```python
import functools
import math

import jax
import jax.numpy as jnp
from jax import lax
from jax.experimental import pallas as pl
from jax.experimental.pallas import tpu as pltpu
from jax.sharding import PartitionSpec as P

D = 1280
HEADS = 20
HEAD_DIM = 64
WINDOW = 1024
STEP = 10


SMALL = 1e-06
NEGATIVE = -1e30
BETA_ONE = 0.9
BETA_TWO = 0.95
RATE = 0.02
GAIN_RATE = 1.0
DECAY = 0.1
TINY = 1e-08
F32 = jnp.float32
BF16 = jnp.bfloat16


def from_behind(block, axis, distance):
    devices = range(lax.axis_size(axis))
    route = [(i - distance, i) for i in devices if i - distance in devices]
    return lax.ppermute(block, axis, route)


def rownorm(value):
    factor = lax.rsqrt(jnp.sum(value * value, -1, keepdims=True) + SMALL)
    return (value * factor, factor)


def norm_back(normed, factor, grad):
    return factor * (grad - normed * jnp.sum(normed * grad, -1, keepdims=True))


def adam(weight, grad, first, second, rate, decay):
    first = BETA_ONE * first + (1.0 - BETA_ONE) * grad
    second = BETA_TWO * second + (1.0 - BETA_TWO) * grad * grad
    fix_one = 1.0 - BETA_ONE**STEP
    fix_two = 1.0 - BETA_TWO**STEP
    change = first / fix_one / (jnp.sqrt(second / fix_two) + TINY) + decay * weight
    return (weight - rate * change, first, second)


def dot(a, b):
    return jnp.dot(a, b, preferred_element_type=F32)


def dot_nt(a, b):
    return lax.dot_general(a, b, (((1,), (1,)), ((), ())), preferred_element_type=F32)


def dot_tn(a, b):
    return lax.dot_general(a, b, (((0,), (0,)), ((), ())), preferred_element_type=F32)


def gather_rows(shard_rows):
    reps = lax.axis_size("rep")
    piece = shard_rows.shape[0] // reps
    mine = lax.dynamic_slice_in_dim(shard_rows, lax.axis_index("rep") * piece, piece, 0)
    column = lax.all_gather(mine, "shard", axis=0)
    return lax.all_gather(column, "rep", axis=1)


def reduce_rows(grad):
    part = lax.psum_scatter(grad, "rep", scatter_dimension=0)
    part = lax.psum_scatter(part, "shard", scatter_dimension=0)
    return lax.all_gather(part, "rep", axis=0, tiled=True)


MESH = pl.DeviceIdType.MESH
HALF = 80


def place():
    rep = lax.axis_index("rep")
    core, chip = lax.rem(rep, 2), rep // 2
    beside, above = chip + 1 - 2 * lax.rem(chip, 2), chip + 2 - 4 * (chip // 2)
    return core, chip, beside, above, 3 - chip


def remote(src, dst, send, recv, rep, shard):
    return pltpu.make_async_remote_copy(
        src_ref=src, dst_ref=dst, send_sem=send, recv_sem=recv,
        device_id=(rep, shard), device_id_type=MESH,
    )


def arrived(ref, sem):
    pltpu.make_async_copy(ref, ref, sem).wait()


def greet(shards):
    rep, line = lax.axis_index("rep"), lax.axis_index("shard")
    barrier = pltpu.get_barrier_semaphore()
    for n in range(1, 8):
        pl.semaphore_signal(barrier, inc=1, device_id=(lax.rem(rep + n, 8), line), device_id_type=MESH)
    for n in range(1, shards):
        pl.semaphore_signal(barrier, inc=1, device_id=(rep, lax.rem(line + n, shards)), device_id_type=MESH)
    pl.semaphore_wait(barrier, 6 + shards)


def add_into(target, sources, rows):
    def step(i, _):
        part = pl.ds(pl.multiple_of(i * 16, 16), 16)
        value = target[part, :].astype(F32)
        for source in sources:
            value = value + source[part, :].astype(F32)
        target[part, :] = value.astype(BF16)
        return 0

    lax.fori_loop(0, rows // 16, step, 0)


def reduction_scratch(count, shards, rows):
    steps = count * shards
    dma = pltpu.SemaphoreType.DMA
    return [
        pltpu.VMEM((steps, 4, rows, D), BF16),
        pltpu.VMEM((2, 4, rows, D), BF16),
        pltpu.VMEM((steps, rows, D), BF16),
        pltpu.VMEM((steps, 2, rows, D), BF16),
        pltpu.VMEM((count, shards + 1, rows, D), BF16),
        dma((2,)), dma(()), dma((steps,)), dma(()), dma((steps, 2)),
        dma(()), dma((steps, 2)), dma(()), dma((count, shards + 1)),
        dma(()), dma((count, 7)), dma(()),
    ]


REDUCTION_SCRATCH = 17


def reduction(grads, out, scratch):
    (acc, own, half, piece, below, own_sem, pair_send, pair_recv, half_send, half_recv,
     piece_send, piece_recv, line_send, line_recv, out_send, out_recv, out_local) = scratch
    count = len(grads)
    rows = own.shape[2]
    shards = below.shape[1] - 1
    core, chip, beside, above, across = place()
    line = lax.axis_index("shard")
    steps = count * shards

    def owner(step):
        i = lax.rem(step, shards)
        back = lax.select(i < shards - 1 - line, shards - 1 - i, i - (shards - 1 - line))
        ahead = lax.select(i < line, i, shards - 1 - (i - line))
        other = lax.select(2 * line < shards, back, ahead)
        return lax.select(i == shards - 1, line, other)

    def begin(step):
        slot = lax.rem(step, 2)
        for m in range(count):
            @pl.when(step // shards == m)
            def _(m=m):
                remote(
                    grads[m].at[owner(step), :, 1 - core], acc.at[step], pair_send, pair_recv.at[step],
                    2 * chip + 1 - core, line,
                ).start()
                pltpu.make_async_copy(grads[m].at[owner(step), :, core], own.at[slot], own_sem.at[slot]).start()

    def first(step):
        slot = lax.rem(step, 2)
        arrived(own.at[slot], own_sem.at[slot])
        arrived(acc.at[step], pair_recv.at[step])
        for q in range(4):
            add_into(acc.at[step, q], (own.at[slot, q],), rows)
        remote(acc.at[step, across, pl.ds(0, HALF)], half.at[step, pl.ds(0, HALF)],
               half_send, half_recv.at[step, 0], 2 * beside + core, line).start()
        remote(acc.at[step, across, pl.ds(HALF, rows - HALF)], half.at[step, pl.ds(HALF, rows - HALF)],
               half_send, half_recv.at[step, 1], 2 * above + core, line).start()

    def second(step):
        arrived(half.at[step, pl.ds(0, HALF)], half_recv.at[step, 0])
        arrived(half.at[step, pl.ds(HALF, rows - HALF)], half_recv.at[step, 1])
        add_into(acc.at[step, above, pl.ds(0, HALF)], (half.at[step, pl.ds(0, HALF)],), HALF)
        add_into(acc.at[step, beside, pl.ds(HALF, rows - HALF)],
                 (half.at[step, pl.ds(HALF, rows - HALF)],), rows - HALF)
        remote(acc.at[step, beside], piece.at[step, 0], piece_send, piece_recv.at[step, 0],
               2 * beside + core, line).start()
        remote(acc.at[step, above], piece.at[step, 1], piece_send, piece_recv.at[step, 1],
               2 * above + core, line).start()

    def wait_line(step, slot):
        m = step // shards
        arrived(below.at[m, slot], line_recv.at[m, slot])
        add_into(acc.at[step, chip], (below.at[m, slot],), rows)

    def third(step):
        m, target = step // shards, owner(step)
        for n in range(2):
            arrived(piece.at[step, n], piece_recv.at[step, n])
        add_into(acc.at[step, chip], (piece.at[step, 0], piece.at[step, 1]), rows)

        @pl.when((target >= line) & (line > 0))
        def _():
            wait_line(step, target)

        @pl.when((target < line) & (line < shards - 1))
        def _():
            wait_line(step, target)

        @pl.when((target == line) & (line < shards - 1))
        def _():
            wait_line(step, shards)

        @pl.when(target > line)
        def _():
            remote(acc.at[step, chip], below.at[m, target], line_send, line_recv.at[m, target],
                   2 * chip + core, line + 1).start()

        @pl.when(target < line)
        def _():
            slot = lax.select(target == line - 1, shards, target)
            remote(acc.at[step, chip], below.at[m, slot], line_send, line_recv.at[m, slot],
                   2 * chip + core, line - 1).start()

        @pl.when(target == line)
        def _():
            mine = 2 * chip + core
            pltpu.make_async_copy(acc.at[step, chip], out.at[m, mine], out_local).start()
            for n, other in enumerate((2 * beside + core, 2 * above + core, 2 * across + core, 2 * chip + 1 - core)):
                remote(acc.at[step, chip], out.at[m, mine], out_send, out_recv.at[m, n], other, line).start()

    def fourth(step):
        m = step // shards
        for n, origin in enumerate((2 * beside + core, 2 * above + core, 2 * across + core)):
            arrived(out.at[m, origin], out_recv.at[m, n])
            remote(out.at[m, origin], out.at[m, origin], out_send, out_recv.at[m, 4 + n],
                   2 * chip + 1 - core, line).start()

    def turn(t):
        @pl.when(t == 0)
        def _():
            begin(0)

        @pl.when(t + 1 < steps)
        def _():
            begin(t + 1)

        @pl.when(t < steps)
        def _():
            first(t)

        @pl.when((t >= 1) & (t < steps + 1))
        def _():
            second(t - 1)

        @pl.when((t >= 2) & (t < steps + 2))
        def _():
            third(t - 2)

        @pl.when((t >= 4) & (t < steps + 4) & (lax.rem(t, shards) == shards - 1))
        def _():
            fourth(t - 4)

    def finish():
        for m in range(count):
            for n in range(4):
                arrived(out.at[m, 0], out_recv.at[m, 3 + n])
        arrived(out.at[:, 0], out_local)
        arrived(out.at[:, pl.ds(0, 7)], out_send)
        arrived(acc, pair_send)
        arrived(half, half_send)
        arrived(piece, piece_send)
        arrived(below.at[:, pl.ds(0, shards - 1)], line_send)

    return steps + 4, turn, finish


def last_kernel(shards, down_ref, attn_ref, gains_ref, out, gains_out, line_got, plane_got, mine,
                line_send, line_recv, plane_send, plane_recv, *scratch):
    rep, line = lax.axis_index("rep"), lax.axis_index("shard")
    turns, turn, finish = reduction((down_ref, attn_ref), out, scratch)
    greet(shards)
    for n in range(1, shards):
        other = lax.rem(line + n, shards)
        remote(gains_ref.at[other], line_got.at[n - 1], line_send, line_recv.at[n - 1], rep, other).start()

    def step(t, _):
        turn(t)

        @pl.when(t == 1)
        def _():
            total = gains_ref[line]
            for n in range(shards - 1):
                arrived(line_got.at[n], line_recv.at[n])
                total = total + line_got[n]
            mine[...] = total
            for n in range(1, 8):
                remote(mine, plane_got.at[n - 1], plane_send, plane_recv.at[n - 1], lax.rem(rep + n, 8), line).start()

        @pl.when(t == 3)
        def _():
            total = mine[...]
            for n in range(7):
                arrived(plane_got.at[n], plane_recv.at[n])
                total = total + plane_got[n]
            gains_out[...] = total

        return 0

    lax.fori_loop(0, turns, step, 0)
    finish()
    arrived(line_got, line_send)
    arrived(plane_got, plane_send)


def reduce_last(down, attn, gains):
    shards, _, _, rows, _ = down.shape
    any_space = pl.BlockSpec(memory_space=pl.ANY)
    vmem = pl.BlockSpec(memory_space=pltpu.VMEM)
    dma = pltpu.SemaphoreType.DMA
    return pl.pallas_call(
        functools.partial(last_kernel, shards),
        out_shape=(
            jax.ShapeDtypeStruct((2, 8, rows, D), BF16),
            jax.ShapeDtypeStruct(gains.shape[1:], F32),
        ),
        in_specs=[any_space, any_space, vmem],
        out_specs=(any_space, vmem),
        scratch_shapes=[
            pltpu.VMEM((shards - 1,) + gains.shape[1:], F32),
            pltpu.VMEM((7,) + gains.shape[1:], F32),
            pltpu.VMEM(gains.shape[1:], F32),
            dma(()), dma((shards - 1,)), dma(()), dma((7,)),
        ] + reduction_scratch(2, shards, rows),
        compiler_params=pltpu.CompilerParams(
            collective_id=2, has_side_effects=True, vmem_limit_bytes=60 * 2**20
        ),
        cost_estimate=pl.CostEstimate(flops=2 * 10**7, bytes_accessed=2 * 10**8, transcendentals=0),
    )(down, attn, gains)


def gather_kernel(shards, attn_ref, ffn_ref, gains_ref, tokens_ref, out, gains_out, before,
                  wide, low, mine, wide_sem, low_sem, mine_sem, line_send, line_recv, plane_send, beside_recv,
                  above_recv, across_recv, pair_send, pair_recv, gains_send, gains_recv, tokens_send,
                  tokens_recv, local_sem):
    core, chip, beside, above, across = place()
    line = lax.axis_index("shard")
    rep = 2 * chip + core
    sibling = 2 * chip + 1 - core
    to_beside, to_above = 2 * beside + core, 2 * above + core
    piece = attn_ref.shape[1]
    others = shards - 1
    steps = 4 * others
    barrier = pltpu.get_barrier_semaphore()
    for other in (sibling, to_beside, to_above):
        pl.semaphore_signal(barrier, inc=1, device_id=(other, line), device_id_type=MESH)
    for n in range(1, shards):
        pl.semaphore_signal(barrier, inc=1, device_id=(rep, lax.rem(line + n, shards)), device_id_type=MESH)
    pl.semaphore_wait(barrier, 3 + others)

    def source(n):
        low_side = 2 * line < shards
        edge = lax.select(low_side, line, shards - 1 - line)
        near = lax.select(lax.rem(n, 2) == 0, edge - 1 - n // 2, edge + 1 + n // 2)
        found = lax.select(n < 2 * edge, near, n + 1)
        return lax.select(low_side, found, shards - 1 - found)

    def own_send(m):
        @pl.when(line < shards - 1)
        def _():
            remote(mine.at[m], out.at[m, line, rep], line_send, line_recv.at[m, line], rep, line + 1).start()

        @pl.when(line > 0)
        def _():
            remote(mine.at[m], out.at[m, line, rep], line_send, line_recv.at[m, line], rep, line - 1).start()

    def fetch(index, slot):
        @pl.when(index < 8)
        def _():
            pltpu.make_async_copy(attn_ref.at[lax.rem(index, 8)], wide.at[slot], wide_sem.at[slot]).start()

        @pl.when(index >= 8)
        def _():
            pltpu.make_async_copy(
                ffn_ref.at[jnp.maximum(index // 8 - 1, 0), lax.rem(index, 8)], wide.at[slot], wide_sem.at[slot]
            ).start()

    def store(index, slot):
        return pltpu.make_async_copy(low.at[slot], out.at[index // 8, line, lax.rem(index, 8)], low_sem.at[slot])

    def lower(src, dst):
        def step(i, _):
            part = pl.ds(pl.multiple_of(i * 32, 32), 32)
            dst[part, :] = src[part, :].astype(BF16)
            return 0

        lax.fori_loop(0, piece // 32, step, 0)

    for n in range(1, shards):
        other = lax.rem(line + n, shards)
        remote(gains_ref, gains_out.at[line], gains_send, gains_recv.at[line], rep, other).start()
    pltpu.make_async_copy(gains_ref, gains_out.at[line], local_sem).start()
    for m in range(4):
        origin = attn_ref.at[rep] if m == 0 else ffn_ref.at[m - 1, rep]
        pltpu.make_async_copy(origin, wide.at[m], mine_sem.at[m]).start()
    for m in range(4):
        arrived(wide.at[m], mine_sem.at[m])
        lower(wide.at[m], mine.at[m])
        if m == 0:
            own_send(0)

            @pl.when(line < shards - 1)
            def _():
                remote(tokens_ref, before.at[1], tokens_send, tokens_recv.at[1], rep, line + 1).start()

    for n in range(2):
        fetch(n, n)

    def begin(c):
        m, origin = c // others, source(lax.rem(c, others))
        got = out.at[m, origin, rep]
        arrived(got, line_recv.at[m, origin])

        @pl.when((origin < line) & (line < shards - 1))
        def _():
            remote(got, got, line_send, line_recv.at[m, origin], rep, line + 1).start()

        @pl.when((origin > line) & (line > 0))
        def _():
            remote(got, got, line_send, line_recv.at[m, origin], rep, line - 1).start()

        remote(got, got, plane_send, beside_recv.at[m, origin], to_beside, line).start()
        remote(got, got, plane_send, above_recv.at[m, origin], to_above, line).start()
        remote(got, got, pair_send, pair_recv.at[m], sibling, line).start()

    def middle(c):
        m, origin = c // others, source(lax.rem(c, others))
        got = out.at[m, origin, to_beside]
        arrived(got, beside_recv.at[m, origin])
        part = out.at[m, origin, to_beside, pl.ds(0, HALF)]
        remote(part, part, plane_send, across_recv.at[m, origin, 0], to_above, line).start()
        remote(got, got, pair_send, pair_recv.at[m], sibling, line).start()
        got = out.at[m, origin, to_above]
        arrived(got, above_recv.at[m, origin])
        part = out.at[m, origin, to_above, pl.ds(HALF, piece - HALF)]
        remote(part, part, plane_send, across_recv.at[m, origin, 1], to_beside, line).start()
        remote(got, got, pair_send, pair_recv.at[m], sibling, line).start()

    def last(c):
        m, origin = c // others, source(lax.rem(c, others))
        got = out.at[m, origin, 2 * across + core]
        arrived(out.at[m, origin, 2 * across + core, pl.ds(0, HALF)], across_recv.at[m, origin, 0])
        arrived(out.at[m, origin, 2 * across + core, pl.ds(HALF, piece - HALF)], across_recv.at[m, origin, 1])
        remote(got, got, pair_send, pair_recv.at[m], sibling, line).start()

    def local(t):
        for n in range(2):
            index = 2 * t + n
            slot = 2 * lax.rem(t, 2) + n
            arrived(wide.at[slot], wide_sem.at[slot])

            @pl.when(index + 2 < 32)
            def _():
                fetch(index + 2, lax.rem(slot + 2, 4))

            @pl.when(t >= 2)
            def _():
                store(index - 4, slot).wait()

            lower(wide.at[slot], low.at[slot])
            store(index, slot).start()

    def turn(t, _):
        @pl.when((lax.rem(t, others) == 0) & (t // others < 3))
        def _():
            own_send(t // others + 1)

        @pl.when(t < steps)
        def _():
            begin(t)

        @pl.when((t == 1) & (line > 0))
        def _():
            arrived(before.at[1], tokens_recv.at[1])

            @pl.when(line < shards - 1)
            def _():
                remote(before.at[1], before.at[0], tokens_send, tokens_recv.at[0], rep, line + 1).start()

        @pl.when((t >= 1) & (t < steps + 1))
        def _():
            middle(t - 1)

        @pl.when((t >= 2) & (t < steps + 2))
        def _():
            last(t - 2)

        local(t)
        return 0

    lax.fori_loop(0, 16, turn, 0)
    for n in range(4):
        store(28 + n, n).wait()
    for m in range(4):
        arrived(out.at[m, pl.ds(0, others), pl.ds(0, 4)], pair_recv.at[m])
    for n in range(1, shards):
        other = lax.rem(line + n, shards)
        arrived(gains_out.at[other], gains_recv.at[other])
    pltpu.make_async_copy(gains_ref, gains_out.at[line], local_sem).wait()

    @pl.when(line > 1)
    def _():
        arrived(before.at[0], tokens_recv.at[0])

    @pl.when((line == 1) | (line == shards - 2))
    def _():
        arrived(before, tokens_send)

    @pl.when(line == 0)
    def _():
        arrived(before.at[0], tokens_send)

    @pl.when((line == 0) | (line == shards - 1))
    def _():
        arrived(out.at[:, 0, pl.ds(0, 1)], line_send)

    @pl.when((line > 0) & (line < shards - 1))
    def _():
        arrived(out.at[:, 0, pl.ds(0, 5)], line_send)

    arrived(out.at[:, pl.ds(0, others), pl.ds(0, 3)], plane_send)
    arrived(out.at[:, pl.ds(0, others), pl.ds(0, 4)], pair_send)
    arrived(gains_out.at[pl.ds(0, others)], gains_send)


def gather_all(attn_w, ffn_w, gains, tokens, shards, collective):
    piece = attn_w.shape[1]
    any_space = pl.BlockSpec(memory_space=pl.ANY)
    dma = pltpu.SemaphoreType.DMA
    return pl.pallas_call(
        functools.partial(gather_kernel, shards),
        out_shape=(
            jax.ShapeDtypeStruct((4, shards, 8, piece, D), BF16),
            jax.ShapeDtypeStruct((shards,) + gains.shape, BF16),
            jax.ShapeDtypeStruct((2,) + tokens.shape, BF16),
        ),
        in_specs=[any_space] * 4,
        out_specs=(any_space,) * 3,
        scratch_shapes=[
            pltpu.VMEM((4, piece, D), F32),
            pltpu.VMEM((4, piece, D), BF16),
            pltpu.VMEM((4, piece, D), BF16),
            dma((4,)), dma((4,)), dma((4,)), dma(()), dma((4, shards)), dma(()), dma((4, shards)),
            dma((4, shards)), dma((4, shards, 2)), dma(()), dma((4,)), dma(()), dma((shards,)), dma(()),
            dma((2,)), dma(()),
        ],
        compiler_params=pltpu.CompilerParams(
            collective_id=collective, has_side_effects=True, vmem_limit_bytes=40 * 2**20
        ),
        cost_estimate=pl.CostEstimate(flops=10**7, bytes_accessed=2 * 10**8, transcendentals=0),
    )(attn_w, ffn_w, gains, tokens)


UNITS = 256


def feed_kernel(blocks, mid_ref, middle_ref, cot_ref, alpha_ref, up_scale_ref, gate_scale_ref, wu_ref, wg_ref, wd_ref,
                out_ref, grad_mid_ref, grad_ref, down_ref, up_sum_ref, gate_sum_ref, alpha_sum_ref,
                up_buf, gate_buf, hidden_buf, total, back):
    turn = pl.program_id(0)
    up_scale, gate_scale = up_scale_ref[...], gate_scale_ref[...] * math.sqrt(D)

    @pl.when(turn < blocks)
    def _():
        up_raw = dot_nt(mid_ref[...], wu_ref[...])
        gate_raw = dot_nt(mid_ref[...], wg_ref[...])
        up_buf[turn] = up_raw
        gate_buf[turn] = gate_raw
        gate = gate_raw * gate_scale
        hidden = (gate * jax.nn.sigmoid(gate) * (up_raw * up_scale)).astype(BF16)
        hidden_buf[turn] = hidden
        part = dot(hidden, wd_ref[...])

        @pl.when(turn == 0)
        def _():
            total[...] = part

        @pl.when(turn > 0)
        def _():
            total[...] += part

    @pl.when(turn == blocks - 1)
    def _():
        alpha = alpha_ref[...]
        rows = total.shape[0]

        def step(i, sums):
            part = pl.ds(pl.multiple_of(i * 32, 32), 32)
            branch, factor = rownorm(total[part, :])
            middle = middle_ref[part, :]
            final, final_factor = rownorm(middle + alpha * (branch - middle))
            out_ref[part, :] = final.astype(BF16)
            grad = norm_back(final, final_factor, cot_ref[part, :].astype(F32))
            grad_mid_ref[part, :] = grad * (1.0 - alpha)
            back[part, :] = norm_back(branch, factor, grad * alpha).astype(BF16)
            return sums + jnp.sum(grad * (branch - middle), 0, keepdims=True)

        alpha_sum_ref[...] = lax.fori_loop(0, rows // 32, step, jnp.zeros((1, D), F32))

    @pl.when(turn >= blocks)
    def _():
        block = turn - blocks
        grads = back[...]
        grad_hidden = dot_nt(grads, wd_ref[...])
        up_raw, gate_raw = up_buf[block], gate_buf[block]
        gate = gate_raw * gate_scale
        sigma = jax.nn.sigmoid(gate)
        active = gate * sigma
        upward = up_raw * up_scale
        grad_upward = grad_hidden * active
        grad_gate = grad_hidden * upward * (sigma * (1.0 + gate * (1.0 - sigma)))
        up_sum_ref[...] = jnp.sum(grad_upward * up_raw, 0, keepdims=True)
        gate_sum_ref[...] = jnp.sum(grad_gate * gate_raw, 0, keepdims=True) * math.sqrt(D)
        grad_u = (grad_upward * up_scale).astype(BF16)
        grad_g = (grad_gate * gate_scale).astype(BF16)
        grad_ref[0] = dot_tn(grad_u, mid_ref[...]).astype(BF16)
        grad_ref[1] = dot_tn(grad_g, mid_ref[...]).astype(BF16)
        down_ref[...] = dot_tn(hidden_buf[block], grads).astype(BF16)
        grad_mid_ref[...] += dot(grad_u, wu_ref[...]) + dot(grad_g, wg_ref[...])


def feed_forward(mid_low, middle, cotangent, alpha_ffn, scales, weights, firsts):
    rows = mid_low.shape[0]
    blocks = scales.shape[1] // UNITS
    whole = lambda *shape: pl.BlockSpec(shape, lambda t: (0,) * len(shape))
    weight = lambda m: pl.BlockSpec((None, UNITS, D), lambda t: (m, lax.rem(t, blocks), 0))
    after = lambda t: jnp.maximum(t - blocks, 0)
    units = pl.BlockSpec((1, UNITS), lambda t: (0, after(t)))
    scale = pl.BlockSpec((1, UNITS), lambda t: (0, lax.rem(t, blocks)))
    return pl.pallas_call(
        functools.partial(feed_kernel, blocks),
        grid=(2 * blocks,),
        out_shape=(
            jax.ShapeDtypeStruct((rows, D), BF16),
            jax.ShapeDtypeStruct((rows, D), F32),
            jax.ShapeDtypeStruct((2, blocks * UNITS, D), BF16),
            jax.ShapeDtypeStruct((blocks * UNITS, D), BF16),
            jax.ShapeDtypeStruct((1, blocks * UNITS), F32),
            jax.ShapeDtypeStruct((1, blocks * UNITS), F32),
            jax.ShapeDtypeStruct((1, D), F32),
        ),
        in_specs=[whole(rows, D), whole(rows, D), whole(rows, D), whole(1, D), scale, scale]
        + [weight(first) for first in firsts],
        out_specs=(
            whole(rows, D), whole(rows, D), pl.BlockSpec((2, UNITS, D), lambda t: (0, after(t), 0)),
            pl.BlockSpec((UNITS, D), lambda t: (after(t), 0)),
            units, units, whole(1, D),
        ),
        scratch_shapes=[
            pltpu.VMEM((blocks, rows, UNITS), F32),
            pltpu.VMEM((blocks, rows, UNITS), F32),
            pltpu.VMEM((blocks, rows, UNITS), BF16),
            pltpu.VMEM((rows, D), F32),
            pltpu.VMEM((rows, D), BF16),
        ],
        compiler_params=pltpu.CompilerParams(vmem_limit_bytes=62 * 2**20),
        cost_estimate=pl.CostEstimate(flops=60 * 10**9, bytes_accessed=120 * 10**6, transcendentals=5 * 10**6),
    )(mid_low, middle, cotangent, alpha_ffn, scales[:1], scales[1:], *weights)


def adam_kernel(places, per, *refs):
    grads = refs[:places]
    w_ref, m_ref, v_ref, w_out, m_out, v_out = refs[places:]

    def update(g_ref):
        def step(i, _):
            part = pl.ds(pl.multiple_of(i * 16, 16), 16)
            new, first, second = adam(
                w_ref[part, :], g_ref[part, :].astype(F32), m_ref[part, :], v_ref[part, :], RATE, DECAY
            )
            w_out[part, :] = rownorm(new)[0]
            m_out[part, :] = first
            v_out[part, :] = second
            return 0

        lax.fori_loop(0, w_ref.shape[0] // 16, step, 0)

    for n in range(places):
        @pl.when(pl.program_id(0) // per == n)
        def _(n=n):
            update(grads[n])


def adam_rows(weight, grads, first, second):
    places = len(grads)
    _, per, piece, _ = grads[0][0].shape
    spec = pl.BlockSpec((None, piece, D), lambda p: (p, 0, 0))

    def grad_spec(n, index):
        return pl.BlockSpec((None, None, piece, D), lambda p: (index, jnp.clip(p - n * per, 0, per - 1), 0, 0))

    shape = jax.ShapeDtypeStruct((places * per, piece, D), F32)
    news = pl.pallas_call(
        functools.partial(adam_kernel, places, per),
        grid=(places * per,),
        out_shape=(shape,) * 3,
        in_specs=[grad_spec(n, index) for n, (_, index) in enumerate(grads)] + [spec] * 3,
        out_specs=(spec,) * 3,
        compiler_params=pltpu.CompilerParams(vmem_limit_bytes=40 * 2**20),
        cost_estimate=pl.CostEstimate(flops=20 * weight.size, bytes_accessed=26 * weight.size, transcendentals=0),
    )(*(array for array, _ in grads), *(old.reshape(shape.shape) for old in (weight, first, second)))
    return tuple(new.reshape(weight.shape) for new in news)


QUERY_BLOCK = 256
PAIR = 2 * HEAD_DIM
PAIRS = HEADS // 2


def head_ones():
    row = lax.broadcasted_iota(jnp.int32, (PAIR, PAIR), 0) // HEAD_DIM
    col = lax.broadcasted_iota(jnp.int32, (PAIR, PAIR), 1) // HEAD_DIM
    return (row == col).astype(F32).astype(BF16)


def head_sum(value, ones):
    high = value.astype(BF16)
    rest = (value - high.astype(F32)).astype(BF16)
    return dot(high, ones) + dot(rest, ones)


def of_head(value, head):
    lane = lax.broadcasted_iota(jnp.int32, value.shape, 1) // HEAD_DIM
    return jnp.where(lane == head, value, jnp.zeros_like(value))


def attend_pair(h_ref, wq_ref, wq2_ref, wk_ref, wk2_ref, wv_ref, wv2_ref, gain_ref, bias_ref, qp_ref, kp_ref, v_ref, o_ref, lse_ref,
                key_buf, query_buf, value_buf):
    cols = h_ref.shape[0]
    rows = qp_ref.shape[0]
    span = bias_ref.shape[1]
    ones = head_ones()
    gain = gain_ref[...]
    weights = jnp.concatenate([wk_ref[...], wk2_ref[...], wv_ref[...], wv2_ref[...]], 0)
    query_weights = jnp.concatenate([wq_ref[...], wq2_ref[...]], 0)

    def project(i, _):
        part = pl.ds(pl.multiple_of(i * QUERY_BLOCK, QUERY_BLOCK), QUERY_BLOCK)
        both = dot_nt(h_ref[part, :], weights)
        keys = both[:, :PAIR]
        kp_ref[part, :] = keys
        factor = lax.rsqrt(head_sum(keys * keys, ones) + SMALL)
        key_buf[part, :] = (keys * factor * gain).astype(BF16)
        values = both[:, PAIR:].astype(BF16)
        v_ref[part, :] = values
        value_buf[part, :PAIR] = values
        value_buf[part, PAIR:] = jnp.ones_like(values)
        return 0

    lax.fori_loop(0, cols // QUERY_BLOCK, project, 0)

    def project_queries(i, _):
        part = pl.ds(pl.multiple_of(i * QUERY_BLOCK, QUERY_BLOCK), QUERY_BLOCK)
        own = pl.ds(pl.multiple_of(cols - rows + i * QUERY_BLOCK, QUERY_BLOCK), QUERY_BLOCK)
        queries = dot_nt(h_ref[own, :], query_weights)
        qp_ref[part, :] = queries
        factor = lax.rsqrt(head_sum(queries * queries, ones) + SMALL)
        scaled = (queries * factor * gain).astype(BF16).astype(F32) * math.sqrt(HEAD_DIM)
        query_buf[part, :] = scaled.astype(BF16)
        return 0

    lax.fori_loop(0, rows // QUERY_BLOCK, project_queries, 0)
    for i in range(rows // QUERY_BLOCK):
        part = pl.ds(i * QUERY_BLOCK, QUERY_BLOCK)
        reach = pl.ds(i * QUERY_BLOCK, span)
        sides = []
        for head in range(2):
            scores = dot_nt(of_head(query_buf[part, :], head), key_buf[reach, :])
            probs = jnp.exp(scores + bias_ref[part, :]).astype(BF16)
            both = dot(probs, value_buf[reach, :])
            total = both[:, PAIR:]
            sides.append(both[:, :PAIR] / total)
            lse_ref[head : head + 1, part] = jnp.log(total).T[:1, :]
        lane = lax.broadcasted_iota(jnp.int32, sides[0].shape, 1)
        o_ref[part, :] = jnp.where(lane < HEAD_DIM, sides[0], sides[1]).astype(BF16)


def back_pair(qp_ref, kp_ref, v_ref, o_ref, da_ref, wo_ref, wo2_ref, gain_ref, bias_ref, lse_ref,
              dq_ref, dk_ref, dv_ref, sum_ref, key_buf, key_turned, k_total, v_total):
    cols = kp_ref.shape[0]
    rows = qp_ref.shape[0]
    span = bias_ref.shape[1]
    ones = head_ones()
    gain = gain_ref[...]
    weights = jnp.concatenate([wo_ref[...], wo2_ref[...]], 0)

    def keys_of(i, _):
        part = pl.ds(pl.multiple_of(i * QUERY_BLOCK, QUERY_BLOCK), QUERY_BLOCK)
        keys = kp_ref[part, :]
        factor = lax.rsqrt(head_sum(keys * keys, ones) + SMALL)
        low = keys * factor * gain
        key_buf[part, :] = low.astype(BF16)
        key_turned[:, part] = low.T.astype(BF16)
        k_total[part, :] = jnp.zeros_like(keys)
        v_total[part, :] = jnp.zeros_like(keys)
        return 0

    lax.fori_loop(0, cols // QUERY_BLOCK, keys_of, 0)
    for i in range(rows // QUERY_BLOCK):
        part = pl.ds(i * QUERY_BLOCK, QUERY_BLOCK)
        reach = pl.ds(i * QUERY_BLOCK, span)
        queries = qp_ref[part, :]
        factor = lax.rsqrt(head_sum(queries * queries, ones) + SMALL)
        hat = queries * factor
        scaled = ((hat * gain).astype(BF16).astype(F32) * math.sqrt(HEAD_DIM)).astype(BF16)
        back = dot_nt(da_ref[part, :], weights).astype(BF16)
        inner = (back.astype(F32) * o_ref[part, :].astype(F32)).T
        sides = []
        for head in range(2):
            mine = slice(head * HEAD_DIM, (head + 1) * HEAD_DIM)
            query, grad = of_head(scaled, head), of_head(back, head)
            scores = dot_nt(key_buf[reach, :], query)
            probs = jnp.exp(scores + bias_ref[i] - lse_ref[head : head + 1, part])
            v_total[reach, :] += dot(probs.astype(BF16), grad)
            delta = jnp.sum(inner[mine, :], 0, keepdims=True)
            grad_scores = (probs * (dot_nt(v_ref[reach, :], grad) - delta)).astype(BF16)
            k_total[reach, :] += dot(grad_scores, query)
            sides.append(dot(key_turned[mine, reach], grad_scores))
        grad_q = jnp.concatenate(sides, 0).T * math.sqrt(HEAD_DIM)
        sums = jnp.sum(grad_q * hat, 0, keepdims=True)
        if i == 0:
            sum_ref[...] = jnp.broadcast_to(sums, sum_ref.shape)
        else:
            sum_ref[...] += jnp.broadcast_to(sums, sum_ref.shape)
        grad_q = grad_q * gain
        dq_ref[part, :] = (factor * (grad_q - hat * head_sum(hat * grad_q, ones))).astype(BF16)

    def finish(i, _):
        part = pl.ds(pl.multiple_of(i * QUERY_BLOCK, QUERY_BLOCK), QUERY_BLOCK)
        keys = kp_ref[part, :]
        factor = lax.rsqrt(head_sum(keys * keys, ones) + SMALL)
        hat = keys * factor
        grad_k = k_total[part, :]
        sum_ref[...] += jnp.broadcast_to(jnp.sum(grad_k * hat, 0, keepdims=True), sum_ref.shape)
        grad_k = grad_k * gain
        dk_ref[part, :] = (factor * (grad_k - hat * head_sum(hat * grad_k, ones))).astype(BF16)
        dv_ref[part, :] = v_total[part, :].astype(BF16)
        return 0

    lax.fori_loop(0, cols // QUERY_BLOCK, finish, 0)


def head_rows(attn_low, matrix, second):
    heads = attn_low.shape[2]

    def index(p):
        head = 2 * p + second
        return (head // heads, matrix, lax.rem(head, heads), 0, 0)

    return pl.BlockSpec((None, None, None, HEAD_DIM, D), index)


def attention_forward(low_all, attn_low, gain_qk, bias, rows):
    cols = low_all.shape[0]
    span = bias.shape[1]
    side = lambda n: pl.BlockSpec((n, PAIR), lambda p: (0, p))
    whole = lambda *shape: pl.BlockSpec(shape, lambda p: (0,) * len(shape))
    return pl.pallas_call(
        attend_pair,
        grid=(PAIRS,),
        out_shape=(
            jax.ShapeDtypeStruct((rows, D), F32),
            jax.ShapeDtypeStruct((cols, D), F32),
            jax.ShapeDtypeStruct((cols, D), BF16),
            jax.ShapeDtypeStruct((rows, D), BF16),
            jax.ShapeDtypeStruct((PAIRS, 8, rows), F32),
        ),
        in_specs=[whole(cols, D)]
        + [head_rows(attn_low, j, second) for j in range(3) for second in range(2)]
        + [side(1), whole(rows, span)],
        out_specs=(side(rows), side(cols), side(cols), side(rows),
                   pl.BlockSpec((None, 8, rows), lambda p: (p, 0, 0))),
        scratch_shapes=[
            pltpu.VMEM((cols, PAIR), BF16),
            pltpu.VMEM((rows, PAIR), BF16),
            pltpu.VMEM((cols, 2 * PAIR), BF16),
        ],
        compiler_params=pltpu.CompilerParams(vmem_limit_bytes=56 * 2**20),
        cost_estimate=pl.CostEstimate(flops=20 * 10**9, bytes_accessed=30 * 10**6, transcendentals=13 * 10**6),
    )(low_all, *[attn_low] * 6, gain_qk, bias)


def attention_backward(q_pre, k_pre, value_all, o_low, grad_spre, attn_low, gain_qk, bias_turned, lse):
    rows, cols = q_pre.shape[0], k_pre.shape[0]
    side = lambda n: pl.BlockSpec((n, PAIR), lambda p: (0, p))
    whole = lambda *shape: pl.BlockSpec(shape, lambda p: (0,) * len(shape))
    stat = pl.BlockSpec((None, 8, rows), lambda p: (p, 0, 0))
    return pl.pallas_call(
        back_pair,
        grid=(PAIRS,),
        out_shape=(
            jax.ShapeDtypeStruct((rows, D), BF16),
            jax.ShapeDtypeStruct((cols, D), BF16),
            jax.ShapeDtypeStruct((cols, D), BF16),
            jax.ShapeDtypeStruct((PAIRS, 8, PAIR), F32),
        ),
        in_specs=[
            side(rows), side(cols), side(cols), side(rows), whole(rows, D),
            head_rows(attn_low, 3, 0), head_rows(attn_low, 3, 1),
            pl.BlockSpec((None, 1, PAIR), lambda p: (p, 0, 0)), whole(*bias_turned.shape), stat,
        ],
        out_specs=(side(rows), side(cols), side(cols), pl.BlockSpec((None, 8, PAIR), lambda p: (p, 0, 0))),
        scratch_shapes=[
            pltpu.VMEM((cols, PAIR), BF16),
            pltpu.VMEM((PAIR, cols), BF16),
            pltpu.VMEM((cols, PAIR), F32),
            pltpu.VMEM((cols, PAIR), F32),
        ],
        compiler_params=pltpu.CompilerParams(vmem_limit_bytes=56 * 2**20),
        cost_estimate=pl.CostEstimate(flops=30 * 10**9, bytes_accessed=40 * 10**6, transcendentals=13 * 10**6),
    )(q_pre, k_pre, value_all, o_low, grad_spre, attn_low, attn_low, gain_qk, bias_turned, lse)


def attention_back_kernel(shards, grads_ref, qp_ref, kp_ref, v_ref, o_ref, weight_ref, da_ref, gain_ref, bias_ref,
                          lse_ref, out, dq_ref, dk_ref, dv_ref, sum_ref,
                          qp_buf, kp_buf, v_buf, o_buf, wo_buf, dq_buf, dk_buf, dv_buf, load_sem, store_sem,
                          key_buf, key_turned, k_total, v_total, *scratch):
    turns, turn, finish = reduction((grads_ref.at[0], grads_ref.at[1]), out, scratch)
    heads = weight_ref.shape[2]

    def loads(p, slot):
        lanes = pl.ds(pl.multiple_of(p * PAIR, PAIR), PAIR)
        copies = [
            pltpu.make_async_copy(ref.at[:, lanes], buf.at[slot], load_sem.at[slot, n])
            for n, (ref, buf) in enumerate(((qp_ref, qp_buf), (kp_ref, kp_buf), (v_ref, v_buf), (o_ref, o_buf)))
        ]
        for second in range(2):
            head = 2 * p + second
            copies.append(
                pltpu.make_async_copy(
                    weight_ref.at[head // heads, 3, lax.rem(head, heads)], wo_buf.at[slot, second],
                    load_sem.at[slot, 4 + second],
                )
            )
        return copies

    def stores(p, slot):
        lanes = pl.ds(pl.multiple_of(p * PAIR, PAIR), PAIR)
        return [
            pltpu.make_async_copy(buf.at[slot], ref.at[:, lanes], store_sem.at[slot, n])
            for n, (ref, buf) in enumerate(((dq_ref, dq_buf), (dk_ref, dk_buf), (dv_ref, dv_buf)))
        ]

    def pair(p):
        slot = lax.rem(p, 2)

        @pl.when(p + 1 < PAIRS)
        def _():
            for copy in loads(p + 1, 1 - slot):
                copy.start()

        for copy in loads(p, slot):
            copy.wait()

        @pl.when(p >= 2)
        def _():
            for copy in stores(p - 2, slot):
                copy.wait()

        back_pair(
            qp_buf.at[slot], kp_buf.at[slot], v_buf.at[slot], o_buf.at[slot], da_ref, wo_buf.at[slot, 0],
            wo_buf.at[slot, 1], gain_ref.at[p], bias_ref, lse_ref.at[p], dq_buf.at[slot], dk_buf.at[slot],
            dv_buf.at[slot], sum_ref.at[p], key_buf, key_turned, k_total, v_total,
        )
        for copy in stores(p, slot):
            copy.start()

    greet(shards)
    for copy in loads(0, 0):
        copy.start()

    def step(t, _):
        turn(t)

        @pl.when(t < PAIRS)
        def _():
            pair(t)

        return 0

    lax.fori_loop(0, max(turns, PAIRS), step, 0)
    for p in (PAIRS - 2, PAIRS - 1):
        for copy in stores(p, p % 2):
            copy.wait()
    finish()


def attention_back_reduce(grads, q_pre, k_pre, value_all, o_low, attn_low, grad_spre, gain_qk, bias_turned, lse):
    _, shards, _, _, rows, _ = grads.shape
    tokens, cols = q_pre.shape[0], k_pre.shape[0]
    any_space = pl.BlockSpec(memory_space=pl.ANY)
    vmem = pl.BlockSpec(memory_space=pltpu.VMEM)
    dma = pltpu.SemaphoreType.DMA
    return pl.pallas_call(
        functools.partial(attention_back_kernel, shards),
        out_shape=(
            jax.ShapeDtypeStruct((2, 8, rows, D), BF16),
            jax.ShapeDtypeStruct((tokens, D), BF16),
            jax.ShapeDtypeStruct((cols, D), BF16),
            jax.ShapeDtypeStruct((cols, D), BF16),
            jax.ShapeDtypeStruct((PAIRS, 8, PAIR), F32),
        ),
        in_specs=[any_space] * 6 + [vmem] * 4,
        out_specs=(any_space,) * 4 + (vmem,),
        scratch_shapes=[
            pltpu.VMEM((2, tokens, PAIR), F32),
            pltpu.VMEM((2, cols, PAIR), F32),
            pltpu.VMEM((2, cols, PAIR), BF16),
            pltpu.VMEM((2, tokens, PAIR), BF16),
            pltpu.VMEM((2, 2, HEAD_DIM, D), BF16),
            pltpu.VMEM((2, tokens, PAIR), BF16),
            pltpu.VMEM((2, cols, PAIR), BF16),
            pltpu.VMEM((2, cols, PAIR), BF16),
            dma((2, 6)), dma((2, 3)),
            pltpu.VMEM((cols, PAIR), BF16),
            pltpu.VMEM((PAIR, cols), BF16),
            pltpu.VMEM((cols, PAIR), F32),
            pltpu.VMEM((cols, PAIR), F32),
        ] + reduction_scratch(2, shards, rows),
        compiler_params=pltpu.CompilerParams(
            collective_id=1, has_side_effects=True, vmem_limit_bytes=62 * 2**20
        ),
        cost_estimate=pl.CostEstimate(flops=30 * 10**9, bytes_accessed=2 * 10**8, transcendentals=13 * 10**6),
    )(grads, q_pre, k_pre, value_all, o_low, attn_low, grad_spre, gain_qk, bias_turned, lse)


def attention_grads_kernel(dq_ref, dk_ref, dv_ref, o_ref, h_ref, da_ref, out):
    matrix = pl.program_id(0)
    rows = dq_ref.shape[0]
    cols = h_ref.shape[0]
    for m, (left, right) in enumerate(
        (
            (dq_ref, h_ref.at[pl.ds(cols - rows, rows)]),
            (dk_ref, h_ref),
            (dv_ref, h_ref),
            (o_ref, da_ref),
        )
    ):
        @pl.when(matrix == m)
        def _(left=left, right=right):
            out[...] = dot_tn(left[...], right[...]).astype(BF16).reshape(out.shape)


def attention_grads(dq, dk, dv, o_low, low_all, grad_spre, shards):
    rows, cols = dq.shape[0], dk.shape[0]
    per = D // shards
    group = math.lcm(per, 2 * HEAD_DIM) if per % (2 * HEAD_DIM) else per
    group = max(group, D // 2) if (D // 2) % group == 0 else group
    whole = lambda *shape: pl.BlockSpec(shape, lambda m, g: (0,) * len(shape))
    side = lambda n, k: pl.BlockSpec((n, group), lambda m, g: (0, lax.select(m == k, g, lax.select(m < k, 0, D // group - 1))))
    return pl.pallas_call(
        attention_grads_kernel,
        grid=(4, D // group),
        out_shape=jax.ShapeDtypeStruct((shards, 4, per, D), BF16),
        in_specs=[side(rows, 0), side(cols, 1), side(cols, 2), side(rows, 3), whole(cols, D), whole(rows, D)],
        out_specs=pl.BlockSpec((group // per, None, per, D), lambda m, g: (g, m, 0, 0)),
        compiler_params=pltpu.CompilerParams(vmem_limit_bytes=56 * 2**20),
        cost_estimate=pl.CostEstimate(flops=14 * 10**9, bytes_accessed=30 * 10**6, transcendentals=0),
    )(dq, dk, dv, o_low, low_all, grad_spre)


def body(
    tokens,
    doc_lengths,
    cotangent,
    attn_w,
    ffn_w,
    attn_m,
    attn_v,
    ffn_m,
    ffn_v,
    gains_d,
    gains_ff,
    gd_m,
    gd_v,
    gf_m,
    gf_v,
):
    shards = lax.axis_size("shard")
    reps = lax.axis_size("rep")
    device_index = lax.axis_index("shard")
    rows = tokens.shape[0]
    reach = WINDOW // rows
    cols = (reach + 1) * rows
    attn_rows = attn_w.shape[1]
    ffn_rows = ffn_w.shape[1]
    ffn_all = shards * ffn_rows
    piece = ffn_rows // reps

    cut = gains_d.size
    small = jnp.concatenate([gains_d.reshape(-1), gains_ff.reshape(-1)]).astype(BF16)
    fast = reps == 8 and shards == 4 and attn_rows % HEAD_DIM == 0
    if fast:
        gathered, small, before = gather_all(
            attn_w.reshape(8, piece, D),
            ffn_w.reshape(3, 8, piece, D),
            jnp.pad(small, (0, 16 * D - small.size)).reshape(16, D),
            tokens,
            shards,
            3,
        )
        attn_low = gathered[0].reshape(shards, 4, attn_rows // HEAD_DIM, HEAD_DIM, D)
        ffn_low = [gathered.reshape(4, ffn_all, D)] * 3
        firsts = (1, 2, 3)
        small = small.reshape(shards, -1)[:, : cut + gains_ff.size]
        present = jnp.arange(reach)[:, None, None] >= reach - device_index
        earlier = [jnp.where(present, before, 0).reshape(reach * rows, D)]
    else:
        attn_low = (
            gather_rows(attn_w.reshape(4 * attn_rows, D).astype(BF16))
            .reshape(shards, 4, attn_rows, D)
            .transpose(1, 0, 2, 3)
            .reshape(1, 4, HEADS, HEAD_DIM, D)
        )
        ffn_low = [gather_rows(ffn_w[m].astype(BF16)).reshape(1, ffn_all, D) for m in range(3)]
        firsts = (0, 0, 0)
        small = lax.all_gather(small, "shard", axis=0)
        earlier = [from_behind(tokens, "shard", offset) for offset in range(reach, 0, -1)]
    small = small.astype(F32)
    query_low, key_low, value_low, out_low = (attn_low[:, j].reshape(D, D) for j in range(4))
    gd_all = small[:, :cut].reshape(shards, 3, -1).transpose(1, 0, 2).reshape(3, D)
    gf_all = small[:, cut:].reshape(shards, 2, ffn_rows).transpose(1, 0, 2).reshape(2, ffn_all)
    gain_qk = gd_all[0]
    alpha_attn = gd_all[1]
    alpha_ffn = gd_all[2]

    lengths_row = doc_lengths[0]
    starts = jnp.cumsum(lengths_row) - lengths_row
    positions = device_index * rows + jnp.arange(rows, dtype=jnp.int32)
    doc_start = jnp.max(
        jnp.where(starts[None, :] <= positions[:, None], starts[None, :], 0), axis=1
    )
    blocks = rows // QUERY_BLOCK
    span = WINDOW + QUERY_BLOCK
    query = jnp.arange(rows, dtype=jnp.int32).reshape(blocks, QUERY_BLOCK)
    lead = query[:, :1] - reach * rows + jnp.arange(span, dtype=jnp.int32)
    ahead = query[:, :, None] - lead[:, None, :]
    floor = (doc_start - device_index * rows).reshape(blocks, QUERY_BLOCK, 1)
    mask = (ahead >= 0) & (ahead < WINDOW) & (lead[:, None, :] >= floor)
    bias = jnp.where(mask, 0.0, NEGATIVE).astype(F32)
    bias_turned = bias.transpose(0, 2, 1)
    bias = bias.reshape(rows, span)
    tokens_all = jnp.concatenate(earlier + [tokens], 0)
    normed_all, factor_all = rownorm(tokens_all.astype(F32))
    low_all = normed_all.astype(BF16)
    normed_in, factor_in = normed_all[-rows:], factor_all[-rows:]
    in_low = low_all[-rows:]
    q_pre, k_pre, value_all, o_low, lse = attention_forward(
        low_all, attn_low, gain_qk[None], bias, rows
    )
    side, side_factor = rownorm(dot(o_low, out_low))
    middle, mid_factor = rownorm(normed_in + alpha_attn * (side - normed_in))
    mid_low = middle.astype(BF16)
    output, grad_mid, ffn_grads, down_grads, grad_scale_up, grad_scale_gate, grad_alpha_ffn = feed_forward(
        mid_low, middle, cotangent, alpha_ffn[None], gf_all, ffn_low, firsts
    )
    grad_mixed = norm_back(middle, mid_factor, grad_mid)
    grad_in = grad_mixed * (1.0 - alpha_attn)
    grad_alpha_attn = jnp.sum(grad_mixed * (side - normed_in), 0)
    grad_spre = norm_back(side, side_factor, grad_mixed * alpha_attn).astype(BF16)
    pair_gain = gain_qk.reshape(PAIRS, 1, PAIR)
    if fast:
        units = (shards, 4, 2, piece, D)
        sum_first, grad_qpre, grad_kpre, grad_vpre, gain_sums = attention_back_reduce(
            ffn_grads.reshape((2,) + units), q_pre, k_pre, value_all, o_low, attn_low, grad_spre,
            pair_gain, bias_turned, lse,
        )
    else:
        grad_qpre, grad_kpre, grad_vpre, gain_sums = attention_backward(
            q_pre, k_pre, value_all, o_low, grad_spre, attn_low, pair_gain, bias_turned, lse
        )
    grad_gain_qk = gain_sums[:, 0].reshape(D)
    grad_gf = jnp.concatenate([grad_scale_up, grad_scale_gate])
    gd_rows = D // shards
    if fast:
        attn_grad = attention_grads(grad_qpre, grad_kpre, grad_vpre, o_low, low_all, grad_spre, shards)
        grad_gd = jnp.stack([grad_gain_qk, grad_alpha_attn, grad_alpha_ffn[0]])
        small = jnp.concatenate(
            [
                grad_gd.reshape(3, shards, gd_rows).transpose(1, 0, 2).reshape(shards, -1),
                grad_gf.reshape(2, shards, ffn_rows).transpose(1, 0, 2).reshape(shards, -1),
            ],
            1,
        )
        small = jnp.pad(small, ((0, 0), (0, 8 * D - small.shape[1]))).reshape(shards, 8, D)
        sum_last, sum_small = reduce_last(down_grads.reshape(units), attn_grad.reshape(units), small)
        sum_small = sum_small.reshape(-1)
        sum_gd = sum_small[: 3 * gd_rows].reshape(3, gd_rows)
        sum_gf = sum_small[3 * gd_rows : 3 * gd_rows + 2 * ffn_rows].reshape(2, ffn_rows)
        attn_sums, ffn_sums = [(sum_last, 1)], [(sum_first, 0), (sum_first, 1), (sum_last, 0)]
    else:
        attn_grad = jnp.stack(
            [
                dot_tn(grad_qpre, in_low),
                dot_tn(grad_kpre, low_all),
                dot_tn(grad_vpre, low_all),
                dot_tn(o_low, grad_spre),
            ]
        ).astype(BF16)
        attn_grad = attn_grad.reshape(4, shards, attn_rows, D).transpose(1, 0, 2, 3)
        attn_grad = attn_grad.reshape(shards, reps, 4 * attn_rows // reps, D).transpose(1, 0, 2, 3)
        attn_sums = [(reduce_rows(attn_grad).reshape(1, 4, attn_rows, D), 0)]
        ready = (shards, reps, piece, D)
        ffn_sums = [
            (reduce_rows(part.reshape(ready).transpose(1, 0, 2, 3)).reshape(1, 1, ffn_rows, D), 0)
            for part in (ffn_grads[0], ffn_grads[1], down_grads)
        ]
        grad_small = jnp.concatenate(
            [grad_gain_qk, grad_alpha_attn, grad_alpha_ffn[0], grad_gf.reshape(-1)]
        )
        grad_small = lax.psum(grad_small, ("rep", "shard"))
        sum_gd = lax.dynamic_slice_in_dim(
            grad_small[: 3 * D].reshape(3, D), device_index * gd_rows, gd_rows, 1
        )
        sum_gf = lax.dynamic_slice_in_dim(
            grad_small[3 * D :].reshape(2, ffn_all), device_index * ffn_rows, ffn_rows, 1
        )
    back_all = dot(grad_kpre, key_low) + dot(grad_vpre, value_low)
    grad_in = grad_in + dot(grad_qpre, query_low) + back_all[reach * rows :]
    for offset in range(1, reach + 1):
        first = (reach - offset) * rows
        part = back_all[first : first + rows].astype(BF16)
        grad_in = grad_in + from_behind(part, "shard", -offset).astype(F32)
    grad_tokens = norm_back(normed_in, factor_in, grad_in)

    attn_unit, attn_m_new, attn_v_new = adam_rows(attn_w, attn_sums, attn_m, attn_v)
    ffn_unit, ffn_m_new, ffn_v_new = adam_rows(ffn_w, ffn_sums, ffn_m, ffn_v)
    gd_new, gd_m_new, gd_v_new = adam(gains_d, sum_gd, gd_m, gd_v, GAIN_RATE, 0.0)
    gf_new, gf_m_new, gf_v_new = adam(gains_ff, sum_gf, gf_m, gf_v, GAIN_RATE, 0.0)
    return (
        output,
        grad_tokens,
        attn_unit,
        attn_m_new,
        attn_v_new,
        ffn_unit,
        ffn_m_new,
        ffn_v_new,
        gd_new,
        gd_m_new,
        gd_v_new,
        gf_new,
        gf_m_new,
        gf_v_new,
    )

def solution(mesh):
    return jax.shard_map(
        body,
        mesh=mesh,
        in_specs=(
            P(("rep", "shard"), None),
            P("rep", None),
            P(("rep", "shard"), None),
            P(None, "shard", None),
            P(None, "shard", None),
            P(None, "shard", None),
            P(None, "shard", None),
            P(None, "shard", None),
            P(None, "shard", None),
            P(None, "shard"),
            P(None, "shard"),
            P(None, "shard"),
            P(None, "shard"),
            P(None, "shard"),
            P(None, "shard"),
        ),
        out_specs=(
            P(("rep", "shard"), None),
            P(("rep", "shard"), None),
            P(None, "shard", None),
            P(None, "shard", None),
            P(None, "shard", None),
            P(None, "shard", None),
            P(None, "shard", None),
            P(None, "shard", None),
            P(None, "shard"),
            P(None, "shard"),
            P(None, "shard"),
            P(None, "shard"),
            P(None, "shard"),
            P(None, "shard"),
        ),
        check_vma=False,
    )
```

```python
import functools
import math

import jax
import jax.numpy as jnp
from jax import lax
from jax.experimental import pallas as pl
from jax.experimental.pallas import tpu as pltpu
from jax.sharding import PartitionSpec as P

D = 1280
HEADS = 20
HEAD_DIM = 64
WINDOW = 1024
STEP = 10


SMALL = 1e-06
NEGATIVE = -1e30
BETA_ONE = 0.9
BETA_TWO = 0.95
RATE = 0.02
GAIN_RATE = 1.0
DECAY = 0.1
TINY = 1e-08
F32 = jnp.float32
BF16 = jnp.bfloat16


def from_behind(block, axis, distance):
    devices = range(lax.axis_size(axis))
    route = [(i - distance, i) for i in devices if i - distance in devices]
    return lax.ppermute(block, axis, route)


def rownorm(value):
    factor = lax.rsqrt(jnp.sum(value * value, -1, keepdims=True) + SMALL)
    return (value * factor, factor)


def norm_back(normed, factor, grad):
    return factor * (grad - normed * jnp.sum(normed * grad, -1, keepdims=True))


def adam(weight, grad, first, second, rate, decay):
    first = BETA_ONE * first + (1.0 - BETA_ONE) * grad
    second = BETA_TWO * second + (1.0 - BETA_TWO) * grad * grad
    fix_one = 1.0 - BETA_ONE**STEP
    fix_two = 1.0 - BETA_TWO**STEP
    change = first / fix_one / (jnp.sqrt(second / fix_two) + TINY) + decay * weight
    return (weight - rate * change, first, second)


def dot(a, b):
    return jnp.dot(a, b, preferred_element_type=F32)


def dot_nt(a, b):
    return lax.dot_general(a, b, (((1,), (1,)), ((), ())), preferred_element_type=F32)


def dot_tn(a, b):
    return lax.dot_general(a, b, (((0,), (0,)), ((), ())), preferred_element_type=F32)


def gather_rows(shard_rows):
    reps = lax.axis_size("rep")
    piece = shard_rows.shape[0] // reps
    mine = lax.dynamic_slice_in_dim(shard_rows, lax.axis_index("rep") * piece, piece, 0)
    column = lax.all_gather(mine, "shard", axis=0)
    return lax.all_gather(column, "rep", axis=1)


def reduce_rows(grad):
    part = lax.psum_scatter(grad, "rep", scatter_dimension=0)
    part = lax.psum_scatter(part, "shard", scatter_dimension=0)
    return lax.all_gather(part, "rep", axis=0, tiled=True)


MESH = pl.DeviceIdType.MESH
HALF = 80


def place():
    rep = lax.axis_index("rep")
    core, chip = lax.rem(rep, 2), rep // 2
    beside, above = chip + 1 - 2 * lax.rem(chip, 2), chip + 2 - 4 * (chip // 2)
    return core, chip, beside, above, 3 - chip


def remote(src, dst, send, recv, rep, shard):
    return pltpu.make_async_remote_copy(
        src_ref=src, dst_ref=dst, send_sem=send, recv_sem=recv,
        device_id=(rep, shard), device_id_type=MESH,
    )


def arrived(ref, sem):
    pltpu.make_async_copy(ref, ref, sem).wait()


def greet(shards):
    rep, line = lax.axis_index("rep"), lax.axis_index("shard")
    barrier = pltpu.get_barrier_semaphore()
    for n in range(1, 8):
        pl.semaphore_signal(barrier, inc=1, device_id=(lax.rem(rep + n, 8), line), device_id_type=MESH)
    for n in range(1, shards):
        pl.semaphore_signal(barrier, inc=1, device_id=(rep, lax.rem(line + n, shards)), device_id_type=MESH)
    pl.semaphore_wait(barrier, 6 + shards)


def add_into(target, sources, rows):
    def step(i, _):
        part = pl.ds(pl.multiple_of(i * 16, 16), 16)
        value = target[part, :].astype(F32)
        for source in sources:
            value = value + source[part, :].astype(F32)
        target[part, :] = value.astype(BF16)
        return 0

    lax.fori_loop(0, rows // 16, step, 0)


def reduction_scratch(count, shards, rows):
    steps = count * shards
    dma = pltpu.SemaphoreType.DMA
    return [
        pltpu.VMEM((steps, 4, rows, D), BF16),
        pltpu.VMEM((2, 4, rows, D), BF16),
        pltpu.VMEM((steps, rows, D), BF16),
        pltpu.VMEM((steps, 2, rows, D), BF16),
        pltpu.VMEM((count, shards + 1, rows, D), BF16),
        dma((2,)), dma(()), dma((steps,)), dma(()), dma((steps, 2)),
        dma(()), dma((steps, 2)), dma(()), dma((count, shards + 1)),
        dma(()), dma((count, 7)), dma(()),
    ]


REDUCTION_SCRATCH = 17


def reduction(grads, out, scratch):
    (acc, own, half, piece, below, own_sem, pair_send, pair_recv, half_send, half_recv,
     piece_send, piece_recv, line_send, line_recv, out_send, out_recv, out_local) = scratch
    count = len(grads)
    rows = own.shape[2]
    shards = below.shape[1] - 1
    core, chip, beside, above, across = place()
    line = lax.axis_index("shard")
    steps = count * shards

    def owner(step):
        i = lax.rem(step, shards)
        back = lax.select(i < shards - 1 - line, shards - 1 - i, i - (shards - 1 - line))
        ahead = lax.select(i < line, i, shards - 1 - (i - line))
        other = lax.select(2 * line < shards, back, ahead)
        return lax.select(i == shards - 1, line, other)

    def begin(step):
        slot = lax.rem(step, 2)
        for m in range(count):
            @pl.when(step // shards == m)
            def _(m=m):
                remote(
                    grads[m].at[owner(step), :, 1 - core], acc.at[step], pair_send, pair_recv.at[step],
                    2 * chip + 1 - core, line,
                ).start()
                pltpu.make_async_copy(grads[m].at[owner(step), :, core], own.at[slot], own_sem.at[slot]).start()

    def first(step):
        slot = lax.rem(step, 2)
        arrived(own.at[slot], own_sem.at[slot])
        arrived(acc.at[step], pair_recv.at[step])
        for q in range(4):
            add_into(acc.at[step, q], (own.at[slot, q],), rows)
        remote(acc.at[step, across, pl.ds(0, HALF)], half.at[step, pl.ds(0, HALF)],
               half_send, half_recv.at[step, 0], 2 * beside + core, line).start()
        remote(acc.at[step, across, pl.ds(HALF, rows - HALF)], half.at[step, pl.ds(HALF, rows - HALF)],
               half_send, half_recv.at[step, 1], 2 * above + core, line).start()

    def second(step):
        arrived(half.at[step, pl.ds(0, HALF)], half_recv.at[step, 0])
        arrived(half.at[step, pl.ds(HALF, rows - HALF)], half_recv.at[step, 1])
        add_into(acc.at[step, above, pl.ds(0, HALF)], (half.at[step, pl.ds(0, HALF)],), HALF)
        add_into(acc.at[step, beside, pl.ds(HALF, rows - HALF)],
                 (half.at[step, pl.ds(HALF, rows - HALF)],), rows - HALF)
        remote(acc.at[step, beside], piece.at[step, 0], piece_send, piece_recv.at[step, 0],
               2 * beside + core, line).start()
        remote(acc.at[step, above], piece.at[step, 1], piece_send, piece_recv.at[step, 1],
               2 * above + core, line).start()

    def pass_on(step):
        m, target = step // shards, owner(step)

        @pl.when(target > line)
        def _():
            remote(acc.at[step, chip], below.at[m, target], line_send, line_recv.at[m, target],
                   2 * chip + core, line + 1).start()

        @pl.when(target < line)
        def _():
            slot = lax.select(target == line - 1, shards, target)
            remote(acc.at[step, chip], below.at[m, slot], line_send, line_recv.at[m, slot],
                   2 * chip + core, line - 1).start()

    def outermost(step):
        target = owner(step)
        return ((target > line) & (line == 0)) | ((target < line) & (line == shards - 1))

    def third(step):
        for n in range(2):
            arrived(piece.at[step, n], piece_recv.at[step, n])
        add_into(acc.at[step, chip], (piece.at[step, 0], piece.at[step, 1]), rows)

        @pl.when(outermost(step))
        def _():
            pass_on(step)

    def along(step):
        m, target = step // shards, owner(step)

        def add_line(slot):
            arrived(below.at[m, slot], line_recv.at[m, slot])
            add_into(acc.at[step, chip], (below.at[m, slot],), rows)

        @pl.when(((target >= line) & (line > 0)) | ((target < line) & (line < shards - 1)))
        def _():
            add_line(target)

        @pl.when((target == line) & (line < shards - 1))
        def _():
            add_line(shards)

        @pl.when(jnp.logical_not(outermost(step)))
        def _():
            pass_on(step)

        @pl.when(target == line)
        def _():
            mine = 2 * chip + core
            pltpu.make_async_copy(acc.at[step, chip], out.at[m, mine], out_local).start()
            for n, other in enumerate((2 * beside + core, 2 * above + core, 2 * across + core, 2 * chip + 1 - core)):
                remote(acc.at[step, chip], out.at[m, mine], out_send, out_recv.at[m, n], other, line).start()

    def fourth(step):
        m = step // shards
        for n, origin in enumerate((2 * beside + core, 2 * above + core, 2 * across + core)):
            arrived(out.at[m, origin], out_recv.at[m, n])
            remote(out.at[m, origin], out.at[m, origin], out_send, out_recv.at[m, 4 + n],
                   2 * chip + 1 - core, line).start()

    def turn(t):
        @pl.when(t == 0)
        def _():
            begin(0)

        @pl.when(t + 1 < steps)
        def _():
            begin(t + 1)

        @pl.when(t < steps)
        def _():
            first(t)

        @pl.when((t >= 1) & (t < steps + 1))
        def _():
            second(t - 1)

        @pl.when((t >= 2) & (t < steps + 2))
        def _():
            third(t - 2)

        @pl.when((t >= 3) & (t < steps + 3))
        def _():
            along(t - 3)

        @pl.when((t >= 5) & (t < steps + 5) & (lax.rem(t - 5, shards) == shards - 1))
        def _():
            fourth(t - 5)

    def finish():
        for m in range(count):
            for n in range(4):
                arrived(out.at[m, 0], out_recv.at[m, 3 + n])
        arrived(out.at[:, 0], out_local)
        arrived(out.at[:, pl.ds(0, 7)], out_send)
        arrived(acc, pair_send)
        arrived(half, half_send)
        arrived(piece, piece_send)
        arrived(below.at[:, pl.ds(0, shards - 1)], line_send)

    return steps + 5, turn, finish


def last_kernel(shards, down_ref, attn_ref, gains_ref, back_ref, out, gains_out, back_out, line_got, plane_got, mine,
                line_send, line_recv, plane_send, plane_recv, back_send, back_recv, *scratch):
    rep, line = lax.axis_index("rep"), lax.axis_index("shard")
    reach = back_ref.shape[0]
    turns, turn, finish = reduction((down_ref, attn_ref), out, scratch)
    greet(shards)
    for n in range(1, shards):
        other = lax.rem(line + n, shards)
        remote(gains_ref.at[other], line_got.at[n - 1], line_send, line_recv.at[n - 1], rep, other).start()

    def step(t, _):
        turn(t)

        @pl.when(t == 1)
        def _():
            total = gains_ref[line]
            for n in range(shards - 1):
                arrived(line_got.at[n], line_recv.at[n])
                total = total + line_got[n]
            mine[...] = total
            for n in range(1, 8):
                remote(mine, plane_got.at[n - 1], plane_send, plane_recv.at[n - 1], lax.rem(rep + n, 8), line).start()

            for n in range(reach):
                @pl.when(line >= reach - n)
                def _(n=n):
                    remote(back_ref.at[n], back_out.at[n], back_send.at[n], back_recv.at[n], rep,
                           line - (reach - n)).start()

        @pl.when(t == 3)
        def _():
            total = mine[...]
            for n in range(7):
                arrived(plane_got.at[n], plane_recv.at[n])
                total = total + plane_got[n]
            gains_out[...] = total

        return 0

    lax.fori_loop(0, turns, step, 0)
    finish()
    arrived(line_got, line_send)
    arrived(plane_got, plane_send)
    for n in range(reach):
        @pl.when(line >= reach - n)
        def _(n=n):
            arrived(back_ref.at[n], back_send.at[n])

        @pl.when(line + reach - n < shards)
        def _(n=n):
            arrived(back_out.at[n], back_recv.at[n])


def reduce_last(down, attn, gains, back):
    shards, _, _, rows, _ = down.shape
    any_space = pl.BlockSpec(memory_space=pl.ANY)
    vmem = pl.BlockSpec(memory_space=pltpu.VMEM)
    dma = pltpu.SemaphoreType.DMA
    return pl.pallas_call(
        functools.partial(last_kernel, shards),
        out_shape=(
            jax.ShapeDtypeStruct((2, 8, rows, D), BF16),
            jax.ShapeDtypeStruct(gains.shape[1:], F32),
            jax.ShapeDtypeStruct(back.shape, BF16),
        ),
        in_specs=[any_space, any_space, vmem, any_space],
        out_specs=(any_space, vmem, any_space),
        scratch_shapes=[
            pltpu.VMEM((shards - 1,) + gains.shape[1:], F32),
            pltpu.VMEM((7,) + gains.shape[1:], F32),
            pltpu.VMEM(gains.shape[1:], F32),
            dma(()), dma((shards - 1,)), dma(()), dma((7,)), dma(back.shape[:1]), dma(back.shape[:1]),
        ] + reduction_scratch(2, shards, rows),
        compiler_params=pltpu.CompilerParams(
            collective_id=2, has_side_effects=True, vmem_limit_bytes=60 * 2**20
        ),
        cost_estimate=pl.CostEstimate(flops=2 * 10**7, bytes_accessed=2 * 10**8, transcendentals=0),
    )(down, attn, gains, back)


UNITS = 256


def feed_kernel(blocks, mid_ref, middle_ref, cot_ref, alpha_ref, up_scale_ref, gate_scale_ref, wu_ref, wg_ref, wd_ref,
                out_ref, grad_mid_ref, grad_ref, down_ref, up_sum_ref, gate_sum_ref, alpha_sum_ref,
                up_buf, gate_buf, hidden_buf, total, back):
    turn = pl.program_id(0)
    up_scale, gate_scale = up_scale_ref[...], gate_scale_ref[...] * math.sqrt(D)

    @pl.when(turn < blocks)
    def _():
        up_raw = dot_nt(mid_ref[...], wu_ref[...])
        gate_raw = dot_nt(mid_ref[...], wg_ref[...])
        up_buf[turn] = up_raw
        gate_buf[turn] = gate_raw
        gate = gate_raw * gate_scale
        hidden = (gate * jax.nn.sigmoid(gate) * (up_raw * up_scale)).astype(BF16)
        hidden_buf[turn] = hidden
        part = dot(hidden, wd_ref[...])

        @pl.when(turn == 0)
        def _():
            total[...] = part

        @pl.when(turn > 0)
        def _():
            total[...] += part

    @pl.when(turn == blocks - 1)
    def _():
        alpha = alpha_ref[...]
        rows = total.shape[0]

        def step(i, sums):
            part = pl.ds(pl.multiple_of(i * 32, 32), 32)
            branch, factor = rownorm(total[part, :])
            middle = middle_ref[part, :]
            final, final_factor = rownorm(middle + alpha * (branch - middle))
            out_ref[part, :] = final.astype(BF16)
            grad = norm_back(final, final_factor, cot_ref[part, :].astype(F32))
            grad_mid_ref[part, :] = grad * (1.0 - alpha)
            back[part, :] = norm_back(branch, factor, grad * alpha).astype(BF16)
            return sums + jnp.sum(grad * (branch - middle), 0, keepdims=True)

        alpha_sum_ref[...] = lax.fori_loop(0, rows // 32, step, jnp.zeros((1, D), F32))

    @pl.when(turn >= blocks)
    def _():
        block = turn - blocks
        grads = back[...]
        grad_hidden = dot_nt(grads, wd_ref[...])
        up_raw, gate_raw = up_buf[block], gate_buf[block]
        gate = gate_raw * gate_scale
        sigma = jax.nn.sigmoid(gate)
        active = gate * sigma
        upward = up_raw * up_scale
        grad_upward = grad_hidden * active
        grad_gate = grad_hidden * upward * (sigma * (1.0 + gate * (1.0 - sigma)))
        up_sum_ref[...] = jnp.sum(grad_upward * up_raw, 0, keepdims=True)
        gate_sum_ref[...] = jnp.sum(grad_gate * gate_raw, 0, keepdims=True) * math.sqrt(D)
        grad_u = (grad_upward * up_scale).astype(BF16)
        grad_g = (grad_gate * gate_scale).astype(BF16)
        grad_ref[0] = dot_tn(grad_u, mid_ref[...]).astype(BF16)
        grad_ref[1] = dot_tn(grad_g, mid_ref[...]).astype(BF16)
        down_ref[...] = dot_tn(hidden_buf[block], grads).astype(BF16)
        grad_mid_ref[...] += dot(grad_u, wu_ref[...]) + dot(grad_g, wg_ref[...])


def feed_forward(mid_low, middle, cotangent, alpha_ffn, scales, weights, firsts):
    rows = mid_low.shape[0]
    blocks = scales.shape[1] // UNITS
    whole = lambda *shape: pl.BlockSpec(shape, lambda t: (0,) * len(shape))
    weight = lambda m: pl.BlockSpec((None, UNITS, D), lambda t: (m, lax.rem(t, blocks), 0))
    after = lambda t: jnp.maximum(t - blocks, 0)
    units = pl.BlockSpec((1, UNITS), lambda t: (0, after(t)))
    scale = pl.BlockSpec((1, UNITS), lambda t: (0, lax.rem(t, blocks)))
    return pl.pallas_call(
        functools.partial(feed_kernel, blocks),
        grid=(2 * blocks,),
        out_shape=(
            jax.ShapeDtypeStruct((rows, D), BF16),
            jax.ShapeDtypeStruct((rows, D), F32),
            jax.ShapeDtypeStruct((2, blocks * UNITS, D), BF16),
            jax.ShapeDtypeStruct((blocks * UNITS, D), BF16),
            jax.ShapeDtypeStruct((1, blocks * UNITS), F32),
            jax.ShapeDtypeStruct((1, blocks * UNITS), F32),
            jax.ShapeDtypeStruct((1, D), F32),
        ),
        in_specs=[whole(rows, D), whole(rows, D), whole(rows, D), whole(1, D), scale, scale]
        + [weight(first) for first in firsts],
        out_specs=(
            whole(rows, D), whole(rows, D), pl.BlockSpec((2, UNITS, D), lambda t: (0, after(t), 0)),
            pl.BlockSpec((UNITS, D), lambda t: (after(t), 0)),
            units, units, whole(1, D),
        ),
        scratch_shapes=[
            pltpu.VMEM((blocks, rows, UNITS), F32),
            pltpu.VMEM((blocks, rows, UNITS), F32),
            pltpu.VMEM((blocks, rows, UNITS), BF16),
            pltpu.VMEM((rows, D), F32),
            pltpu.VMEM((rows, D), BF16),
        ],
        compiler_params=pltpu.CompilerParams(vmem_limit_bytes=62 * 2**20),
        cost_estimate=pl.CostEstimate(flops=60 * 10**9, bytes_accessed=120 * 10**6, transcendentals=5 * 10**6),
    )(mid_low, middle, cotangent, alpha_ffn, scales[:1], scales[1:], *weights)


def adam_kernel(places, per, *refs):
    grads = refs[:places]
    w_ref, m_ref, v_ref, w_out, m_out, v_out = refs[places:]

    def update(g_ref):
        def step(i, _):
            part = pl.ds(pl.multiple_of(i * 16, 16), 16)
            new, first, second = adam(
                w_ref[part, :], g_ref[part, :].astype(F32), m_ref[part, :], v_ref[part, :], RATE, DECAY
            )
            w_out[part, :] = rownorm(new)[0]
            m_out[part, :] = first
            v_out[part, :] = second
            return 0

        lax.fori_loop(0, w_ref.shape[0] // 16, step, 0)

    for n in range(places):
        @pl.when(pl.program_id(0) // per == n)
        def _(n=n):
            update(grads[n])


def adam_rows(weight, grads, first, second):
    places = len(grads)
    _, per, piece, _ = grads[0][0].shape
    spec = pl.BlockSpec((None, piece, D), lambda p: (p, 0, 0))

    def grad_spec(n, index):
        return pl.BlockSpec((None, None, piece, D), lambda p: (index, jnp.clip(p - n * per, 0, per - 1), 0, 0))

    shape = jax.ShapeDtypeStruct((places * per, piece, D), F32)
    news = pl.pallas_call(
        functools.partial(adam_kernel, places, per),
        grid=(places * per,),
        out_shape=(shape,) * 3,
        in_specs=[grad_spec(n, index) for n, (_, index) in enumerate(grads)] + [spec] * 3,
        out_specs=(spec,) * 3,
        compiler_params=pltpu.CompilerParams(vmem_limit_bytes=40 * 2**20),
        cost_estimate=pl.CostEstimate(flops=20 * weight.size, bytes_accessed=26 * weight.size, transcendentals=0),
    )(*(array for array, _ in grads), *(old.reshape(shape.shape) for old in (weight, first, second)))
    return tuple(new.reshape(weight.shape) for new in news)


QUERY_BLOCK = 256
PAIR = 2 * HEAD_DIM
PAIRS = HEADS // 2


def head_ones():
    row = lax.broadcasted_iota(jnp.int32, (PAIR, PAIR), 0) // HEAD_DIM
    col = lax.broadcasted_iota(jnp.int32, (PAIR, PAIR), 1) // HEAD_DIM
    return (row == col).astype(F32).astype(BF16)


def head_sum(value, ones):
    high = value.astype(BF16)
    rest = (value - high.astype(F32)).astype(BF16)
    return dot(high, ones) + dot(rest, ones)


def of_head(value, head):
    lane = lax.broadcasted_iota(jnp.int32, value.shape, 1) // HEAD_DIM
    return jnp.where(lane == head, value, jnp.zeros_like(value))


def attend_pair(h_ref, wq_ref, wq2_ref, wk_ref, wk2_ref, wv_ref, wv2_ref, gain_ref, bias_ref, qp_ref, kp_ref, v_ref, o_ref, lse_ref,
                key_buf, query_buf, value_buf):
    cols = h_ref.shape[0]
    rows = qp_ref.shape[0]
    span = bias_ref.shape[1]
    ones = head_ones()
    gain = gain_ref[...]
    weights = jnp.concatenate([wk_ref[...], wk2_ref[...], wv_ref[...], wv2_ref[...]], 0)
    query_weights = jnp.concatenate([wq_ref[...], wq2_ref[...]], 0)

    def project(i, _):
        part = pl.ds(pl.multiple_of(i * QUERY_BLOCK, QUERY_BLOCK), QUERY_BLOCK)
        both = dot_nt(h_ref[part, :], weights)
        keys = both[:, :PAIR]
        kp_ref[part, :] = keys
        factor = lax.rsqrt(head_sum(keys * keys, ones) + SMALL)
        key_buf[part, :] = (keys * factor * gain).astype(BF16)
        values = both[:, PAIR:].astype(BF16)
        v_ref[part, :] = values
        value_buf[part, :PAIR] = values
        value_buf[part, PAIR:] = jnp.ones_like(values)
        return 0

    lax.fori_loop(0, cols // QUERY_BLOCK, project, 0)

    def project_queries(i, _):
        part = pl.ds(pl.multiple_of(i * QUERY_BLOCK, QUERY_BLOCK), QUERY_BLOCK)
        own = pl.ds(pl.multiple_of(cols - rows + i * QUERY_BLOCK, QUERY_BLOCK), QUERY_BLOCK)
        queries = dot_nt(h_ref[own, :], query_weights)
        qp_ref[part, :] = queries
        factor = lax.rsqrt(head_sum(queries * queries, ones) + SMALL)
        scaled = (queries * factor * gain).astype(BF16).astype(F32) * math.sqrt(HEAD_DIM)
        query_buf[part, :] = scaled.astype(BF16)
        return 0

    lax.fori_loop(0, rows // QUERY_BLOCK, project_queries, 0)
    for i in range(rows // QUERY_BLOCK):
        part = pl.ds(i * QUERY_BLOCK, QUERY_BLOCK)
        reach = pl.ds(i * QUERY_BLOCK, span)
        sides = []
        for head in range(2):
            scores = dot_nt(of_head(query_buf[part, :], head), key_buf[reach, :])
            probs = jnp.exp(scores + bias_ref[part, :]).astype(BF16)
            both = dot(probs, value_buf[reach, :])
            total = both[:, PAIR:]
            sides.append(both[:, :PAIR] / total)
            lse_ref[head : head + 1, part] = jnp.log(total).T[:1, :]
        lane = lax.broadcasted_iota(jnp.int32, sides[0].shape, 1)
        o_ref[part, :] = jnp.where(lane < HEAD_DIM, sides[0], sides[1]).astype(BF16)


def back_pair(qp_ref, kp_ref, v_ref, o_ref, da_ref, wo_ref, wo2_ref, gain_ref, bias_ref, lse_ref,
              dq_ref, dk_ref, dv_ref, sum_ref, key_buf, key_turned, k_total, v_total):
    cols = kp_ref.shape[0]
    rows = qp_ref.shape[0]
    span = bias_ref.shape[1]
    ones = head_ones()
    gain = gain_ref[...]
    weights = jnp.concatenate([wo_ref[...], wo2_ref[...]], 0)

    def keys_of(i, _):
        part = pl.ds(pl.multiple_of(i * QUERY_BLOCK, QUERY_BLOCK), QUERY_BLOCK)
        keys = kp_ref[part, :]
        factor = lax.rsqrt(head_sum(keys * keys, ones) + SMALL)
        low = keys * factor * gain
        key_buf[part, :] = low.astype(BF16)
        key_turned[:, part] = low.T.astype(BF16)
        k_total[part, :] = jnp.zeros_like(keys)
        v_total[part, :] = jnp.zeros_like(keys)
        return 0

    lax.fori_loop(0, cols // QUERY_BLOCK, keys_of, 0)
    for i in range(rows // QUERY_BLOCK):
        part = pl.ds(i * QUERY_BLOCK, QUERY_BLOCK)
        reach = pl.ds(i * QUERY_BLOCK, span)
        queries = qp_ref[part, :]
        factor = lax.rsqrt(head_sum(queries * queries, ones) + SMALL)
        hat = queries * factor
        scaled = ((hat * gain).astype(BF16).astype(F32) * math.sqrt(HEAD_DIM)).astype(BF16)
        back = dot_nt(da_ref[part, :], weights).astype(BF16)
        inner = (back.astype(F32) * o_ref[part, :].astype(F32)).T
        sides = []
        for head in range(2):
            mine = slice(head * HEAD_DIM, (head + 1) * HEAD_DIM)
            query, grad = of_head(scaled, head), of_head(back, head)
            scores = dot_nt(key_buf[reach, :], query)
            probs = jnp.exp(scores + bias_ref[i] - lse_ref[head : head + 1, part])
            v_total[reach, :] += dot(probs.astype(BF16), grad)
            delta = jnp.sum(inner[mine, :], 0, keepdims=True)
            grad_scores = (probs * (dot_nt(v_ref[reach, :], grad) - delta)).astype(BF16)
            k_total[reach, :] += dot(grad_scores, query)
            sides.append(dot(key_turned[mine, reach], grad_scores))
        grad_q = jnp.concatenate(sides, 0).T * math.sqrt(HEAD_DIM)
        sums = jnp.sum(grad_q * hat, 0, keepdims=True)
        if i == 0:
            sum_ref[...] = jnp.broadcast_to(sums, sum_ref.shape)
        else:
            sum_ref[...] += jnp.broadcast_to(sums, sum_ref.shape)
        grad_q = grad_q * gain
        dq_ref[part, :] = (factor * (grad_q - hat * head_sum(hat * grad_q, ones))).astype(BF16)

    def finish(i, _):
        part = pl.ds(pl.multiple_of(i * QUERY_BLOCK, QUERY_BLOCK), QUERY_BLOCK)
        keys = kp_ref[part, :]
        factor = lax.rsqrt(head_sum(keys * keys, ones) + SMALL)
        hat = keys * factor
        grad_k = k_total[part, :]
        sum_ref[...] += jnp.broadcast_to(jnp.sum(grad_k * hat, 0, keepdims=True), sum_ref.shape)
        grad_k = grad_k * gain
        dk_ref[part, :] = (factor * (grad_k - hat * head_sum(hat * grad_k, ones))).astype(BF16)
        dv_ref[part, :] = v_total[part, :].astype(BF16)
        return 0

    lax.fori_loop(0, cols // QUERY_BLOCK, finish, 0)


def head_rows(attn_low, matrix, second):
    heads = attn_low.shape[2]

    def index(p):
        head = 2 * p + second
        return (head // heads, matrix, lax.rem(head, heads), 0, 0)

    return pl.BlockSpec((None, None, None, HEAD_DIM, D), index)


def attention_forward(low_all, attn_low, gain_qk, bias, rows):
    cols = low_all.shape[0]
    span = bias.shape[1]
    side = lambda n: pl.BlockSpec((n, PAIR), lambda p: (0, p))
    whole = lambda *shape: pl.BlockSpec(shape, lambda p: (0,) * len(shape))
    return pl.pallas_call(
        attend_pair,
        grid=(PAIRS,),
        out_shape=(
            jax.ShapeDtypeStruct((rows, D), F32),
            jax.ShapeDtypeStruct((cols, D), F32),
            jax.ShapeDtypeStruct((cols, D), BF16),
            jax.ShapeDtypeStruct((rows, D), BF16),
            jax.ShapeDtypeStruct((PAIRS, 8, rows), F32),
        ),
        in_specs=[whole(cols, D)]
        + [head_rows(attn_low, j, second) for j in range(3) for second in range(2)]
        + [side(1), whole(rows, span)],
        out_specs=(side(rows), side(cols), side(cols), side(rows),
                   pl.BlockSpec((None, 8, rows), lambda p: (p, 0, 0))),
        scratch_shapes=[
            pltpu.VMEM((cols, PAIR), BF16),
            pltpu.VMEM((rows, PAIR), BF16),
            pltpu.VMEM((cols, 2 * PAIR), BF16),
        ],
        compiler_params=pltpu.CompilerParams(vmem_limit_bytes=56 * 2**20),
        cost_estimate=pl.CostEstimate(flops=20 * 10**9, bytes_accessed=30 * 10**6, transcendentals=13 * 10**6),
    )(low_all, *[attn_low] * 6, gain_qk, bias)


def attention_backward(q_pre, k_pre, value_all, o_low, grad_spre, attn_low, gain_qk, bias_turned, lse):
    rows, cols = q_pre.shape[0], k_pre.shape[0]
    side = lambda n: pl.BlockSpec((n, PAIR), lambda p: (0, p))
    whole = lambda *shape: pl.BlockSpec(shape, lambda p: (0,) * len(shape))
    stat = pl.BlockSpec((None, 8, rows), lambda p: (p, 0, 0))
    return pl.pallas_call(
        back_pair,
        grid=(PAIRS,),
        out_shape=(
            jax.ShapeDtypeStruct((rows, D), BF16),
            jax.ShapeDtypeStruct((cols, D), BF16),
            jax.ShapeDtypeStruct((cols, D), BF16),
            jax.ShapeDtypeStruct((PAIRS, 8, PAIR), F32),
        ),
        in_specs=[
            side(rows), side(cols), side(cols), side(rows), whole(rows, D),
            head_rows(attn_low, 3, 0), head_rows(attn_low, 3, 1),
            pl.BlockSpec((None, 1, PAIR), lambda p: (p, 0, 0)), whole(*bias_turned.shape), stat,
        ],
        out_specs=(side(rows), side(cols), side(cols), pl.BlockSpec((None, 8, PAIR), lambda p: (p, 0, 0))),
        scratch_shapes=[
            pltpu.VMEM((cols, PAIR), BF16),
            pltpu.VMEM((PAIR, cols), BF16),
            pltpu.VMEM((cols, PAIR), F32),
            pltpu.VMEM((cols, PAIR), F32),
        ],
        compiler_params=pltpu.CompilerParams(vmem_limit_bytes=56 * 2**20),
        cost_estimate=pl.CostEstimate(flops=30 * 10**9, bytes_accessed=40 * 10**6, transcendentals=13 * 10**6),
    )(q_pre, k_pre, value_all, o_low, grad_spre, attn_low, attn_low, gain_qk, bias_turned, lse)


START = 5


def gather_kernel(shards, attn_ref, ffn_ref, gains_ref, tokens_ref, bias_ref,
                  out, gains_out, h_out, qp_out, kp_out, v_out, o_out, lse_ref,
                  wide, low, mine, wide_sem, low_sem, mine_sem, line_send, line_recv, plane_send, beside_recv,
                  above_recv, across_recv, pair_send, pair_recv, gains_send, gains_recv, tokens_send,
                  tokens_recv, local_sem, gains_buf, before, h_buf, load_sem, store_sem,
                  weight_buf, gain_row, qp_buf, kp_buf, v_buf, o_buf, key_buf, query_buf, value_buf):
    core, chip, beside, above, across = place()
    line = lax.axis_index("shard")
    rep = 2 * chip + core
    sibling = 2 * chip + 1 - core
    to_beside, to_above = 2 * beside + core, 2 * above + core
    piece = attn_ref.shape[1]
    rows = tokens_ref.shape[0]
    heads = 2 * piece // HEAD_DIM
    others = shards - 1
    steps = 4 * others
    greet(shards)

    def rows_of(m, shard, rep, start=0, size=None):
        first = pl.multiple_of(rep * piece + start, 16)
        return out.at[m, shard, pl.ds(first, piece if size is None else size)]

    def source(n):
        low_side = 2 * line < shards
        edge = lax.select(low_side, line, shards - 1 - line)
        near = lax.select(lax.rem(n, 2) == 0, edge - 1 - n // 2, edge + 1 + n // 2)
        found = lax.select(n < 2 * edge, near, n + 1)
        return lax.select(low_side, found, shards - 1 - found)

    def own_send(m):
        @pl.when(line < shards - 1)
        def _():
            remote(mine.at[m], rows_of(m, line, rep), line_send, line_recv.at[m, line], rep, line + 1).start()

        @pl.when(line > 0)
        def _():
            remote(mine.at[m], rows_of(m, line, rep), line_send, line_recv.at[m, line], rep, line - 1).start()

    def fetch(index, slot):
        @pl.when(index < 8)
        def _():
            pltpu.make_async_copy(attn_ref.at[lax.rem(index, 8)], wide.at[slot], wide_sem.at[slot]).start()

        @pl.when(index >= 8)
        def _():
            pltpu.make_async_copy(
                ffn_ref.at[jnp.maximum(index // 8 - 1, 0), lax.rem(index, 8)], wide.at[slot], wide_sem.at[slot]
            ).start()

    def store(index, slot):
        return pltpu.make_async_copy(low.at[slot], rows_of(index // 8, line, lax.rem(index, 8)), low_sem.at[slot])

    def lower(src, dst):
        def step(i, _):
            part = pl.ds(pl.multiple_of(i * 32, 32), 32)
            dst[part, :] = src[part, :].astype(BF16)
            return 0

        lax.fori_loop(0, piece // 32, step, 0)

    for n in range(1, shards):
        other = lax.rem(line + n, shards)
        remote(gains_ref, gains_buf.at[line], gains_send, gains_recv.at[line], rep, other).start()
    pltpu.make_async_copy(gains_ref, gains_buf.at[line], local_sem).start()
    own = pl.ds(2 * rows, rows)
    pltpu.make_async_copy(tokens_ref, h_buf.at[own], load_sem.at[0, 0]).start()
    for m in range(4):
        origin = attn_ref.at[rep] if m == 0 else ffn_ref.at[m - 1, rep]
        pltpu.make_async_copy(origin, wide.at[m], mine_sem.at[m]).start()
    for m in range(4):
        arrived(wide.at[m], mine_sem.at[m])
        lower(wide.at[m], mine.at[m])
        if m == 0:
            own_send(0)

            @pl.when(line < shards - 1)
            def _():
                remote(tokens_ref, before.at[1], tokens_send, tokens_recv.at[1], rep, line + 1).start()

    for n in range(2):
        fetch(n, n)

    def norm_rows(source, first):
        def step(i, _):
            at = pl.multiple_of(first + i * 32, 32)
            value = source[pl.ds(pl.multiple_of(i * 32, 32), 32), :].astype(F32)
            h_buf[pl.ds(at, 32), :] = rownorm(value)[0].astype(BF16)
            return 0

        lax.fori_loop(0, rows // 32, step, 0)

    def clear_rows(first):
        h_buf[pl.ds(first, rows), :] = jnp.zeros((rows, D), BF16)

    arrived(h_buf.at[own], load_sem.at[0, 0])
    norm_rows(h_buf.at[own], 2 * rows)

    def loads(p, slot):
        copies = []
        for j in range(3):
            for second in range(2):
                head = 2 * p + second
                first = pl.multiple_of(2 * piece * j + HEAD_DIM * lax.rem(head, heads), HEAD_DIM)
                copies.append(
                    pltpu.make_async_copy(
                        out.at[0, head // heads, pl.ds(first, HEAD_DIM)], weight_buf.at[slot, 2 * j + second],
                        load_sem.at[slot, 2 * j + second],
                    )
                )
        return copies

    def stores(p, slot):
        lanes = pl.ds(pl.multiple_of(p * PAIR, PAIR), PAIR)
        return [
            pltpu.make_async_copy(buf.at[slot], ref.at[:, lanes], store_sem.at[slot, n])
            for n, (ref, buf) in enumerate(((qp_out, qp_buf), (kp_out, kp_buf), (v_out, v_buf), (o_out, o_buf)))
        ]

    def pair(p):
        slot = lax.rem(p, 2)

        @pl.when(p + 1 < PAIRS)
        def _():
            for copy in loads(p + 1, 1 - slot):
                copy.start()

        for copy in loads(p, slot):
            copy.wait()

        @pl.when(p >= 2)
        def _():
            for copy in stores(p - 2, slot):
                copy.wait()

        row = lax.broadcasted_iota(jnp.int32, (8, PAIR), 0)
        left, right = (
            jnp.sum(
                jnp.where(row == lax.rem(2 * p + n, heads), gains_buf[(2 * p + n) // heads, :8, :PAIR], 0.0),
                0, keepdims=True,
            )
            for n in range(2)
        )
        lane = lax.broadcasted_iota(jnp.int32, (1, PAIR), 1)
        gain_row[...] = jnp.where(lane < HEAD_DIM, left, right)
        attend_pair(
            h_buf, *(weight_buf.at[slot, n] for n in range(6)), gain_row, bias_ref, qp_buf.at[slot],
            kp_buf.at[slot], v_buf.at[slot], o_buf.at[slot], lse_ref.at[p], key_buf, query_buf, value_buf,
        )
        for copy in stores(p, slot):
            copy.start()

    def begin(c):
        m, origin = c // others, source(lax.rem(c, others))
        got = rows_of(m, origin, rep)
        arrived(got, line_recv.at[m, origin])

        @pl.when((origin < line) & (line < shards - 1))
        def _():
            remote(got, got, line_send, line_recv.at[m, origin], rep, line + 1).start()

        @pl.when((origin > line) & (line > 0))
        def _():
            remote(got, got, line_send, line_recv.at[m, origin], rep, line - 1).start()

        remote(got, got, plane_send, beside_recv.at[m, origin], to_beside, line).start()
        remote(got, got, plane_send, above_recv.at[m, origin], to_above, line).start()
        remote(got, got, pair_send, pair_recv.at[m], sibling, line).start()

    def middle(c):
        m, origin = c // others, source(lax.rem(c, others))
        got = rows_of(m, origin, to_beside)
        arrived(got, beside_recv.at[m, origin])
        part = rows_of(m, origin, to_beside, 0, HALF)
        remote(part, part, plane_send, across_recv.at[m, origin, 0], to_above, line).start()
        remote(got, got, pair_send, pair_recv.at[m], sibling, line).start()
        got = rows_of(m, origin, to_above)
        arrived(got, above_recv.at[m, origin])
        part = rows_of(m, origin, to_above, HALF, piece - HALF)
        remote(part, part, plane_send, across_recv.at[m, origin, 1], to_beside, line).start()
        remote(got, got, pair_send, pair_recv.at[m], sibling, line).start()

    def last(c):
        m, origin = c // others, source(lax.rem(c, others))
        got = rows_of(m, origin, 2 * across + core)
        arrived(rows_of(m, origin, 2 * across + core, 0, HALF), across_recv.at[m, origin, 0])
        arrived(rows_of(m, origin, 2 * across + core, HALF, piece - HALF), across_recv.at[m, origin, 1])
        remote(got, got, pair_send, pair_recv.at[m], sibling, line).start()

    def local(t):
        for n in range(2):
            index = 2 * t + n
            slot = 2 * lax.rem(t, 2) + n
            arrived(wide.at[slot], wide_sem.at[slot])

            @pl.when(index + 2 < 32)
            def _():
                fetch(index + 2, lax.rem(slot + 2, 4))

            @pl.when(t >= 2)
            def _():
                store(index - 4, slot).wait()

            lower(wide.at[slot], low.at[slot])
            store(index, slot).start()

    def turn(t, _):
        @pl.when((lax.rem(t, others) == 0) & (t // others < 3))
        def _():
            own_send(t // others + 1)

        @pl.when(t < steps)
        def _():
            begin(t)

        @pl.when((t == 1) & (line > 0))
        def _():
            arrived(before.at[1], tokens_recv.at[1])

            @pl.when(line < shards - 1)
            def _():
                remote(before.at[1], before.at[0], tokens_send, tokens_recv.at[0], rep, line + 1).start()

            norm_rows(before.at[1], rows)

        @pl.when((t == 1) & (line == 0))
        def _():
            clear_rows(rows)

        @pl.when((t == 3) & (line > 1))
        def _():
            arrived(before.at[0], tokens_recv.at[0])
            norm_rows(before.at[0], 0)

        @pl.when((t == 3) & (line <= 1))
        def _():
            clear_rows(0)

        @pl.when((t >= 1) & (t < steps + 1))
        def _():
            middle(t - 1)

        @pl.when((t >= 2) & (t < steps + 2))
        def _():
            last(t - 2)

        local(t)

        @pl.when(t == START)
        def _():
            pltpu.make_async_copy(gains_ref, gains_buf.at[line], local_sem).wait()
            for n in range(1, shards):
                other = lax.rem(line + n, shards)
                arrived(gains_buf.at[other], gains_recv.at[other])
            arrived(out.at[0, pl.ds(0, others), pl.ds(0, 4 * piece)], pair_recv.at[0])
            for copy in loads(0, 0):
                copy.start()

        @pl.when((t >= START) & (t < START + PAIRS))
        def _():
            pair(t - START)

        return 0

    lax.fori_loop(0, 16, turn, 0)
    for n in range(4):
        store(28 + n, n).wait()
    gains_copy = pltpu.make_async_copy(gains_buf, gains_out, local_sem)
    h_copy = pltpu.make_async_copy(h_buf, h_out, load_sem.at[0, 0])
    gains_copy.start()
    h_copy.start()
    for p in (PAIRS - 2, PAIRS - 1):
        for copy in stores(p, p % 2):
            copy.wait()
    for m in range(1, 4):
        arrived(out.at[m, pl.ds(0, others), pl.ds(0, 4 * piece)], pair_recv.at[m])
    gains_copy.wait()
    h_copy.wait()

    @pl.when((line == 1) | (line == shards - 2))
    def _():
        arrived(before, tokens_send)

    @pl.when(line == 0)
    def _():
        arrived(before.at[0], tokens_send)

    @pl.when((line == 0) | (line == shards - 1))
    def _():
        arrived(out.at[:, 0, pl.ds(0, piece)], line_send)

    @pl.when((line > 0) & (line < shards - 1))
    def _():
        arrived(out.at[:, 0, pl.ds(0, 5 * piece)], line_send)

    arrived(out.at[:, pl.ds(0, others), pl.ds(0, 3 * piece)], plane_send)
    arrived(out.at[:, pl.ds(0, others), pl.ds(0, 4 * piece)], pair_send)
    arrived(gains_buf.at[pl.ds(0, others)], gains_send)


def gather_attend(attn_w, ffn_w, gains, tokens, bias, shards):
    piece = attn_w.shape[1]
    rows = tokens.shape[0]
    cols = rows + WINDOW
    any_space = pl.BlockSpec(memory_space=pl.ANY)
    vmem = pl.BlockSpec(memory_space=pltpu.VMEM)
    dma = pltpu.SemaphoreType.DMA
    return pl.pallas_call(
        functools.partial(gather_kernel, shards),
        out_shape=(
            jax.ShapeDtypeStruct((4, shards, 8 * piece, D), BF16),
            jax.ShapeDtypeStruct((shards,) + gains.shape, F32),
            jax.ShapeDtypeStruct((cols, D), BF16),
            jax.ShapeDtypeStruct((rows, D), F32),
            jax.ShapeDtypeStruct((cols, D), F32),
            jax.ShapeDtypeStruct((cols, D), BF16),
            jax.ShapeDtypeStruct((rows, D), BF16),
            jax.ShapeDtypeStruct((PAIRS, 8, rows), F32),
        ),
        in_specs=[any_space] * 4 + [vmem],
        out_specs=(any_space,) * 7 + (vmem,),
        scratch_shapes=[
            pltpu.VMEM((4, piece, D), F32),
            pltpu.VMEM((4, piece, D), BF16),
            pltpu.VMEM((4, piece, D), BF16),
            dma((4,)), dma((4,)), dma((4,)), dma(()), dma((4, shards)), dma(()), dma((4, shards)),
            dma((4, shards)), dma((4, shards, 2)), dma(()), dma((4,)), dma(()), dma((shards,)), dma(()),
            dma((2,)), dma(()),
            pltpu.VMEM((shards,) + gains.shape, F32),
            pltpu.VMEM((2, rows, D), BF16),
            pltpu.VMEM((cols, D), BF16),
            dma((2, 6)), dma((2, 4)),
            pltpu.VMEM((2, 6, HEAD_DIM, D), BF16),
            pltpu.VMEM((1, PAIR), F32),
            pltpu.VMEM((2, rows, PAIR), F32),
            pltpu.VMEM((2, cols, PAIR), F32),
            pltpu.VMEM((2, cols, PAIR), BF16),
            pltpu.VMEM((2, rows, PAIR), BF16),
            pltpu.VMEM((cols, PAIR), BF16),
            pltpu.VMEM((rows, PAIR), BF16),
            pltpu.VMEM((cols, 2 * PAIR), BF16),
        ],
        compiler_params=pltpu.CompilerParams(
            collective_id=3, has_side_effects=True, vmem_limit_bytes=60 * 2**20
        ),
        cost_estimate=pl.CostEstimate(flops=20 * 10**9, bytes_accessed=2 * 10**8, transcendentals=13 * 10**6),
    )(attn_w, ffn_w, gains, tokens, bias)


def attention_back_kernel(shards, grads_ref, qp_ref, kp_ref, v_ref, o_ref, weight_ref, da_ref, gain_ref, bias_ref,
                          lse_ref, out, dq_ref, dk_ref, dv_ref, sum_ref,
                          qp_buf, kp_buf, v_buf, o_buf, wo_buf, dq_buf, dk_buf, dv_buf, load_sem, store_sem,
                          key_buf, key_turned, k_total, v_total, *scratch):
    turns, turn, finish = reduction((grads_ref.at[0], grads_ref.at[1]), out, scratch)
    height = weight_ref.shape[2] // 4
    heads = height // HEAD_DIM

    def loads(p, slot):
        lanes = pl.ds(pl.multiple_of(p * PAIR, PAIR), PAIR)
        copies = [
            pltpu.make_async_copy(ref.at[:, lanes], buf.at[slot], load_sem.at[slot, n])
            for n, (ref, buf) in enumerate(((qp_ref, qp_buf), (kp_ref, kp_buf), (v_ref, v_buf), (o_ref, o_buf)))
        ]
        for second in range(2):
            head = 2 * p + second
            copies.append(
                pltpu.make_async_copy(
                    weight_ref.at[
                        0, head // heads,
                        pl.ds(pl.multiple_of(3 * height + HEAD_DIM * lax.rem(head, heads), HEAD_DIM), HEAD_DIM),
                    ],
                    wo_buf.at[slot, second], load_sem.at[slot, 4 + second],
                )
            )
        return copies

    def stores(p, slot):
        lanes = pl.ds(pl.multiple_of(p * PAIR, PAIR), PAIR)
        return [
            pltpu.make_async_copy(buf.at[slot], ref.at[:, lanes], store_sem.at[slot, n])
            for n, (ref, buf) in enumerate(((dq_ref, dq_buf), (dk_ref, dk_buf), (dv_ref, dv_buf)))
        ]

    def pair(p):
        slot = lax.rem(p, 2)

        @pl.when(p + 1 < PAIRS)
        def _():
            for copy in loads(p + 1, 1 - slot):
                copy.start()

        for copy in loads(p, slot):
            copy.wait()

        @pl.when(p >= 2)
        def _():
            for copy in stores(p - 2, slot):
                copy.wait()

        back_pair(
            qp_buf.at[slot], kp_buf.at[slot], v_buf.at[slot], o_buf.at[slot], da_ref, wo_buf.at[slot, 0],
            wo_buf.at[slot, 1], gain_ref.at[p], bias_ref, lse_ref.at[p], dq_buf.at[slot], dk_buf.at[slot],
            dv_buf.at[slot], sum_ref.at[p], key_buf, key_turned, k_total, v_total,
        )
        for copy in stores(p, slot):
            copy.start()

    greet(shards)
    for copy in loads(0, 0):
        copy.start()

    def step(t, _):
        turn(t)

        @pl.when(t < PAIRS)
        def _():
            pair(t)

        return 0

    lax.fori_loop(0, max(turns, PAIRS), step, 0)
    for p in (PAIRS - 2, PAIRS - 1):
        for copy in stores(p, p % 2):
            copy.wait()
    finish()


def attention_back_reduce(grads, q_pre, k_pre, value_all, o_low, attn_low, grad_spre, gain_qk, bias_turned, lse):
    _, shards, _, _, rows, _ = grads.shape
    tokens, cols = q_pre.shape[0], k_pre.shape[0]
    any_space = pl.BlockSpec(memory_space=pl.ANY)
    vmem = pl.BlockSpec(memory_space=pltpu.VMEM)
    dma = pltpu.SemaphoreType.DMA
    return pl.pallas_call(
        functools.partial(attention_back_kernel, shards),
        out_shape=(
            jax.ShapeDtypeStruct((2, 8, rows, D), BF16),
            jax.ShapeDtypeStruct((tokens, D), BF16),
            jax.ShapeDtypeStruct((cols, D), BF16),
            jax.ShapeDtypeStruct((cols, D), BF16),
            jax.ShapeDtypeStruct((PAIRS, 8, PAIR), F32),
        ),
        in_specs=[any_space] * 6 + [vmem] * 4,
        out_specs=(any_space,) * 4 + (vmem,),
        scratch_shapes=[
            pltpu.VMEM((2, tokens, PAIR), F32),
            pltpu.VMEM((2, cols, PAIR), F32),
            pltpu.VMEM((2, cols, PAIR), BF16),
            pltpu.VMEM((2, tokens, PAIR), BF16),
            pltpu.VMEM((2, 2, HEAD_DIM, D), BF16),
            pltpu.VMEM((2, tokens, PAIR), BF16),
            pltpu.VMEM((2, cols, PAIR), BF16),
            pltpu.VMEM((2, cols, PAIR), BF16),
            dma((2, 6)), dma((2, 3)),
            pltpu.VMEM((cols, PAIR), BF16),
            pltpu.VMEM((PAIR, cols), BF16),
            pltpu.VMEM((cols, PAIR), F32),
            pltpu.VMEM((cols, PAIR), F32),
        ] + reduction_scratch(2, shards, rows),
        compiler_params=pltpu.CompilerParams(
            collective_id=1, has_side_effects=True, vmem_limit_bytes=62 * 2**20
        ),
        cost_estimate=pl.CostEstimate(flops=30 * 10**9, bytes_accessed=2 * 10**8, transcendentals=13 * 10**6),
    )(grads, q_pre, k_pre, value_all, o_low, attn_low, grad_spre, gain_qk, bias_turned, lse)


def attention_grads_kernel(dq_ref, dk_ref, dv_ref, o_ref, h_ref, da_ref, out):
    matrix = pl.program_id(0)
    rows = dq_ref.shape[0]
    cols = h_ref.shape[0]
    for m, (left, right) in enumerate(
        (
            (dq_ref, h_ref.at[pl.ds(cols - rows, rows)]),
            (dk_ref, h_ref),
            (dv_ref, h_ref),
            (o_ref, da_ref),
        )
    ):
        @pl.when(matrix == m)
        def _(left=left, right=right):
            out[...] = dot_tn(left[...], right[...]).astype(BF16).reshape(out.shape)


def attention_grads(dq, dk, dv, o_low, low_all, grad_spre, shards):
    rows, cols = dq.shape[0], dk.shape[0]
    per = D // shards
    group = math.lcm(per, 2 * HEAD_DIM) if per % (2 * HEAD_DIM) else per
    group = max(group, D // 2) if (D // 2) % group == 0 else group
    whole = lambda *shape: pl.BlockSpec(shape, lambda m, g: (0,) * len(shape))
    side = lambda n, k: pl.BlockSpec((n, group), lambda m, g: (0, lax.select(m == k, g, lax.select(m < k, 0, D // group - 1))))
    return pl.pallas_call(
        attention_grads_kernel,
        grid=(4, D // group),
        out_shape=jax.ShapeDtypeStruct((shards, 4, per, D), BF16),
        in_specs=[side(rows, 0), side(cols, 1), side(cols, 2), side(rows, 3), whole(cols, D), whole(rows, D)],
        out_specs=pl.BlockSpec((group // per, None, per, D), lambda m, g: (g, m, 0, 0)),
        compiler_params=pltpu.CompilerParams(vmem_limit_bytes=56 * 2**20),
        cost_estimate=pl.CostEstimate(flops=14 * 10**9, bytes_accessed=30 * 10**6, transcendentals=0),
    )(dq, dk, dv, o_low, low_all, grad_spre)


def body(
    tokens,
    doc_lengths,
    cotangent,
    attn_w,
    ffn_w,
    attn_m,
    attn_v,
    ffn_m,
    ffn_v,
    gains_d,
    gains_ff,
    gd_m,
    gd_v,
    gf_m,
    gf_v,
):
    shards = lax.axis_size("shard")
    reps = lax.axis_size("rep")
    device_index = lax.axis_index("shard")
    rows = tokens.shape[0]
    reach = WINDOW // rows
    cols = (reach + 1) * rows
    attn_rows = attn_w.shape[1]
    ffn_rows = ffn_w.shape[1]
    ffn_all = shards * ffn_rows
    piece = ffn_rows // reps

    lengths_row = doc_lengths[0]
    starts = jnp.cumsum(lengths_row) - lengths_row
    positions = device_index * rows + jnp.arange(rows, dtype=jnp.int32)
    doc_start = jnp.max(
        jnp.where(starts[None, :] <= positions[:, None], starts[None, :], 0), axis=1
    )
    blocks = rows // QUERY_BLOCK
    span = WINDOW + QUERY_BLOCK
    query = jnp.arange(rows, dtype=jnp.int32).reshape(blocks, QUERY_BLOCK)
    lead = query[:, :1] - reach * rows + jnp.arange(span, dtype=jnp.int32)
    ahead = query[:, :, None] - lead[:, None, :]
    floor = (doc_start - device_index * rows).reshape(blocks, QUERY_BLOCK, 1)
    mask = (ahead >= 0) & (ahead < WINDOW) & (lead[:, None, :] >= floor)
    bias = jnp.where(mask, 0.0, NEGATIVE).astype(F32)
    bias_turned = bias.transpose(0, 2, 1)
    bias = bias.reshape(rows, span)
    cut = gains_d.size
    small = jnp.concatenate([gains_d.reshape(-1), gains_ff.reshape(-1)]).astype(BF16)
    normed_in, factor_in = rownorm(tokens.astype(F32))
    fast = reps == 8 and shards == 4 and attn_rows % HEAD_DIM == 0 and reach == 2
    if fast:
        small = small.astype(F32)
        qk_heads = small[:attn_rows].reshape(-1, HEAD_DIM)
        qk_heads = jnp.pad(
            jnp.concatenate([qk_heads, qk_heads], 1), ((0, 8 - qk_heads.shape[0]), (0, D - PAIR))
        )
        small = jnp.pad(small, (0, 8 * D - small.size)).reshape(8, D)
        gathered, small, low_all, q_pre, k_pre, value_all, o_low, lse = gather_attend(
            attn_w.reshape(8, piece, D),
            ffn_w.reshape(3, 8, piece, D),
            jnp.concatenate([qk_heads, small]),
            tokens,
            bias,
            shards,
        )
        small = small[:, 8:].reshape(shards, -1)[:, : cut + gains_ff.size]
        query_low, key_low, value_low, out_low = (
            gathered[0, :, j * attn_rows : (j + 1) * attn_rows].reshape(D, D) for j in range(4)
        )
        ffn_low = [gathered.reshape(4, ffn_all, D)] * 3
        firsts = (1, 2, 3)
    else:
        attn_low = (
            gather_rows(attn_w.reshape(4 * attn_rows, D).astype(BF16))
            .reshape(shards, 4, attn_rows, D)
            .transpose(1, 0, 2, 3)
            .reshape(1, 4, HEADS, HEAD_DIM, D)
        )
        ffn_low = [gather_rows(ffn_w[m].astype(BF16)).reshape(1, ffn_all, D) for m in range(3)]
        firsts = (0, 0, 0)
        small = lax.all_gather(small, "shard", axis=0).astype(F32)
        query_low, key_low, value_low, out_low = (attn_low[0, j].reshape(D, D) for j in range(4))
    gd_all = small[:, :cut].reshape(shards, 3, -1).transpose(1, 0, 2).reshape(3, D)
    gf_all = small[:, cut:].reshape(shards, 2, ffn_rows).transpose(1, 0, 2).reshape(2, ffn_all)
    gain_qk = gd_all[0]
    alpha_attn = gd_all[1]
    alpha_ffn = gd_all[2]

    if not fast:
        earlier = [from_behind(tokens, "shard", offset) for offset in range(reach, 0, -1)]
        low_all = rownorm(jnp.concatenate(earlier + [tokens], 0).astype(F32))[0].astype(BF16)
        q_pre, k_pre, value_all, o_low, lse = attention_forward(
            low_all, attn_low, gain_qk[None], bias, rows
        )
    in_low = low_all[-rows:]
    side, side_factor = rownorm(dot(o_low, out_low))
    middle, mid_factor = rownorm(normed_in + alpha_attn * (side - normed_in))
    mid_low = middle.astype(BF16)
    output, grad_mid, ffn_grads, down_grads, grad_scale_up, grad_scale_gate, grad_alpha_ffn = feed_forward(
        mid_low, middle, cotangent, alpha_ffn[None], gf_all, ffn_low, firsts
    )
    grad_mixed = norm_back(middle, mid_factor, grad_mid)
    grad_in = grad_mixed * (1.0 - alpha_attn)
    grad_alpha_attn = jnp.sum(grad_mixed * (side - normed_in), 0)
    grad_spre = norm_back(side, side_factor, grad_mixed * alpha_attn).astype(BF16)
    pair_gain = gain_qk.reshape(PAIRS, 1, PAIR)
    if fast:
        units = (shards, 4, 2, piece, D)
        sum_first, grad_qpre, grad_kpre, grad_vpre, gain_sums = attention_back_reduce(
            ffn_grads.reshape((2,) + units), q_pre, k_pre, value_all, o_low, gathered, grad_spre,
            pair_gain, bias_turned, lse,
        )
    else:
        grad_qpre, grad_kpre, grad_vpre, gain_sums = attention_backward(
            q_pre, k_pre, value_all, o_low, grad_spre, attn_low, pair_gain, bias_turned, lse
        )
    back_all = dot(grad_kpre, key_low) + dot(grad_vpre, value_low)
    grad_in = grad_in + dot(grad_qpre, query_low) + back_all[reach * rows :]
    back_parts = back_all[: reach * rows].reshape(reach, rows, D).astype(BF16)
    grad_gain_qk = gain_sums[:, 0].reshape(D)
    grad_gf = jnp.concatenate([grad_scale_up, grad_scale_gate])
    gd_rows = D // shards
    if fast:
        attn_grad = attention_grads(grad_qpre, grad_kpre, grad_vpre, o_low, low_all, grad_spre, shards)
        grad_gd = jnp.stack([grad_gain_qk, grad_alpha_attn, grad_alpha_ffn[0]])
        small = jnp.concatenate(
            [
                grad_gd.reshape(3, shards, gd_rows).transpose(1, 0, 2).reshape(shards, -1),
                grad_gf.reshape(2, shards, ffn_rows).transpose(1, 0, 2).reshape(shards, -1),
            ],
            1,
        )
        small = jnp.pad(small, ((0, 0), (0, 8 * D - small.shape[1]))).reshape(shards, 8, D)
        sum_last, sum_small, back_got = reduce_last(
            down_grads.reshape(units), attn_grad.reshape(units), small, back_parts
        )
        for n in range(reach):
            sent = device_index + reach - n < shards
            grad_in = grad_in + jnp.where(sent, back_got[n], 0).astype(F32)
        sum_small = sum_small.reshape(-1)
        sum_gd = sum_small[: 3 * gd_rows].reshape(3, gd_rows)
        sum_gf = sum_small[3 * gd_rows : 3 * gd_rows + 2 * ffn_rows].reshape(2, ffn_rows)
        attn_sums, ffn_sums = [(sum_last, 1)], [(sum_first, 0), (sum_first, 1), (sum_last, 0)]
    else:
        for n in range(reach):
            grad_in = grad_in + from_behind(back_parts[n], "shard", n - reach).astype(F32)
        attn_grad = jnp.stack(
            [
                dot_tn(grad_qpre, in_low),
                dot_tn(grad_kpre, low_all),
                dot_tn(grad_vpre, low_all),
                dot_tn(o_low, grad_spre),
            ]
        ).astype(BF16)
        attn_grad = attn_grad.reshape(4, shards, attn_rows, D).transpose(1, 0, 2, 3)
        attn_grad = attn_grad.reshape(shards, reps, 4 * attn_rows // reps, D).transpose(1, 0, 2, 3)
        attn_sums = [(reduce_rows(attn_grad).reshape(1, 4, attn_rows, D), 0)]
        ready = (shards, reps, piece, D)
        ffn_sums = [
            (reduce_rows(part.reshape(ready).transpose(1, 0, 2, 3)).reshape(1, 1, ffn_rows, D), 0)
            for part in (ffn_grads[0], ffn_grads[1], down_grads)
        ]
        grad_small = jnp.concatenate(
            [grad_gain_qk, grad_alpha_attn, grad_alpha_ffn[0], grad_gf.reshape(-1)]
        )
        grad_small = lax.psum(grad_small, ("rep", "shard"))
        sum_gd = lax.dynamic_slice_in_dim(
            grad_small[: 3 * D].reshape(3, D), device_index * gd_rows, gd_rows, 1
        )
        sum_gf = lax.dynamic_slice_in_dim(
            grad_small[3 * D :].reshape(2, ffn_all), device_index * ffn_rows, ffn_rows, 1
        )
    grad_tokens = norm_back(normed_in, factor_in, grad_in)

    attn_unit, attn_m_new, attn_v_new = adam_rows(attn_w, attn_sums, attn_m, attn_v)
    ffn_unit, ffn_m_new, ffn_v_new = adam_rows(ffn_w, ffn_sums, ffn_m, ffn_v)
    gd_new, gd_m_new, gd_v_new = adam(gains_d, sum_gd, gd_m, gd_v, GAIN_RATE, 0.0)
    gf_new, gf_m_new, gf_v_new = adam(gains_ff, sum_gf, gf_m, gf_v, GAIN_RATE, 0.0)
    return (
        output,
        grad_tokens,
        attn_unit,
        attn_m_new,
        attn_v_new,
        ffn_unit,
        ffn_m_new,
        ffn_v_new,
        gd_new,
        gd_m_new,
        gd_v_new,
        gf_new,
        gf_m_new,
        gf_v_new,
    )

def solution(mesh):
    return jax.shard_map(
        body,
        mesh=mesh,
        in_specs=(
            P(("rep", "shard"), None),
            P("rep", None),
            P(("rep", "shard"), None),
            P(None, "shard", None),
            P(None, "shard", None),
            P(None, "shard", None),
            P(None, "shard", None),
            P(None, "shard", None),
            P(None, "shard", None),
            P(None, "shard"),
            P(None, "shard"),
            P(None, "shard"),
            P(None, "shard"),
            P(None, "shard"),
            P(None, "shard"),
        ),
        out_specs=(
            P(("rep", "shard"), None),
            P(("rep", "shard"), None),
            P(None, "shard", None),
            P(None, "shard", None),
            P(None, "shard", None),
            P(None, "shard", None),
            P(None, "shard", None),
            P(None, "shard", None),
            P(None, "shard"),
            P(None, "shard"),
            P(None, "shard"),
            P(None, "shard"),
            P(None, "shard"),
            P(None, "shard"),
        ),
        check_vma=False,
    )
```

```python
import functools
import math

import jax
import jax.numpy as jnp
from jax import lax
from jax.experimental import pallas as pl
from jax.experimental.pallas import tpu as pltpu
from jax.sharding import PartitionSpec as P

D = 1280
HEADS = 20
HEAD_DIM = 64
WINDOW = 1024
STEP = 10


SMALL = 1e-06
NEGATIVE = -1e30
BETA_ONE = 0.9
BETA_TWO = 0.95
RATE = 0.02
GAIN_RATE = 1.0
DECAY = 0.1
TINY = 1e-08
F32 = jnp.float32
BF16 = jnp.bfloat16


def from_behind(block, axis, distance):
    devices = range(lax.axis_size(axis))
    route = [(i - distance, i) for i in devices if i - distance in devices]
    return lax.ppermute(block, axis, route)


def rownorm(value):
    factor = lax.rsqrt(jnp.sum(value * value, -1, keepdims=True) + SMALL)
    return (value * factor, factor)


def norm_back(normed, factor, grad):
    return factor * (grad - normed * jnp.sum(normed * grad, -1, keepdims=True))


def adam(weight, grad, first, second, rate, decay):
    first = BETA_ONE * first + (1.0 - BETA_ONE) * grad
    second = BETA_TWO * second + (1.0 - BETA_TWO) * grad * grad
    fix_one = 1.0 - BETA_ONE**STEP
    fix_two = 1.0 - BETA_TWO**STEP
    change = first / fix_one / (jnp.sqrt(second / fix_two) + TINY) + decay * weight
    return (weight - rate * change, first, second)


def dot(a, b):
    return jnp.dot(a, b, preferred_element_type=F32)


def dot_nt(a, b):
    return lax.dot_general(a, b, (((1,), (1,)), ((), ())), preferred_element_type=F32)


def dot_tn(a, b):
    return lax.dot_general(a, b, (((0,), (0,)), ((), ())), preferred_element_type=F32)


def gather_rows(shard_rows):
    reps = lax.axis_size("rep")
    piece = shard_rows.shape[0] // reps
    mine = lax.dynamic_slice_in_dim(shard_rows, lax.axis_index("rep") * piece, piece, 0)
    column = lax.all_gather(mine, "shard", axis=0)
    return lax.all_gather(column, "rep", axis=1)


def reduce_rows(grad):
    part = lax.psum_scatter(grad, "rep", scatter_dimension=0)
    part = lax.psum_scatter(part, "shard", scatter_dimension=0)
    return lax.all_gather(part, "rep", axis=0, tiled=True)


MESH = pl.DeviceIdType.MESH
HALF = 80


def place():
    rep = lax.axis_index("rep")
    core, chip = lax.rem(rep, 2), rep // 2
    beside, above = chip + 1 - 2 * lax.rem(chip, 2), chip + 2 - 4 * (chip // 2)
    return core, chip, beside, above, 3 - chip


def remote(src, dst, send, recv, rep, shard):
    return pltpu.make_async_remote_copy(
        src_ref=src, dst_ref=dst, send_sem=send, recv_sem=recv,
        device_id=(rep, shard), device_id_type=MESH,
    )


def arrived(ref, sem):
    pltpu.make_async_copy(ref, ref, sem).wait()


def greet(shards):
    rep, line = lax.axis_index("rep"), lax.axis_index("shard")
    barrier = pltpu.get_barrier_semaphore()
    for n in range(1, 8):
        pl.semaphore_signal(barrier, inc=1, device_id=(lax.rem(rep + n, 8), line), device_id_type=MESH)
    for n in range(1, shards):
        pl.semaphore_signal(barrier, inc=1, device_id=(rep, lax.rem(line + n, shards)), device_id_type=MESH)
    pl.semaphore_wait(barrier, 6 + shards)


def add_into(target, sources, rows):
    def step(i, _):
        part = pl.ds(pl.multiple_of(i * 16, 16), 16)
        if len(sources) == 1:
            target[part, :] = target[part, :] + sources[0][part, :]
        else:
            value = target[part, :].astype(F32)
            for source in sources:
                value = value + source[part, :].astype(F32)
            target[part, :] = value.astype(BF16)
        return 0

    lax.fori_loop(0, rows // 16, step, 0, unroll=5)


def reduction_scratch(count, shards, rows):
    steps = count * shards
    dma = pltpu.SemaphoreType.DMA
    return [
        pltpu.VMEM((steps, 4, rows, D), BF16),
        pltpu.VMEM((2, 4, rows, D), BF16),
        pltpu.VMEM((steps, rows, D), BF16),
        pltpu.VMEM((steps, 2, rows, D), BF16),
        pltpu.VMEM((count, shards + 1, rows, D), BF16),
        dma((2,)), dma(()), dma((steps,)), dma(()), dma((steps, 2)),
        dma(()), dma((steps, 2)), dma(()), dma((count, shards + 1)),
        dma(()), dma((count, 7)), dma(()),
    ]


REDUCTION_SCRATCH = 17


def reduction(grads, out, scratch):
    (acc, own, half, piece, below, own_sem, pair_send, pair_recv, half_send, half_recv,
     piece_send, piece_recv, line_send, line_recv, out_send, out_recv, out_local) = scratch
    count = len(grads)
    rows = own.shape[2]
    shards = below.shape[1] - 1
    core, chip, beside, above, across = place()
    line = lax.axis_index("shard")
    steps = count * shards

    def owner(step):
        i = lax.rem(step, shards)
        back = lax.select(i < shards - 1 - line, shards - 1 - i, i - (shards - 1 - line))
        ahead = lax.select(i < line, i, shards - 1 - (i - line))
        other = lax.select(2 * line < shards, back, ahead)
        return lax.select(i == shards - 1, line, other)

    def begin(step):
        slot = lax.rem(step, 2)
        for m in range(count):
            @pl.when(step // shards == m)
            def _(m=m):
                remote(
                    grads[m].at[owner(step), :, 1 - core], acc.at[step], pair_send, pair_recv.at[step],
                    2 * chip + 1 - core, line,
                ).start()
                pltpu.make_async_copy(grads[m].at[owner(step), :, core], own.at[slot], own_sem.at[slot]).start()

    def first(step):
        slot = lax.rem(step, 2)
        arrived(own.at[slot], own_sem.at[slot])
        arrived(acc.at[step], pair_recv.at[step])
        for q in range(4):
            add_into(acc.at[step, q], (own.at[slot, q],), rows)
        remote(acc.at[step, across, pl.ds(0, HALF)], half.at[step, pl.ds(0, HALF)],
               half_send, half_recv.at[step, 0], 2 * beside + core, line).start()
        remote(acc.at[step, across, pl.ds(HALF, rows - HALF)], half.at[step, pl.ds(HALF, rows - HALF)],
               half_send, half_recv.at[step, 1], 2 * above + core, line).start()

    def second(step):
        arrived(half.at[step, pl.ds(0, HALF)], half_recv.at[step, 0])
        arrived(half.at[step, pl.ds(HALF, rows - HALF)], half_recv.at[step, 1])
        add_into(acc.at[step, above, pl.ds(0, HALF)], (half.at[step, pl.ds(0, HALF)],), HALF)
        add_into(acc.at[step, beside, pl.ds(HALF, rows - HALF)],
                 (half.at[step, pl.ds(HALF, rows - HALF)],), rows - HALF)
        remote(acc.at[step, beside], piece.at[step, 0], piece_send, piece_recv.at[step, 0],
               2 * beside + core, line).start()
        remote(acc.at[step, above], piece.at[step, 1], piece_send, piece_recv.at[step, 1],
               2 * above + core, line).start()

    def pass_on(step):
        m, target = step // shards, owner(step)

        @pl.when(target > line)
        def _():
            remote(acc.at[step, chip], below.at[m, target], line_send, line_recv.at[m, target],
                   2 * chip + core, line + 1).start()

        @pl.when(target < line)
        def _():
            slot = lax.select(target == line - 1, shards, target)
            remote(acc.at[step, chip], below.at[m, slot], line_send, line_recv.at[m, slot],
                   2 * chip + core, line - 1).start()

    def outermost(step):
        target = owner(step)
        return ((target > line) & (line == 0)) | ((target < line) & (line == shards - 1))

    def third(step):
        for n in range(2):
            arrived(piece.at[step, n], piece_recv.at[step, n])
        add_into(acc.at[step, chip], (piece.at[step, 0], piece.at[step, 1]), rows)

        @pl.when(outermost(step))
        def _():
            pass_on(step)

    def along(step):
        m, target = step // shards, owner(step)

        def add_line(slot):
            arrived(below.at[m, slot], line_recv.at[m, slot])
            add_into(acc.at[step, chip], (below.at[m, slot],), rows)

        @pl.when(((target >= line) & (line > 0)) | ((target < line) & (line < shards - 1)))
        def _():
            add_line(target)

        @pl.when((target == line) & (line < shards - 1))
        def _():
            add_line(shards)

        @pl.when(jnp.logical_not(outermost(step)))
        def _():
            pass_on(step)

        @pl.when(target == line)
        def _():
            mine = 2 * chip + core
            pltpu.make_async_copy(acc.at[step, chip], out.at[m, mine], out_local).start()
            for n, other in enumerate((2 * beside + core, 2 * above + core, 2 * across + core, 2 * chip + 1 - core)):
                remote(acc.at[step, chip], out.at[m, mine], out_send, out_recv.at[m, n], other, line).start()

    def fourth(step):
        m = step // shards
        for n, origin in enumerate((2 * beside + core, 2 * above + core, 2 * across + core)):
            arrived(out.at[m, origin], out_recv.at[m, n])
            remote(out.at[m, origin], out.at[m, origin], out_send, out_recv.at[m, 4 + n],
                   2 * chip + 1 - core, line).start()

    def turn(t):
        @pl.when(t == 0)
        def _():
            begin(0)

        @pl.when(t + 1 < steps)
        def _():
            begin(t + 1)

        @pl.when(t < steps)
        def _():
            first(t)

        @pl.when((t >= 1) & (t < steps + 1))
        def _():
            second(t - 1)

        @pl.when((t >= 2) & (t < steps + 2))
        def _():
            third(t - 2)

        @pl.when((t >= 3) & (t < steps + 3))
        def _():
            along(t - 3)

        @pl.when((t >= 5) & (t < steps + 5) & (lax.rem(t - 5, shards) == shards - 1))
        def _():
            fourth(t - 5)

    def finish():
        for m in range(count):
            for n in range(4):
                arrived(out.at[m, 0], out_recv.at[m, 3 + n])
        arrived(out.at[:, 0], out_local)
        arrived(out.at[:, pl.ds(0, 7)], out_send)
        arrived(acc, pair_send)
        arrived(half, half_send)
        arrived(piece, piece_send)
        arrived(below.at[:, pl.ds(0, shards - 1)], line_send)

    return steps + 5, turn, finish


def last_kernel(shards, down_ref, attn_ref, gains_ref, dq_ref, dk_ref, dv_ref, weight_ref,
                out, gains_out, back_out, own_out,
                line_got, plane_got, mine, line_send, line_recv, plane_send, plane_recv, back_send, back_recv,
                weight_buf, left_buf, parts, weight_sem, left_sem, *scratch):
    rep, line = lax.axis_index("rep"), lax.axis_index("shard")
    rows, cols = dq_ref.shape[0], dk_ref.shape[0]
    reach = back_out.shape[0]
    per = rows // BACK_BLOCK
    height = weight_ref.shape[2] // 4
    turns, turn, finish = reduction((down_ref, attn_ref), out, scratch)
    greet(shards)
    for n in range(1, shards):
        other = lax.rem(line + n, shards)
        remote(gains_ref.at[other], line_got.at[n - 1], line_send, line_recv.at[n - 1], rep, other).start()
    for j in range(3):
        for shard in range(shards):
            pltpu.make_async_copy(
                weight_ref.at[0, shard, pl.ds(j * height, height)],
                weight_buf.at[j, pl.ds(shard * height, height)], weight_sem,
            ).start()

    def lefts(block):
        slot = lax.rem(block, 2)
        part = pl.ds(pl.multiple_of(block * BACK_BLOCK, BACK_BLOCK), BACK_BLOCK)
        return [
            pltpu.make_async_copy(ref.at[part], left_buf.at[slot, n], left_sem.at[slot, n])
            for n, ref in ((1, dk_ref), (2, dv_ref))
        ]

    def own_left(block):
        slot = lax.rem(block, 2)
        part = pl.ds(pl.multiple_of((block - reach * per) * BACK_BLOCK, BACK_BLOCK), BACK_BLOCK)
        return pltpu.make_async_copy(dq_ref.at[part], left_buf.at[slot, 0], left_sem.at[slot, 0])

    def fetch(block):
        for copy in lefts(block):
            copy.start()

        @pl.when(block >= reach * per)
        def _():
            own_left(block).start()

    def product(block):
        slot = lax.rem(block, 2)

        @pl.when(block + 1 < cols // BACK_BLOCK)
        def _():
            fetch(block + 1)

        for copy in lefts(block):
            copy.wait()
        total = dot(left_buf[slot, 1], weight_buf[1]) + dot(left_buf[slot, 2], weight_buf[2])

        @pl.when(block < reach * per)
        def _():
            parts[block] = total.astype(BF16)
            n = block // per
            part = pl.ds(pl.multiple_of(lax.rem(block, per) * BACK_BLOCK, BACK_BLOCK), BACK_BLOCK)

            @pl.when(line >= reach - n)
            def _():
                remote(parts.at[block], back_out.at[n, part], back_send.at[n], back_recv.at[n], rep,
                       line - (reach - n)).start()

        @pl.when(block >= reach * per)
        def _():
            own_left(block).wait()
            part = pl.ds(pl.multiple_of((block - reach * per) * BACK_BLOCK, BACK_BLOCK), BACK_BLOCK)
            own_out[part, :] = total + dot(left_buf[slot, 0], weight_buf[0])

    fetch(0)

    def step(t, _):
        turn(t)

        @pl.when(t == 1)
        def _():
            arrived(weight_buf, weight_sem)
            total = gains_ref[line]
            for n in range(shards - 1):
                arrived(line_got.at[n], line_recv.at[n])
                total = total + line_got[n]
            mine[...] = total
            for n in range(1, 8):
                remote(mine, plane_got.at[n - 1], plane_send, plane_recv.at[n - 1], lax.rem(rep + n, 8), line).start()

        @pl.when(t == 3)
        def _():
            total = mine[...]
            for n in range(7):
                arrived(plane_got.at[n], plane_recv.at[n])
                total = total + plane_got[n]
            gains_out[...] = total

        @pl.when((t >= 1) & (t <= 2 * (cols // BACK_BLOCK) - 1) & (lax.rem(t, 2) == 1))
        def _():
            product(t // 2)

        return 0

    lax.fori_loop(0, max(turns, 2 * (cols // BACK_BLOCK)), step, 0)
    finish()
    arrived(line_got, line_send)
    arrived(plane_got, plane_send)
    for n in range(reach):
        @pl.when(line >= reach - n)
        def _(n=n):
            arrived(parts.at[pl.ds(0, per)], back_send.at[n])

        @pl.when(line + reach - n < shards)
        def _(n=n):
            arrived(back_out.at[n], back_recv.at[n])


BACK_BLOCK = 256


def reduce_last(down, attn, gains, grad_q, grad_k, grad_v, gathered):
    shards, _, _, rows, _ = down.shape
    tokens, cols = grad_q.shape[0], grad_k.shape[0]
    reach = (cols - tokens) // tokens
    any_space = pl.BlockSpec(memory_space=pl.ANY)
    vmem = pl.BlockSpec(memory_space=pltpu.VMEM)
    dma = pltpu.SemaphoreType.DMA
    return pl.pallas_call(
        functools.partial(last_kernel, shards),
        out_shape=(
            jax.ShapeDtypeStruct((2, 8, rows, D), BF16),
            jax.ShapeDtypeStruct(gains.shape[1:], F32),
            jax.ShapeDtypeStruct((reach, tokens, D), BF16),
            jax.ShapeDtypeStruct((tokens, D), F32),
        ),
        in_specs=[any_space, any_space, vmem] + [any_space] * 4,
        out_specs=(any_space, vmem, any_space, vmem),
        scratch_shapes=[
            pltpu.VMEM((shards - 1,) + gains.shape[1:], F32),
            pltpu.VMEM((7,) + gains.shape[1:], F32),
            pltpu.VMEM(gains.shape[1:], F32),
            dma(()), dma((shards - 1,)), dma(()), dma((7,)), dma((reach,)), dma((reach,)),
            pltpu.VMEM((3, D, D), BF16),
            pltpu.VMEM((2, 3, BACK_BLOCK, D), BF16),
            pltpu.VMEM((reach * tokens // BACK_BLOCK, BACK_BLOCK, D), BF16),
            dma(()), dma((2, 3)),
        ] + reduction_scratch(2, shards, rows),
        compiler_params=pltpu.CompilerParams(
            collective_id=2, has_side_effects=True, vmem_limit_bytes=62 * 2**20
        ),
        cost_estimate=pl.CostEstimate(flops=12 * 10**9, bytes_accessed=2 * 10**8, transcendentals=0),
    )(down, attn, gains, grad_q, grad_k, grad_v, gathered)


UNITS = 256


def feed_kernel(blocks, mid_ref, middle_ref, cot_ref, alpha_ref, up_scale_ref, gate_scale_ref, wu_ref, wg_ref, wd_ref,
                out_ref, grad_mid_ref, grad_ref, down_ref, up_sum_ref, gate_sum_ref, alpha_sum_ref,
                up_buf, gate_buf, hidden_buf, total, back, grad_hidden_buf, grad_u_buf, grad_g_buf):
    turn = pl.program_id(0)
    after = turn - blocks - 2

    def raw(block):
        up_buf[block] = dot_nt(mid_ref[...], wu_ref[...])
        gate_buf[block] = dot_nt(mid_ref[...], wg_ref[...])

    def activate(block):
        gate = gate_buf[block] * (gate_scale_ref[...] * math.sqrt(D))
        hidden = gate * jax.nn.sigmoid(gate) * (up_buf[block] * up_scale_ref[...])
        hidden_buf[block] = hidden.astype(BF16)

    def project(block, first):
        part = dot(hidden_buf[block], wd_ref[...])
        total[...] = part if first else total[...] + part

    def middle_step():
        alpha = alpha_ref[...]
        rows = total.shape[0]

        def step(i, sums):
            part = pl.ds(pl.multiple_of(i * 32, 32), 32)
            branch, factor = rownorm(total[part, :])
            middle = middle_ref[part, :]
            final, final_factor = rownorm(middle + alpha * (branch - middle))
            out_ref[part, :] = final.astype(BF16)
            grad = norm_back(final, final_factor, cot_ref[part, :].astype(F32))
            grad_mid_ref[part, :] = grad * (1.0 - alpha)
            back[part, :] = norm_back(branch, factor, grad * alpha).astype(BF16)
            return sums + jnp.sum(grad * (branch - middle), 0, keepdims=True)

        alpha_sum_ref[...] = lax.fori_loop(0, rows // 32, step, jnp.zeros((1, D), F32))

    def back_raw():
        grad_hidden_buf[...] = dot_nt(back[...], wd_ref[...])

    def back_activate(block):
        up_scale, gate_scale = up_scale_ref[...], gate_scale_ref[...] * math.sqrt(D)
        grad_hidden = grad_hidden_buf[...]
        up_raw, gate_raw = up_buf[block], gate_buf[block]
        gate = gate_raw * gate_scale
        sigma = jax.nn.sigmoid(gate)
        active = gate * sigma
        upward = up_raw * up_scale
        grad_upward = grad_hidden * active
        grad_gate = grad_hidden * upward * (sigma * (1.0 + gate * (1.0 - sigma)))
        up_sum_ref[...] = jnp.sum(grad_upward * up_raw, 0, keepdims=True)
        gate_sum_ref[...] = jnp.sum(grad_gate * gate_raw, 0, keepdims=True) * math.sqrt(D)
        grad_u_buf[...] = (grad_upward * up_scale).astype(BF16)
        grad_g_buf[...] = (grad_gate * gate_scale).astype(BF16)

    def back_project(block):
        grad_u, grad_g = grad_u_buf[...], grad_g_buf[...]
        grad_ref[0] = dot_tn(grad_u, mid_ref[...]).astype(BF16)
        grad_ref[1] = dot_tn(grad_g, mid_ref[...]).astype(BF16)
        down_ref[...] = dot_tn(hidden_buf[block], back[...]).astype(BF16)
        grad_mid_ref[...] += dot(grad_u, wu_ref[...]) + dot(grad_g, wg_ref[...])

    @pl.when(turn == 0)
    def _():
        raw(0)

    @pl.when(turn == 1)
    def _():
        activate(0)
        raw(1)

    @pl.when(turn == 2)
    def _():
        project(0, True)
        activate(1)
        raw(2)

    @pl.when((turn > 2) & (turn < blocks))
    def _():
        project(turn - 2, False)
        activate(turn - 1)
        raw(turn)

    @pl.when(turn == blocks)
    def _():
        project(turn - 2, False)
        activate(turn - 1)

    @pl.when(turn == blocks + 1)
    def _():
        project(turn - 2, False)
        middle_step()

    @pl.when(after == 0)
    def _():
        back_raw()

    @pl.when(after == 1)
    def _():
        back_activate(0)
        back_raw()

    @pl.when((after > 1) & (after < blocks))
    def _():
        back_project(after - 2)
        back_activate(after - 1)
        back_raw()

    @pl.when(after == blocks)
    def _():
        back_project(after - 2)
        back_activate(after - 1)

    @pl.when(after == blocks + 1)
    def _():
        back_project(after - 2)


def feed_forward(mid_low, middle, cotangent, alpha_ffn, scales, weights, firsts):
    rows = mid_low.shape[0]
    blocks = scales.shape[1] // UNITS
    whole = lambda *shape: pl.BlockSpec(shape, lambda t: (0,) * len(shape))
    half = blocks + 2

    def stage(t, early, late):
        return jnp.clip(lax.select(t < half, t - early, t - half - late), 0, blocks - 1)

    weight = lambda m, early, late: pl.BlockSpec((None, UNITS, D), lambda t: (m, stage(t, early, late), 0))
    done = lambda t, lag: jnp.clip(t - half - lag, 0, blocks - 1)
    units = pl.BlockSpec((1, UNITS), lambda t: (0, done(t, 1)))
    scale = pl.BlockSpec((1, UNITS), lambda t: (0, stage(t, 1, 1)))
    return pl.pallas_call(
        functools.partial(feed_kernel, blocks),
        grid=(2 * half,),
        out_shape=(
            jax.ShapeDtypeStruct((rows, D), BF16),
            jax.ShapeDtypeStruct((rows, D), F32),
            jax.ShapeDtypeStruct((2, blocks * UNITS, D), BF16),
            jax.ShapeDtypeStruct((blocks * UNITS, D), BF16),
            jax.ShapeDtypeStruct((1, blocks * UNITS), F32),
            jax.ShapeDtypeStruct((1, blocks * UNITS), F32),
            jax.ShapeDtypeStruct((1, D), F32),
        ),
        in_specs=[whole(rows, D), whole(rows, D), whole(rows, D), whole(1, D), scale, scale]
        + [weight(firsts[0], 0, 2), weight(firsts[1], 0, 2), weight(firsts[2], 2, 0)],
        out_specs=(
            whole(rows, D), whole(rows, D), pl.BlockSpec((2, UNITS, D), lambda t: (0, done(t, 2), 0)),
            pl.BlockSpec((UNITS, D), lambda t: (done(t, 2), 0)),
            units, units, whole(1, D),
        ),
        scratch_shapes=[
            pltpu.VMEM((blocks, rows, UNITS), F32),
            pltpu.VMEM((blocks, rows, UNITS), F32),
            pltpu.VMEM((blocks, rows, UNITS), BF16),
            pltpu.VMEM((rows, D), F32),
            pltpu.VMEM((rows, D), BF16),
            pltpu.VMEM((rows, UNITS), F32),
            pltpu.VMEM((rows, UNITS), BF16),
            pltpu.VMEM((rows, UNITS), BF16),
        ],
        compiler_params=pltpu.CompilerParams(vmem_limit_bytes=62 * 2**20),
        cost_estimate=pl.CostEstimate(flops=60 * 10**9, bytes_accessed=120 * 10**6, transcendentals=5 * 10**6),
    )(mid_low, middle, cotangent, alpha_ffn, scales[:1], scales[1:], *weights)


def adam_kernel(places, per, *refs):
    grads = refs[:places]
    w_ref, m_ref, v_ref, w_out, m_out, v_out = refs[places:]

    def update(g_ref):
        def step(i, _):
            part = pl.ds(pl.multiple_of(i * 16, 16), 16)
            new, first, second = adam(
                w_ref[part, :], g_ref[part, :].astype(F32), m_ref[part, :], v_ref[part, :], RATE, DECAY
            )
            w_out[part, :] = rownorm(new)[0]
            m_out[part, :] = first
            v_out[part, :] = second
            return 0

        lax.fori_loop(0, w_ref.shape[0] // 16, step, 0, unroll=5)

    for n in range(places):
        @pl.when(pl.program_id(0) // per == n)
        def _(n=n):
            update(grads[n])


def adam_rows(weight, grads, first, second):
    places = len(grads)
    _, per, piece, _ = grads[0][0].shape
    spec = pl.BlockSpec((None, piece, D), lambda p: (p, 0, 0))

    def grad_spec(n, index):
        return pl.BlockSpec((None, None, piece, D), lambda p: (index, jnp.clip(p - n * per, 0, per - 1), 0, 0))

    shape = jax.ShapeDtypeStruct((places * per, piece, D), F32)
    news = pl.pallas_call(
        functools.partial(adam_kernel, places, per),
        grid=(places * per,),
        out_shape=(shape,) * 3,
        in_specs=[grad_spec(n, index) for n, (_, index) in enumerate(grads)] + [spec] * 3,
        out_specs=(spec,) * 3,
        compiler_params=pltpu.CompilerParams(vmem_limit_bytes=40 * 2**20),
        cost_estimate=pl.CostEstimate(flops=20 * weight.size, bytes_accessed=26 * weight.size, transcendentals=0),
    )(*(array for array, _ in grads), *(old.reshape(shape.shape) for old in (weight, first, second)))
    return tuple(new.reshape(weight.shape) for new in news)


QUERY_BLOCK = 256
PAIR = 2 * HEAD_DIM
PAIRS = HEADS // 2


def head_ones():
    row = lax.broadcasted_iota(jnp.int32, (PAIR, PAIR), 0) // HEAD_DIM
    col = lax.broadcasted_iota(jnp.int32, (PAIR, PAIR), 1) // HEAD_DIM
    return (row == col).astype(F32).astype(BF16)


def head_sum(value, ones):
    high = value.astype(BF16)
    rest = (value - high.astype(F32)).astype(BF16)
    return dot(high, ones) + dot(rest, ones)


def of_head(value, head):
    lane = lax.broadcasted_iota(jnp.int32, value.shape, 1) // HEAD_DIM
    return jnp.where(lane == head, value, jnp.zeros_like(value))


def attend_pair(h_ref, wq_ref, wq2_ref, wk_ref, wk2_ref, wv_ref, wv2_ref, gain_ref, bias_ref, qp_ref, kp_ref, v_ref, o_ref, lse_ref,
                key_buf, query_buf, value_buf):
    cols = h_ref.shape[0]
    rows = qp_ref.shape[0]
    span = bias_ref.shape[1]
    ones = head_ones()
    gain = gain_ref[...]
    weights = jnp.concatenate([wk_ref[...], wk2_ref[...], wv_ref[...], wv2_ref[...]], 0)
    query_weights = jnp.concatenate([wq_ref[...], wq2_ref[...]], 0)

    def project(i, _):
        part = pl.ds(pl.multiple_of(i * QUERY_BLOCK, QUERY_BLOCK), QUERY_BLOCK)
        both = dot_nt(h_ref[part, :], weights)
        keys = both[:, :PAIR]
        kp_ref[part, :] = keys
        factor = lax.rsqrt(head_sum(keys * keys, ones) + SMALL)
        key_buf[part, :] = (keys * factor * gain).astype(BF16)
        values = both[:, PAIR:].astype(BF16)
        v_ref[part, :] = values
        value_buf[part, :PAIR] = values
        value_buf[part, PAIR:] = jnp.ones_like(values)
        return 0

    lax.fori_loop(0, cols // QUERY_BLOCK, project, 0)

    def project_queries(i, _):
        part = pl.ds(pl.multiple_of(i * QUERY_BLOCK, QUERY_BLOCK), QUERY_BLOCK)
        own = pl.ds(pl.multiple_of(cols - rows + i * QUERY_BLOCK, QUERY_BLOCK), QUERY_BLOCK)
        queries = dot_nt(h_ref[own, :], query_weights)
        qp_ref[part, :] = queries
        factor = lax.rsqrt(head_sum(queries * queries, ones) + SMALL)
        scaled = (queries * factor * gain).astype(BF16).astype(F32) * math.sqrt(HEAD_DIM)
        query_buf[part, :] = scaled.astype(BF16)
        return 0

    lax.fori_loop(0, rows // QUERY_BLOCK, project_queries, 0)
    for i in range(rows // QUERY_BLOCK):
        part = pl.ds(i * QUERY_BLOCK, QUERY_BLOCK)
        reach = pl.ds(i * QUERY_BLOCK, span)
        sides = []
        for head in range(2):
            scores = dot_nt(of_head(query_buf[part, :], head), key_buf[reach, :])
            probs = jnp.exp(scores + bias_ref[part, :]).astype(BF16)
            both = dot(probs, value_buf[reach, :])
            total = both[:, PAIR:]
            sides.append(both[:, :PAIR] / total)
            lse_ref[head : head + 1, part] = jnp.log(total).T[:1, :]
        lane = lax.broadcasted_iota(jnp.int32, sides[0].shape, 1)
        o_ref[part, :] = jnp.where(lane < HEAD_DIM, sides[0], sides[1]).astype(BF16)


def back_pair(qp_ref, kp_ref, v_ref, o_ref, da_ref, wo_ref, wo2_ref, gain_ref, bias_ref, lse_ref,
              dq_ref, dk_ref, dv_ref, sum_ref, key_buf, key_turned, k_total, v_total):
    cols = kp_ref.shape[0]
    rows = qp_ref.shape[0]
    span = bias_ref.shape[1]
    ones = head_ones()
    gain = gain_ref[...]
    weights = jnp.concatenate([wo_ref[...], wo2_ref[...]], 0)

    def keys_of(i, _):
        part = pl.ds(pl.multiple_of(i * QUERY_BLOCK, QUERY_BLOCK), QUERY_BLOCK)
        keys = kp_ref[part, :]
        factor = lax.rsqrt(head_sum(keys * keys, ones) + SMALL)
        low = keys * factor * gain
        key_buf[part, :] = low.astype(BF16)
        key_turned[:, part] = low.T.astype(BF16)
        k_total[part, :] = jnp.zeros_like(keys)
        v_total[part, :] = jnp.zeros_like(keys)
        return 0

    lax.fori_loop(0, cols // QUERY_BLOCK, keys_of, 0)
    for i in range(rows // QUERY_BLOCK):
        part = pl.ds(i * QUERY_BLOCK, QUERY_BLOCK)
        reach = pl.ds(i * QUERY_BLOCK, span)
        queries = qp_ref[part, :]
        factor = lax.rsqrt(head_sum(queries * queries, ones) + SMALL)
        hat = queries * factor
        scaled = ((hat * gain).astype(BF16).astype(F32) * math.sqrt(HEAD_DIM)).astype(BF16)
        back = dot_nt(da_ref[part, :], weights).astype(BF16)
        inner = (back.astype(F32) * o_ref[part, :].astype(F32)).T
        sides = []
        for head in range(2):
            mine = slice(head * HEAD_DIM, (head + 1) * HEAD_DIM)
            query, grad = of_head(scaled, head), of_head(back, head)
            scores = dot_nt(key_buf[reach, :], query)
            probs = jnp.exp(scores + bias_ref[i] - lse_ref[head : head + 1, part])
            v_total[reach, :] += dot(probs.astype(BF16), grad)
            delta = jnp.sum(inner[mine, :], 0, keepdims=True)
            grad_scores = (probs * (dot_nt(v_ref[reach, :], grad) - delta)).astype(BF16)
            k_total[reach, :] += dot(grad_scores, query)
            sides.append(dot(key_turned[mine, reach], grad_scores))
        grad_q = jnp.concatenate(sides, 0).T * math.sqrt(HEAD_DIM)
        sums = jnp.sum(grad_q * hat, 0, keepdims=True)
        if i == 0:
            sum_ref[...] = jnp.broadcast_to(sums, sum_ref.shape)
        else:
            sum_ref[...] += jnp.broadcast_to(sums, sum_ref.shape)
        grad_q = grad_q * gain
        dq_ref[part, :] = (factor * (grad_q - hat * head_sum(hat * grad_q, ones))).astype(BF16)

    def finish(i, _):
        part = pl.ds(pl.multiple_of(i * QUERY_BLOCK, QUERY_BLOCK), QUERY_BLOCK)
        keys = kp_ref[part, :]
        factor = lax.rsqrt(head_sum(keys * keys, ones) + SMALL)
        hat = keys * factor
        grad_k = k_total[part, :]
        sum_ref[...] += jnp.broadcast_to(jnp.sum(grad_k * hat, 0, keepdims=True), sum_ref.shape)
        grad_k = grad_k * gain
        dk_ref[part, :] = (factor * (grad_k - hat * head_sum(hat * grad_k, ones))).astype(BF16)
        dv_ref[part, :] = v_total[part, :].astype(BF16)
        return 0

    lax.fori_loop(0, cols // QUERY_BLOCK, finish, 0)


def head_rows(attn_low, matrix, second):
    heads = attn_low.shape[2]

    def index(p):
        head = 2 * p + second
        return (head // heads, matrix, lax.rem(head, heads), 0, 0)

    return pl.BlockSpec((None, None, None, HEAD_DIM, D), index)


def attention_forward(low_all, attn_low, gain_qk, bias, rows):
    cols = low_all.shape[0]
    span = bias.shape[1]
    side = lambda n: pl.BlockSpec((n, PAIR), lambda p: (0, p))
    whole = lambda *shape: pl.BlockSpec(shape, lambda p: (0,) * len(shape))
    return pl.pallas_call(
        attend_pair,
        grid=(PAIRS,),
        out_shape=(
            jax.ShapeDtypeStruct((rows, D), F32),
            jax.ShapeDtypeStruct((cols, D), F32),
            jax.ShapeDtypeStruct((cols, D), BF16),
            jax.ShapeDtypeStruct((rows, D), BF16),
            jax.ShapeDtypeStruct((PAIRS, 8, rows), F32),
        ),
        in_specs=[whole(cols, D)]
        + [head_rows(attn_low, j, second) for j in range(3) for second in range(2)]
        + [side(1), whole(rows, span)],
        out_specs=(side(rows), side(cols), side(cols), side(rows),
                   pl.BlockSpec((None, 8, rows), lambda p: (p, 0, 0))),
        scratch_shapes=[
            pltpu.VMEM((cols, PAIR), BF16),
            pltpu.VMEM((rows, PAIR), BF16),
            pltpu.VMEM((cols, 2 * PAIR), BF16),
        ],
        compiler_params=pltpu.CompilerParams(vmem_limit_bytes=56 * 2**20),
        cost_estimate=pl.CostEstimate(flops=20 * 10**9, bytes_accessed=30 * 10**6, transcendentals=13 * 10**6),
    )(low_all, *[attn_low] * 6, gain_qk, bias)


def attention_backward(q_pre, k_pre, value_all, o_low, grad_spre, attn_low, gain_qk, bias_turned, lse):
    rows, cols = q_pre.shape[0], k_pre.shape[0]
    side = lambda n: pl.BlockSpec((n, PAIR), lambda p: (0, p))
    whole = lambda *shape: pl.BlockSpec(shape, lambda p: (0,) * len(shape))
    stat = pl.BlockSpec((None, 8, rows), lambda p: (p, 0, 0))
    return pl.pallas_call(
        back_pair,
        grid=(PAIRS,),
        out_shape=(
            jax.ShapeDtypeStruct((rows, D), BF16),
            jax.ShapeDtypeStruct((cols, D), BF16),
            jax.ShapeDtypeStruct((cols, D), BF16),
            jax.ShapeDtypeStruct((PAIRS, 8, PAIR), F32),
        ),
        in_specs=[
            side(rows), side(cols), side(cols), side(rows), whole(rows, D),
            head_rows(attn_low, 3, 0), head_rows(attn_low, 3, 1),
            pl.BlockSpec((None, 1, PAIR), lambda p: (p, 0, 0)), whole(*bias_turned.shape), stat,
        ],
        out_specs=(side(rows), side(cols), side(cols), pl.BlockSpec((None, 8, PAIR), lambda p: (p, 0, 0))),
        scratch_shapes=[
            pltpu.VMEM((cols, PAIR), BF16),
            pltpu.VMEM((PAIR, cols), BF16),
            pltpu.VMEM((cols, PAIR), F32),
            pltpu.VMEM((cols, PAIR), F32),
        ],
        compiler_params=pltpu.CompilerParams(vmem_limit_bytes=56 * 2**20),
        cost_estimate=pl.CostEstimate(flops=30 * 10**9, bytes_accessed=40 * 10**6, transcendentals=13 * 10**6),
    )(q_pre, k_pre, value_all, o_low, grad_spre, attn_low, attn_low, gain_qk, bias_turned, lse)


START = 4


def gather_kernel(shards, attn_ref, ffn_ref, gains_ref, tokens_ref, bias_ref,
                  out, gains_out, h_out, qp_out, kp_out, v_out, o_out, lse_ref,
                  wide, low, mine, wide_sem, low_sem, mine_sem, line_send, line_recv, plane_send, beside_recv,
                  above_recv, across_recv, pair_send, pair_recv, gains_send, gains_recv, tokens_send,
                  tokens_recv, local_sem, gains_buf, before, h_buf, load_sem, store_sem,
                  weight_buf, gain_row, qp_buf, kp_buf, v_buf, o_buf, key_buf, query_buf, value_buf):
    core, chip, beside, above, across = place()
    line = lax.axis_index("shard")
    rep = 2 * chip + core
    sibling = 2 * chip + 1 - core
    to_beside, to_above = 2 * beside + core, 2 * above + core
    piece = attn_ref.shape[1]
    rows = tokens_ref.shape[0]
    heads = 2 * piece // HEAD_DIM
    others = shards - 1
    steps = 4 * others
    greet(shards)

    def rows_of(m, shard, rep, start=0, size=None):
        first = pl.multiple_of(rep * piece + start, 16)
        return out.at[m, shard, pl.ds(first, piece if size is None else size)]

    def source(n):
        low_side = 2 * line < shards
        edge = lax.select(low_side, line, shards - 1 - line)
        near = lax.select(lax.rem(n, 2) == 0, edge - 1 - n // 2, edge + 1 + n // 2)
        found = lax.select(n < 2 * edge, near, n + 1)
        return lax.select(low_side, found, shards - 1 - found)

    def own_send(m):
        @pl.when(line < shards - 1)
        def _():
            remote(mine.at[m], rows_of(m, line, rep), line_send, line_recv.at[m, line], rep, line + 1).start()

        @pl.when(line > 0)
        def _():
            remote(mine.at[m], rows_of(m, line, rep), line_send, line_recv.at[m, line], rep, line - 1).start()

    def fetch(index, slot):
        @pl.when(index < 8)
        def _():
            pltpu.make_async_copy(attn_ref.at[lax.rem(index, 8)], wide.at[slot], wide_sem.at[slot]).start()

        @pl.when(index >= 8)
        def _():
            pltpu.make_async_copy(
                ffn_ref.at[jnp.maximum(index // 8 - 1, 0), lax.rem(index, 8)], wide.at[slot], wide_sem.at[slot]
            ).start()

    def store(index, slot):
        return pltpu.make_async_copy(low.at[slot], rows_of(index // 8, line, lax.rem(index, 8)), low_sem.at[slot])

    def lower(src, dst):
        def step(i, _):
            part = pl.ds(pl.multiple_of(i * 32, 32), 32)
            dst[part, :] = src[part, :].astype(BF16)
            return 0

        lax.fori_loop(0, piece // 32, step, 0)

    for n in range(1, shards):
        other = lax.rem(line + n, shards)
        remote(gains_ref, gains_buf.at[line], gains_send, gains_recv.at[line], rep, other).start()
    pltpu.make_async_copy(gains_ref, gains_buf.at[line], local_sem).start()
    own = pl.ds(2 * rows, rows)
    pltpu.make_async_copy(tokens_ref, h_buf.at[own], load_sem.at[0, 0]).start()
    for m in range(4):
        origin = attn_ref.at[rep] if m == 0 else ffn_ref.at[m - 1, rep]
        pltpu.make_async_copy(origin, wide.at[m], mine_sem.at[m]).start()
    for m in range(4):
        arrived(wide.at[m], mine_sem.at[m])
        lower(wide.at[m], mine.at[m])
        if m == 0:
            own_send(0)

            @pl.when(line < shards - 1)
            def _():
                remote(tokens_ref, before.at[1], tokens_send, tokens_recv.at[1], rep, line + 1).start()

    for n in range(2):
        fetch(n, n)

    def norm_rows(source, first):
        def step(i, _):
            at = pl.multiple_of(first + i * 32, 32)
            value = source[pl.ds(pl.multiple_of(i * 32, 32), 32), :].astype(F32)
            h_buf[pl.ds(at, 32), :] = rownorm(value)[0].astype(BF16)
            return 0

        lax.fori_loop(0, rows // 32, step, 0)

    def clear_rows(first):
        h_buf[pl.ds(first, rows), :] = jnp.zeros((rows, D), BF16)

    arrived(h_buf.at[own], load_sem.at[0, 0])
    norm_rows(h_buf.at[own], 2 * rows)

    def loads(p, slot):
        copies = []
        for j in range(3):
            for second in range(2):
                head = 2 * p + second
                first = pl.multiple_of(2 * piece * j + HEAD_DIM * lax.rem(head, heads), HEAD_DIM)
                copies.append(
                    pltpu.make_async_copy(
                        out.at[0, head // heads, pl.ds(first, HEAD_DIM)], weight_buf.at[slot, 2 * j + second],
                        load_sem.at[slot, 2 * j + second],
                    )
                )
        return copies

    def stores(p, slot):
        lanes = pl.ds(pl.multiple_of(p * PAIR, PAIR), PAIR)
        return [
            pltpu.make_async_copy(buf.at[slot], ref.at[:, lanes], store_sem.at[slot, n])
            for n, (ref, buf) in enumerate(((qp_out, qp_buf), (kp_out, kp_buf), (v_out, v_buf), (o_out, o_buf)))
        ]

    def pair(p):
        slot = lax.rem(p, 2)

        @pl.when(p + 1 < PAIRS)
        def _():
            for copy in loads(p + 1, 1 - slot):
                copy.start()

        for copy in loads(p, slot):
            copy.wait()

        @pl.when(p >= 2)
        def _():
            for copy in stores(p - 2, slot):
                copy.wait()

        row = lax.broadcasted_iota(jnp.int32, (8, PAIR), 0)
        left, right = (
            jnp.sum(
                jnp.where(row == lax.rem(2 * p + n, heads), gains_buf[(2 * p + n) // heads, :8, :PAIR], 0.0),
                0, keepdims=True,
            )
            for n in range(2)
        )
        lane = lax.broadcasted_iota(jnp.int32, (1, PAIR), 1)
        gain_row[...] = jnp.where(lane < HEAD_DIM, left, right)
        attend_pair(
            h_buf, *(weight_buf.at[slot, n] for n in range(6)), gain_row, bias_ref, qp_buf.at[slot],
            kp_buf.at[slot], v_buf.at[slot], o_buf.at[slot], lse_ref.at[p], key_buf, query_buf, value_buf,
        )
        for copy in stores(p, slot):
            copy.start()

    def begin(c):
        m, origin = c // others, source(lax.rem(c, others))
        got = rows_of(m, origin, rep)
        arrived(got, line_recv.at[m, origin])

        @pl.when((origin < line) & (line < shards - 1))
        def _():
            remote(got, got, line_send, line_recv.at[m, origin], rep, line + 1).start()

        @pl.when((origin > line) & (line > 0))
        def _():
            remote(got, got, line_send, line_recv.at[m, origin], rep, line - 1).start()

        remote(got, got, plane_send, beside_recv.at[m, origin], to_beside, line).start()
        remote(got, got, plane_send, above_recv.at[m, origin], to_above, line).start()
        remote(got, got, pair_send, pair_recv.at[m], sibling, line).start()

    def middle(c):
        m, origin = c // others, source(lax.rem(c, others))
        got = rows_of(m, origin, to_beside)
        arrived(got, beside_recv.at[m, origin])
        part = rows_of(m, origin, to_beside, 0, HALF)
        remote(part, part, plane_send, across_recv.at[m, origin, 0], to_above, line).start()
        remote(got, got, pair_send, pair_recv.at[m], sibling, line).start()
        got = rows_of(m, origin, to_above)
        arrived(got, above_recv.at[m, origin])
        part = rows_of(m, origin, to_above, HALF, piece - HALF)
        remote(part, part, plane_send, across_recv.at[m, origin, 1], to_beside, line).start()
        remote(got, got, pair_send, pair_recv.at[m], sibling, line).start()

    def last(c):
        m, origin = c // others, source(lax.rem(c, others))
        got = rows_of(m, origin, 2 * across + core)
        arrived(rows_of(m, origin, 2 * across + core, 0, HALF), across_recv.at[m, origin, 0])
        arrived(rows_of(m, origin, 2 * across + core, HALF, piece - HALF), across_recv.at[m, origin, 1])
        remote(got, got, pair_send, pair_recv.at[m], sibling, line).start()

    def local(t):
        for n in range(2):
            index = 2 * t + n
            slot = 2 * lax.rem(t, 2) + n
            arrived(wide.at[slot], wide_sem.at[slot])

            @pl.when(index + 2 < 32)
            def _():
                fetch(index + 2, lax.rem(slot + 2, 4))

            @pl.when(t >= 2)
            def _():
                store(index - 4, slot).wait()

            lower(wide.at[slot], low.at[slot])
            store(index, slot).start()

    def turn(t, _):
        @pl.when((lax.rem(t, others) == 0) & (t // others < 3))
        def _():
            own_send(t // others + 1)

        @pl.when(t < steps)
        def _():
            begin(t)

        @pl.when((t == 1) & (line > 0))
        def _():
            arrived(before.at[1], tokens_recv.at[1])

            @pl.when(line < shards - 1)
            def _():
                remote(before.at[1], before.at[0], tokens_send, tokens_recv.at[0], rep, line + 1).start()

            norm_rows(before.at[1], rows)

        @pl.when((t == 1) & (line == 0))
        def _():
            clear_rows(rows)

        @pl.when((t == 3) & (line > 1))
        def _():
            arrived(before.at[0], tokens_recv.at[0])
            norm_rows(before.at[0], 0)

        @pl.when((t == 3) & (line <= 1))
        def _():
            clear_rows(0)

        @pl.when((t >= 1) & (t < steps + 1))
        def _():
            middle(t - 1)

        @pl.when((t >= 2) & (t < steps + 2))
        def _():
            last(t - 2)

        @pl.when(t < 2)
        def _():
            local(2 * t)
            local(2 * t + 1)

        @pl.when(t >= 2)
        def _():
            local(t + 2)

        @pl.when(t == START)
        def _():
            pltpu.make_async_copy(gains_ref, gains_buf.at[line], local_sem).wait()
            for n in range(1, shards):
                other = lax.rem(line + n, shards)
                arrived(gains_buf.at[other], gains_recv.at[other])
            arrived(out.at[0, pl.ds(0, others), pl.ds(0, 4 * piece)], pair_recv.at[0])
            for copy in loads(0, 0):
                copy.start()

        @pl.when((t >= START) & (t < START + PAIRS))
        def _():
            pair(t - START)

        return 0

    lax.fori_loop(0, 14, turn, 0)
    for n in range(4):
        store(28 + n, n).wait()
    gains_copy = pltpu.make_async_copy(gains_buf, gains_out, local_sem)
    h_copy = pltpu.make_async_copy(h_buf, h_out, load_sem.at[0, 0])
    gains_copy.start()
    h_copy.start()
    for p in (PAIRS - 2, PAIRS - 1):
        for copy in stores(p, p % 2):
            copy.wait()
    for m in range(1, 4):
        arrived(out.at[m, pl.ds(0, others), pl.ds(0, 4 * piece)], pair_recv.at[m])
    gains_copy.wait()
    h_copy.wait()

    @pl.when((line == 1) | (line == shards - 2))
    def _():
        arrived(before, tokens_send)

    @pl.when(line == 0)
    def _():
        arrived(before.at[0], tokens_send)

    @pl.when((line == 0) | (line == shards - 1))
    def _():
        arrived(out.at[:, 0, pl.ds(0, piece)], line_send)

    @pl.when((line > 0) & (line < shards - 1))
    def _():
        arrived(out.at[:, 0, pl.ds(0, 5 * piece)], line_send)

    arrived(out.at[:, pl.ds(0, others), pl.ds(0, 3 * piece)], plane_send)
    arrived(out.at[:, pl.ds(0, others), pl.ds(0, 4 * piece)], pair_send)
    arrived(gains_buf.at[pl.ds(0, others)], gains_send)


def gather_attend(attn_w, ffn_w, gains, tokens, bias, shards):
    piece = attn_w.shape[1]
    rows = tokens.shape[0]
    cols = rows + WINDOW
    any_space = pl.BlockSpec(memory_space=pl.ANY)
    vmem = pl.BlockSpec(memory_space=pltpu.VMEM)
    dma = pltpu.SemaphoreType.DMA
    return pl.pallas_call(
        functools.partial(gather_kernel, shards),
        out_shape=(
            jax.ShapeDtypeStruct((4, shards, 8 * piece, D), BF16),
            jax.ShapeDtypeStruct((shards,) + gains.shape, F32),
            jax.ShapeDtypeStruct((cols, D), BF16),
            jax.ShapeDtypeStruct((rows, D), F32),
            jax.ShapeDtypeStruct((cols, D), F32),
            jax.ShapeDtypeStruct((cols, D), BF16),
            jax.ShapeDtypeStruct((rows, D), BF16),
            jax.ShapeDtypeStruct((PAIRS, 8, rows), F32),
        ),
        in_specs=[any_space] * 4 + [vmem],
        out_specs=(any_space,) * 7 + (vmem,),
        scratch_shapes=[
            pltpu.VMEM((4, piece, D), F32),
            pltpu.VMEM((4, piece, D), BF16),
            pltpu.VMEM((4, piece, D), BF16),
            dma((4,)), dma((4,)), dma((4,)), dma(()), dma((4, shards)), dma(()), dma((4, shards)),
            dma((4, shards)), dma((4, shards, 2)), dma(()), dma((4,)), dma(()), dma((shards,)), dma(()),
            dma((2,)), dma(()),
            pltpu.VMEM((shards,) + gains.shape, F32),
            pltpu.VMEM((2, rows, D), BF16),
            pltpu.VMEM((cols, D), BF16),
            dma((2, 6)), dma((2, 4)),
            pltpu.VMEM((2, 6, HEAD_DIM, D), BF16),
            pltpu.VMEM((1, PAIR), F32),
            pltpu.VMEM((2, rows, PAIR), F32),
            pltpu.VMEM((2, cols, PAIR), F32),
            pltpu.VMEM((2, cols, PAIR), BF16),
            pltpu.VMEM((2, rows, PAIR), BF16),
            pltpu.VMEM((cols, PAIR), BF16),
            pltpu.VMEM((rows, PAIR), BF16),
            pltpu.VMEM((cols, 2 * PAIR), BF16),
        ],
        compiler_params=pltpu.CompilerParams(
            collective_id=3, has_side_effects=True, vmem_limit_bytes=60 * 2**20
        ),
        cost_estimate=pl.CostEstimate(flops=20 * 10**9, bytes_accessed=2 * 10**8, transcendentals=13 * 10**6),
    )(attn_w, ffn_w, gains, tokens, bias)


def attention_back_kernel(shards, grads_ref, qp_ref, kp_ref, v_ref, o_ref, weight_ref, da_ref, gain_ref, bias_ref,
                          lse_ref, h_ref, out, dq_ref, dk_ref, dv_ref, turned_ref, sum_ref,
                          qp_buf, kp_buf, v_buf, o_buf, wo_buf, dq_buf, dk_buf, dv_buf, turned_buf, load_sem, store_sem,
                          key_buf, key_turned, k_total, v_total, *scratch):
    turns, turn, finish = reduction((grads_ref.at[0], grads_ref.at[1]), out, scratch)
    height = weight_ref.shape[2] // 4
    heads = height // HEAD_DIM

    def loads(p, slot):
        lanes = pl.ds(pl.multiple_of(p * PAIR, PAIR), PAIR)
        copies = [
            pltpu.make_async_copy(ref.at[:, lanes], buf.at[slot], load_sem.at[slot, n])
            for n, (ref, buf) in enumerate(((qp_ref, qp_buf), (kp_ref, kp_buf), (v_ref, v_buf), (o_ref, o_buf)))
        ]
        for second in range(2):
            head = 2 * p + second
            copies.append(
                pltpu.make_async_copy(
                    weight_ref.at[
                        0, head // heads,
                        pl.ds(pl.multiple_of(3 * height + HEAD_DIM * lax.rem(head, heads), HEAD_DIM), HEAD_DIM),
                    ],
                    wo_buf.at[slot, second], load_sem.at[slot, 4 + second],
                )
            )
        return copies

    def stores(p, slot):
        lanes = pl.ds(pl.multiple_of(p * PAIR, PAIR), PAIR)
        copies = [
            pltpu.make_async_copy(buf.at[slot], ref.at[:, lanes], store_sem.at[slot, n])
            for n, (ref, buf) in enumerate(((dq_ref, dq_buf), (dk_ref, dk_buf), (dv_ref, dv_buf)))
        ]
        for j in range(4):
            for second in range(2):
                head = 2 * p + second
                first = pl.multiple_of(height * j + HEAD_DIM * lax.rem(head, heads), HEAD_DIM)
                copies.append(
                    pltpu.make_async_copy(
                        turned_buf.at[slot, j, pl.ds(second * HEAD_DIM, HEAD_DIM)],
                        turned_ref.at[head // heads, pl.ds(first, HEAD_DIM)],
                        store_sem.at[slot, 3 + 2 * j + second],
                    )
                )
        return copies

    def pair(p):
        slot = lax.rem(p, 2)

        @pl.when(p + 1 < PAIRS)
        def _():
            for copy in loads(p + 1, 1 - slot):
                copy.start()

        for copy in loads(p, slot):
            copy.wait()

        @pl.when(p >= 2)
        def _():
            for copy in stores(p - 2, slot):
                copy.wait()

        back_pair(
            qp_buf.at[slot], kp_buf.at[slot], v_buf.at[slot], o_buf.at[slot], da_ref, wo_buf.at[slot, 0],
            wo_buf.at[slot, 1], gain_ref.at[p], bias_ref, lse_ref.at[p], dq_buf.at[slot], dk_buf.at[slot],
            dv_buf.at[slot], sum_ref.at[p], key_buf, key_turned, k_total, v_total,
        )
        cols, rows = h_ref.shape[0], da_ref.shape[0]
        turned_buf[slot, 0] = dot_tn(dq_buf[slot], h_ref[pl.ds(cols - rows, rows), :]).astype(BF16)
        turned_buf[slot, 1] = dot_tn(dk_buf[slot], h_ref[...]).astype(BF16)
        turned_buf[slot, 2] = dot_tn(dv_buf[slot], h_ref[...]).astype(BF16)
        turned_buf[slot, 3] = dot_tn(o_buf[slot], da_ref[...]).astype(BF16)
        for copy in stores(p, slot):
            copy.start()

    greet(shards)
    for copy in loads(0, 0):
        copy.start()

    def step(t, _):
        turn(t)

        @pl.when(t < PAIRS)
        def _():
            pair(t)

        return 0

    lax.fori_loop(0, max(turns, PAIRS), step, 0)
    for p in (PAIRS - 2, PAIRS - 1):
        for copy in stores(p, p % 2):
            copy.wait()
    finish()


def attention_back_reduce(grads, q_pre, k_pre, value_all, o_low, attn_low, grad_spre, gain_qk, bias_turned, lse, low_all):
    _, shards, _, _, rows, _ = grads.shape
    tokens, cols = q_pre.shape[0], k_pre.shape[0]
    any_space = pl.BlockSpec(memory_space=pl.ANY)
    vmem = pl.BlockSpec(memory_space=pltpu.VMEM)
    dma = pltpu.SemaphoreType.DMA
    return pl.pallas_call(
        functools.partial(attention_back_kernel, shards),
        out_shape=(
            jax.ShapeDtypeStruct((2, 8, rows, D), BF16),
            jax.ShapeDtypeStruct((tokens, D), BF16),
            jax.ShapeDtypeStruct((cols, D), BF16),
            jax.ShapeDtypeStruct((cols, D), BF16),
            jax.ShapeDtypeStruct((shards, 8 * rows, D), BF16),
            jax.ShapeDtypeStruct((PAIRS, 8, PAIR), F32),
        ),
        in_specs=[any_space] * 6 + [vmem] * 5,
        out_specs=(any_space,) * 5 + (vmem,),
        scratch_shapes=[
            pltpu.VMEM((2, tokens, PAIR), F32),
            pltpu.VMEM((2, cols, PAIR), F32),
            pltpu.VMEM((2, cols, PAIR), BF16),
            pltpu.VMEM((2, tokens, PAIR), BF16),
            pltpu.VMEM((2, 2, HEAD_DIM, D), BF16),
            pltpu.VMEM((2, tokens, PAIR), BF16),
            pltpu.VMEM((2, cols, PAIR), BF16),
            pltpu.VMEM((2, cols, PAIR), BF16),
            pltpu.VMEM((2, 4, PAIR, D), BF16),
            dma((2, 6)), dma((2, 11)),
            pltpu.VMEM((cols, PAIR), BF16),
            pltpu.VMEM((PAIR, cols), BF16),
            pltpu.VMEM((cols, PAIR), F32),
            pltpu.VMEM((cols, PAIR), F32),
        ] + reduction_scratch(2, shards, rows),
        compiler_params=pltpu.CompilerParams(
            collective_id=1, has_side_effects=True, vmem_limit_bytes=62 * 2**20
        ),
        cost_estimate=pl.CostEstimate(flops=30 * 10**9, bytes_accessed=2 * 10**8, transcendentals=13 * 10**6),
    )(grads, q_pre, k_pre, value_all, o_low, attn_low, grad_spre, gain_qk, bias_turned, lse, low_all)


def body(
    tokens,
    doc_lengths,
    cotangent,
    attn_w,
    ffn_w,
    attn_m,
    attn_v,
    ffn_m,
    ffn_v,
    gains_d,
    gains_ff,
    gd_m,
    gd_v,
    gf_m,
    gf_v,
):
    shards = lax.axis_size("shard")
    reps = lax.axis_size("rep")
    device_index = lax.axis_index("shard")
    rows = tokens.shape[0]
    reach = WINDOW // rows
    cols = (reach + 1) * rows
    attn_rows = attn_w.shape[1]
    ffn_rows = ffn_w.shape[1]
    ffn_all = shards * ffn_rows
    piece = ffn_rows // reps

    lengths_row = doc_lengths[0]
    starts = jnp.cumsum(lengths_row) - lengths_row
    positions = device_index * rows + jnp.arange(rows, dtype=jnp.int32)
    doc_start = jnp.max(
        jnp.where(starts[None, :] <= positions[:, None], starts[None, :], 0), axis=1
    )
    blocks = rows // QUERY_BLOCK
    span = WINDOW + QUERY_BLOCK
    query = jnp.arange(rows, dtype=jnp.int32).reshape(blocks, QUERY_BLOCK)
    lead = query[:, :1] - reach * rows + jnp.arange(span, dtype=jnp.int32)
    ahead = query[:, :, None] - lead[:, None, :]
    floor = (doc_start - device_index * rows).reshape(blocks, QUERY_BLOCK, 1)
    mask = (ahead >= 0) & (ahead < WINDOW) & (lead[:, None, :] >= floor)
    bias = jnp.where(mask, 0.0, NEGATIVE).astype(F32)
    bias_turned = bias.transpose(0, 2, 1)
    bias = bias.reshape(rows, span)
    cut = gains_d.size
    small = jnp.concatenate([gains_d.reshape(-1), gains_ff.reshape(-1)]).astype(BF16)
    normed_in, factor_in = rownorm(tokens.astype(F32))
    fast = reps == 8 and shards == 4 and attn_rows % HEAD_DIM == 0 and reach == 2
    if fast:
        small = small.astype(F32)
        qk_heads = small[:attn_rows].reshape(-1, HEAD_DIM)
        qk_heads = jnp.pad(
            jnp.concatenate([qk_heads, qk_heads], 1), ((0, 8 - qk_heads.shape[0]), (0, D - PAIR))
        )
        small = jnp.pad(small, (0, 8 * D - small.size)).reshape(8, D)
        gathered, small, low_all, q_pre, k_pre, value_all, o_low, lse = gather_attend(
            attn_w.reshape(8, piece, D),
            ffn_w.reshape(3, 8, piece, D),
            jnp.concatenate([qk_heads, small]),
            tokens,
            bias,
            shards,
        )
        small = small[:, 8:].reshape(shards, -1)[:, : cut + gains_ff.size]
        out_low = gathered[0, :, 3 * attn_rows :].reshape(D, D)
        ffn_low = [gathered.reshape(4, ffn_all, D)] * 3
        firsts = (1, 2, 3)
    else:
        attn_low = (
            gather_rows(attn_w.reshape(4 * attn_rows, D).astype(BF16))
            .reshape(shards, 4, attn_rows, D)
            .transpose(1, 0, 2, 3)
            .reshape(1, 4, HEADS, HEAD_DIM, D)
        )
        ffn_low = [gather_rows(ffn_w[m].astype(BF16)).reshape(1, ffn_all, D) for m in range(3)]
        firsts = (0, 0, 0)
        small = lax.all_gather(small, "shard", axis=0).astype(F32)
        query_low, key_low, value_low, out_low = (attn_low[0, j].reshape(D, D) for j in range(4))
    gd_all = small[:, :cut].reshape(shards, 3, -1).transpose(1, 0, 2).reshape(3, D)
    gf_all = small[:, cut:].reshape(shards, 2, ffn_rows).transpose(1, 0, 2).reshape(2, ffn_all)
    gain_qk = gd_all[0]
    alpha_attn = gd_all[1]
    alpha_ffn = gd_all[2]

    if not fast:
        earlier = [from_behind(tokens, "shard", offset) for offset in range(reach, 0, -1)]
        low_all = rownorm(jnp.concatenate(earlier + [tokens], 0).astype(F32))[0].astype(BF16)
        q_pre, k_pre, value_all, o_low, lse = attention_forward(
            low_all, attn_low, gain_qk[None], bias, rows
        )
    in_low = low_all[-rows:]
    side, side_factor = rownorm(dot(o_low, out_low))
    middle, mid_factor = rownorm(normed_in + alpha_attn * (side - normed_in))
    mid_low = middle.astype(BF16)
    output, grad_mid, ffn_grads, down_grads, grad_scale_up, grad_scale_gate, grad_alpha_ffn = feed_forward(
        mid_low, middle, cotangent, alpha_ffn[None], gf_all, ffn_low, firsts
    )
    grad_mixed = norm_back(middle, mid_factor, grad_mid)
    grad_in = grad_mixed * (1.0 - alpha_attn)
    grad_alpha_attn = jnp.sum(grad_mixed * (side - normed_in), 0)
    grad_spre = norm_back(side, side_factor, grad_mixed * alpha_attn).astype(BF16)
    pair_gain = gain_qk.reshape(PAIRS, 1, PAIR)
    if fast:
        units = (shards, 4, 2, piece, D)
        sum_first, grad_qpre, grad_kpre, grad_vpre, attn_grad, gain_sums = attention_back_reduce(
            ffn_grads.reshape((2,) + units), q_pre, k_pre, value_all, o_low, gathered, grad_spre,
            pair_gain, bias_turned, lse, low_all,
        )
    else:
        grad_qpre, grad_kpre, grad_vpre, gain_sums = attention_backward(
            q_pre, k_pre, value_all, o_low, grad_spre, attn_low, pair_gain, bias_turned, lse
        )
    grad_gain_qk = gain_sums[:, 0].reshape(D)
    grad_gf = jnp.concatenate([grad_scale_up, grad_scale_gate])
    gd_rows = D // shards
    if fast:
        grad_gd = jnp.stack([grad_gain_qk, grad_alpha_attn, grad_alpha_ffn[0]])
        small = jnp.concatenate(
            [
                grad_gd.reshape(3, shards, gd_rows).transpose(1, 0, 2).reshape(shards, -1),
                grad_gf.reshape(2, shards, ffn_rows).transpose(1, 0, 2).reshape(shards, -1),
            ],
            1,
        )
        small = jnp.pad(small, ((0, 0), (0, 8 * D - small.shape[1]))).reshape(shards, 8, D)
        sum_last, sum_small, back_got, back_own = reduce_last(
            down_grads.reshape(units), attn_grad.reshape(units), small, grad_qpre, grad_kpre, grad_vpre, gathered
        )
        grad_in = grad_in + back_own
        for n in range(reach):
            sent = device_index + reach - n < shards
            grad_in = grad_in + jnp.where(sent, back_got[n], 0).astype(F32)
        sum_small = sum_small.reshape(-1)
        sum_gd = sum_small[: 3 * gd_rows].reshape(3, gd_rows)
        sum_gf = sum_small[3 * gd_rows : 3 * gd_rows + 2 * ffn_rows].reshape(2, ffn_rows)
        attn_sums, ffn_sums = [(sum_last, 1)], [(sum_first, 0), (sum_first, 1), (sum_last, 0)]
    else:
        back_all = dot(grad_kpre, key_low) + dot(grad_vpre, value_low)
        grad_in = grad_in + dot(grad_qpre, query_low) + back_all[reach * rows :]
        back_parts = back_all[: reach * rows].reshape(reach, rows, D).astype(BF16)
        for n in range(reach):
            grad_in = grad_in + from_behind(back_parts[n], "shard", n - reach).astype(F32)
        attn_grad = jnp.stack(
            [
                dot_tn(grad_qpre, in_low),
                dot_tn(grad_kpre, low_all),
                dot_tn(grad_vpre, low_all),
                dot_tn(o_low, grad_spre),
            ]
        ).astype(BF16)
        attn_grad = attn_grad.reshape(4, shards, attn_rows, D).transpose(1, 0, 2, 3)
        attn_grad = attn_grad.reshape(shards, reps, 4 * attn_rows // reps, D).transpose(1, 0, 2, 3)
        attn_sums = [(reduce_rows(attn_grad).reshape(1, 4, attn_rows, D), 0)]
        ready = (shards, reps, piece, D)
        ffn_sums = [
            (reduce_rows(part.reshape(ready).transpose(1, 0, 2, 3)).reshape(1, 1, ffn_rows, D), 0)
            for part in (ffn_grads[0], ffn_grads[1], down_grads)
        ]
        grad_small = jnp.concatenate(
            [grad_gain_qk, grad_alpha_attn, grad_alpha_ffn[0], grad_gf.reshape(-1)]
        )
        grad_small = lax.psum(grad_small, ("rep", "shard"))
        sum_gd = lax.dynamic_slice_in_dim(
            grad_small[: 3 * D].reshape(3, D), device_index * gd_rows, gd_rows, 1
        )
        sum_gf = lax.dynamic_slice_in_dim(
            grad_small[3 * D :].reshape(2, ffn_all), device_index * ffn_rows, ffn_rows, 1
        )
    grad_tokens = norm_back(normed_in, factor_in, grad_in)

    attn_unit, attn_m_new, attn_v_new = adam_rows(attn_w, attn_sums, attn_m, attn_v)
    ffn_unit, ffn_m_new, ffn_v_new = adam_rows(ffn_w, ffn_sums, ffn_m, ffn_v)
    gd_new, gd_m_new, gd_v_new = adam(gains_d, sum_gd, gd_m, gd_v, GAIN_RATE, 0.0)
    gf_new, gf_m_new, gf_v_new = adam(gains_ff, sum_gf, gf_m, gf_v, GAIN_RATE, 0.0)
    return (
        output,
        grad_tokens,
        attn_unit,
        attn_m_new,
        attn_v_new,
        ffn_unit,
        ffn_m_new,
        ffn_v_new,
        gd_new,
        gd_m_new,
        gd_v_new,
        gf_new,
        gf_m_new,
        gf_v_new,
    )

def solution(mesh):
    return jax.shard_map(
        body,
        mesh=mesh,
        in_specs=(
            P(("rep", "shard"), None),
            P("rep", None),
            P(("rep", "shard"), None),
            P(None, "shard", None),
            P(None, "shard", None),
            P(None, "shard", None),
            P(None, "shard", None),
            P(None, "shard", None),
            P(None, "shard", None),
            P(None, "shard"),
            P(None, "shard"),
            P(None, "shard"),
            P(None, "shard"),
            P(None, "shard"),
            P(None, "shard"),
        ),
        out_specs=(
            P(("rep", "shard"), None),
            P(("rep", "shard"), None),
            P(None, "shard", None),
            P(None, "shard", None),
            P(None, "shard", None),
            P(None, "shard", None),
            P(None, "shard", None),
            P(None, "shard", None),
            P(None, "shard"),
            P(None, "shard"),
            P(None, "shard"),
            P(None, "shard"),
            P(None, "shard"),
            P(None, "shard"),
        ),
        check_vma=False,
    )
```

```python
import functools
import math

import jax
import jax.numpy as jnp
from jax import lax
from jax.experimental import pallas as pl
from jax.experimental.pallas import tpu as pltpu
from jax.sharding import PartitionSpec as P

D = 1280
HEADS = 20
HEAD_DIM = 64
WINDOW = 1024
STEP = 10


SMALL = 1e-06
NEGATIVE = -1e30
BETA_ONE = 0.9
BETA_TWO = 0.95
RATE = 0.02
GAIN_RATE = 1.0
DECAY = 0.1
TINY = 1e-08
F32 = jnp.float32
BF16 = jnp.bfloat16


def from_behind(block, axis, distance):
    devices = range(lax.axis_size(axis))
    route = [(i - distance, i) for i in devices if i - distance in devices]
    return lax.ppermute(block, axis, route)


def rownorm(value):
    factor = lax.rsqrt(jnp.sum(value * value, -1, keepdims=True) + SMALL)
    return (value * factor, factor)


def norm_back(normed, factor, grad):
    return factor * (grad - normed * jnp.sum(normed * grad, -1, keepdims=True))


def adam(weight, grad, first, second, rate, decay):
    first = BETA_ONE * first + (1.0 - BETA_ONE) * grad
    second = BETA_TWO * second + (1.0 - BETA_TWO) * grad * grad
    fix_one = 1.0 - BETA_ONE**STEP
    fix_two = 1.0 - BETA_TWO**STEP
    change = first / fix_one / (jnp.sqrt(second / fix_two) + TINY) + decay * weight
    return (weight - rate * change, first, second)


def dot(a, b):
    return jnp.dot(a, b, preferred_element_type=F32)


def dot_nt(a, b):
    return lax.dot_general(a, b, (((1,), (1,)), ((), ())), preferred_element_type=F32)


def dot_tn(a, b):
    return lax.dot_general(a, b, (((0,), (0,)), ((), ())), preferred_element_type=F32)


def gather_rows(shard_rows):
    reps = lax.axis_size("rep")
    piece = shard_rows.shape[0] // reps
    mine = lax.dynamic_slice_in_dim(shard_rows, lax.axis_index("rep") * piece, piece, 0)
    column = lax.all_gather(mine, "shard", axis=0)
    return lax.all_gather(column, "rep", axis=1)


def reduce_rows(grad):
    part = lax.psum_scatter(grad, "rep", scatter_dimension=0)
    part = lax.psum_scatter(part, "shard", scatter_dimension=0)
    return lax.all_gather(part, "rep", axis=0, tiled=True)


MESH = pl.DeviceIdType.MESH
HALF = 80
CUTS = 2
PART = 32


def place():
    rep = lax.axis_index("rep")
    core, chip = lax.rem(rep, 2), rep // 2
    beside, above = chip + 1 - 2 * lax.rem(chip, 2), chip + 2 - 4 * (chip // 2)
    return core, chip, beside, above, 3 - chip


def remote(src, dst, send, recv, rep, shard):
    return pltpu.make_async_remote_copy(
        src_ref=src, dst_ref=dst, send_sem=send, recv_sem=recv,
        device_id=(rep, shard), device_id_type=MESH,
    )


def arrived(ref, sem):
    pltpu.make_async_copy(ref, ref, sem).wait()


def greet(shards):
    rep, line = lax.axis_index("rep"), lax.axis_index("shard")
    barrier = pltpu.get_barrier_semaphore()
    for n in range(1, 8):
        pl.semaphore_signal(barrier, inc=1, device_id=(lax.rem(rep + n, 8), line), device_id_type=MESH)
    for n in range(1, shards):
        pl.semaphore_signal(barrier, inc=1, device_id=(rep, lax.rem(line + n, shards)), device_id_type=MESH)
    pl.semaphore_wait(barrier, 6 + shards)


def add_into(target, sources, rows):
    def step(i, _):
        part = pl.ds(pl.multiple_of(i * 16, 16), 16)
        if len(sources) == 1:
            target[part, :] = target[part, :] + sources[0][part, :]
        else:
            value = target[part, :].astype(F32)
            for source in sources:
                value = value + source[part, :].astype(F32)
            target[part, :] = value.astype(BF16)
        return 0

    lax.fori_loop(0, rows // 16, step, 0, unroll=min(5, rows // 16))


def reduction_scratch(count, shards, rows):
    count, rows = CUTS * count, rows // CUTS
    steps = count * shards
    dma = pltpu.SemaphoreType.DMA
    return [
        pltpu.VMEM((steps, 4, rows, D), BF16),
        pltpu.VMEM((2, 4, rows, D), BF16),
        pltpu.VMEM((steps, rows, D), BF16),
        pltpu.VMEM((steps, 2, rows, D), BF16),
        pltpu.VMEM((count, shards + 1, rows, D), BF16),
        dma((2,)), dma(()), dma((steps,)), dma(()), dma((steps, 2)),
        dma(()), dma((steps, 2)), dma(()), dma((count, shards + 1)),
        dma(()), dma((count, 7)), dma(()),
    ]


REDUCTION_SCRATCH = 17


def reduction(grads, out, scratch):
    (acc, own, half, piece, below, own_sem, pair_send, pair_recv, half_send, half_recv,
     piece_send, piece_recv, line_send, line_recv, out_send, out_recv, out_local) = scratch
    count = CUTS * len(grads)
    rows = own.shape[2]
    shards = below.shape[1] - 1
    core, chip, beside, above, across = place()
    line = lax.axis_index("shard")
    steps = count * shards

    def owner(step):
        i = lax.rem(step, shards)
        back = lax.select(i < shards - 1 - line, shards - 1 - i, i - (shards - 1 - line))
        ahead = lax.select(i < line, i, shards - 1 - (i - line))
        other = lax.select(2 * line < shards, back, ahead)
        return lax.select(i == shards - 1, line, other)

    def cut(m):
        return pl.ds(pl.multiple_of(lax.rem(m, CUTS) * rows, rows), rows)

    def result(m, rep):
        return out.at[m // CUTS, rep, cut(m)]

    def ways(step):
        odd = lax.rem(step // shards, 2) == 1
        return lax.select(odd, above, beside), lax.select(odd, beside, above)

    def begin(step):
        slot, m = lax.rem(step, 2), step // shards
        for n, grad in enumerate(grads):
            @pl.when(m // CUTS == n)
            def _(grad=grad):
                remote(
                    grad.at[owner(step), :, 1 - core, cut(m)], acc.at[step], pair_send, pair_recv.at[step],
                    2 * chip + 1 - core, line,
                ).start()
                pltpu.make_async_copy(
                    grad.at[owner(step), :, core, cut(m)], own.at[slot], own_sem.at[slot]
                ).start()

    def first(step):
        slot = lax.rem(step, 2)
        arrived(own.at[slot], own_sem.at[slot])
        arrived(acc.at[step], pair_recv.at[step])
        for q in range(4):
            add_into(acc.at[step, q], (own.at[slot, q],), rows)
        one, two = ways(step)
        remote(acc.at[step, across, pl.ds(0, PART)], half.at[step, pl.ds(0, PART)],
               half_send, half_recv.at[step, 0], 2 * one + core, line).start()
        remote(acc.at[step, across, pl.ds(PART, rows - PART)], half.at[step, pl.ds(PART, rows - PART)],
               half_send, half_recv.at[step, 1], 2 * two + core, line).start()

    def second(step):
        one, two = ways(step)
        arrived(half.at[step, pl.ds(0, PART)], half_recv.at[step, 0])
        arrived(half.at[step, pl.ds(PART, rows - PART)], half_recv.at[step, 1])
        add_into(acc.at[step, two, pl.ds(0, PART)], (half.at[step, pl.ds(0, PART)],), PART)
        add_into(acc.at[step, one, pl.ds(PART, rows - PART)],
                 (half.at[step, pl.ds(PART, rows - PART)],), rows - PART)
        remote(acc.at[step, beside], piece.at[step, 0], piece_send, piece_recv.at[step, 0],
               2 * beside + core, line).start()
        remote(acc.at[step, above], piece.at[step, 1], piece_send, piece_recv.at[step, 1],
               2 * above + core, line).start()

    def pass_on(step):
        m, target = step // shards, owner(step)

        @pl.when(target > line)
        def _():
            remote(acc.at[step, chip], below.at[m, target], line_send, line_recv.at[m, target],
                   2 * chip + core, line + 1).start()

        @pl.when(target < line)
        def _():
            slot = lax.select(target == line - 1, shards, target)
            remote(acc.at[step, chip], below.at[m, slot], line_send, line_recv.at[m, slot],
                   2 * chip + core, line - 1).start()

    def outermost(step):
        target = owner(step)
        return ((target > line) & (line == 0)) | ((target < line) & (line == shards - 1))

    def third(step):
        for n in range(2):
            arrived(piece.at[step, n], piece_recv.at[step, n])
        add_into(acc.at[step, chip], (piece.at[step, 0], piece.at[step, 1]), rows)

        @pl.when(outermost(step))
        def _():
            pass_on(step)

    def along(step):
        m, target = step // shards, owner(step)

        def add_line(slot):
            arrived(below.at[m, slot], line_recv.at[m, slot])
            add_into(acc.at[step, chip], (below.at[m, slot],), rows)

        @pl.when(((target >= line) & (line > 0)) | ((target < line) & (line < shards - 1)))
        def _():
            add_line(target)

        @pl.when((target == line) & (line < shards - 1))
        def _():
            add_line(shards)

        @pl.when(jnp.logical_not(outermost(step)))
        def _():
            pass_on(step)

        @pl.when(target == line)
        def _():
            mine = 2 * chip + core
            pltpu.make_async_copy(acc.at[step, chip], result(m, mine), out_local).start()
            for n, other in enumerate((2 * beside + core, 2 * above + core, 2 * across + core, 2 * chip + 1 - core)):
                remote(acc.at[step, chip], result(m, mine), out_send, out_recv.at[m, n], other, line).start()

    def fourth(step):
        m = step // shards
        for n, origin in enumerate((2 * beside + core, 2 * above + core, 2 * across + core)):
            arrived(result(m, origin), out_recv.at[m, n])
            remote(result(m, origin), result(m, origin), out_send, out_recv.at[m, 4 + n],
                   2 * chip + 1 - core, line).start()

    def lead(t):
        @pl.when(t == 0)
        def _():
            begin(0)

        @pl.when(t + 1 < steps)
        def _():
            begin(t + 1)

        @pl.when(t < steps)
        def _():
            first(t)

    def follow(t):
        @pl.when((t >= 1) & (t < steps + 1))
        def _():
            second(t - 1)

        @pl.when((t >= 2) & (t < steps + 2))
        def _():
            third(t - 2)

        @pl.when((t >= 3) & (t < steps + 3))
        def _():
            along(t - 3)

        @pl.when((t >= 5) & (t < steps + 5) & (lax.rem(t - 5, shards) == shards - 1))
        def _():
            fourth(t - 5)

    def finish():
        for m in range(count):
            for n in range(4):
                arrived(result(m, 0), out_recv.at[m, 3 + n])
        arrived(out.at[:, 0], out_local)
        arrived(out.at[:, pl.ds(0, 7)], out_send)
        arrived(acc, pair_send)
        arrived(half, half_send)
        arrived(piece, piece_send)
        arrived(below.at[:, pl.ds(0, shards - 1)], line_send)

    return steps + 5, lead, follow, finish


def last_kernel(shards, down_ref, attn_ref, gains_ref, dq_ref, dk_ref, dv_ref, weight_ref,
                out, gains_out, back_out, own_out,
                line_got, plane_got, mine, line_send, line_recv, plane_send, plane_recv, back_send, back_recv,
                weight_buf, left_buf, parts, weight_sem, left_sem, *scratch):
    rep, line = lax.axis_index("rep"), lax.axis_index("shard")
    rows, cols = dq_ref.shape[0], dk_ref.shape[0]
    reach = back_out.shape[0]
    per = rows // BACK_BLOCK
    height = weight_ref.shape[2] // 4
    turns, lead, follow, finish = reduction((down_ref, attn_ref), out, scratch)
    greet(shards)
    for n in range(1, shards):
        other = lax.rem(line + n, shards)
        remote(gains_ref.at[other], line_got.at[n - 1], line_send, line_recv.at[n - 1], rep, other).start()
    for j in range(3):
        for shard in range(shards):
            pltpu.make_async_copy(
                weight_ref.at[0, shard, pl.ds(j * height, height)],
                weight_buf.at[j, pl.ds(shard * height, height)], weight_sem,
            ).start()

    def lefts(block):
        slot = lax.rem(block, 2)
        part = pl.ds(pl.multiple_of(block * BACK_BLOCK, BACK_BLOCK), BACK_BLOCK)
        return [
            pltpu.make_async_copy(ref.at[part], left_buf.at[slot, n], left_sem.at[slot, n])
            for n, ref in ((1, dk_ref), (2, dv_ref))
        ]

    def own_left(block):
        slot = lax.rem(block, 2)
        part = pl.ds(pl.multiple_of((block - reach * per) * BACK_BLOCK, BACK_BLOCK), BACK_BLOCK)
        return pltpu.make_async_copy(dq_ref.at[part], left_buf.at[slot, 0], left_sem.at[slot, 0])

    def fetch(block):
        for copy in lefts(block):
            copy.start()

        @pl.when(block >= reach * per)
        def _():
            own_left(block).start()

    def product(block):
        slot = lax.rem(block, 2)

        @pl.when(block + 1 < cols // BACK_BLOCK)
        def _():
            fetch(block + 1)

        for copy in lefts(block):
            copy.wait()
        total = dot(left_buf[slot, 1], weight_buf[1]) + dot(left_buf[slot, 2], weight_buf[2])

        @pl.when(block < reach * per)
        def _():
            parts[block] = total.astype(BF16)
            n = block // per
            part = pl.ds(pl.multiple_of(lax.rem(block, per) * BACK_BLOCK, BACK_BLOCK), BACK_BLOCK)

            @pl.when(line >= reach - n)
            def _():
                remote(parts.at[block], back_out.at[n, part], back_send.at[n], back_recv.at[n], rep,
                       line - (reach - n)).start()

        @pl.when(block >= reach * per)
        def _():
            own_left(block).wait()
            part = pl.ds(pl.multiple_of((block - reach * per) * BACK_BLOCK, BACK_BLOCK), BACK_BLOCK)
            own_out[part, :] = total + dot(left_buf[slot, 0], weight_buf[0])

    fetch(0)

    def step(t, _):
        lead(t)

        @pl.when(t == 2)
        def _():
            arrived(weight_buf, weight_sem)
            total = gains_ref[line]
            for n in range(shards - 1):
                arrived(line_got.at[n], line_recv.at[n])
                total = total + line_got[n]
            mine[...] = total
            for n in range(1, 8):
                remote(mine, plane_got.at[n - 1], plane_send, plane_recv.at[n - 1], lax.rem(rep + n, 8), line).start()

        @pl.when(t == 5)
        def _():
            total = mine[...]
            for n in range(7):
                arrived(plane_got.at[n], plane_recv.at[n])
                total = total + plane_got[n]
            gains_out[...] = total

        @pl.when((t < 3 * (cols // BACK_BLOCK)) & (lax.rem(t, 3) == 2))
        def _():
            product(t // 3)

        follow(t)
        return 0

    lax.fori_loop(0, max(turns, 3 * (cols // BACK_BLOCK)), step, 0)
    finish()
    arrived(line_got, line_send)
    arrived(plane_got, plane_send)
    for n in range(reach):
        @pl.when(line >= reach - n)
        def _(n=n):
            arrived(parts.at[pl.ds(0, per)], back_send.at[n])

        @pl.when(line + reach - n < shards)
        def _(n=n):
            arrived(back_out.at[n], back_recv.at[n])


BACK_BLOCK = 256


def reduce_last(down, attn, gains, grad_q, grad_k, grad_v, gathered):
    shards, _, _, rows, _ = down.shape
    tokens, cols = grad_q.shape[0], grad_k.shape[0]
    reach = (cols - tokens) // tokens
    any_space = pl.BlockSpec(memory_space=pl.ANY)
    vmem = pl.BlockSpec(memory_space=pltpu.VMEM)
    dma = pltpu.SemaphoreType.DMA
    return pl.pallas_call(
        functools.partial(last_kernel, shards),
        out_shape=(
            jax.ShapeDtypeStruct((2, 8, rows, D), BF16),
            jax.ShapeDtypeStruct(gains.shape[1:], F32),
            jax.ShapeDtypeStruct((reach, tokens, D), BF16),
            jax.ShapeDtypeStruct((tokens, D), F32),
        ),
        in_specs=[any_space, any_space, vmem] + [any_space] * 4,
        out_specs=(any_space, vmem, any_space, vmem),
        scratch_shapes=[
            pltpu.VMEM((shards - 1,) + gains.shape[1:], F32),
            pltpu.VMEM((7,) + gains.shape[1:], F32),
            pltpu.VMEM(gains.shape[1:], F32),
            dma(()), dma((shards - 1,)), dma(()), dma((7,)), dma((reach,)), dma((reach,)),
            pltpu.VMEM((3, D, D), BF16),
            pltpu.VMEM((2, 3, BACK_BLOCK, D), BF16),
            pltpu.VMEM((reach * tokens // BACK_BLOCK, BACK_BLOCK, D), BF16),
            dma(()), dma((2, 3)),
        ] + reduction_scratch(2, shards, rows),
        compiler_params=pltpu.CompilerParams(
            collective_id=2, has_side_effects=True, vmem_limit_bytes=62 * 2**20
        ),
        cost_estimate=pl.CostEstimate(flops=12 * 10**9, bytes_accessed=2 * 10**8, transcendentals=0),
    )(down, attn, gains, grad_q, grad_k, grad_v, gathered)


UNITS = 256


def feed_kernel(blocks, mid_ref, middle_ref, cot_ref, alpha_ref, up_scale_ref, gate_scale_ref, wu_ref, wg_ref, wd_ref,
                out_ref, grad_mid_ref, grad_ref, down_ref, up_sum_ref, gate_sum_ref, alpha_sum_ref,
                up_buf, gate_buf, hidden_buf, total, back, grad_hidden_buf, grad_u_buf, grad_g_buf):
    turn = pl.program_id(0)
    after = turn - blocks - 2

    def raw(block):
        up_buf[block] = dot_nt(mid_ref[...], wu_ref[...])
        gate_buf[block] = dot_nt(mid_ref[...], wg_ref[...])

    def activate(block):
        gate = gate_buf[block] * (gate_scale_ref[...] * math.sqrt(D))
        hidden = gate * jax.nn.sigmoid(gate) * (up_buf[block] * up_scale_ref[...])
        hidden_buf[block] = hidden.astype(BF16)

    def project(block, first):
        part = dot(hidden_buf[block], wd_ref[...])
        total[...] = part if first else total[...] + part

    def middle_step():
        alpha = alpha_ref[...]
        rows = total.shape[0]

        def step(i, sums):
            part = pl.ds(pl.multiple_of(i * 32, 32), 32)
            branch, factor = rownorm(total[part, :])
            middle = middle_ref[part, :]
            final, final_factor = rownorm(middle + alpha * (branch - middle))
            out_ref[part, :] = final.astype(BF16)
            grad = norm_back(final, final_factor, cot_ref[part, :].astype(F32))
            grad_mid_ref[part, :] = grad * (1.0 - alpha)
            back[part, :] = norm_back(branch, factor, grad * alpha).astype(BF16)
            return sums + jnp.sum(grad * (branch - middle), 0, keepdims=True)

        alpha_sum_ref[...] = lax.fori_loop(0, rows // 32, step, jnp.zeros((1, D), F32))

    def back_raw():
        grad_hidden_buf[...] = dot_nt(back[...], wd_ref[...])

    def back_activate(block):
        up_scale, gate_scale = up_scale_ref[...], gate_scale_ref[...] * math.sqrt(D)
        grad_hidden = grad_hidden_buf[...]
        up_raw, gate_raw = up_buf[block], gate_buf[block]
        gate = gate_raw * gate_scale
        sigma = jax.nn.sigmoid(gate)
        active = gate * sigma
        upward = up_raw * up_scale
        grad_upward = grad_hidden * active
        grad_gate = grad_hidden * upward * (sigma * (1.0 + gate * (1.0 - sigma)))
        up_sum_ref[...] = jnp.sum(grad_upward * up_raw, 0, keepdims=True)
        gate_sum_ref[...] = jnp.sum(grad_gate * gate_raw, 0, keepdims=True) * math.sqrt(D)
        grad_u_buf[...] = (grad_upward * up_scale).astype(BF16)
        grad_g_buf[...] = (grad_gate * gate_scale).astype(BF16)

    def back_project(block):
        grad_u, grad_g = grad_u_buf[...], grad_g_buf[...]
        grad_ref[0] = dot_tn(grad_u, mid_ref[...]).astype(BF16)
        grad_ref[1] = dot_tn(grad_g, mid_ref[...]).astype(BF16)
        down_ref[...] = dot_tn(hidden_buf[block], back[...]).astype(BF16)
        grad_mid_ref[...] += dot(grad_u, wu_ref[...]) + dot(grad_g, wg_ref[...])

    @pl.when(turn == 0)
    def _():
        raw(0)

    @pl.when(turn == 1)
    def _():
        activate(0)
        raw(1)

    @pl.when(turn == 2)
    def _():
        project(0, True)
        activate(1)
        raw(2)

    @pl.when((turn > 2) & (turn < blocks))
    def _():
        project(turn - 2, False)
        activate(turn - 1)
        raw(turn)

    @pl.when(turn == blocks)
    def _():
        project(turn - 2, False)
        activate(turn - 1)

    @pl.when(turn == blocks + 1)
    def _():
        project(turn - 2, False)
        middle_step()

    @pl.when(after == 0)
    def _():
        back_raw()

    @pl.when(after == 1)
    def _():
        back_activate(0)
        back_raw()

    @pl.when((after > 1) & (after < blocks))
    def _():
        back_project(after - 2)
        back_activate(after - 1)
        back_raw()

    @pl.when(after == blocks)
    def _():
        back_project(after - 2)
        back_activate(after - 1)

    @pl.when(after == blocks + 1)
    def _():
        back_project(after - 2)


def feed_forward(mid_low, middle, cotangent, alpha_ffn, scales, weights, firsts):
    rows = mid_low.shape[0]
    blocks = scales.shape[1] // UNITS
    whole = lambda *shape: pl.BlockSpec(shape, lambda t: (0,) * len(shape))
    half = blocks + 2

    def stage(t, early, late):
        return jnp.clip(lax.select(t < half, t - early, t - half - late), 0, blocks - 1)

    weight = lambda m, early, late: pl.BlockSpec((None, UNITS, D), lambda t: (m, stage(t, early, late), 0))
    done = lambda t, lag: jnp.clip(t - half - lag, 0, blocks - 1)
    units = pl.BlockSpec((1, UNITS), lambda t: (0, done(t, 1)))
    scale = pl.BlockSpec((1, UNITS), lambda t: (0, stage(t, 1, 1)))
    return pl.pallas_call(
        functools.partial(feed_kernel, blocks),
        grid=(2 * half,),
        out_shape=(
            jax.ShapeDtypeStruct((rows, D), BF16),
            jax.ShapeDtypeStruct((rows, D), F32),
            jax.ShapeDtypeStruct((2, blocks * UNITS, D), BF16),
            jax.ShapeDtypeStruct((blocks * UNITS, D), BF16),
            jax.ShapeDtypeStruct((1, blocks * UNITS), F32),
            jax.ShapeDtypeStruct((1, blocks * UNITS), F32),
            jax.ShapeDtypeStruct((1, D), F32),
        ),
        in_specs=[whole(rows, D), whole(rows, D), whole(rows, D), whole(1, D), scale, scale]
        + [weight(firsts[0], 0, 2), weight(firsts[1], 0, 2), weight(firsts[2], 2, 0)],
        out_specs=(
            whole(rows, D), whole(rows, D), pl.BlockSpec((2, UNITS, D), lambda t: (0, done(t, 2), 0)),
            pl.BlockSpec((UNITS, D), lambda t: (done(t, 2), 0)),
            units, units, whole(1, D),
        ),
        scratch_shapes=[
            pltpu.VMEM((blocks, rows, UNITS), F32),
            pltpu.VMEM((blocks, rows, UNITS), F32),
            pltpu.VMEM((blocks, rows, UNITS), BF16),
            pltpu.VMEM((rows, D), F32),
            pltpu.VMEM((rows, D), BF16),
            pltpu.VMEM((rows, UNITS), F32),
            pltpu.VMEM((rows, UNITS), BF16),
            pltpu.VMEM((rows, UNITS), BF16),
        ],
        compiler_params=pltpu.CompilerParams(vmem_limit_bytes=62 * 2**20),
        cost_estimate=pl.CostEstimate(flops=60 * 10**9, bytes_accessed=120 * 10**6, transcendentals=5 * 10**6),
    )(mid_low, middle, cotangent, alpha_ffn, scales[:1], scales[1:], *weights)


def adam_kernel(places, per, *refs):
    grads = refs[:places]
    w_ref, m_ref, v_ref, w_out, m_out, v_out = refs[places:]
    group, piece, _ = w_ref.shape

    def update(g_ref):
        for n in range(group):
            def step(i, _, n=n):
                part = (n, pl.ds(pl.multiple_of(i * 16, 16), 16), slice(None))
                new, first, second = adam(
                    w_ref[part], g_ref[part].astype(F32), m_ref[part], v_ref[part], RATE, DECAY
                )
                w_out[part] = rownorm(new)[0]
                m_out[part] = first
                v_out[part] = second
                return 0

            lax.fori_loop(0, piece // 16, step, 0, unroll=5)

    for n in range(places):
        @pl.when(pl.program_id(0) // per == n)
        def _(n=n):
            update(grads[n])


def adam_rows(weight, grads, first, second):
    places = len(grads)
    _, per, piece, _ = grads[0][0].shape
    group = 2 if per % 2 == 0 else 1
    steps = per // group
    spec = pl.BlockSpec((group, piece, D), lambda p: (p, 0, 0))

    def grad_spec(n, index):
        return pl.BlockSpec(
            (None, group, piece, D), lambda p: (index, jnp.clip(p - n * steps, 0, steps - 1), 0, 0)
        )

    shape = jax.ShapeDtypeStruct((places * per, piece, D), F32)
    news = pl.pallas_call(
        functools.partial(adam_kernel, places, steps),
        grid=(places * steps,),
        out_shape=(shape,) * 3,
        in_specs=[grad_spec(n, index) for n, (_, index) in enumerate(grads)] + [spec] * 3,
        out_specs=(spec,) * 3,
        compiler_params=pltpu.CompilerParams(vmem_limit_bytes=60 * 2**20),
        cost_estimate=pl.CostEstimate(flops=20 * weight.size, bytes_accessed=26 * weight.size, transcendentals=0),
    )(*(array for array, _ in grads), *(old.reshape(shape.shape) for old in (weight, first, second)))
    return tuple(new.reshape(weight.shape) for new in news)


QUERY_BLOCK = 256
PAIR = 2 * HEAD_DIM
PAIRS = HEADS // 2


def head_ones():
    row = lax.broadcasted_iota(jnp.int32, (PAIR, PAIR), 0) // HEAD_DIM
    col = lax.broadcasted_iota(jnp.int32, (PAIR, PAIR), 1) // HEAD_DIM
    return (row == col).astype(F32).astype(BF16)


def head_sum(value, ones):
    high = value.astype(BF16)
    rest = (value - high.astype(F32)).astype(BF16)
    return dot(high, ones) + dot(rest, ones)


def of_head(value, head):
    lane = lax.broadcasted_iota(jnp.int32, value.shape, 1) // HEAD_DIM
    return jnp.where(lane == head, value, jnp.zeros_like(value))


def attend_pair(h_ref, wq_ref, wq2_ref, wk_ref, wk2_ref, wv_ref, wv2_ref, gain_ref, bias_ref, qp_ref, kp_ref, v_ref, o_ref, lse_ref,
                key_buf, query_buf, value_buf):
    cols = h_ref.shape[0]
    rows = qp_ref.shape[0]
    span = bias_ref.shape[1]
    ones = head_ones()
    gain = gain_ref[...]
    weights = jnp.concatenate([wk_ref[...], wk2_ref[...], wv_ref[...], wv2_ref[...]], 0)
    query_weights = jnp.concatenate([wq_ref[...], wq2_ref[...]], 0)

    def project(i, _):
        part = pl.ds(pl.multiple_of(i * QUERY_BLOCK, QUERY_BLOCK), QUERY_BLOCK)
        both = dot_nt(h_ref[part, :], weights)
        keys = both[:, :PAIR]
        kp_ref[part, :] = keys
        factor = lax.rsqrt(head_sum(keys * keys, ones) + SMALL)
        key_buf[part, :] = (keys * factor * gain).astype(BF16)
        values = both[:, PAIR:].astype(BF16)
        v_ref[part, :] = values
        value_buf[part, :PAIR] = values
        value_buf[part, PAIR:] = jnp.ones_like(values)
        return 0

    lax.fori_loop(0, cols // QUERY_BLOCK, project, 0)

    def project_queries(i, _):
        part = pl.ds(pl.multiple_of(i * QUERY_BLOCK, QUERY_BLOCK), QUERY_BLOCK)
        own = pl.ds(pl.multiple_of(cols - rows + i * QUERY_BLOCK, QUERY_BLOCK), QUERY_BLOCK)
        queries = dot_nt(h_ref[own, :], query_weights)
        qp_ref[part, :] = queries
        factor = lax.rsqrt(head_sum(queries * queries, ones) + SMALL)
        scaled = (queries * factor * gain).astype(BF16).astype(F32) * math.sqrt(HEAD_DIM)
        query_buf[part, :] = scaled.astype(BF16)
        return 0

    lax.fori_loop(0, rows // QUERY_BLOCK, project_queries, 0)
    for i in range(rows // QUERY_BLOCK):
        part = pl.ds(i * QUERY_BLOCK, QUERY_BLOCK)
        reach = pl.ds(i * QUERY_BLOCK, span)
        sides = []
        for head in range(2):
            scores = dot_nt(of_head(query_buf[part, :], head), key_buf[reach, :])
            probs = jnp.exp(scores + bias_ref[part, :]).astype(BF16)
            both = dot(probs, value_buf[reach, :])
            total = both[:, PAIR:]
            sides.append(both[:, :PAIR] / total)
            lse_ref[head : head + 1, part] = jnp.log(total).T[:1, :]
        lane = lax.broadcasted_iota(jnp.int32, sides[0].shape, 1)
        o_ref[part, :] = jnp.where(lane < HEAD_DIM, sides[0], sides[1]).astype(BF16)


def back_pair(*refs):
    start, block, finish = back_parts(*refs)
    start()
    for i in range(refs[0].shape[0] // QUERY_BLOCK):
        block(i)
    finish()


def back_parts(qp_ref, kp_ref, v_ref, o_ref, da_ref, wo_ref, wo2_ref, gain_ref, bias_ref, lse_ref,
               dq_ref, dk_ref, dv_ref, sum_ref, key_buf, key_turned, k_total, v_total):
    cols = kp_ref.shape[0]
    rows = qp_ref.shape[0]
    span = bias_ref.shape[1]

    def keys_of(i, _):
        ones, gain = head_ones(), gain_ref[...]
        part = pl.ds(pl.multiple_of(i * QUERY_BLOCK, QUERY_BLOCK), QUERY_BLOCK)
        keys = kp_ref[part, :]
        factor = lax.rsqrt(head_sum(keys * keys, ones) + SMALL)
        low = keys * factor * gain
        key_buf[part, :] = low.astype(BF16)
        key_turned[:, part] = low.T.astype(BF16)
        k_total[part, :] = jnp.zeros_like(keys)
        v_total[part, :] = jnp.zeros_like(keys)
        return 0

    def start():
        lax.fori_loop(0, cols // QUERY_BLOCK, keys_of, 0)

    def block(i):
        ones, gain = head_ones(), gain_ref[...]
        weights = jnp.concatenate([wo_ref[...], wo2_ref[...]], 0)
        part = pl.ds(i * QUERY_BLOCK, QUERY_BLOCK)
        reach = pl.ds(i * QUERY_BLOCK, span)
        queries = qp_ref[part, :]
        factor = lax.rsqrt(head_sum(queries * queries, ones) + SMALL)
        hat = queries * factor
        scaled = ((hat * gain).astype(BF16).astype(F32) * math.sqrt(HEAD_DIM)).astype(BF16)
        back = dot_nt(da_ref[part, :], weights).astype(BF16)
        inner = (back.astype(F32) * o_ref[part, :].astype(F32)).T
        sides = []
        for head in range(2):
            mine = slice(head * HEAD_DIM, (head + 1) * HEAD_DIM)
            query, grad = of_head(scaled, head), of_head(back, head)
            scores = dot_nt(key_buf[reach, :], query)
            probs = jnp.exp(scores + bias_ref[i] - lse_ref[head : head + 1, part])
            v_total[reach, :] += dot(probs.astype(BF16), grad)
            delta = jnp.sum(inner[mine, :], 0, keepdims=True)
            grad_scores = (probs * (dot_nt(v_ref[reach, :], grad) - delta)).astype(BF16)
            k_total[reach, :] += dot(grad_scores, query)
            sides.append(dot(key_turned[mine, reach], grad_scores))
        grad_q = jnp.concatenate(sides, 0).T * math.sqrt(HEAD_DIM)
        sums = jnp.sum(grad_q * hat, 0, keepdims=True)
        if i == 0:
            sum_ref[...] = jnp.broadcast_to(sums, sum_ref.shape)
        else:
            sum_ref[...] += jnp.broadcast_to(sums, sum_ref.shape)
        grad_q = grad_q * gain
        dq_ref[part, :] = (factor * (grad_q - hat * head_sum(hat * grad_q, ones))).astype(BF16)

    def close(i, _):
        ones, gain = head_ones(), gain_ref[...]
        part = pl.ds(pl.multiple_of(i * QUERY_BLOCK, QUERY_BLOCK), QUERY_BLOCK)
        keys = kp_ref[part, :]
        factor = lax.rsqrt(head_sum(keys * keys, ones) + SMALL)
        hat = keys * factor
        grad_k = k_total[part, :]
        sum_ref[...] += jnp.broadcast_to(jnp.sum(grad_k * hat, 0, keepdims=True), sum_ref.shape)
        grad_k = grad_k * gain
        dk_ref[part, :] = (factor * (grad_k - hat * head_sum(hat * grad_k, ones))).astype(BF16)
        dv_ref[part, :] = v_total[part, :].astype(BF16)
        return 0

    def finish():
        lax.fori_loop(0, cols // QUERY_BLOCK, close, 0)

    return start, block, finish


def head_rows(attn_low, matrix, second):
    heads = attn_low.shape[2]

    def index(p):
        head = 2 * p + second
        return (head // heads, matrix, lax.rem(head, heads), 0, 0)

    return pl.BlockSpec((None, None, None, HEAD_DIM, D), index)


def attention_forward(low_all, attn_low, gain_qk, bias, rows):
    cols = low_all.shape[0]
    span = bias.shape[1]
    side = lambda n: pl.BlockSpec((n, PAIR), lambda p: (0, p))
    whole = lambda *shape: pl.BlockSpec(shape, lambda p: (0,) * len(shape))
    return pl.pallas_call(
        attend_pair,
        grid=(PAIRS,),
        out_shape=(
            jax.ShapeDtypeStruct((rows, D), F32),
            jax.ShapeDtypeStruct((cols, D), F32),
            jax.ShapeDtypeStruct((cols, D), BF16),
            jax.ShapeDtypeStruct((rows, D), BF16),
            jax.ShapeDtypeStruct((PAIRS, 8, rows), F32),
        ),
        in_specs=[whole(cols, D)]
        + [head_rows(attn_low, j, second) for j in range(3) for second in range(2)]
        + [side(1), whole(rows, span)],
        out_specs=(side(rows), side(cols), side(cols), side(rows),
                   pl.BlockSpec((None, 8, rows), lambda p: (p, 0, 0))),
        scratch_shapes=[
            pltpu.VMEM((cols, PAIR), BF16),
            pltpu.VMEM((rows, PAIR), BF16),
            pltpu.VMEM((cols, 2 * PAIR), BF16),
        ],
        compiler_params=pltpu.CompilerParams(vmem_limit_bytes=56 * 2**20),
        cost_estimate=pl.CostEstimate(flops=20 * 10**9, bytes_accessed=30 * 10**6, transcendentals=13 * 10**6),
    )(low_all, *[attn_low] * 6, gain_qk, bias)


def attention_backward(q_pre, k_pre, value_all, o_low, grad_spre, attn_low, gain_qk, bias_turned, lse):
    rows, cols = q_pre.shape[0], k_pre.shape[0]
    side = lambda n: pl.BlockSpec((n, PAIR), lambda p: (0, p))
    whole = lambda *shape: pl.BlockSpec(shape, lambda p: (0,) * len(shape))
    stat = pl.BlockSpec((None, 8, rows), lambda p: (p, 0, 0))
    return pl.pallas_call(
        back_pair,
        grid=(PAIRS,),
        out_shape=(
            jax.ShapeDtypeStruct((rows, D), BF16),
            jax.ShapeDtypeStruct((cols, D), BF16),
            jax.ShapeDtypeStruct((cols, D), BF16),
            jax.ShapeDtypeStruct((PAIRS, 8, PAIR), F32),
        ),
        in_specs=[
            side(rows), side(cols), side(cols), side(rows), whole(rows, D),
            head_rows(attn_low, 3, 0), head_rows(attn_low, 3, 1),
            pl.BlockSpec((None, 1, PAIR), lambda p: (p, 0, 0)), whole(*bias_turned.shape), stat,
        ],
        out_specs=(side(rows), side(cols), side(cols), pl.BlockSpec((None, 8, PAIR), lambda p: (p, 0, 0))),
        scratch_shapes=[
            pltpu.VMEM((cols, PAIR), BF16),
            pltpu.VMEM((PAIR, cols), BF16),
            pltpu.VMEM((cols, PAIR), F32),
            pltpu.VMEM((cols, PAIR), F32),
        ],
        compiler_params=pltpu.CompilerParams(vmem_limit_bytes=56 * 2**20),
        cost_estimate=pl.CostEstimate(flops=30 * 10**9, bytes_accessed=40 * 10**6, transcendentals=13 * 10**6),
    )(q_pre, k_pre, value_all, o_low, grad_spre, attn_low, attn_low, gain_qk, bias_turned, lse)


START = 5


def gather_kernel(shards, attn_ref, ffn_ref, gains_ref, tokens_ref, bias_ref,
                  out, gains_out, h_out, qp_out, kp_out, v_out, o_out, lse_ref,
                  wide, low, mine, wide_sem, low_sem, mine_sem, line_send, line_recv, plane_send, beside_recv,
                  above_recv, across_recv, pair_send, pair_recv, gains_send, gains_recv, tokens_send,
                  tokens_recv, local_sem, gains_buf, before, h_buf, load_sem, store_sem,
                  weight_buf, gain_row, qp_buf, kp_buf, v_buf, o_buf, key_buf, query_buf, value_buf):
    core, chip, beside, above, across = place()
    line = lax.axis_index("shard")
    rep = 2 * chip + core
    sibling = 2 * chip + 1 - core
    to_beside, to_above = 2 * beside + core, 2 * above + core
    piece = attn_ref.shape[1]
    rows = tokens_ref.shape[0]
    heads = 2 * piece // HEAD_DIM
    others = shards - 1
    steps = 4 * others
    greet(shards)

    def rows_of(m, shard, rep, start=0, size=None):
        first = pl.multiple_of(rep * piece + start, 16)
        return out.at[m, shard, pl.ds(first, piece if size is None else size)]

    def source(n):
        low_side = 2 * line < shards
        edge = lax.select(low_side, line, shards - 1 - line)
        near = lax.select(lax.rem(n, 2) == 0, edge - 1 - n // 2, edge + 1 + n // 2)
        found = lax.select(n < 2 * edge, near, n + 1)
        return lax.select(low_side, found, shards - 1 - found)

    def own_send(m):
        @pl.when(line < shards - 1)
        def _():
            remote(mine.at[m], rows_of(m, line, rep), line_send, line_recv.at[m, line], rep, line + 1).start()

        @pl.when(line > 0)
        def _():
            remote(mine.at[m], rows_of(m, line, rep), line_send, line_recv.at[m, line], rep, line - 1).start()

    def fetch(index, slot):
        @pl.when(index < 8)
        def _():
            pltpu.make_async_copy(attn_ref.at[lax.rem(index, 8)], wide.at[slot], wide_sem.at[slot]).start()

        @pl.when(index >= 8)
        def _():
            pltpu.make_async_copy(
                ffn_ref.at[jnp.maximum(index // 8 - 1, 0), lax.rem(index, 8)], wide.at[slot], wide_sem.at[slot]
            ).start()

    def store(index, slot):
        return pltpu.make_async_copy(low.at[slot], rows_of(index // 8, line, lax.rem(index, 8)), low_sem.at[slot])

    def lower(src, dst):
        def step(i, _):
            part = pl.ds(pl.multiple_of(i * 32, 32), 32)
            dst[part, :] = src[part, :].astype(BF16)
            return 0

        lax.fori_loop(0, piece // 32, step, 0)

    for n in range(1, shards):
        other = lax.rem(line + n, shards)
        remote(gains_ref, gains_buf.at[line], gains_send, gains_recv.at[line], rep, other).start()
    pltpu.make_async_copy(gains_ref, gains_buf.at[line], local_sem).start()
    own = pl.ds(2 * rows, rows)
    pltpu.make_async_copy(tokens_ref, h_buf.at[own], load_sem.at[0, 0]).start()
    for m in range(4):
        origin = attn_ref.at[rep] if m == 0 else ffn_ref.at[m - 1, rep]
        pltpu.make_async_copy(origin, wide.at[m], mine_sem.at[m]).start()
    for m in range(4):
        arrived(wide.at[m], mine_sem.at[m])
        lower(wide.at[m], mine.at[m])
        if m == 0:
            own_send(0)

            @pl.when(line < shards - 1)
            def _():
                remote(tokens_ref, before.at[1], tokens_send, tokens_recv.at[1], rep, line + 1).start()

    for n in range(2):
        fetch(n, n)

    def norm_rows(source, first):
        def step(i, _):
            at = pl.multiple_of(first + i * 32, 32)
            value = source[pl.ds(pl.multiple_of(i * 32, 32), 32), :].astype(F32)
            h_buf[pl.ds(at, 32), :] = rownorm(value)[0].astype(BF16)
            return 0

        lax.fori_loop(0, rows // 32, step, 0)

    def clear_rows(first):
        h_buf[pl.ds(first, rows), :] = jnp.zeros((rows, D), BF16)

    arrived(h_buf.at[own], load_sem.at[0, 0])
    norm_rows(h_buf.at[own], 2 * rows)

    def loads(p, slot):
        copies = []
        for j in range(3):
            for second in range(2):
                head = 2 * p + second
                first = pl.multiple_of(2 * piece * j + HEAD_DIM * lax.rem(head, heads), HEAD_DIM)
                copies.append(
                    pltpu.make_async_copy(
                        out.at[0, head // heads, pl.ds(first, HEAD_DIM)], weight_buf.at[slot, 2 * j + second],
                        load_sem.at[slot, 2 * j + second],
                    )
                )
        return copies

    def stores(p, slot):
        lanes = pl.ds(pl.multiple_of(p * PAIR, PAIR), PAIR)
        return [
            pltpu.make_async_copy(buf.at[slot], ref.at[:, lanes], store_sem.at[slot, n])
            for n, (ref, buf) in enumerate(((qp_out, qp_buf), (kp_out, kp_buf), (v_out, v_buf), (o_out, o_buf)))
        ]

    def pair(p):
        slot = lax.rem(p, 2)

        @pl.when(p + 1 < PAIRS)
        def _():
            for copy in loads(p + 1, 1 - slot):
                copy.start()

        for copy in loads(p, slot):
            copy.wait()

        @pl.when(p >= 2)
        def _():
            for copy in stores(p - 2, slot):
                copy.wait()

        row = lax.broadcasted_iota(jnp.int32, (8, PAIR), 0)
        left, right = (
            jnp.sum(
                jnp.where(row == lax.rem(2 * p + n, heads), gains_buf[(2 * p + n) // heads, :8, :PAIR], 0.0),
                0, keepdims=True,
            )
            for n in range(2)
        )
        lane = lax.broadcasted_iota(jnp.int32, (1, PAIR), 1)
        gain_row[...] = jnp.where(lane < HEAD_DIM, left, right)
        attend_pair(
            h_buf, *(weight_buf.at[slot, n] for n in range(6)), gain_row, bias_ref, qp_buf.at[slot],
            kp_buf.at[slot], v_buf.at[slot], o_buf.at[slot], lse_ref.at[p], key_buf, query_buf, value_buf,
        )
        for copy in stores(p, slot):
            copy.start()

    def begin(c):
        m, origin = c // others, source(lax.rem(c, others))
        got = rows_of(m, origin, rep)
        arrived(got, line_recv.at[m, origin])

        @pl.when((origin < line) & (line < shards - 1))
        def _():
            remote(got, got, line_send, line_recv.at[m, origin], rep, line + 1).start()

        @pl.when((origin > line) & (line > 0))
        def _():
            remote(got, got, line_send, line_recv.at[m, origin], rep, line - 1).start()

        remote(got, got, plane_send, beside_recv.at[m, origin], to_beside, line).start()
        remote(got, got, plane_send, above_recv.at[m, origin], to_above, line).start()
        remote(got, got, pair_send, pair_recv.at[m], sibling, line).start()

    def middle(c):
        m, origin = c // others, source(lax.rem(c, others))
        got = rows_of(m, origin, to_beside)
        arrived(got, beside_recv.at[m, origin])
        part = rows_of(m, origin, to_beside, 0, HALF)
        remote(part, part, plane_send, across_recv.at[m, origin, 0], to_above, line).start()
        remote(got, got, pair_send, pair_recv.at[m], sibling, line).start()
        got = rows_of(m, origin, to_above)
        arrived(got, above_recv.at[m, origin])
        part = rows_of(m, origin, to_above, HALF, piece - HALF)
        remote(part, part, plane_send, across_recv.at[m, origin, 1], to_beside, line).start()
        remote(got, got, pair_send, pair_recv.at[m], sibling, line).start()

    def last(c):
        m, origin = c // others, source(lax.rem(c, others))
        got = rows_of(m, origin, 2 * across + core)
        arrived(rows_of(m, origin, 2 * across + core, 0, HALF), across_recv.at[m, origin, 0])
        arrived(rows_of(m, origin, 2 * across + core, HALF, piece - HALF), across_recv.at[m, origin, 1])
        remote(got, got, pair_send, pair_recv.at[m], sibling, line).start()

    def local(t):
        for n in range(2):
            index = 2 * t + n
            slot = 2 * lax.rem(t, 2) + n
            arrived(wide.at[slot], wide_sem.at[slot])

            @pl.when(index + 2 < 32)
            def _():
                fetch(index + 2, lax.rem(slot + 2, 4))

            @pl.when(t >= 2)
            def _():
                store(index - 4, slot).wait()

            lower(wide.at[slot], low.at[slot])
            store(index, slot).start()

    def turn(t, _):
        @pl.when((lax.rem(t, others) == 0) & (t // others < 3))
        def _():
            own_send(t // others + 1)

        @pl.when(t < steps)
        def _():
            begin(t)

        @pl.when((t == 1) & (line > 0))
        def _():
            arrived(before.at[1], tokens_recv.at[1])

            @pl.when(line < shards - 1)
            def _():
                remote(before.at[1], before.at[0], tokens_send, tokens_recv.at[0], rep, line + 1).start()

            norm_rows(before.at[1], rows)

        @pl.when((t == 1) & (line == 0))
        def _():
            clear_rows(rows)

        @pl.when((t == 3) & (line > 1))
        def _():
            arrived(before.at[0], tokens_recv.at[0])
            norm_rows(before.at[0], 0)

        @pl.when((t == 3) & (line <= 1))
        def _():
            clear_rows(0)

        @pl.when(t < 2)
        def _():
            local(2 * t)
            local(2 * t + 1)

        @pl.when(t >= 2)
        def _():
            local(t + 2)

        @pl.when(t == START)
        def _():
            pltpu.make_async_copy(gains_ref, gains_buf.at[line], local_sem).wait()
            for n in range(1, shards):
                other = lax.rem(line + n, shards)
                arrived(gains_buf.at[other], gains_recv.at[other])
            arrived(out.at[0, pl.ds(0, others), pl.ds(0, 4 * piece)], pair_recv.at[0])
            for copy in loads(0, 0):
                copy.start()

        early = (t > START + 3).astype(jnp.int32) + (t > START + 6).astype(jnp.int32)
        most = lax.select((t == START + 3) | (t == START + 6), 2, 1)

        def one(n, _):
            pair(t - START + early + n)
            return 0

        lax.fori_loop(0, lax.select((t >= START) & (t < START + PAIRS - 2), most, 0), one, 0)

        @pl.when((t >= 1) & (t < steps + 1))
        def _():
            middle(t - 1)

        @pl.when((t >= 2) & (t < steps + 2))
        def _():
            last(t - 2)

        return 0

    lax.fori_loop(0, 14, turn, 0)
    for n in range(4):
        store(28 + n, n).wait()
    gains_copy = pltpu.make_async_copy(gains_buf, gains_out, local_sem)
    h_copy = pltpu.make_async_copy(h_buf, h_out, load_sem.at[0, 0])
    gains_copy.start()
    h_copy.start()
    for p in (PAIRS - 2, PAIRS - 1):
        for copy in stores(p, p % 2):
            copy.wait()
    for m in range(1, 4):
        arrived(out.at[m, pl.ds(0, others), pl.ds(0, 4 * piece)], pair_recv.at[m])
    gains_copy.wait()
    h_copy.wait()

    @pl.when((line == 1) | (line == shards - 2))
    def _():
        arrived(before, tokens_send)

    @pl.when(line == 0)
    def _():
        arrived(before.at[0], tokens_send)

    @pl.when((line == 0) | (line == shards - 1))
    def _():
        arrived(out.at[:, 0, pl.ds(0, piece)], line_send)

    @pl.when((line > 0) & (line < shards - 1))
    def _():
        arrived(out.at[:, 0, pl.ds(0, 5 * piece)], line_send)

    arrived(out.at[:, pl.ds(0, others), pl.ds(0, 3 * piece)], plane_send)
    arrived(out.at[:, pl.ds(0, others), pl.ds(0, 4 * piece)], pair_send)
    arrived(gains_buf.at[pl.ds(0, others)], gains_send)


def gather_attend(attn_w, ffn_w, gains, tokens, bias, shards):
    piece = attn_w.shape[1]
    rows = tokens.shape[0]
    cols = rows + WINDOW
    any_space = pl.BlockSpec(memory_space=pl.ANY)
    vmem = pl.BlockSpec(memory_space=pltpu.VMEM)
    dma = pltpu.SemaphoreType.DMA
    return pl.pallas_call(
        functools.partial(gather_kernel, shards),
        out_shape=(
            jax.ShapeDtypeStruct((4, shards, 8 * piece, D), BF16),
            jax.ShapeDtypeStruct((shards,) + gains.shape, F32),
            jax.ShapeDtypeStruct((cols, D), BF16),
            jax.ShapeDtypeStruct((rows, D), F32),
            jax.ShapeDtypeStruct((cols, D), F32),
            jax.ShapeDtypeStruct((cols, D), BF16),
            jax.ShapeDtypeStruct((rows, D), BF16),
            jax.ShapeDtypeStruct((PAIRS, 8, rows), F32),
        ),
        in_specs=[any_space] * 4 + [vmem],
        out_specs=(any_space,) * 7 + (vmem,),
        scratch_shapes=[
            pltpu.VMEM((4, piece, D), F32),
            pltpu.VMEM((4, piece, D), BF16),
            pltpu.VMEM((4, piece, D), BF16),
            dma((4,)), dma((4,)), dma((4,)), dma(()), dma((4, shards)), dma(()), dma((4, shards)),
            dma((4, shards)), dma((4, shards, 2)), dma(()), dma((4,)), dma(()), dma((shards,)), dma(()),
            dma((2,)), dma(()),
            pltpu.VMEM((shards,) + gains.shape, F32),
            pltpu.VMEM((2, rows, D), BF16),
            pltpu.VMEM((cols, D), BF16),
            dma((2, 6)), dma((2, 4)),
            pltpu.VMEM((2, 6, HEAD_DIM, D), BF16),
            pltpu.VMEM((1, PAIR), F32),
            pltpu.VMEM((2, rows, PAIR), F32),
            pltpu.VMEM((2, cols, PAIR), F32),
            pltpu.VMEM((2, cols, PAIR), BF16),
            pltpu.VMEM((2, rows, PAIR), BF16),
            pltpu.VMEM((cols, PAIR), BF16),
            pltpu.VMEM((rows, PAIR), BF16),
            pltpu.VMEM((cols, 2 * PAIR), BF16),
        ],
        compiler_params=pltpu.CompilerParams(
            collective_id=3, has_side_effects=True, vmem_limit_bytes=60 * 2**20
        ),
        cost_estimate=pl.CostEstimate(flops=20 * 10**9, bytes_accessed=2 * 10**8, transcendentals=13 * 10**6),
    )(attn_w, ffn_w, gains, tokens, bias)


def attention_back_kernel(shards, grads_ref, qp_ref, kp_ref, v_ref, o_ref, weight_ref, da_ref, gain_ref, bias_ref,
                          lse_ref, h_ref, out, dq_ref, dk_ref, dv_ref, turned_ref, sum_ref,
                          qp_buf, kp_buf, v_buf, o_buf, wo_buf, dq_buf, dk_buf, dv_buf, turned_buf, load_sem, store_sem,
                          key_buf, key_turned, k_total, v_total, *scratch):
    turns, lead, follow, finish = reduction((grads_ref.at[0], grads_ref.at[1]), out, scratch)
    height = weight_ref.shape[2] // 4
    heads = height // HEAD_DIM

    def loads(p, slot):
        lanes = pl.ds(pl.multiple_of(p * PAIR, PAIR), PAIR)
        copies = [
            pltpu.make_async_copy(ref.at[:, lanes], buf.at[slot], load_sem.at[slot, n])
            for n, (ref, buf) in enumerate(((qp_ref, qp_buf), (kp_ref, kp_buf), (v_ref, v_buf), (o_ref, o_buf)))
        ]
        for second in range(2):
            head = 2 * p + second
            copies.append(
                pltpu.make_async_copy(
                    weight_ref.at[
                        0, head // heads,
                        pl.ds(pl.multiple_of(3 * height + HEAD_DIM * lax.rem(head, heads), HEAD_DIM), HEAD_DIM),
                    ],
                    wo_buf.at[slot, second], load_sem.at[slot, 4 + second],
                )
            )
        return copies

    def stores(p, slot):
        lanes = pl.ds(pl.multiple_of(p * PAIR, PAIR), PAIR)
        copies = [
            pltpu.make_async_copy(buf.at[slot], ref.at[:, lanes], store_sem.at[slot, n])
            for n, (ref, buf) in enumerate(((dq_ref, dq_buf), (dk_ref, dk_buf), (dv_ref, dv_buf)))
        ]
        for j in range(4):
            for second in range(2):
                head = 2 * p + second
                first = pl.multiple_of(height * j + HEAD_DIM * lax.rem(head, heads), HEAD_DIM)
                copies.append(
                    pltpu.make_async_copy(
                        turned_buf.at[slot, j, pl.ds(second * HEAD_DIM, HEAD_DIM)],
                        turned_ref.at[head // heads, pl.ds(first, HEAD_DIM)],
                        store_sem.at[slot, 3 + 2 * j + second],
                    )
                )
        return copies

    def unit(u):
        p = u // 2
        slot = lax.rem(p, 2)
        begin, block, close = back_parts(
            qp_buf.at[slot], kp_buf.at[slot], v_buf.at[slot], o_buf.at[slot], da_ref, wo_buf.at[slot, 0],
            wo_buf.at[slot, 1], gain_ref.at[p], bias_ref, lse_ref.at[p], dq_buf.at[slot], dk_buf.at[slot],
            dv_buf.at[slot], sum_ref.at[p], key_buf, key_turned, k_total, v_total,
        )

        @pl.when(lax.rem(u, 2) == 0)
        def _():
            @pl.when(p + 1 < PAIRS)
            def _():
                for copy in loads(p + 1, 1 - slot):
                    copy.start()

            for copy in loads(p, slot):
                copy.wait()

            @pl.when(p >= 2)
            def _():
                for copy in stores(p - 2, slot):
                    copy.wait()

            begin()
            block(0)

        @pl.when(lax.rem(u, 2) == 1)
        def _():
            block(1)
            close()
            cols, rows = h_ref.shape[0], da_ref.shape[0]
            turned_buf[slot, 0] = dot_tn(dq_buf[slot], h_ref[pl.ds(cols - rows, rows), :]).astype(BF16)
            turned_buf[slot, 1] = dot_tn(dk_buf[slot], h_ref[...]).astype(BF16)
            turned_buf[slot, 2] = dot_tn(dv_buf[slot], h_ref[...]).astype(BF16)
            turned_buf[slot, 3] = dot_tn(o_buf[slot], da_ref[...]).astype(BF16)
            for copy in stores(p, slot):
                copy.start()

    greet(shards)
    for copy in loads(0, 0):
        copy.start()

    def step(t, _):
        lead(t)
        most = lax.select(lax.rem(t, 4) == 3, 2, 1)

        def one(n, _):
            unit(t + t // 4 + n)
            return 0

        lax.fori_loop(0, lax.select(t < 8 * PAIRS // 5, most, 0), one, 0)
        follow(t)
        return 0

    lax.fori_loop(0, max(turns, 8 * PAIRS // 5), step, 0)
    for p in (PAIRS - 2, PAIRS - 1):
        for copy in stores(p, p % 2):
            copy.wait()
    finish()


def attention_back_reduce(grads, q_pre, k_pre, value_all, o_low, attn_low, grad_spre, gain_qk, bias_turned, lse, low_all):
    _, shards, _, _, rows, _ = grads.shape
    tokens, cols = q_pre.shape[0], k_pre.shape[0]
    any_space = pl.BlockSpec(memory_space=pl.ANY)
    vmem = pl.BlockSpec(memory_space=pltpu.VMEM)
    dma = pltpu.SemaphoreType.DMA
    return pl.pallas_call(
        functools.partial(attention_back_kernel, shards),
        out_shape=(
            jax.ShapeDtypeStruct((2, 8, rows, D), BF16),
            jax.ShapeDtypeStruct((tokens, D), BF16),
            jax.ShapeDtypeStruct((cols, D), BF16),
            jax.ShapeDtypeStruct((cols, D), BF16),
            jax.ShapeDtypeStruct((shards, 8 * rows, D), BF16),
            jax.ShapeDtypeStruct((PAIRS, 8, PAIR), F32),
        ),
        in_specs=[any_space] * 6 + [vmem] * 5,
        out_specs=(any_space,) * 5 + (vmem,),
        scratch_shapes=[
            pltpu.VMEM((2, tokens, PAIR), F32),
            pltpu.VMEM((2, cols, PAIR), F32),
            pltpu.VMEM((2, cols, PAIR), BF16),
            pltpu.VMEM((2, tokens, PAIR), BF16),
            pltpu.VMEM((2, 2, HEAD_DIM, D), BF16),
            pltpu.VMEM((2, tokens, PAIR), BF16),
            pltpu.VMEM((2, cols, PAIR), BF16),
            pltpu.VMEM((2, cols, PAIR), BF16),
            pltpu.VMEM((2, 4, PAIR, D), BF16),
            dma((2, 6)), dma((2, 11)),
            pltpu.VMEM((cols, PAIR), BF16),
            pltpu.VMEM((PAIR, cols), BF16),
            pltpu.VMEM((cols, PAIR), F32),
            pltpu.VMEM((cols, PAIR), F32),
        ] + reduction_scratch(2, shards, rows),
        compiler_params=pltpu.CompilerParams(
            collective_id=1, has_side_effects=True, vmem_limit_bytes=62 * 2**20
        ),
        cost_estimate=pl.CostEstimate(flops=30 * 10**9, bytes_accessed=2 * 10**8, transcendentals=13 * 10**6),
    )(grads, q_pre, k_pre, value_all, o_low, attn_low, grad_spre, gain_qk, bias_turned, lse, low_all)


def body(
    tokens,
    doc_lengths,
    cotangent,
    attn_w,
    ffn_w,
    attn_m,
    attn_v,
    ffn_m,
    ffn_v,
    gains_d,
    gains_ff,
    gd_m,
    gd_v,
    gf_m,
    gf_v,
):
    shards = lax.axis_size("shard")
    reps = lax.axis_size("rep")
    device_index = lax.axis_index("shard")
    rows = tokens.shape[0]
    reach = WINDOW // rows
    cols = (reach + 1) * rows
    attn_rows = attn_w.shape[1]
    ffn_rows = ffn_w.shape[1]
    ffn_all = shards * ffn_rows
    piece = ffn_rows // reps

    lengths_row = doc_lengths[0]
    starts = jnp.cumsum(lengths_row) - lengths_row
    positions = device_index * rows + jnp.arange(rows, dtype=jnp.int32)
    doc_start = jnp.max(
        jnp.where(starts[None, :] <= positions[:, None], starts[None, :], 0), axis=1
    )
    blocks = rows // QUERY_BLOCK
    span = WINDOW + QUERY_BLOCK
    query = jnp.arange(rows, dtype=jnp.int32).reshape(blocks, QUERY_BLOCK)
    lead = query[:, :1] - reach * rows + jnp.arange(span, dtype=jnp.int32)
    ahead = query[:, :, None] - lead[:, None, :]
    floor = (doc_start - device_index * rows).reshape(blocks, QUERY_BLOCK, 1)
    mask = (ahead >= 0) & (ahead < WINDOW) & (lead[:, None, :] >= floor)
    bias = jnp.where(mask, 0.0, NEGATIVE).astype(F32)
    bias_turned = bias.transpose(0, 2, 1)
    bias = bias.reshape(rows, span)
    cut = gains_d.size
    small = jnp.concatenate([gains_d.reshape(-1), gains_ff.reshape(-1)]).astype(BF16)
    normed_in, factor_in = rownorm(tokens.astype(F32))
    fast = reps == 8 and shards == 4 and attn_rows % HEAD_DIM == 0 and reach == 2
    if fast:
        small = small.astype(F32)
        qk_heads = small[:attn_rows].reshape(-1, HEAD_DIM)
        qk_heads = jnp.pad(
            jnp.concatenate([qk_heads, qk_heads], 1), ((0, 8 - qk_heads.shape[0]), (0, D - PAIR))
        )
        small = jnp.pad(small, (0, 8 * D - small.size)).reshape(8, D)
        gathered, small, low_all, q_pre, k_pre, value_all, o_low, lse = gather_attend(
            attn_w.reshape(8, piece, D),
            ffn_w.reshape(3, 8, piece, D),
            jnp.concatenate([qk_heads, small]),
            tokens,
            bias,
            shards,
        )
        small = small[:, 8:].reshape(shards, -1)[:, : cut + gains_ff.size]
        out_low = gathered[0, :, 3 * attn_rows :].reshape(D, D)
        ffn_low = [gathered.reshape(4, ffn_all, D)] * 3
        firsts = (1, 2, 3)
    else:
        attn_low = (
            gather_rows(attn_w.reshape(4 * attn_rows, D).astype(BF16))
            .reshape(shards, 4, attn_rows, D)
            .transpose(1, 0, 2, 3)
            .reshape(1, 4, HEADS, HEAD_DIM, D)
        )
        ffn_low = [gather_rows(ffn_w[m].astype(BF16)).reshape(1, ffn_all, D) for m in range(3)]
        firsts = (0, 0, 0)
        small = lax.all_gather(small, "shard", axis=0).astype(F32)
        query_low, key_low, value_low, out_low = (attn_low[0, j].reshape(D, D) for j in range(4))
    gd_all = small[:, :cut].reshape(shards, 3, -1).transpose(1, 0, 2).reshape(3, D)
    gf_all = small[:, cut:].reshape(shards, 2, ffn_rows).transpose(1, 0, 2).reshape(2, ffn_all)
    gain_qk = gd_all[0]
    alpha_attn = gd_all[1]
    alpha_ffn = gd_all[2]

    if not fast:
        earlier = [from_behind(tokens, "shard", offset) for offset in range(reach, 0, -1)]
        low_all = rownorm(jnp.concatenate(earlier + [tokens], 0).astype(F32))[0].astype(BF16)
        q_pre, k_pre, value_all, o_low, lse = attention_forward(
            low_all, attn_low, gain_qk[None], bias, rows
        )
    in_low = low_all[-rows:]
    side, side_factor = rownorm(dot(o_low, out_low))
    middle, mid_factor = rownorm(normed_in + alpha_attn * (side - normed_in))
    mid_low = middle.astype(BF16)
    output, grad_mid, ffn_grads, down_grads, grad_scale_up, grad_scale_gate, grad_alpha_ffn = feed_forward(
        mid_low, middle, cotangent, alpha_ffn[None], gf_all, ffn_low, firsts
    )
    grad_mixed = norm_back(middle, mid_factor, grad_mid)
    grad_in = grad_mixed * (1.0 - alpha_attn)
    grad_alpha_attn = jnp.sum(grad_mixed * (side - normed_in), 0)
    grad_spre = norm_back(side, side_factor, grad_mixed * alpha_attn).astype(BF16)
    pair_gain = gain_qk.reshape(PAIRS, 1, PAIR)
    if fast:
        units = (shards, 4, 2, piece, D)
        sum_first, grad_qpre, grad_kpre, grad_vpre, attn_grad, gain_sums = attention_back_reduce(
            ffn_grads.reshape((2,) + units), q_pre, k_pre, value_all, o_low, gathered, grad_spre,
            pair_gain, bias_turned, lse, low_all,
        )
    else:
        grad_qpre, grad_kpre, grad_vpre, gain_sums = attention_backward(
            q_pre, k_pre, value_all, o_low, grad_spre, attn_low, pair_gain, bias_turned, lse
        )
    grad_gain_qk = gain_sums[:, 0].reshape(D)
    grad_gf = jnp.concatenate([grad_scale_up, grad_scale_gate])
    gd_rows = D // shards
    if fast:
        grad_gd = jnp.stack([grad_gain_qk, grad_alpha_attn, grad_alpha_ffn[0]])
        small = jnp.concatenate(
            [
                grad_gd.reshape(3, shards, gd_rows).transpose(1, 0, 2).reshape(shards, -1),
                grad_gf.reshape(2, shards, ffn_rows).transpose(1, 0, 2).reshape(shards, -1),
            ],
            1,
        )
        small = jnp.pad(small, ((0, 0), (0, 8 * D - small.shape[1]))).reshape(shards, 8, D)
        sum_last, sum_small, back_got, back_own = reduce_last(
            down_grads.reshape(units), attn_grad.reshape(units), small, grad_qpre, grad_kpre, grad_vpre, gathered
        )
        grad_in = grad_in + back_own
        for n in range(reach):
            sent = device_index + reach - n < shards
            grad_in = grad_in + jnp.where(sent, back_got[n], 0).astype(F32)
        sum_small = sum_small.reshape(-1)
        sum_gd = sum_small[: 3 * gd_rows].reshape(3, gd_rows)
        sum_gf = sum_small[3 * gd_rows : 3 * gd_rows + 2 * ffn_rows].reshape(2, ffn_rows)
        attn_sums, ffn_sums = [(sum_last, 1)], [(sum_first, 0), (sum_first, 1), (sum_last, 0)]
    else:
        back_all = dot(grad_kpre, key_low) + dot(grad_vpre, value_low)
        grad_in = grad_in + dot(grad_qpre, query_low) + back_all[reach * rows :]
        back_parts = back_all[: reach * rows].reshape(reach, rows, D).astype(BF16)
        for n in range(reach):
            grad_in = grad_in + from_behind(back_parts[n], "shard", n - reach).astype(F32)
        attn_grad = jnp.stack(
            [
                dot_tn(grad_qpre, in_low),
                dot_tn(grad_kpre, low_all),
                dot_tn(grad_vpre, low_all),
                dot_tn(o_low, grad_spre),
            ]
        ).astype(BF16)
        attn_grad = attn_grad.reshape(4, shards, attn_rows, D).transpose(1, 0, 2, 3)
        attn_grad = attn_grad.reshape(shards, reps, 4 * attn_rows // reps, D).transpose(1, 0, 2, 3)
        attn_sums = [(reduce_rows(attn_grad).reshape(1, 4, attn_rows, D), 0)]
        ready = (shards, reps, piece, D)
        ffn_sums = [
            (reduce_rows(part.reshape(ready).transpose(1, 0, 2, 3)).reshape(1, 1, ffn_rows, D), 0)
            for part in (ffn_grads[0], ffn_grads[1], down_grads)
        ]
        grad_small = jnp.concatenate(
            [grad_gain_qk, grad_alpha_attn, grad_alpha_ffn[0], grad_gf.reshape(-1)]
        )
        grad_small = lax.psum(grad_small, ("rep", "shard"))
        sum_gd = lax.dynamic_slice_in_dim(
            grad_small[: 3 * D].reshape(3, D), device_index * gd_rows, gd_rows, 1
        )
        sum_gf = lax.dynamic_slice_in_dim(
            grad_small[3 * D :].reshape(2, ffn_all), device_index * ffn_rows, ffn_rows, 1
        )
    grad_tokens = norm_back(normed_in, factor_in, grad_in)

    attn_unit, attn_m_new, attn_v_new = adam_rows(attn_w, attn_sums, attn_m, attn_v)
    ffn_unit, ffn_m_new, ffn_v_new = adam_rows(ffn_w, ffn_sums, ffn_m, ffn_v)
    gd_new, gd_m_new, gd_v_new = adam(gains_d, sum_gd, gd_m, gd_v, GAIN_RATE, 0.0)
    gf_new, gf_m_new, gf_v_new = adam(gains_ff, sum_gf, gf_m, gf_v, GAIN_RATE, 0.0)
    return (
        output,
        grad_tokens,
        attn_unit,
        attn_m_new,
        attn_v_new,
        ffn_unit,
        ffn_m_new,
        ffn_v_new,
        gd_new,
        gd_m_new,
        gd_v_new,
        gf_new,
        gf_m_new,
        gf_v_new,
    )

def solution(mesh):
    return jax.shard_map(
        body,
        mesh=mesh,
        in_specs=(
            P(("rep", "shard"), None),
            P("rep", None),
            P(("rep", "shard"), None),
            P(None, "shard", None),
            P(None, "shard", None),
            P(None, "shard", None),
            P(None, "shard", None),
            P(None, "shard", None),
            P(None, "shard", None),
            P(None, "shard"),
            P(None, "shard"),
            P(None, "shard"),
            P(None, "shard"),
            P(None, "shard"),
            P(None, "shard"),
        ),
        out_specs=(
            P(("rep", "shard"), None),
            P(("rep", "shard"), None),
            P(None, "shard", None),
            P(None, "shard", None),
            P(None, "shard", None),
            P(None, "shard", None),
            P(None, "shard", None),
            P(None, "shard", None),
            P(None, "shard"),
            P(None, "shard"),
            P(None, "shard"),
            P(None, "shard"),
            P(None, "shard"),
            P(None, "shard"),
        ),
        check_vma=False,
    )
```

```python
import functools
import math

import jax
import jax.numpy as jnp
from jax import lax
from jax.experimental import pallas as pl
from jax.experimental.pallas import tpu as pltpu
from jax.sharding import PartitionSpec as P

D = 1280
HEADS = 20
HEAD_DIM = 64
WINDOW = 1024
STEP = 10


SMALL = 1e-06
NEGATIVE = -1e30
BETA_ONE = 0.9
BETA_TWO = 0.95
RATE = 0.02
GAIN_RATE = 1.0
DECAY = 0.1
TINY = 1e-08
F32 = jnp.float32
BF16 = jnp.bfloat16


def from_behind(block, axis, distance):
    devices = range(lax.axis_size(axis))
    route = [(i - distance, i) for i in devices if i - distance in devices]
    return lax.ppermute(block, axis, route)


def rownorm(value):
    factor = lax.rsqrt(jnp.sum(value * value, -1, keepdims=True) + SMALL)
    return (value * factor, factor)


def norm_back(normed, factor, grad):
    return factor * (grad - normed * jnp.sum(normed * grad, -1, keepdims=True))


def adam(weight, grad, first, second, rate, decay):
    first = BETA_ONE * first + (1.0 - BETA_ONE) * grad
    second = BETA_TWO * second + (1.0 - BETA_TWO) * grad * grad
    fix_one = 1.0 - BETA_ONE**STEP
    fix_two = 1.0 - BETA_TWO**STEP
    change = first / fix_one / (jnp.sqrt(second / fix_two) + TINY) + decay * weight
    return (weight - rate * change, first, second)


def dot(a, b):
    return jnp.dot(a, b, preferred_element_type=F32)


def dot_nt(a, b):
    return lax.dot_general(a, b, (((1,), (1,)), ((), ())), preferred_element_type=F32)


def dot_tn(a, b):
    return lax.dot_general(a, b, (((0,), (0,)), ((), ())), preferred_element_type=F32)


def gather_rows(shard_rows):
    reps = lax.axis_size("rep")
    piece = shard_rows.shape[0] // reps
    mine = lax.dynamic_slice_in_dim(shard_rows, lax.axis_index("rep") * piece, piece, 0)
    column = lax.all_gather(mine, "shard", axis=0)
    return lax.all_gather(column, "rep", axis=1)


def reduce_rows(grad):
    part = lax.psum_scatter(grad, "rep", scatter_dimension=0)
    part = lax.psum_scatter(part, "shard", scatter_dimension=0)
    return lax.all_gather(part, "rep", axis=0, tiled=True)


MESH = pl.DeviceIdType.MESH
HALF = 80
RING = 8
HALF_RING = 4


def place():
    rep = lax.axis_index("rep")
    core, chip = lax.rem(rep, 2), rep // 2
    beside, above = chip + 1 - 2 * lax.rem(chip, 2), chip + 2 - 4 * (chip // 2)
    return core, chip, beside, above, 3 - chip


def remote(src, dst, send, recv, rep, shard):
    return pltpu.make_async_remote_copy(
        src_ref=src, dst_ref=dst, send_sem=send, recv_sem=recv,
        device_id=(rep, shard), device_id_type=MESH,
    )


def arrived(ref, sem):
    pltpu.make_async_copy(ref, ref, sem).wait()


def greet(shards):
    rep, line = lax.axis_index("rep"), lax.axis_index("shard")
    barrier = pltpu.get_barrier_semaphore()
    for n in range(1, 8):
        pl.semaphore_signal(barrier, inc=1, device_id=(lax.rem(rep + n, 8), line), device_id_type=MESH)
    for n in range(1, shards):
        pl.semaphore_signal(barrier, inc=1, device_id=(rep, lax.rem(line + n, shards)), device_id_type=MESH)
    pl.semaphore_wait(barrier, 6 + shards)


def add_into(target, sources, rows):
    def step(i, _):
        part = pl.ds(pl.multiple_of(i * 16, 16), 16)
        if len(sources) == 1:
            target[part, :] = target[part, :] + sources[0][part, :]
        else:
            value = target[part, :].astype(F32)
            for source in sources:
                value = value + source[part, :].astype(F32)
            target[part, :] = value.astype(BF16)
        return 0

    lax.fori_loop(0, rows // 16, step, 0, unroll=min(5, rows // 16))


def reduction_scratch(count, shards, rows):
    steps = count * shards
    dma = pltpu.SemaphoreType.DMA
    return [
        pltpu.VMEM((RING, 4, rows, D), BF16),
        pltpu.VMEM((2, 4, rows, D), BF16),
        pltpu.VMEM((HALF_RING, rows, D), BF16),
        pltpu.VMEM((HALF_RING, 2, rows, D), BF16),
        pltpu.VMEM((count, shards + 1, rows, D), BF16),
        dma((2,)), dma(()), dma((steps,)), dma((steps,)), dma((steps, 2)),
        dma((steps,)), dma((steps, 2)), dma((steps,)), dma((count, shards + 1)),
        dma((count,)), dma((count, 7)), dma((count,)), dma(()), pltpu.SemaphoreType.REGULAR,
    ]


def reduction(grads, out, scratch):
    (acc, own, half, piece, below, own_sem, pair_send, pair_recv, half_send, half_recv,
     piece_send, piece_recv, line_send, line_recv, out_send, out_recv, out_local, on_send, credit) = scratch
    count = len(grads)
    rows = own.shape[2]
    shards = below.shape[1] - 1
    core, chip, beside, above, across = place()
    line = lax.axis_index("shard")
    steps = count * shards
    mine, sibling = 2 * chip + core, 2 * chip + 1 - core
    one = piece.at[0, 0]

    def owner(step):
        i = lax.rem(step, shards)
        back = lax.select(i < shards - 1 - line, shards - 1 - i, i - (shards - 1 - line))
        ahead = lax.select(i < line, i, shards - 1 - (i - line))
        other = lax.select(2 * line < shards, back, ahead)
        return lax.select(i == shards - 1, line, other)

    def room(step):
        return acc.at[lax.rem(step, RING)]

    def begin(step):
        slot = lax.rem(step, 2)

        @pl.when(step >= RING)
        def _():
            pl.semaphore_wait(credit, 1)

        for n, grad in enumerate(grads):
            @pl.when(step // shards == n)
            def _(grad=grad):
                remote(grad.at[owner(step), :, 1 - core], room(step), pair_send, pair_recv.at[step], sibling, line).start()
                pltpu.make_async_copy(grad.at[owner(step), :, core], own.at[slot], own_sem.at[slot]).start()

    def first(step):
        slot, part = lax.rem(step, 2), lax.rem(step, HALF_RING)
        total = room(step)
        arrived(own.at[slot], own_sem.at[slot])
        arrived(total, pair_recv.at[step])
        for q in range(4):
            add_into(total.at[q], (own.at[slot, q],), rows)
        remote(total.at[across, pl.ds(0, HALF)], half.at[part, pl.ds(0, HALF)],
               half_send.at[step], half_recv.at[step, 0], 2 * beside + core, line).start()
        remote(total.at[across, pl.ds(HALF, rows - HALF)], half.at[part, pl.ds(HALF, rows - HALF)],
               half_send.at[step], half_recv.at[step, 1], 2 * above + core, line).start()

    def second(step):
        part = lax.rem(step, HALF_RING)
        total = room(step)
        low, high = half.at[part, pl.ds(0, HALF)], half.at[part, pl.ds(HALF, rows - HALF)]
        arrived(low, half_recv.at[step, 0])
        arrived(high, half_recv.at[step, 1])
        add_into(total.at[above, pl.ds(0, HALF)], (low,), HALF)
        add_into(total.at[beside, pl.ds(HALF, rows - HALF)], (high,), rows - HALF)
        remote(total.at[beside], piece.at[part, 0], piece_send.at[step], piece_recv.at[step, 0],
               2 * beside + core, line).start()
        remote(total.at[above], piece.at[part, 1], piece_send.at[step], piece_recv.at[step, 1],
               2 * above + core, line).start()

    def pass_on(step):
        m, target = step // shards, owner(step)

        @pl.when(target > line)
        def _():
            remote(room(step).at[chip], below.at[m, target], line_send.at[step], line_recv.at[m, target],
                   mine, line + 1).start()

        @pl.when(target < line)
        def _():
            slot = lax.select(target == line - 1, shards, target)
            remote(room(step).at[chip], below.at[m, slot], line_send.at[step], line_recv.at[m, slot],
                   mine, line - 1).start()

    def outermost(step):
        target = owner(step)
        return ((target > line) & (line == 0)) | ((target < line) & (line == shards - 1))

    def third(step):
        part = lax.rem(step, HALF_RING)
        for n in range(2):
            arrived(piece.at[part, n], piece_recv.at[step, n])
        add_into(room(step).at[chip], (piece.at[part, 0], piece.at[part, 1]), rows)

        @pl.when(outermost(step))
        def _():
            pass_on(step)

    def along(step):
        m, target = step // shards, owner(step)

        def add_line(slot):
            arrived(below.at[m, slot], line_recv.at[m, slot])
            add_into(room(step).at[chip], (below.at[m, slot],), rows)

        @pl.when(((target >= line) & (line > 0)) | ((target < line) & (line < shards - 1)))
        def _():
            add_line(target)

        @pl.when((target == line) & (line < shards - 1))
        def _():
            add_line(shards)

        @pl.when(jnp.logical_not(outermost(step)))
        def _():
            pass_on(step)

        @pl.when(target == line)
        def _():
            total = room(step).at[chip]
            pltpu.make_async_copy(total, out.at[m, mine], out_local.at[m]).start()
            for n, other in enumerate((2 * beside + core, 2 * above + core, 2 * across + core, sibling)):
                remote(total, out.at[m, mine], out_send.at[m], out_recv.at[m, n], other, line).start()

    def fourth(step):
        m = step // shards
        for n, origin in enumerate((2 * beside + core, 2 * above + core, 2 * across + core)):
            arrived(out.at[m, origin], out_recv.at[m, n])
            remote(out.at[m, origin], out.at[m, origin], on_send, out_recv.at[m, 4 + n], sibling, line).start()

    def retire(step):
        m, target = step // shards, owner(step)
        arrived(one, half_send.at[step])
        arrived(piece.at[0], piece_send.at[step])

        @pl.when(target != line)
        def _():
            arrived(one, line_send.at[step])

        @pl.when(target == line)
        def _():
            arrived(acc.at[0], out_send.at[m])
            arrived(one, out_local.at[m])

        @pl.when(step + RING < steps)
        def _():
            pl.semaphore_signal(credit, inc=1, device_id=(sibling, line), device_id_type=MESH)

    def lead(t):
        @pl.when(t >= 5)
        def _():
            retire(t - 5)

        @pl.when(t == 0)
        def _():
            begin(0)

        @pl.when(t + 1 < steps)
        def _():
            begin(t + 1)

        @pl.when(t < steps)
        def _():
            first(t)

    def follow(t):
        @pl.when((t >= 1) & (t < steps + 1))
        def _():
            second(t - 1)

        @pl.when((t >= 2) & (t < steps + 2))
        def _():
            third(t - 2)

        @pl.when((t >= 3) & (t < steps + 3))
        def _():
            along(t - 3)

        @pl.when((t >= 5) & (lax.rem(t - 5, shards) == shards - 1))
        def _():
            fourth(t - 5)

    def finish():
        for m in range(count):
            for n in range(4):
                arrived(out.at[m, 0], out_recv.at[m, 3 + n])
        arrived(out.at[:, pl.ds(0, 3)], on_send)

    return steps + 5, lead, follow, finish, pair_send


UNITS = 256


def feed_kernel(blocks, mid_ref, middle_ref, cot_ref, alpha_ref, up_scale_ref, gate_scale_ref, wu_ref, wg_ref, wd_ref,
                out_ref, grad_mid_ref, grad_ref, down_ref, up_sum_ref, gate_sum_ref, alpha_sum_ref,
                up_buf, gate_buf, hidden_buf, total, back, grad_hidden_buf, grad_u_buf, grad_g_buf):
    turn = pl.program_id(0)
    after = turn - blocks - 2

    def raw(block):
        up_buf[block] = dot_nt(mid_ref[...], wu_ref[...])
        gate_buf[block] = dot_nt(mid_ref[...], wg_ref[...])

    def activate(block):
        gate = gate_buf[block] * (gate_scale_ref[...] * math.sqrt(D))
        hidden = gate * jax.nn.sigmoid(gate) * (up_buf[block] * up_scale_ref[...])
        hidden_buf[block] = hidden.astype(BF16)

    def project(block, first):
        part = dot(hidden_buf[block], wd_ref[...])
        total[...] = part if first else total[...] + part

    def middle_step():
        alpha = alpha_ref[...]
        rows = total.shape[0]

        def step(i, sums):
            part = pl.ds(pl.multiple_of(i * 32, 32), 32)
            branch, factor = rownorm(total[part, :])
            middle = middle_ref[part, :]
            final, final_factor = rownorm(middle + alpha * (branch - middle))
            out_ref[part, :] = final.astype(BF16)
            grad = norm_back(final, final_factor, cot_ref[part, :].astype(F32))
            grad_mid_ref[part, :] = grad * (1.0 - alpha)
            back[part, :] = norm_back(branch, factor, grad * alpha).astype(BF16)
            return sums + jnp.sum(grad * (branch - middle), 0, keepdims=True)

        alpha_sum_ref[...] = lax.fori_loop(0, rows // 32, step, jnp.zeros((1, D), F32))

    def back_raw():
        grad_hidden_buf[...] = dot_nt(back[...], wd_ref[...])

    def back_activate(block):
        up_scale, gate_scale = up_scale_ref[...], gate_scale_ref[...] * math.sqrt(D)
        grad_hidden = grad_hidden_buf[...]
        up_raw, gate_raw = up_buf[block], gate_buf[block]
        gate = gate_raw * gate_scale
        sigma = jax.nn.sigmoid(gate)
        active = gate * sigma
        upward = up_raw * up_scale
        grad_upward = grad_hidden * active
        grad_gate = grad_hidden * upward * (sigma * (1.0 + gate * (1.0 - sigma)))
        up_sum_ref[...] = jnp.sum(grad_upward * up_raw, 0, keepdims=True)
        gate_sum_ref[...] = jnp.sum(grad_gate * gate_raw, 0, keepdims=True) * math.sqrt(D)
        grad_u_buf[...] = (grad_upward * up_scale).astype(BF16)
        grad_g_buf[...] = (grad_gate * gate_scale).astype(BF16)

    def back_project(block):
        grad_u, grad_g = grad_u_buf[...], grad_g_buf[...]
        grad_ref[0] = dot_tn(grad_u, mid_ref[...]).astype(BF16)
        grad_ref[1] = dot_tn(grad_g, mid_ref[...]).astype(BF16)
        down_ref[...] = dot_tn(hidden_buf[block], back[...]).astype(BF16)
        grad_mid_ref[...] += dot(grad_u, wu_ref[...]) + dot(grad_g, wg_ref[...])

    @pl.when(turn == 0)
    def _():
        raw(0)

    @pl.when(turn == 1)
    def _():
        activate(0)
        raw(1)

    @pl.when(turn == 2)
    def _():
        project(0, True)
        activate(1)
        raw(2)

    @pl.when((turn > 2) & (turn < blocks))
    def _():
        project(turn - 2, False)
        activate(turn - 1)
        raw(turn)

    @pl.when(turn == blocks)
    def _():
        project(turn - 2, False)
        activate(turn - 1)

    @pl.when(turn == blocks + 1)
    def _():
        project(turn - 2, False)
        middle_step()

    @pl.when(after == 0)
    def _():
        back_raw()

    @pl.when(after == 1)
    def _():
        back_activate(0)
        back_raw()

    @pl.when((after > 1) & (after < blocks))
    def _():
        back_project(after - 2)
        back_activate(after - 1)
        back_raw()

    @pl.when(after == blocks)
    def _():
        back_project(after - 2)
        back_activate(after - 1)

    @pl.when(after == blocks + 1)
    def _():
        back_project(after - 2)


def feed_forward(mid_low, middle, cotangent, alpha_ffn, scales, weights, firsts):
    rows = mid_low.shape[0]
    blocks = scales.shape[1] // UNITS
    whole = lambda *shape: pl.BlockSpec(shape, lambda t: (0,) * len(shape))
    half = blocks + 2

    def stage(t, early, late):
        return jnp.clip(lax.select(t < half, t - early, t - half - late), 0, blocks - 1)

    weight = lambda m, early, late: pl.BlockSpec((None, UNITS, D), lambda t: (m, stage(t, early, late), 0))
    done = lambda t, lag: jnp.clip(t - half - lag, 0, blocks - 1)
    units = pl.BlockSpec((1, UNITS), lambda t: (0, done(t, 1)))
    scale = pl.BlockSpec((1, UNITS), lambda t: (0, stage(t, 1, 1)))
    return pl.pallas_call(
        functools.partial(feed_kernel, blocks),
        grid=(2 * half,),
        out_shape=(
            jax.ShapeDtypeStruct((rows, D), BF16),
            jax.ShapeDtypeStruct((rows, D), F32),
            jax.ShapeDtypeStruct((2, blocks * UNITS, D), BF16),
            jax.ShapeDtypeStruct((blocks * UNITS, D), BF16),
            jax.ShapeDtypeStruct((1, blocks * UNITS), F32),
            jax.ShapeDtypeStruct((1, blocks * UNITS), F32),
            jax.ShapeDtypeStruct((1, D), F32),
        ),
        in_specs=[whole(rows, D), whole(rows, D), whole(rows, D), whole(1, D), scale, scale]
        + [weight(firsts[0], 0, 2), weight(firsts[1], 0, 2), weight(firsts[2], 2, 0)],
        out_specs=(
            whole(rows, D), whole(rows, D), pl.BlockSpec((2, UNITS, D), lambda t: (0, done(t, 2), 0)),
            pl.BlockSpec((UNITS, D), lambda t: (done(t, 2), 0)),
            units, units, whole(1, D),
        ),
        scratch_shapes=[
            pltpu.VMEM((blocks, rows, UNITS), F32),
            pltpu.VMEM((blocks, rows, UNITS), F32),
            pltpu.VMEM((blocks, rows, UNITS), BF16),
            pltpu.VMEM((rows, D), F32),
            pltpu.VMEM((rows, D), BF16),
            pltpu.VMEM((rows, UNITS), F32),
            pltpu.VMEM((rows, UNITS), BF16),
            pltpu.VMEM((rows, UNITS), BF16),
        ],
        compiler_params=pltpu.CompilerParams(vmem_limit_bytes=62 * 2**20),
        cost_estimate=pl.CostEstimate(flops=60 * 10**9, bytes_accessed=120 * 10**6, transcendentals=5 * 10**6),
    )(mid_low, middle, cotangent, alpha_ffn, scales[:1], scales[1:], *weights)


def adam_kernel(places, per, *refs):
    grads = refs[:places]
    w_ref, m_ref, v_ref, w_out, m_out, v_out = refs[places:]
    group, piece, _ = w_ref.shape

    def update(g_ref):
        for n in range(group):
            def step(i, _, n=n):
                part = (n, pl.ds(pl.multiple_of(i * 16, 16), 16), slice(None))
                new, first, second = adam(
                    w_ref[part], g_ref[part].astype(F32), m_ref[part], v_ref[part], RATE, DECAY
                )
                w_out[part] = rownorm(new)[0]
                m_out[part] = first
                v_out[part] = second
                return 0

            lax.fori_loop(0, piece // 16, step, 0, unroll=5)

    for n in range(places):
        @pl.when(pl.program_id(0) // per == n)
        def _(n=n):
            update(grads[n])


def adam_rows(weight, grads, first, second):
    places = len(grads)
    _, per, piece, _ = grads[0][0].shape
    group = 2 if per % 2 == 0 else 1
    steps = per // group
    spec = pl.BlockSpec((group, piece, D), lambda p: (p, 0, 0))

    def grad_spec(n, index):
        return pl.BlockSpec(
            (None, group, piece, D), lambda p: (index, jnp.clip(p - n * steps, 0, steps - 1), 0, 0)
        )

    shape = jax.ShapeDtypeStruct((places * per, piece, D), F32)
    news = pl.pallas_call(
        functools.partial(adam_kernel, places, steps),
        grid=(places * steps,),
        out_shape=(shape,) * 3,
        in_specs=[grad_spec(n, index) for n, (_, index) in enumerate(grads)] + [spec] * 3,
        out_specs=(spec,) * 3,
        compiler_params=pltpu.CompilerParams(vmem_limit_bytes=60 * 2**20),
        cost_estimate=pl.CostEstimate(flops=20 * weight.size, bytes_accessed=26 * weight.size, transcendentals=0),
    )(*(array for array, _ in grads), *(old.reshape(shape.shape) for old in (weight, first, second)))
    return tuple(new.reshape(weight.shape) for new in news)


QUERY_BLOCK = 256
PAIR = 2 * HEAD_DIM
PAIRS = HEADS // 2


def head_ones():
    row = lax.broadcasted_iota(jnp.int32, (PAIR, PAIR), 0) // HEAD_DIM
    col = lax.broadcasted_iota(jnp.int32, (PAIR, PAIR), 1) // HEAD_DIM
    return (row == col).astype(F32).astype(BF16)


def head_sum(value, ones):
    high = value.astype(BF16)
    rest = (value - high.astype(F32)).astype(BF16)
    return dot(high, ones) + dot(rest, ones)


def of_head(value, head):
    lane = lax.broadcasted_iota(jnp.int32, value.shape, 1) // HEAD_DIM
    return jnp.where(lane == head, value, jnp.zeros_like(value))


def attend_pair(h_ref, wq_ref, wq2_ref, wk_ref, wk2_ref, wv_ref, wv2_ref, gain_ref, bias_ref, qp_ref, kp_ref, v_ref, o_ref, lse_ref,
                key_buf, query_buf, value_buf):
    cols = h_ref.shape[0]
    rows = qp_ref.shape[0]
    span = bias_ref.shape[1]
    ones = head_ones()
    gain = gain_ref[...]
    weights = jnp.concatenate([wk_ref[...], wk2_ref[...], wv_ref[...], wv2_ref[...]], 0)
    query_weights = jnp.concatenate([wq_ref[...], wq2_ref[...]], 0)

    def project(i, _):
        part = pl.ds(pl.multiple_of(i * QUERY_BLOCK, QUERY_BLOCK), QUERY_BLOCK)
        both = dot_nt(h_ref[part, :], weights)
        keys = both[:, :PAIR]
        kp_ref[part, :] = keys
        factor = lax.rsqrt(head_sum(keys * keys, ones) + SMALL)
        key_buf[part, :] = (keys * factor * gain).astype(BF16)
        values = both[:, PAIR:].astype(BF16)
        v_ref[part, :] = values
        value_buf[part, :PAIR] = values
        value_buf[part, PAIR:] = jnp.ones_like(values)
        return 0

    lax.fori_loop(0, cols // QUERY_BLOCK, project, 0)

    def project_queries(i, _):
        part = pl.ds(pl.multiple_of(i * QUERY_BLOCK, QUERY_BLOCK), QUERY_BLOCK)
        own = pl.ds(pl.multiple_of(cols - rows + i * QUERY_BLOCK, QUERY_BLOCK), QUERY_BLOCK)
        queries = dot_nt(h_ref[own, :], query_weights)
        qp_ref[part, :] = queries
        factor = lax.rsqrt(head_sum(queries * queries, ones) + SMALL)
        scaled = (queries * factor * gain).astype(BF16).astype(F32) * math.sqrt(HEAD_DIM)
        query_buf[part, :] = scaled.astype(BF16)
        return 0

    lax.fori_loop(0, rows // QUERY_BLOCK, project_queries, 0)
    for i in range(rows // QUERY_BLOCK):
        part = pl.ds(i * QUERY_BLOCK, QUERY_BLOCK)
        reach = pl.ds(i * QUERY_BLOCK, span)
        sides = []
        for head in range(2):
            scores = dot_nt(of_head(query_buf[part, :], head), key_buf[reach, :])
            probs = jnp.exp(scores + bias_ref[part, :]).astype(BF16)
            both = dot(probs, value_buf[reach, :])
            total = both[:, PAIR:]
            sides.append(both[:, :PAIR] / total)
            lse_ref[head : head + 1, part] = jnp.log(total).T[:1, :]
        lane = lax.broadcasted_iota(jnp.int32, sides[0].shape, 1)
        o_ref[part, :] = jnp.where(lane < HEAD_DIM, sides[0], sides[1]).astype(BF16)


def back_pair(*refs):
    start, block, finish = back_parts(*refs)
    start()
    for i in range(refs[0].shape[0] // QUERY_BLOCK):
        block(i)
    finish()


def back_parts(qp_ref, kp_ref, v_ref, o_ref, da_ref, wo_ref, wo2_ref, gain_ref, bias_ref, lse_ref,
               dq_ref, dk_ref, dv_ref, sum_ref, key_buf, key_turned, k_total, v_total):
    cols = kp_ref.shape[0]
    rows = qp_ref.shape[0]
    span = bias_ref.shape[1]

    def keys_of(i, _):
        ones, gain = head_ones(), gain_ref[...]
        part = pl.ds(pl.multiple_of(i * QUERY_BLOCK, QUERY_BLOCK), QUERY_BLOCK)
        keys = kp_ref[part, :]
        factor = lax.rsqrt(head_sum(keys * keys, ones) + SMALL)
        low = keys * factor * gain
        key_buf[part, :] = low.astype(BF16)
        key_turned[:, part] = low.T.astype(BF16)
        k_total[part, :] = jnp.zeros_like(keys)
        v_total[part, :] = jnp.zeros_like(keys)
        return 0

    def start():
        lax.fori_loop(0, cols // QUERY_BLOCK, keys_of, 0)

    def block(i):
        ones, gain = head_ones(), gain_ref[...]
        weights = jnp.concatenate([wo_ref[...], wo2_ref[...]], 0)
        part = pl.ds(i * QUERY_BLOCK, QUERY_BLOCK)
        reach = pl.ds(i * QUERY_BLOCK, span)
        queries = qp_ref[part, :]
        factor = lax.rsqrt(head_sum(queries * queries, ones) + SMALL)
        hat = queries * factor
        scaled = ((hat * gain).astype(BF16).astype(F32) * math.sqrt(HEAD_DIM)).astype(BF16)
        back = dot_nt(da_ref[part, :], weights).astype(BF16)
        inner = (back.astype(F32) * o_ref[part, :].astype(F32)).T
        sides = []
        for head in range(2):
            mine = slice(head * HEAD_DIM, (head + 1) * HEAD_DIM)
            query, grad = of_head(scaled, head), of_head(back, head)
            scores = dot_nt(key_buf[reach, :], query)
            probs = jnp.exp(scores + bias_ref[i] - lse_ref[head : head + 1, part])
            v_total[reach, :] += dot(probs.astype(BF16), grad)
            delta = jnp.sum(inner[mine, :], 0, keepdims=True)
            grad_scores = (probs * (dot_nt(v_ref[reach, :], grad) - delta)).astype(BF16)
            k_total[reach, :] += dot(grad_scores, query)
            sides.append(dot(key_turned[mine, reach], grad_scores))
        grad_q = jnp.concatenate(sides, 0).T * math.sqrt(HEAD_DIM)
        sums = jnp.sum(grad_q * hat, 0, keepdims=True)
        if i == 0:
            sum_ref[...] = jnp.broadcast_to(sums, sum_ref.shape)
        else:
            sum_ref[...] += jnp.broadcast_to(sums, sum_ref.shape)
        grad_q = grad_q * gain
        dq_ref[part, :] = (factor * (grad_q - hat * head_sum(hat * grad_q, ones))).astype(BF16)

    def close(i, _):
        ones, gain = head_ones(), gain_ref[...]
        part = pl.ds(pl.multiple_of(i * QUERY_BLOCK, QUERY_BLOCK), QUERY_BLOCK)
        keys = kp_ref[part, :]
        factor = lax.rsqrt(head_sum(keys * keys, ones) + SMALL)
        hat = keys * factor
        grad_k = k_total[part, :]
        sum_ref[...] += jnp.broadcast_to(jnp.sum(grad_k * hat, 0, keepdims=True), sum_ref.shape)
        grad_k = grad_k * gain
        dk_ref[part, :] = (factor * (grad_k - hat * head_sum(hat * grad_k, ones))).astype(BF16)
        dv_ref[part, :] = v_total[part, :].astype(BF16)
        return 0

    def finish():
        lax.fori_loop(0, cols // QUERY_BLOCK, close, 0)

    return start, block, finish


def head_rows(attn_low, matrix, second):
    heads = attn_low.shape[2]

    def index(p):
        head = 2 * p + second
        return (head // heads, matrix, lax.rem(head, heads), 0, 0)

    return pl.BlockSpec((None, None, None, HEAD_DIM, D), index)


def attention_forward(low_all, attn_low, gain_qk, bias, rows):
    cols = low_all.shape[0]
    span = bias.shape[1]
    side = lambda n: pl.BlockSpec((n, PAIR), lambda p: (0, p))
    whole = lambda *shape: pl.BlockSpec(shape, lambda p: (0,) * len(shape))
    return pl.pallas_call(
        attend_pair,
        grid=(PAIRS,),
        out_shape=(
            jax.ShapeDtypeStruct((rows, D), F32),
            jax.ShapeDtypeStruct((cols, D), F32),
            jax.ShapeDtypeStruct((cols, D), BF16),
            jax.ShapeDtypeStruct((rows, D), BF16),
            jax.ShapeDtypeStruct((PAIRS, 8, rows), F32),
        ),
        in_specs=[whole(cols, D)]
        + [head_rows(attn_low, j, second) for j in range(3) for second in range(2)]
        + [side(1), whole(rows, span)],
        out_specs=(side(rows), side(cols), side(cols), side(rows),
                   pl.BlockSpec((None, 8, rows), lambda p: (p, 0, 0))),
        scratch_shapes=[
            pltpu.VMEM((cols, PAIR), BF16),
            pltpu.VMEM((rows, PAIR), BF16),
            pltpu.VMEM((cols, 2 * PAIR), BF16),
        ],
        compiler_params=pltpu.CompilerParams(vmem_limit_bytes=56 * 2**20),
        cost_estimate=pl.CostEstimate(flops=20 * 10**9, bytes_accessed=30 * 10**6, transcendentals=13 * 10**6),
    )(low_all, *[attn_low] * 6, gain_qk, bias)


def attention_backward(q_pre, k_pre, value_all, o_low, grad_spre, attn_low, gain_qk, bias_turned, lse):
    rows, cols = q_pre.shape[0], k_pre.shape[0]
    side = lambda n: pl.BlockSpec((n, PAIR), lambda p: (0, p))
    whole = lambda *shape: pl.BlockSpec(shape, lambda p: (0,) * len(shape))
    stat = pl.BlockSpec((None, 8, rows), lambda p: (p, 0, 0))
    return pl.pallas_call(
        back_pair,
        grid=(PAIRS,),
        out_shape=(
            jax.ShapeDtypeStruct((rows, D), BF16),
            jax.ShapeDtypeStruct((cols, D), BF16),
            jax.ShapeDtypeStruct((cols, D), BF16),
            jax.ShapeDtypeStruct((PAIRS, 8, PAIR), F32),
        ),
        in_specs=[
            side(rows), side(cols), side(cols), side(rows), whole(rows, D),
            head_rows(attn_low, 3, 0), head_rows(attn_low, 3, 1),
            pl.BlockSpec((None, 1, PAIR), lambda p: (p, 0, 0)), whole(*bias_turned.shape), stat,
        ],
        out_specs=(side(rows), side(cols), side(cols), pl.BlockSpec((None, 8, PAIR), lambda p: (p, 0, 0))),
        scratch_shapes=[
            pltpu.VMEM((cols, PAIR), BF16),
            pltpu.VMEM((PAIR, cols), BF16),
            pltpu.VMEM((cols, PAIR), F32),
            pltpu.VMEM((cols, PAIR), F32),
        ],
        compiler_params=pltpu.CompilerParams(vmem_limit_bytes=56 * 2**20),
        cost_estimate=pl.CostEstimate(flops=30 * 10**9, bytes_accessed=40 * 10**6, transcendentals=13 * 10**6),
    )(q_pre, k_pre, value_all, o_low, grad_spre, attn_low, attn_low, gain_qk, bias_turned, lse)


START = 5


def gather_kernel(shards, attn_ref, ffn_ref, gains_ref, tokens_ref, bias_ref,
                  out, gains_out, h_out, qp_out, kp_out, v_out, o_out, lse_ref,
                  wide, low, mine, wide_sem, low_sem, mine_sem, line_send, line_recv, plane_send, beside_recv,
                  above_recv, across_recv, pair_send, pair_recv, gains_send, gains_recv, tokens_send,
                  tokens_recv, local_sem, gains_buf, before, h_buf, load_sem, store_sem,
                  weight_buf, gain_row, qp_buf, kp_buf, v_buf, o_buf, key_buf, query_buf, value_buf):
    core, chip, beside, above, across = place()
    line = lax.axis_index("shard")
    rep = 2 * chip + core
    sibling = 2 * chip + 1 - core
    to_beside, to_above = 2 * beside + core, 2 * above + core
    piece = attn_ref.shape[1]
    rows = tokens_ref.shape[0]
    heads = 2 * piece // HEAD_DIM
    others = shards - 1
    steps = 4 * others
    greet(shards)

    def rows_of(m, shard, rep, start=0, size=None):
        first = pl.multiple_of(rep * piece + start, 16)
        return out.at[m, shard, pl.ds(first, piece if size is None else size)]

    def source(n):
        low_side = 2 * line < shards
        edge = lax.select(low_side, line, shards - 1 - line)
        near = lax.select(lax.rem(n, 2) == 0, edge - 1 - n // 2, edge + 1 + n // 2)
        found = lax.select(n < 2 * edge, near, n + 1)
        return lax.select(low_side, found, shards - 1 - found)

    def own_send(m):
        @pl.when(line < shards - 1)
        def _():
            remote(mine.at[m], rows_of(m, line, rep), line_send, line_recv.at[m, line], rep, line + 1).start()

        @pl.when(line > 0)
        def _():
            remote(mine.at[m], rows_of(m, line, rep), line_send, line_recv.at[m, line], rep, line - 1).start()

    def fetch(index, slot):
        @pl.when(index < 8)
        def _():
            pltpu.make_async_copy(attn_ref.at[lax.rem(index, 8)], wide.at[slot], wide_sem.at[slot]).start()

        @pl.when(index >= 8)
        def _():
            pltpu.make_async_copy(
                ffn_ref.at[jnp.maximum(index // 8 - 1, 0), lax.rem(index, 8)], wide.at[slot], wide_sem.at[slot]
            ).start()

    def store(index, slot):
        return pltpu.make_async_copy(low.at[slot], rows_of(index // 8, line, lax.rem(index, 8)), low_sem.at[slot])

    def lower(src, dst):
        def step(i, _):
            part = pl.ds(pl.multiple_of(i * 32, 32), 32)
            dst[part, :] = src[part, :].astype(BF16)
            return 0

        lax.fori_loop(0, piece // 32, step, 0)

    for n in range(1, shards):
        other = lax.rem(line + n, shards)
        remote(gains_ref, gains_buf.at[line], gains_send, gains_recv.at[line], rep, other).start()
    pltpu.make_async_copy(gains_ref, gains_buf.at[line], local_sem).start()
    own = pl.ds(2 * rows, rows)
    pltpu.make_async_copy(tokens_ref, h_buf.at[own], load_sem.at[0, 0]).start()
    for m in range(4):
        origin = attn_ref.at[rep] if m == 0 else ffn_ref.at[m - 1, rep]
        pltpu.make_async_copy(origin, wide.at[m], mine_sem.at[m]).start()
    for m in range(4):
        arrived(wide.at[m], mine_sem.at[m])
        lower(wide.at[m], mine.at[m])
        if m == 0:
            own_send(0)

            @pl.when(line < shards - 1)
            def _():
                remote(tokens_ref, before.at[1], tokens_send, tokens_recv.at[1], rep, line + 1).start()

    for n in range(2):
        fetch(n, n)

    def norm_rows(source, first):
        def step(i, _):
            at = pl.multiple_of(first + i * 32, 32)
            value = source[pl.ds(pl.multiple_of(i * 32, 32), 32), :].astype(F32)
            h_buf[pl.ds(at, 32), :] = rownorm(value)[0].astype(BF16)
            return 0

        lax.fori_loop(0, rows // 32, step, 0)

    def clear_rows(first):
        h_buf[pl.ds(first, rows), :] = jnp.zeros((rows, D), BF16)

    arrived(h_buf.at[own], load_sem.at[0, 0])
    norm_rows(h_buf.at[own], 2 * rows)

    def loads(p, slot):
        copies = []
        for j in range(3):
            for second in range(2):
                head = 2 * p + second
                first = pl.multiple_of(2 * piece * j + HEAD_DIM * lax.rem(head, heads), HEAD_DIM)
                copies.append(
                    pltpu.make_async_copy(
                        out.at[0, head // heads, pl.ds(first, HEAD_DIM)], weight_buf.at[slot, 2 * j + second],
                        load_sem.at[slot, 2 * j + second],
                    )
                )
        return copies

    def stores(p, slot):
        lanes = pl.ds(pl.multiple_of(p * PAIR, PAIR), PAIR)
        return [
            pltpu.make_async_copy(buf.at[slot], ref.at[:, lanes], store_sem.at[slot, n])
            for n, (ref, buf) in enumerate(((qp_out, qp_buf), (kp_out, kp_buf), (v_out, v_buf), (o_out, o_buf)))
        ]

    def pair(p):
        slot = lax.rem(p, 2)

        @pl.when(p + 1 < PAIRS)
        def _():
            for copy in loads(p + 1, 1 - slot):
                copy.start()

        for copy in loads(p, slot):
            copy.wait()

        @pl.when(p >= 2)
        def _():
            for copy in stores(p - 2, slot):
                copy.wait()

        row = lax.broadcasted_iota(jnp.int32, (8, PAIR), 0)
        left, right = (
            jnp.sum(
                jnp.where(row == lax.rem(2 * p + n, heads), gains_buf[(2 * p + n) // heads, :8, :PAIR], 0.0),
                0, keepdims=True,
            )
            for n in range(2)
        )
        lane = lax.broadcasted_iota(jnp.int32, (1, PAIR), 1)
        gain_row[...] = jnp.where(lane < HEAD_DIM, left, right)
        attend_pair(
            h_buf, *(weight_buf.at[slot, n] for n in range(6)), gain_row, bias_ref, qp_buf.at[slot],
            kp_buf.at[slot], v_buf.at[slot], o_buf.at[slot], lse_ref.at[p], key_buf, query_buf, value_buf,
        )
        for copy in stores(p, slot):
            copy.start()

    def begin(c):
        m, origin = c // others, source(lax.rem(c, others))
        got = rows_of(m, origin, rep)
        arrived(got, line_recv.at[m, origin])

        @pl.when((origin < line) & (line < shards - 1))
        def _():
            remote(got, got, line_send, line_recv.at[m, origin], rep, line + 1).start()

        @pl.when((origin > line) & (line > 0))
        def _():
            remote(got, got, line_send, line_recv.at[m, origin], rep, line - 1).start()

        remote(got, got, plane_send, beside_recv.at[m, origin], to_beside, line).start()
        remote(got, got, plane_send, above_recv.at[m, origin], to_above, line).start()
        remote(got, got, pair_send, pair_recv.at[m], sibling, line).start()

    def middle(c):
        m, origin = c // others, source(lax.rem(c, others))
        got = rows_of(m, origin, to_beside)
        arrived(got, beside_recv.at[m, origin])
        part = rows_of(m, origin, to_beside, 0, HALF)
        remote(part, part, plane_send, across_recv.at[m, origin, 0], to_above, line).start()
        remote(got, got, pair_send, pair_recv.at[m], sibling, line).start()
        got = rows_of(m, origin, to_above)
        arrived(got, above_recv.at[m, origin])
        part = rows_of(m, origin, to_above, HALF, piece - HALF)
        remote(part, part, plane_send, across_recv.at[m, origin, 1], to_beside, line).start()
        remote(got, got, pair_send, pair_recv.at[m], sibling, line).start()

    def last(c):
        m, origin = c // others, source(lax.rem(c, others))
        got = rows_of(m, origin, 2 * across + core)
        arrived(rows_of(m, origin, 2 * across + core, 0, HALF), across_recv.at[m, origin, 0])
        arrived(rows_of(m, origin, 2 * across + core, HALF, piece - HALF), across_recv.at[m, origin, 1])
        remote(got, got, pair_send, pair_recv.at[m], sibling, line).start()

    def local(t):
        for n in range(2):
            index = 2 * t + n
            slot = 2 * lax.rem(t, 2) + n
            arrived(wide.at[slot], wide_sem.at[slot])

            @pl.when(index + 2 < 32)
            def _():
                fetch(index + 2, lax.rem(slot + 2, 4))

            @pl.when(t >= 2)
            def _():
                store(index - 4, slot).wait()

            lower(wide.at[slot], low.at[slot])
            store(index, slot).start()

    def turn(t, _):
        @pl.when((lax.rem(t, others) == 0) & (t // others < 3))
        def _():
            own_send(t // others + 1)

        @pl.when(t < steps)
        def _():
            begin(t)

        @pl.when((t == 1) & (line > 0))
        def _():
            arrived(before.at[1], tokens_recv.at[1])

            @pl.when(line < shards - 1)
            def _():
                remote(before.at[1], before.at[0], tokens_send, tokens_recv.at[0], rep, line + 1).start()

            norm_rows(before.at[1], rows)

        @pl.when((t == 1) & (line == 0))
        def _():
            clear_rows(rows)

        @pl.when((t == 3) & (line > 1))
        def _():
            arrived(before.at[0], tokens_recv.at[0])
            norm_rows(before.at[0], 0)

        @pl.when((t == 3) & (line <= 1))
        def _():
            clear_rows(0)

        @pl.when(t < 2)
        def _():
            local(2 * t)
            local(2 * t + 1)

        @pl.when(t >= 2)
        def _():
            local(t + 2)

        @pl.when(t == START)
        def _():
            pltpu.make_async_copy(gains_ref, gains_buf.at[line], local_sem).wait()
            for n in range(1, shards):
                other = lax.rem(line + n, shards)
                arrived(gains_buf.at[other], gains_recv.at[other])
            arrived(out.at[0, pl.ds(0, others), pl.ds(0, 4 * piece)], pair_recv.at[0])
            for copy in loads(0, 0):
                copy.start()

        early = (t > START + 3).astype(jnp.int32) + (t > START + 6).astype(jnp.int32)
        most = lax.select((t == START + 3) | (t == START + 6), 2, 1)

        def one(n, _):
            pair(t - START + early + n)
            return 0

        lax.fori_loop(0, lax.select((t >= START) & (t < START + PAIRS - 2), most, 0), one, 0)

        @pl.when((t >= 1) & (t < steps + 1))
        def _():
            middle(t - 1)

        @pl.when((t >= 2) & (t < steps + 2))
        def _():
            last(t - 2)

        return 0

    lax.fori_loop(0, 14, turn, 0)
    for n in range(4):
        store(28 + n, n).wait()
    gains_copy = pltpu.make_async_copy(gains_buf, gains_out, local_sem)
    h_copy = pltpu.make_async_copy(h_buf, h_out, load_sem.at[0, 0])
    gains_copy.start()
    h_copy.start()
    for p in (PAIRS - 2, PAIRS - 1):
        for copy in stores(p, p % 2):
            copy.wait()
    for m in range(1, 4):
        arrived(out.at[m, pl.ds(0, others), pl.ds(0, 4 * piece)], pair_recv.at[m])
    gains_copy.wait()
    h_copy.wait()

    @pl.when((line == 1) | (line == shards - 2))
    def _():
        arrived(before, tokens_send)

    @pl.when(line == 0)
    def _():
        arrived(before.at[0], tokens_send)

    @pl.when((line == 0) | (line == shards - 1))
    def _():
        arrived(out.at[:, 0, pl.ds(0, piece)], line_send)

    @pl.when((line > 0) & (line < shards - 1))
    def _():
        arrived(out.at[:, 0, pl.ds(0, 5 * piece)], line_send)

    arrived(out.at[:, pl.ds(0, others), pl.ds(0, 3 * piece)], plane_send)
    arrived(out.at[:, pl.ds(0, others), pl.ds(0, 4 * piece)], pair_send)
    arrived(gains_buf.at[pl.ds(0, others)], gains_send)


def gather_attend(attn_w, ffn_w, gains, tokens, bias, shards):
    piece = attn_w.shape[1]
    rows = tokens.shape[0]
    cols = rows + WINDOW
    any_space = pl.BlockSpec(memory_space=pl.ANY)
    vmem = pl.BlockSpec(memory_space=pltpu.VMEM)
    dma = pltpu.SemaphoreType.DMA
    return pl.pallas_call(
        functools.partial(gather_kernel, shards),
        out_shape=(
            jax.ShapeDtypeStruct((4, shards, 8 * piece, D), BF16),
            jax.ShapeDtypeStruct((shards,) + gains.shape, F32),
            jax.ShapeDtypeStruct((cols, D), BF16),
            jax.ShapeDtypeStruct((rows, D), F32),
            jax.ShapeDtypeStruct((cols, D), F32),
            jax.ShapeDtypeStruct((cols, D), BF16),
            jax.ShapeDtypeStruct((rows, D), BF16),
            jax.ShapeDtypeStruct((PAIRS, 8, rows), F32),
        ),
        in_specs=[any_space] * 4 + [vmem],
        out_specs=(any_space,) * 7 + (vmem,),
        scratch_shapes=[
            pltpu.VMEM((4, piece, D), F32),
            pltpu.VMEM((4, piece, D), BF16),
            pltpu.VMEM((4, piece, D), BF16),
            dma((4,)), dma((4,)), dma((4,)), dma(()), dma((4, shards)), dma(()), dma((4, shards)),
            dma((4, shards)), dma((4, shards, 2)), dma(()), dma((4,)), dma(()), dma((shards,)), dma(()),
            dma((2,)), dma(()),
            pltpu.VMEM((shards,) + gains.shape, F32),
            pltpu.VMEM((2, rows, D), BF16),
            pltpu.VMEM((cols, D), BF16),
            dma((2, 6)), dma((2, 4)),
            pltpu.VMEM((2, 6, HEAD_DIM, D), BF16),
            pltpu.VMEM((1, PAIR), F32),
            pltpu.VMEM((2, rows, PAIR), F32),
            pltpu.VMEM((2, cols, PAIR), F32),
            pltpu.VMEM((2, cols, PAIR), BF16),
            pltpu.VMEM((2, rows, PAIR), BF16),
            pltpu.VMEM((cols, PAIR), BF16),
            pltpu.VMEM((rows, PAIR), BF16),
            pltpu.VMEM((cols, 2 * PAIR), BF16),
        ],
        compiler_params=pltpu.CompilerParams(
            collective_id=3, has_side_effects=True, vmem_limit_bytes=60 * 2**20
        ),
        cost_estimate=pl.CostEstimate(flops=20 * 10**9, bytes_accessed=2 * 10**8, transcendentals=13 * 10**6),
    )(attn_w, ffn_w, gains, tokens, bias)


BACK_BLOCK = 256


def backward_kernel(shards, grads_ref, down_ref, qp_ref, kp_ref, v_ref, o_ref, weight_ref, gains_ref, da_ref, gain_ref,
                    bias_ref, lse_ref, h_ref, out, dq_ref, dk_ref, dv_ref, turned_ref, gains_out, sums_out, back_out,
                    own_out, sums, line_got, plane_got, line_sums, plane_sums, mine_gains, mine_sums, line_send, line_recv, plane_send,
                    plane_recv, back_send, back_recv, *scratch):
    rep, line = lax.axis_index("rep"), lax.axis_index("shard")
    grads = (grads_ref.at[0], grads_ref.at[1], down_ref, turned_ref)
    turns, lead, follow, finish, pair_send = reduction(grads, out, scratch)
    height = weight_ref.shape[2] // 4
    heads = height // HEAD_DIM
    rows, cols = da_ref.shape[0], h_ref.shape[0]
    reach = back_out.shape[0]
    per = rows // BACK_BLOCK
    attended = PAIRS + 1
    dma = pltpu.SemaphoreType.DMA
    greet(shards)

    def attention(qp_buf, kp_buf, v_buf, o_buf, wo_buf, dq_buf, dk_buf, dv_buf, turned_buf, load_sem, store_sem,
                  key_buf, key_turned, k_total, v_total):
        def loads(p, slot):
            lanes = pl.ds(pl.multiple_of(p * PAIR, PAIR), PAIR)
            copies = [
                pltpu.make_async_copy(ref.at[:, lanes], buf.at[slot], load_sem.at[slot, n])
                for n, (ref, buf) in enumerate(((qp_ref, qp_buf), (kp_ref, kp_buf), (v_ref, v_buf), (o_ref, o_buf)))
            ]
            for second in range(2):
                head = 2 * p + second
                first = pl.multiple_of(3 * height + HEAD_DIM * lax.rem(head, heads), HEAD_DIM)
                copies.append(
                    pltpu.make_async_copy(
                        weight_ref.at[0, head // heads, pl.ds(first, HEAD_DIM)], wo_buf.at[slot, second],
                        load_sem.at[slot, 4 + second],
                    )
                )
            return copies

        def lane_stores(p, slot):
            lanes = pl.ds(pl.multiple_of(p * PAIR, PAIR), PAIR)
            return [
                pltpu.make_async_copy(buf.at[slot], ref.at[:, lanes], store_sem.at[slot, n])
                for n, (ref, buf) in enumerate(((dq_ref, dq_buf), (dk_ref, dk_buf), (dv_ref, dv_buf)))
            ]

        def start_stores(p, slot):
            for copy in lane_stores(p, slot):
                copy.start()
            for second in range(2):
                head = 2 * p + second
                for n in range(HEAD_DIM // 32):
                    row = HEAD_DIM * lax.rem(head, heads) + 32 * n
                    place_of = pl.ds(pl.multiple_of(lax.rem(row, height // 2), 32), 32)
                    for j in range(4):
                        pltpu.make_async_copy(
                            turned_buf.at[slot, j, pl.ds(second * HEAD_DIM + 32 * n, 32)],
                            turned_ref.at[head // heads, j, row // (height // 2), place_of], store_sem.at[slot, 3],
                        ).start()

        def wait_stores(p, slot):
            for copy in lane_stores(p, slot):
                copy.wait()
            arrived(turned_buf.at[slot], store_sem.at[slot, 3])

        def pair(p):
            slot = lax.rem(p, 2)

            @pl.when(p + 1 < PAIRS)
            def _():
                for copy in loads(p + 1, 1 - slot):
                    copy.start()

            for copy in loads(p, slot):
                copy.wait()

            @pl.when(p >= 2)
            def _():
                wait_stores(p - 2, slot)

            back_pair(
                qp_buf.at[slot], kp_buf.at[slot], v_buf.at[slot], o_buf.at[slot], da_ref, wo_buf.at[slot, 0],
                wo_buf.at[slot, 1], gain_ref.at[p], bias_ref, lse_ref.at[p], dq_buf.at[slot], dk_buf.at[slot],
                dv_buf.at[slot], sums.at[p], key_buf, key_turned, k_total, v_total,
            )
            turned_buf[slot, 0] = dot_tn(dq_buf[slot], h_ref[pl.ds(cols - rows, rows), :]).astype(BF16)
            turned_buf[slot, 1] = dot_tn(dk_buf[slot], h_ref[...]).astype(BF16)
            turned_buf[slot, 2] = dot_tn(dv_buf[slot], h_ref[...]).astype(BF16)
            turned_buf[slot, 3] = dot_tn(o_buf[slot], da_ref[...]).astype(BF16)
            start_stores(p, slot)

        for copy in loads(0, 0):
            copy.start()

        def step(t, _):
            lead(t)

            @pl.when(t < PAIRS)
            def _():
                pair(t)

            follow(t)
            return 0

        lax.fori_loop(0, attended, step, 0)
        for p in (PAIRS - 2, PAIRS - 1):
            wait_stores(p, p % 2)

    pl.run_scoped(
        attention,
        pltpu.VMEM((2, rows, PAIR), F32),
        pltpu.VMEM((2, cols, PAIR), F32),
        pltpu.VMEM((2, cols, PAIR), BF16),
        pltpu.VMEM((2, rows, PAIR), BF16),
        pltpu.VMEM((2, 2, HEAD_DIM, D), BF16),
        pltpu.VMEM((2, rows, PAIR), BF16),
        pltpu.VMEM((2, cols, PAIR), BF16),
        pltpu.VMEM((2, cols, PAIR), BF16),
        pltpu.VMEM((2, 4, PAIR, D), BF16),
        dma((2, 6)), dma((2, 4)),
        pltpu.VMEM((cols, PAIR), BF16),
        pltpu.VMEM((PAIR, cols), BF16),
        pltpu.VMEM((cols, PAIR), F32),
        pltpu.VMEM((cols, PAIR), F32),
    )

    def inputs(weight_buf, left_buf, parts, weight_sem, left_sem):
        for j in range(3):
            for shard in range(shards):
                pltpu.make_async_copy(
                    weight_ref.at[0, shard, pl.ds(j * height, height)],
                    weight_buf.at[j, pl.ds(shard * height, height)], weight_sem,
                ).start()
        for n in range(1, shards):
            other = lax.rem(line + n, shards)
            remote(gains_ref.at[other], line_got.at[n - 1], line_send.at[0], line_recv.at[0, n - 1], rep, other).start()
            remote(sums, line_sums.at[n - 1], line_send.at[1], line_recv.at[1, n - 1], rep, other).start()

        def lefts(block):
            slot = lax.rem(block, 2)
            part = pl.ds(pl.multiple_of(block * BACK_BLOCK, BACK_BLOCK), BACK_BLOCK)
            return [
                pltpu.make_async_copy(ref.at[part], left_buf.at[slot, n], left_sem.at[slot, n])
                for n, ref in ((1, dk_ref), (2, dv_ref))
            ]

        def own_left(block):
            slot = lax.rem(block, 2)
            part = pl.ds(pl.multiple_of((block - reach * per) * BACK_BLOCK, BACK_BLOCK), BACK_BLOCK)
            return pltpu.make_async_copy(dq_ref.at[part], left_buf.at[slot, 0], left_sem.at[slot, 0])

        def fetch(block):
            for copy in lefts(block):
                copy.start()

            @pl.when(block >= reach * per)
            def _():
                own_left(block).start()

        def product(block):
            slot = lax.rem(block, 2)

            @pl.when(block + 1 < cols // BACK_BLOCK)
            def _():
                fetch(block + 1)

            for copy in lefts(block):
                copy.wait()
            total = dot(left_buf[slot, 1], weight_buf[1]) + dot(left_buf[slot, 2], weight_buf[2])

            @pl.when(block < reach * per)
            def _():
                parts[block] = total.astype(BF16)
                n = block // per
                part = pl.ds(pl.multiple_of(lax.rem(block, per) * BACK_BLOCK, BACK_BLOCK), BACK_BLOCK)

                @pl.when(line >= reach - n)
                def _():
                    remote(parts.at[block], back_out.at[n, part], back_send.at[n], back_recv.at[n], rep,
                           line - (reach - n)).start()

            @pl.when(block >= reach * per)
            def _():
                own_left(block).wait()
                part = pl.ds(pl.multiple_of((block - reach * per) * BACK_BLOCK, BACK_BLOCK), BACK_BLOCK)
                own_out[part, :] = total + dot(left_buf[slot, 0], weight_buf[0])

        fetch(0)

        def step(t, _):
            lead(t)

            @pl.when(t == attended + 1)
            def _():
                arrived(weight_buf, weight_sem)
                for pair_of, (whole, got, got_plane, mine) in enumerate(
                    ((gains_ref.at[line], line_got, plane_got, mine_gains), (sums, line_sums, plane_sums, mine_sums))
                ):
                    total = whole[...]
                    for n in range(shards - 1):
                        arrived(got.at[n], line_recv.at[pair_of, n])
                        total = total + got[n]
                    mine[...] = total
                    for n in range(1, 8):
                        remote(mine, got_plane.at[n - 1], plane_send.at[pair_of], plane_recv.at[pair_of, n - 1],
                               lax.rem(rep + n, 8), line).start()

            @pl.when(t == attended + 3)
            def _():
                for pair_of, (got_plane, mine, result) in enumerate(
                    ((plane_got, mine_gains, gains_out), (plane_sums, mine_sums, sums_out))
                ):
                    total = mine[...]
                    for n in range(7):
                        arrived(got_plane.at[n], plane_recv.at[pair_of, n])
                        total = total + got_plane[n]
                    result[...] = total

            @pl.when((t > attended + 1) & (t < attended + 2 + cols // BACK_BLOCK))
            def _():
                product(t - attended - 2)

            follow(t)
            return 0

        lax.fori_loop(attended, turns, step, 0)
        for n in range(reach):
            @pl.when(line >= reach - n)
            def _(n=n):
                arrived(parts.at[pl.ds(0, per)], back_send.at[n])

            @pl.when(line + reach - n < shards)
            def _(n=n):
                arrived(back_out.at[n], back_recv.at[n])

    pl.run_scoped(
        inputs,
        pltpu.VMEM((3, D, D), BF16),
        pltpu.VMEM((2, 3, BACK_BLOCK, D), BF16),
        pltpu.VMEM((reach * per, BACK_BLOCK, D), BF16),
        dma(()), dma((2, 3)),
    )
    finish()
    arrived(grads_ref, pair_send)
    arrived(line_got, line_send.at[0])
    arrived(line_sums, line_send.at[1])
    arrived(plane_got, plane_send.at[0])
    arrived(plane_sums, plane_send.at[1])


def backward_reduce(grads, down, q_pre, k_pre, value_all, o_low, gathered, gains, grad_spre, gain_qk, bias_turned, lse,
                    low_all):
    _, shards, _, _, rows, _ = grads.shape
    tokens, cols = q_pre.shape[0], k_pre.shape[0]
    reach = (cols - tokens) // tokens
    lines = gains.shape[1:]
    any_space = pl.BlockSpec(memory_space=pl.ANY)
    vmem = pl.BlockSpec(memory_space=pltpu.VMEM)
    dma = pltpu.SemaphoreType.DMA
    return pl.pallas_call(
        functools.partial(backward_kernel, shards),
        out_shape=(
            jax.ShapeDtypeStruct((4, 8, rows, D), BF16),
            jax.ShapeDtypeStruct((tokens, D), BF16),
            jax.ShapeDtypeStruct((cols, D), BF16),
            jax.ShapeDtypeStruct((cols, D), BF16),
            jax.ShapeDtypeStruct(grads.shape[1:], BF16),
            jax.ShapeDtypeStruct(lines, F32),
            jax.ShapeDtypeStruct((PAIRS, 8, PAIR), F32),
            jax.ShapeDtypeStruct((reach, tokens, D), BF16),
            jax.ShapeDtypeStruct((tokens, D), F32),
        ),
        in_specs=[any_space] * 7 + [vmem] * 6,
        out_specs=(any_space,) * 5 + (vmem, vmem, any_space, vmem),
        scratch_shapes=[
            pltpu.VMEM((PAIRS, 8, PAIR), F32),
            pltpu.VMEM((shards - 1,) + lines, F32),
            pltpu.VMEM((7,) + lines, F32),
            pltpu.VMEM((shards - 1, PAIRS, 8, PAIR), F32),
            pltpu.VMEM((7, PAIRS, 8, PAIR), F32),
            pltpu.VMEM(lines, F32),
            pltpu.VMEM((PAIRS, 8, PAIR), F32),
            dma((2,)), dma((2, shards - 1)), dma((2,)), dma((2, 7)), dma((reach,)), dma((reach,)),
        ] + reduction_scratch(4, shards, rows),
        compiler_params=pltpu.CompilerParams(
            collective_id=1, has_side_effects=True, vmem_limit_bytes=63 * 2**20
        ),
        cost_estimate=pl.CostEstimate(flops=55 * 10**9, bytes_accessed=4 * 10**8, transcendentals=13 * 10**6),
    )(grads, down, q_pre, k_pre, value_all, o_low, gathered, gains, grad_spre, gain_qk, bias_turned, lse, low_all)


def body(
    tokens,
    doc_lengths,
    cotangent,
    attn_w,
    ffn_w,
    attn_m,
    attn_v,
    ffn_m,
    ffn_v,
    gains_d,
    gains_ff,
    gd_m,
    gd_v,
    gf_m,
    gf_v,
):
    shards = lax.axis_size("shard")
    reps = lax.axis_size("rep")
    device_index = lax.axis_index("shard")
    rows = tokens.shape[0]
    reach = WINDOW // rows
    cols = (reach + 1) * rows
    attn_rows = attn_w.shape[1]
    ffn_rows = ffn_w.shape[1]
    ffn_all = shards * ffn_rows
    piece = ffn_rows // reps

    lengths_row = doc_lengths[0]
    starts = jnp.cumsum(lengths_row) - lengths_row
    positions = device_index * rows + jnp.arange(rows, dtype=jnp.int32)
    doc_start = jnp.max(
        jnp.where(starts[None, :] <= positions[:, None], starts[None, :], 0), axis=1
    )
    blocks = rows // QUERY_BLOCK
    span = WINDOW + QUERY_BLOCK
    query = jnp.arange(rows, dtype=jnp.int32).reshape(blocks, QUERY_BLOCK)
    lead = query[:, :1] - reach * rows + jnp.arange(span, dtype=jnp.int32)
    ahead = query[:, :, None] - lead[:, None, :]
    floor = (doc_start - device_index * rows).reshape(blocks, QUERY_BLOCK, 1)
    mask = (ahead >= 0) & (ahead < WINDOW) & (lead[:, None, :] >= floor)
    bias = jnp.where(mask, 0.0, NEGATIVE).astype(F32)
    bias_turned = bias.transpose(0, 2, 1)
    bias = bias.reshape(rows, span)
    cut = gains_d.size
    small = jnp.concatenate([gains_d.reshape(-1), gains_ff.reshape(-1)]).astype(BF16)
    normed_in, factor_in = rownorm(tokens.astype(F32))
    fast = reps == 8 and shards == 4 and attn_rows % HEAD_DIM == 0 and reach == 2
    if fast:
        small = small.astype(F32)
        qk_heads = small[:attn_rows].reshape(-1, HEAD_DIM)
        qk_heads = jnp.pad(
            jnp.concatenate([qk_heads, qk_heads], 1), ((0, 8 - qk_heads.shape[0]), (0, D - PAIR))
        )
        small = jnp.pad(small, (0, 8 * D - small.size)).reshape(8, D)
        gathered, small, low_all, q_pre, k_pre, value_all, o_low, lse = gather_attend(
            attn_w.reshape(8, piece, D),
            ffn_w.reshape(3, 8, piece, D),
            jnp.concatenate([qk_heads, small]),
            tokens,
            bias,
            shards,
        )
        small = small[:, 8:].reshape(shards, -1)[:, : cut + gains_ff.size]
        out_low = gathered[0, :, 3 * attn_rows :].reshape(D, D)
        ffn_low = [gathered.reshape(4, ffn_all, D)] * 3
        firsts = (1, 2, 3)
    else:
        attn_low = (
            gather_rows(attn_w.reshape(4 * attn_rows, D).astype(BF16))
            .reshape(shards, 4, attn_rows, D)
            .transpose(1, 0, 2, 3)
            .reshape(1, 4, HEADS, HEAD_DIM, D)
        )
        ffn_low = [gather_rows(ffn_w[m].astype(BF16)).reshape(1, ffn_all, D) for m in range(3)]
        firsts = (0, 0, 0)
        small = lax.all_gather(small, "shard", axis=0).astype(F32)
        query_low, key_low, value_low, out_low = (attn_low[0, j].reshape(D, D) for j in range(4))
    gd_all = small[:, :cut].reshape(shards, 3, -1).transpose(1, 0, 2).reshape(3, D)
    gf_all = small[:, cut:].reshape(shards, 2, ffn_rows).transpose(1, 0, 2).reshape(2, ffn_all)
    gain_qk = gd_all[0]
    alpha_attn = gd_all[1]
    alpha_ffn = gd_all[2]

    if not fast:
        earlier = [from_behind(tokens, "shard", offset) for offset in range(reach, 0, -1)]
        low_all = rownorm(jnp.concatenate(earlier + [tokens], 0).astype(F32))[0].astype(BF16)
        q_pre, k_pre, value_all, o_low, lse = attention_forward(
            low_all, attn_low, gain_qk[None], bias, rows
        )
    in_low = low_all[-rows:]
    side, side_factor = rownorm(dot(o_low, out_low))
    middle, mid_factor = rownorm(normed_in + alpha_attn * (side - normed_in))
    mid_low = middle.astype(BF16)
    output, grad_mid, ffn_grads, down_grads, grad_scale_up, grad_scale_gate, grad_alpha_ffn = feed_forward(
        mid_low, middle, cotangent, alpha_ffn[None], gf_all, ffn_low, firsts
    )
    grad_mixed = norm_back(middle, mid_factor, grad_mid)
    grad_in = grad_mixed * (1.0 - alpha_attn)
    grad_alpha_attn = jnp.sum(grad_mixed * (side - normed_in), 0)
    grad_spre = norm_back(side, side_factor, grad_mixed * alpha_attn).astype(BF16)
    pair_gain = gain_qk.reshape(PAIRS, 1, PAIR)
    grad_gf = jnp.concatenate([grad_scale_up, grad_scale_gate])
    gd_rows = D // shards
    if fast:
        units = (shards, 4, 2, piece, D)
        grad_gd = jnp.stack([grad_alpha_attn, grad_alpha_ffn[0]])
        small = jnp.concatenate(
            [
                grad_gd.reshape(2, shards, gd_rows).transpose(1, 0, 2).reshape(shards, -1),
                grad_gf.reshape(2, shards, ffn_rows).transpose(1, 0, 2).reshape(shards, -1),
            ],
            1,
        )
        small = jnp.pad(small, ((0, 0), (0, 8 * D - small.shape[1]))).reshape(shards, 8, D)
        summed, _, _, _, _, sum_small, sum_qk, back_got, back_own = backward_reduce(
            ffn_grads.reshape((2,) + units), down_grads.reshape(units), q_pre, k_pre, value_all, o_low, gathered,
            small, grad_spre, pair_gain, bias_turned, lse, low_all,
        )
        grad_in = grad_in + back_own
        for n in range(reach):
            sent = device_index + reach - n < shards
            grad_in = grad_in + jnp.where(sent, back_got[n], 0).astype(F32)
        sum_small = sum_small.reshape(-1)
        sum_qk = lax.dynamic_slice_in_dim(sum_qk[:, 0].reshape(D), device_index * gd_rows, gd_rows, 0)
        sum_gd = jnp.concatenate([sum_qk, sum_small[: 2 * gd_rows]]).reshape(3, gd_rows)
        sum_gf = sum_small[2 * gd_rows : 2 * gd_rows + 2 * ffn_rows].reshape(2, ffn_rows)
        attn_sums, ffn_sums = [(summed, 3)], [(summed, 0), (summed, 1), (summed, 2)]
    else:
        grad_qpre, grad_kpre, grad_vpre, gain_sums = attention_backward(
            q_pre, k_pre, value_all, o_low, grad_spre, attn_low, pair_gain, bias_turned, lse
        )
        grad_gain_qk = gain_sums[:, 0].reshape(D)
        back_all = dot(grad_kpre, key_low) + dot(grad_vpre, value_low)
        grad_in = grad_in + dot(grad_qpre, query_low) + back_all[reach * rows :]
        back_parts = back_all[: reach * rows].reshape(reach, rows, D).astype(BF16)
        for n in range(reach):
            grad_in = grad_in + from_behind(back_parts[n], "shard", n - reach).astype(F32)
        attn_grad = jnp.stack(
            [
                dot_tn(grad_qpre, in_low),
                dot_tn(grad_kpre, low_all),
                dot_tn(grad_vpre, low_all),
                dot_tn(o_low, grad_spre),
            ]
        ).astype(BF16)
        attn_grad = attn_grad.reshape(4, shards, attn_rows, D).transpose(1, 0, 2, 3)
        attn_grad = attn_grad.reshape(shards, reps, 4 * attn_rows // reps, D).transpose(1, 0, 2, 3)
        attn_sums = [(reduce_rows(attn_grad).reshape(1, 4, attn_rows, D), 0)]
        ready = (shards, reps, piece, D)
        ffn_sums = [
            (reduce_rows(part.reshape(ready).transpose(1, 0, 2, 3)).reshape(1, 1, ffn_rows, D), 0)
            for part in (ffn_grads[0], ffn_grads[1], down_grads)
        ]
        grad_small = jnp.concatenate(
            [grad_gain_qk, grad_alpha_attn, grad_alpha_ffn[0], grad_gf.reshape(-1)]
        )
        grad_small = lax.psum(grad_small, ("rep", "shard"))
        sum_gd = lax.dynamic_slice_in_dim(
            grad_small[: 3 * D].reshape(3, D), device_index * gd_rows, gd_rows, 1
        )
        sum_gf = lax.dynamic_slice_in_dim(
            grad_small[3 * D :].reshape(2, ffn_all), device_index * ffn_rows, ffn_rows, 1
        )
    grad_tokens = norm_back(normed_in, factor_in, grad_in)

    attn_unit, attn_m_new, attn_v_new = adam_rows(attn_w, attn_sums, attn_m, attn_v)
    ffn_unit, ffn_m_new, ffn_v_new = adam_rows(ffn_w, ffn_sums, ffn_m, ffn_v)
    gd_new, gd_m_new, gd_v_new = adam(gains_d, sum_gd, gd_m, gd_v, GAIN_RATE, 0.0)
    gf_new, gf_m_new, gf_v_new = adam(gains_ff, sum_gf, gf_m, gf_v, GAIN_RATE, 0.0)
    return (
        output,
        grad_tokens,
        attn_unit,
        attn_m_new,
        attn_v_new,
        ffn_unit,
        ffn_m_new,
        ffn_v_new,
        gd_new,
        gd_m_new,
        gd_v_new,
        gf_new,
        gf_m_new,
        gf_v_new,
    )

def solution(mesh):
    return jax.shard_map(
        body,
        mesh=mesh,
        in_specs=(
            P(("rep", "shard"), None),
            P("rep", None),
            P(("rep", "shard"), None),
            P(None, "shard", None),
            P(None, "shard", None),
            P(None, "shard", None),
            P(None, "shard", None),
            P(None, "shard", None),
            P(None, "shard", None),
            P(None, "shard"),
            P(None, "shard"),
            P(None, "shard"),
            P(None, "shard"),
            P(None, "shard"),
            P(None, "shard"),
        ),
        out_specs=(
            P(("rep", "shard"), None),
            P(("rep", "shard"), None),
            P(None, "shard", None),
            P(None, "shard", None),
            P(None, "shard", None),
            P(None, "shard", None),
            P(None, "shard", None),
            P(None, "shard", None),
            P(None, "shard"),
            P(None, "shard"),
            P(None, "shard"),
            P(None, "shard"),
            P(None, "shard"),
            P(None, "shard"),
        ),
        check_vma=False,
    )
```

```python
import functools
import math

import jax
import jax.numpy as jnp
from jax import lax
from jax.experimental import pallas as pl
from jax.experimental.pallas import tpu as pltpu
from jax.sharding import PartitionSpec as P

D = 1280
HEADS = 20
HEAD_DIM = 64
WINDOW = 1024
STEP = 10


SMALL = 1e-06
NEGATIVE = -1e30
BETA_ONE = 0.9
BETA_TWO = 0.95
RATE = 0.02
GAIN_RATE = 1.0
DECAY = 0.1
TINY = 1e-08
F32 = jnp.float32
BF16 = jnp.bfloat16


def from_behind(block, axis, distance):
    devices = range(lax.axis_size(axis))
    route = [(i - distance, i) for i in devices if i - distance in devices]
    return lax.ppermute(block, axis, route)


def rownorm(value):
    factor = lax.rsqrt(jnp.sum(value * value, -1, keepdims=True) + SMALL)
    return (value * factor, factor)


def norm_back(normed, factor, grad):
    return factor * (grad - normed * jnp.sum(normed * grad, -1, keepdims=True))


def adam(weight, grad, first, second, rate, decay):
    first = BETA_ONE * first + (1.0 - BETA_ONE) * grad
    second = BETA_TWO * second + (1.0 - BETA_TWO) * grad * grad
    fix_one = 1.0 - BETA_ONE**STEP
    fix_two = 1.0 - BETA_TWO**STEP
    change = first / fix_one / (jnp.sqrt(second / fix_two) + TINY) + decay * weight
    return (weight - rate * change, first, second)


def dot(a, b):
    return jnp.dot(a, b, preferred_element_type=F32)


def dot_nt(a, b):
    return lax.dot_general(a, b, (((1,), (1,)), ((), ())), preferred_element_type=F32)


def dot_tn(a, b):
    return lax.dot_general(a, b, (((0,), (0,)), ((), ())), preferred_element_type=F32)


def gather_rows(shard_rows):
    reps = lax.axis_size("rep")
    piece = shard_rows.shape[0] // reps
    mine = lax.dynamic_slice_in_dim(shard_rows, lax.axis_index("rep") * piece, piece, 0)
    column = lax.all_gather(mine, "shard", axis=0)
    return lax.all_gather(column, "rep", axis=1)


def reduce_rows(grad):
    part = lax.psum_scatter(grad, "rep", scatter_dimension=0)
    part = lax.psum_scatter(part, "shard", scatter_dimension=0)
    return lax.all_gather(part, "rep", axis=0, tiled=True)


MESH = pl.DeviceIdType.MESH
HALF = 80
RING = 8
HALF_RING = 4


def place():
    rep = lax.axis_index("rep")
    core, chip = lax.rem(rep, 2), rep // 2
    beside, above = chip + 1 - 2 * lax.rem(chip, 2), chip + 2 - 4 * (chip // 2)
    return core, chip, beside, above, 3 - chip


def remote(src, dst, send, recv, rep, shard):
    return pltpu.make_async_remote_copy(
        src_ref=src, dst_ref=dst, send_sem=send, recv_sem=recv,
        device_id=(rep, shard), device_id_type=MESH,
    )


def arrived(ref, sem):
    pltpu.make_async_copy(ref, ref, sem).wait()


def greet(shards):
    rep, line = lax.axis_index("rep"), lax.axis_index("shard")
    barrier = pltpu.get_barrier_semaphore()
    for n in range(1, 8):
        pl.semaphore_signal(barrier, inc=1, device_id=(lax.rem(rep + n, 8), line), device_id_type=MESH)
    for n in range(1, shards):
        pl.semaphore_signal(barrier, inc=1, device_id=(rep, lax.rem(line + n, shards)), device_id_type=MESH)
    pl.semaphore_wait(barrier, 6 + shards)


def add_into(target, sources, rows):
    def step(i, _):
        part = pl.ds(pl.multiple_of(i * 16, 16), 16)
        if len(sources) == 1:
            target[part, :] = target[part, :] + sources[0][part, :]
        else:
            value = target[part, :].astype(F32)
            for source in sources:
                value = value + source[part, :].astype(F32)
            target[part, :] = value.astype(BF16)
        return 0

    lax.fori_loop(0, rows // 16, step, 0, unroll=min(5, rows // 16))


def reduction_scratch(count, shards, rows):
    steps = count * shards
    dma = pltpu.SemaphoreType.DMA
    return [
        pltpu.VMEM((RING, 4, rows, D), BF16),
        pltpu.VMEM((2, 4, rows, D), BF16),
        pltpu.VMEM((HALF_RING, rows, D), BF16),
        pltpu.VMEM((HALF_RING, 2, rows, D), BF16),
        pltpu.VMEM((count, shards + 1, rows, D), BF16),
        dma((2,)), dma(()), dma((steps,)), dma((steps,)), dma((steps, 2)),
        dma((steps,)), dma((steps, 2)), dma((steps,)), dma((count, shards + 1)),
        dma((count,)), dma((count, 8)), dma((count,)), dma(()), pltpu.SemaphoreType.REGULAR,
    ]


def reduction(grads, out, scratch):
    (acc, own, half, piece, below, own_sem, pair_send, pair_recv, half_send, half_recv,
     piece_send, piece_recv, line_send, line_recv, out_send, out_recv, out_local, on_send, credit) = scratch
    count = len(grads)
    rows = own.shape[2]
    shards = below.shape[1] - 1
    core, chip, beside, above, across = place()
    line = lax.axis_index("shard")
    steps = count * shards
    mine, sibling = 2 * chip + core, 2 * chip + 1 - core
    one = piece.at[0, 0]

    def owner(step):
        i = lax.rem(step, shards)
        back = lax.select(i < shards - 1 - line, shards - 1 - i, i - (shards - 1 - line))
        ahead = lax.select(i < line, i, shards - 1 - (i - line))
        other = lax.select(2 * line < shards, back, ahead)
        return lax.select(i == shards - 1, line, other)

    def room(step):
        return acc.at[lax.rem(step, RING)]

    def begin(step):
        slot = lax.rem(step, 2)

        @pl.when(step >= RING)
        def _():
            pl.semaphore_wait(credit, 1)

        for n, grad in enumerate(grads):
            @pl.when(step // shards == n)
            def _(grad=grad):
                remote(grad.at[owner(step), :, 1 - core], room(step), pair_send, pair_recv.at[step], sibling, line).start()
                pltpu.make_async_copy(grad.at[owner(step), :, core], own.at[slot], own_sem.at[slot]).start()

    def first(step):
        slot, part = lax.rem(step, 2), lax.rem(step, HALF_RING)
        total = room(step)
        arrived(own.at[slot], own_sem.at[slot])
        arrived(total, pair_recv.at[step])
        for q in range(4):
            add_into(total.at[q], (own.at[slot, q],), rows)
        remote(total.at[across, pl.ds(0, HALF)], half.at[part, pl.ds(0, HALF)],
               half_send.at[step], half_recv.at[step, 0], 2 * beside + core, line).start()
        remote(total.at[across, pl.ds(HALF, rows - HALF)], half.at[part, pl.ds(HALF, rows - HALF)],
               half_send.at[step], half_recv.at[step, 1], 2 * above + core, line).start()

    def second(step):
        part = lax.rem(step, HALF_RING)
        total = room(step)
        low, high = half.at[part, pl.ds(0, HALF)], half.at[part, pl.ds(HALF, rows - HALF)]
        arrived(low, half_recv.at[step, 0])
        arrived(high, half_recv.at[step, 1])
        add_into(total.at[above, pl.ds(0, HALF)], (low,), HALF)
        add_into(total.at[beside, pl.ds(HALF, rows - HALF)], (high,), rows - HALF)
        remote(total.at[beside], piece.at[part, 0], piece_send.at[step], piece_recv.at[step, 0],
               2 * beside + core, line).start()
        remote(total.at[above], piece.at[part, 1], piece_send.at[step], piece_recv.at[step, 1],
               2 * above + core, line).start()

    def pass_on(step):
        m, target = step // shards, owner(step)

        @pl.when(target > line)
        def _():
            remote(room(step).at[chip], below.at[m, target], line_send.at[step], line_recv.at[m, target],
                   mine, line + 1).start()

        @pl.when(target < line)
        def _():
            slot = lax.select(target == line - 1, shards, target)
            remote(room(step).at[chip], below.at[m, slot], line_send.at[step], line_recv.at[m, slot],
                   mine, line - 1).start()

    def outermost(step):
        target = owner(step)
        return ((target > line) & (line == 0)) | ((target < line) & (line == shards - 1))

    def third(step):
        part = lax.rem(step, HALF_RING)
        for n in range(2):
            arrived(piece.at[part, n], piece_recv.at[step, n])
        add_into(room(step).at[chip], (piece.at[part, 0], piece.at[part, 1]), rows)

        @pl.when(outermost(step))
        def _():
            pass_on(step)

    def along(step):
        m, target = step // shards, owner(step)

        def add_line(slot):
            arrived(below.at[m, slot], line_recv.at[m, slot])
            add_into(room(step).at[chip], (below.at[m, slot],), rows)

        @pl.when(((target >= line) & (line > 0)) | ((target < line) & (line < shards - 1)))
        def _():
            add_line(target)

        @pl.when((target == line) & (line < shards - 1))
        def _():
            add_line(shards)

        @pl.when(jnp.logical_not(outermost(step)))
        def _():
            pass_on(step)

        @pl.when(target == line)
        def _():
            total = room(step).at[chip]
            pltpu.make_async_copy(total, out.at[m, mine], out_local.at[m]).start()
            for n, other in enumerate((2 * beside + core, 2 * above + core, sibling)):
                remote(total, out.at[m, mine], out_send.at[m], out_recv.at[m, n], other, line).start()

    def fourth(step):
        m = step // shards
        for n, (origin, other, part) in enumerate(
            (
                (2 * beside + core, 2 * above + core, pl.ds(0, HALF)),
                (2 * above + core, 2 * beside + core, pl.ds(HALF, rows - HALF)),
            )
        ):
            arrived(out.at[m, origin], out_recv.at[m, n])
            share = out.at[m, origin, part]
            remote(share, share, on_send, out_recv.at[m, 3 + n], other, line).start()
            remote(out.at[m, origin], out.at[m, origin], on_send, out_recv.at[m, 5 + n], sibling, line).start()

    def fifth(step):
        m, origin = step // shards, 2 * across + core
        arrived(out.at[m, origin, pl.ds(0, HALF)], out_recv.at[m, 3])
        arrived(out.at[m, origin, pl.ds(HALF, rows - HALF)], out_recv.at[m, 4])
        remote(out.at[m, origin], out.at[m, origin], on_send, out_recv.at[m, 7], sibling, line).start()

    def retire(step):
        m, target = step // shards, owner(step)
        arrived(one, half_send.at[step])
        arrived(piece.at[0], piece_send.at[step])

        @pl.when(target != line)
        def _():
            arrived(one, line_send.at[step])

        @pl.when(target == line)
        def _():
            arrived(acc.at[0, pl.ds(0, 3)], out_send.at[m])
            arrived(one, out_local.at[m])

        @pl.when(step + RING < steps)
        def _():
            pl.semaphore_signal(credit, inc=1, device_id=(sibling, line), device_id_type=MESH)

    def lead(t):
        @pl.when((t >= 6) & (t < steps + 6))
        def _():
            retire(t - 6)

        @pl.when(t == 0)
        def _():
            begin(0)

        @pl.when(t + 1 < steps)
        def _():
            begin(t + 1)

        @pl.when(t < steps)
        def _():
            first(t)

    def follow(t):
        @pl.when((t >= 1) & (t < steps + 1))
        def _():
            second(t - 1)

        @pl.when((t >= 3) & (t < steps + 3))
        def _():
            third(t - 3)

        @pl.when((t >= 4) & (t < steps + 4))
        def _():
            along(t - 4)

        @pl.when((t >= 5) & (t < steps + 5) & (lax.rem(t - 5, shards) == shards - 1))
        def _():
            fourth(t - 5)

        @pl.when((t >= 6) & (t < steps + 6) & (lax.rem(t - 6, shards) == shards - 1))
        def _():
            fifth(t - 6)

    def finish():
        for m in range(count):
            for n in (2, 5, 6, 7):
                arrived(out.at[m, 0], out_recv.at[m, n])
        arrived(out.at[:, pl.ds(0, 4)], on_send)

    return steps + 6, lead, follow, finish, pair_send


UNITS = 256


def feed_kernel(blocks, mid_ref, middle_ref, cot_ref, alpha_ref, up_scale_ref, gate_scale_ref, wu_ref, wg_ref, wd_ref,
                out_ref, grad_mid_ref, grad_ref, down_ref, up_sum_ref, gate_sum_ref, alpha_sum_ref,
                up_buf, gate_buf, hidden_buf, total, back, grad_hidden_buf, grad_u_buf, grad_g_buf):
    turn = pl.program_id(0)
    after = turn - blocks - 2

    def raw(block):
        up_buf[block] = dot_nt(mid_ref[...], wu_ref[...])
        gate_buf[block] = dot_nt(mid_ref[...], wg_ref[...])

    def activate(block):
        gate = gate_buf[block] * (gate_scale_ref[...] * math.sqrt(D))
        hidden = gate * jax.nn.sigmoid(gate) * (up_buf[block] * up_scale_ref[...])
        hidden_buf[block] = hidden.astype(BF16)

    def project(block, first):
        part = dot(hidden_buf[block], wd_ref[...])
        total[...] = part if first else total[...] + part

    def middle_step():
        alpha = alpha_ref[...]
        rows = total.shape[0]

        def step(i, sums):
            part = pl.ds(pl.multiple_of(i * 32, 32), 32)
            branch, factor = rownorm(total[part, :])
            middle = middle_ref[part, :]
            final, final_factor = rownorm(middle + alpha * (branch - middle))
            out_ref[part, :] = final.astype(BF16)
            grad = norm_back(final, final_factor, cot_ref[part, :].astype(F32))
            grad_mid_ref[part, :] = grad * (1.0 - alpha)
            back[part, :] = norm_back(branch, factor, grad * alpha).astype(BF16)
            return sums + jnp.sum(grad * (branch - middle), 0, keepdims=True)

        alpha_sum_ref[...] = lax.fori_loop(0, rows // 32, step, jnp.zeros((1, D), F32))

    def back_raw():
        grad_hidden_buf[...] = dot_nt(back[...], wd_ref[...])

    def back_activate(block):
        up_scale, gate_scale = up_scale_ref[...], gate_scale_ref[...] * math.sqrt(D)
        grad_hidden = grad_hidden_buf[...]
        up_raw, gate_raw = up_buf[block], gate_buf[block]
        gate = gate_raw * gate_scale
        sigma = jax.nn.sigmoid(gate)
        active = gate * sigma
        upward = up_raw * up_scale
        grad_upward = grad_hidden * active
        grad_gate = grad_hidden * upward * (sigma * (1.0 + gate * (1.0 - sigma)))
        up_sum_ref[...] = jnp.sum(grad_upward * up_raw, 0, keepdims=True)
        gate_sum_ref[...] = jnp.sum(grad_gate * gate_raw, 0, keepdims=True) * math.sqrt(D)
        grad_u_buf[...] = (grad_upward * up_scale).astype(BF16)
        grad_g_buf[...] = (grad_gate * gate_scale).astype(BF16)

    def back_project(block):
        grad_u, grad_g = grad_u_buf[...], grad_g_buf[...]
        grad_ref[0] = dot_tn(grad_u, mid_ref[...]).astype(BF16)
        grad_ref[1] = dot_tn(grad_g, mid_ref[...]).astype(BF16)
        down_ref[...] = dot_tn(hidden_buf[block], back[...]).astype(BF16)
        grad_mid_ref[...] += dot(grad_u, wu_ref[...]) + dot(grad_g, wg_ref[...])

    @pl.when(turn == 0)
    def _():
        raw(0)

    @pl.when(turn == 1)
    def _():
        activate(0)
        raw(1)

    @pl.when(turn == 2)
    def _():
        project(0, True)
        activate(1)
        raw(2)

    @pl.when((turn > 2) & (turn < blocks))
    def _():
        project(turn - 2, False)
        activate(turn - 1)
        raw(turn)

    @pl.when(turn == blocks)
    def _():
        project(turn - 2, False)
        activate(turn - 1)

    @pl.when(turn == blocks + 1)
    def _():
        project(turn - 2, False)
        middle_step()

    @pl.when(after == 0)
    def _():
        back_raw()

    @pl.when(after == 1)
    def _():
        back_activate(0)
        back_raw()

    @pl.when((after > 1) & (after < blocks))
    def _():
        back_project(after - 2)
        back_activate(after - 1)
        back_raw()

    @pl.when(after == blocks)
    def _():
        back_project(after - 2)
        back_activate(after - 1)

    @pl.when(after == blocks + 1)
    def _():
        back_project(after - 2)


def feed_forward(mid_low, middle, cotangent, alpha_ffn, scales, weights, firsts):
    rows = mid_low.shape[0]
    blocks = scales.shape[1] // UNITS
    whole = lambda *shape: pl.BlockSpec(shape, lambda t: (0,) * len(shape))
    half = blocks + 2

    def stage(t, early, late):
        return jnp.clip(lax.select(t < half, t - early, t - half - late), 0, blocks - 1)

    weight = lambda m, early, late: pl.BlockSpec((None, UNITS, D), lambda t: (m, stage(t, early, late), 0))
    done = lambda t, lag: jnp.clip(t - half - lag, 0, blocks - 1)
    units = pl.BlockSpec((1, UNITS), lambda t: (0, done(t, 1)))
    scale = pl.BlockSpec((1, UNITS), lambda t: (0, stage(t, 1, 1)))
    return pl.pallas_call(
        functools.partial(feed_kernel, blocks),
        grid=(2 * half,),
        out_shape=(
            jax.ShapeDtypeStruct((rows, D), BF16),
            jax.ShapeDtypeStruct((rows, D), F32),
            jax.ShapeDtypeStruct((2, blocks * UNITS, D), BF16),
            jax.ShapeDtypeStruct((blocks * UNITS, D), BF16),
            jax.ShapeDtypeStruct((1, blocks * UNITS), F32),
            jax.ShapeDtypeStruct((1, blocks * UNITS), F32),
            jax.ShapeDtypeStruct((1, D), F32),
        ),
        in_specs=[whole(rows, D), whole(rows, D), whole(rows, D), whole(1, D), scale, scale]
        + [weight(firsts[0], 0, 2), weight(firsts[1], 0, 2), weight(firsts[2], 2, 0)],
        out_specs=(
            whole(rows, D), whole(rows, D), pl.BlockSpec((2, UNITS, D), lambda t: (0, done(t, 2), 0)),
            pl.BlockSpec((UNITS, D), lambda t: (done(t, 2), 0)),
            units, units, whole(1, D),
        ),
        scratch_shapes=[
            pltpu.VMEM((blocks, rows, UNITS), F32),
            pltpu.VMEM((blocks, rows, UNITS), F32),
            pltpu.VMEM((blocks, rows, UNITS), BF16),
            pltpu.VMEM((rows, D), F32),
            pltpu.VMEM((rows, D), BF16),
            pltpu.VMEM((rows, UNITS), F32),
            pltpu.VMEM((rows, UNITS), BF16),
            pltpu.VMEM((rows, UNITS), BF16),
        ],
        compiler_params=pltpu.CompilerParams(vmem_limit_bytes=62 * 2**20),
        cost_estimate=pl.CostEstimate(flops=60 * 10**9, bytes_accessed=120 * 10**6, transcendentals=5 * 10**6),
    )(mid_low, middle, cotangent, alpha_ffn, scales[:1], scales[1:], *weights)


def adam_kernel(places, per, *refs):
    grads = refs[:places]
    w_ref, m_ref, v_ref, w_out, m_out, v_out = refs[places:]
    group, piece, _ = w_ref.shape

    def update(g_ref):
        for n in range(group):
            def step(i, _, n=n):
                part = (n, pl.ds(pl.multiple_of(i * 16, 16), 16), slice(None))
                new, first, second = adam(
                    w_ref[part], g_ref[part].astype(F32), m_ref[part], v_ref[part], RATE, DECAY
                )
                w_out[part] = rownorm(new)[0]
                m_out[part] = first
                v_out[part] = second
                return 0

            lax.fori_loop(0, piece // 16, step, 0, unroll=5)

    for n in range(places):
        @pl.when(pl.program_id(0) // per == n)
        def _(n=n):
            update(grads[n])


def adam_rows(weight, grads, first, second):
    places = len(grads)
    _, per, piece, _ = grads[0][0].shape
    group = 2 if per % 2 == 0 else 1
    steps = per // group
    spec = pl.BlockSpec((group, piece, D), lambda p: (p, 0, 0))

    def grad_spec(n, index):
        return pl.BlockSpec(
            (None, group, piece, D), lambda p: (index, jnp.clip(p - n * steps, 0, steps - 1), 0, 0)
        )

    shape = jax.ShapeDtypeStruct((places * per, piece, D), F32)
    news = pl.pallas_call(
        functools.partial(adam_kernel, places, steps),
        grid=(places * steps,),
        out_shape=(shape,) * 3,
        in_specs=[grad_spec(n, index) for n, (_, index) in enumerate(grads)] + [spec] * 3,
        out_specs=(spec,) * 3,
        compiler_params=pltpu.CompilerParams(vmem_limit_bytes=60 * 2**20),
        cost_estimate=pl.CostEstimate(flops=20 * weight.size, bytes_accessed=26 * weight.size, transcendentals=0),
    )(*(array for array, _ in grads), *(old.reshape(shape.shape) for old in (weight, first, second)))
    return tuple(new.reshape(weight.shape) for new in news)


QUERY_BLOCK = 256
PAIR = 2 * HEAD_DIM
PAIRS = HEADS // 2


def head_ones():
    row = lax.broadcasted_iota(jnp.int32, (PAIR, PAIR), 0) // HEAD_DIM
    col = lax.broadcasted_iota(jnp.int32, (PAIR, PAIR), 1) // HEAD_DIM
    return (row == col).astype(F32).astype(BF16)


def head_sum(value, ones):
    high = value.astype(BF16)
    rest = (value - high.astype(F32)).astype(BF16)
    return dot(high, ones) + dot(rest, ones)


def of_head(value, head):
    lane = lax.broadcasted_iota(jnp.int32, value.shape, 1) // HEAD_DIM
    return jnp.where(lane == head, value, jnp.zeros_like(value))


def attend_pair(h_ref, wq_ref, wq2_ref, wk_ref, wk2_ref, wv_ref, wv2_ref, gain_ref, bias_ref, qp_ref, kp_ref, v_ref, o_ref, lse_ref,
                key_buf, query_buf, value_buf):
    cols = h_ref.shape[0]
    rows = qp_ref.shape[0]
    span = bias_ref.shape[1]
    ones = head_ones()
    gain = gain_ref[...]
    weights = jnp.concatenate([wk_ref[...], wk2_ref[...], wv_ref[...], wv2_ref[...]], 0)
    query_weights = jnp.concatenate([wq_ref[...], wq2_ref[...]], 0)

    def project(i, _):
        part = pl.ds(pl.multiple_of(i * QUERY_BLOCK, QUERY_BLOCK), QUERY_BLOCK)
        both = dot_nt(h_ref[part, :], weights)
        keys = both[:, :PAIR]
        kp_ref[part, :] = keys
        factor = lax.rsqrt(head_sum(keys * keys, ones) + SMALL)
        key_buf[part, :] = (keys * factor * gain).astype(BF16)
        values = both[:, PAIR:].astype(BF16)
        v_ref[part, :] = values
        value_buf[part, :PAIR] = values
        value_buf[part, PAIR:] = jnp.ones_like(values)
        return 0

    lax.fori_loop(0, cols // QUERY_BLOCK, project, 0)

    def project_queries(i, _):
        part = pl.ds(pl.multiple_of(i * QUERY_BLOCK, QUERY_BLOCK), QUERY_BLOCK)
        own = pl.ds(pl.multiple_of(cols - rows + i * QUERY_BLOCK, QUERY_BLOCK), QUERY_BLOCK)
        queries = dot_nt(h_ref[own, :], query_weights)
        qp_ref[part, :] = queries
        factor = lax.rsqrt(head_sum(queries * queries, ones) + SMALL)
        scaled = (queries * factor * gain).astype(BF16).astype(F32) * math.sqrt(HEAD_DIM)
        query_buf[part, :] = scaled.astype(BF16)
        return 0

    lax.fori_loop(0, rows // QUERY_BLOCK, project_queries, 0)
    for i in range(rows // QUERY_BLOCK):
        part = pl.ds(i * QUERY_BLOCK, QUERY_BLOCK)
        reach = pl.ds(i * QUERY_BLOCK, span)
        sides = []
        for head in range(2):
            scores = dot_nt(of_head(query_buf[part, :], head), key_buf[reach, :])
            probs = jnp.exp(scores + bias_ref[part, :]).astype(BF16)
            both = dot(probs, value_buf[reach, :])
            total = both[:, PAIR:]
            sides.append(both[:, :PAIR] / total)
            lse_ref[head : head + 1, part] = jnp.log(total).T[:1, :]
        lane = lax.broadcasted_iota(jnp.int32, sides[0].shape, 1)
        o_ref[part, :] = jnp.where(lane < HEAD_DIM, sides[0], sides[1]).astype(BF16)


def back_pair(*refs):
    start, block, finish = back_parts(*refs)
    start()
    for i in range(refs[0].shape[0] // QUERY_BLOCK):
        block(i)
    finish()


def back_parts(qp_ref, kp_ref, v_ref, o_ref, da_ref, wo_ref, wo2_ref, gain_ref, bias_ref, lse_ref,
               dq_ref, dk_ref, dv_ref, sum_ref, key_buf, key_turned, k_total, v_total):
    cols = kp_ref.shape[0]
    rows = qp_ref.shape[0]
    span = bias_ref.shape[1]

    def keys_of(i, _):
        ones, gain = head_ones(), gain_ref[...]
        part = pl.ds(pl.multiple_of(i * QUERY_BLOCK, QUERY_BLOCK), QUERY_BLOCK)
        keys = kp_ref[part, :]
        factor = lax.rsqrt(head_sum(keys * keys, ones) + SMALL)
        low = keys * factor * gain
        key_buf[part, :] = low.astype(BF16)
        key_turned[:, part] = low.T.astype(BF16)
        k_total[part, :] = jnp.zeros_like(keys)
        v_total[part, :] = jnp.zeros_like(keys)
        return 0

    def start():
        lax.fori_loop(0, cols // QUERY_BLOCK, keys_of, 0)

    def block(i):
        ones, gain = head_ones(), gain_ref[...]
        weights = jnp.concatenate([wo_ref[...], wo2_ref[...]], 0)
        part = pl.ds(i * QUERY_BLOCK, QUERY_BLOCK)
        reach = pl.ds(i * QUERY_BLOCK, span)
        queries = qp_ref[part, :]
        factor = lax.rsqrt(head_sum(queries * queries, ones) + SMALL)
        hat = queries * factor
        scaled = ((hat * gain).astype(BF16).astype(F32) * math.sqrt(HEAD_DIM)).astype(BF16)
        back = dot_nt(da_ref[part, :], weights).astype(BF16)
        inner = (back.astype(F32) * o_ref[part, :].astype(F32)).T
        sides = []
        for head in range(2):
            mine = slice(head * HEAD_DIM, (head + 1) * HEAD_DIM)
            query, grad = of_head(scaled, head), of_head(back, head)
            scores = dot_nt(key_buf[reach, :], query)
            probs = jnp.exp(scores + bias_ref[i] - lse_ref[head : head + 1, part])
            v_total[reach, :] += dot(probs.astype(BF16), grad)
            delta = jnp.sum(inner[mine, :], 0, keepdims=True)
            grad_scores = (probs * (dot_nt(v_ref[reach, :], grad) - delta)).astype(BF16)
            k_total[reach, :] += dot(grad_scores, query)
            sides.append(dot(key_turned[mine, reach], grad_scores))
        grad_q = jnp.concatenate(sides, 0).T * math.sqrt(HEAD_DIM)
        sums = jnp.sum(grad_q * hat, 0, keepdims=True)
        if i == 0:
            sum_ref[...] = jnp.broadcast_to(sums, sum_ref.shape)
        else:
            sum_ref[...] += jnp.broadcast_to(sums, sum_ref.shape)
        grad_q = grad_q * gain
        dq_ref[part, :] = (factor * (grad_q - hat * head_sum(hat * grad_q, ones))).astype(BF16)

    def close(i, _):
        ones, gain = head_ones(), gain_ref[...]
        part = pl.ds(pl.multiple_of(i * QUERY_BLOCK, QUERY_BLOCK), QUERY_BLOCK)
        keys = kp_ref[part, :]
        factor = lax.rsqrt(head_sum(keys * keys, ones) + SMALL)
        hat = keys * factor
        grad_k = k_total[part, :]
        sum_ref[...] += jnp.broadcast_to(jnp.sum(grad_k * hat, 0, keepdims=True), sum_ref.shape)
        grad_k = grad_k * gain
        dk_ref[part, :] = (factor * (grad_k - hat * head_sum(hat * grad_k, ones))).astype(BF16)
        dv_ref[part, :] = v_total[part, :].astype(BF16)
        return 0

    def finish():
        lax.fori_loop(0, cols // QUERY_BLOCK, close, 0)

    return start, block, finish


def head_rows(attn_low, matrix, second):
    heads = attn_low.shape[2]

    def index(p):
        head = 2 * p + second
        return (head // heads, matrix, lax.rem(head, heads), 0, 0)

    return pl.BlockSpec((None, None, None, HEAD_DIM, D), index)


def attention_forward(low_all, attn_low, gain_qk, bias, rows):
    cols = low_all.shape[0]
    span = bias.shape[1]
    side = lambda n: pl.BlockSpec((n, PAIR), lambda p: (0, p))
    whole = lambda *shape: pl.BlockSpec(shape, lambda p: (0,) * len(shape))
    return pl.pallas_call(
        attend_pair,
        grid=(PAIRS,),
        out_shape=(
            jax.ShapeDtypeStruct((rows, D), F32),
            jax.ShapeDtypeStruct((cols, D), F32),
            jax.ShapeDtypeStruct((cols, D), BF16),
            jax.ShapeDtypeStruct((rows, D), BF16),
            jax.ShapeDtypeStruct((PAIRS, 8, rows), F32),
        ),
        in_specs=[whole(cols, D)]
        + [head_rows(attn_low, j, second) for j in range(3) for second in range(2)]
        + [side(1), whole(rows, span)],
        out_specs=(side(rows), side(cols), side(cols), side(rows),
                   pl.BlockSpec((None, 8, rows), lambda p: (p, 0, 0))),
        scratch_shapes=[
            pltpu.VMEM((cols, PAIR), BF16),
            pltpu.VMEM((rows, PAIR), BF16),
            pltpu.VMEM((cols, 2 * PAIR), BF16),
        ],
        compiler_params=pltpu.CompilerParams(vmem_limit_bytes=56 * 2**20),
        cost_estimate=pl.CostEstimate(flops=20 * 10**9, bytes_accessed=30 * 10**6, transcendentals=13 * 10**6),
    )(low_all, *[attn_low] * 6, gain_qk, bias)


def attention_backward(q_pre, k_pre, value_all, o_low, grad_spre, attn_low, gain_qk, bias_turned, lse):
    rows, cols = q_pre.shape[0], k_pre.shape[0]
    side = lambda n: pl.BlockSpec((n, PAIR), lambda p: (0, p))
    whole = lambda *shape: pl.BlockSpec(shape, lambda p: (0,) * len(shape))
    stat = pl.BlockSpec((None, 8, rows), lambda p: (p, 0, 0))
    return pl.pallas_call(
        back_pair,
        grid=(PAIRS,),
        out_shape=(
            jax.ShapeDtypeStruct((rows, D), BF16),
            jax.ShapeDtypeStruct((cols, D), BF16),
            jax.ShapeDtypeStruct((cols, D), BF16),
            jax.ShapeDtypeStruct((PAIRS, 8, PAIR), F32),
        ),
        in_specs=[
            side(rows), side(cols), side(cols), side(rows), whole(rows, D),
            head_rows(attn_low, 3, 0), head_rows(attn_low, 3, 1),
            pl.BlockSpec((None, 1, PAIR), lambda p: (p, 0, 0)), whole(*bias_turned.shape), stat,
        ],
        out_specs=(side(rows), side(cols), side(cols), pl.BlockSpec((None, 8, PAIR), lambda p: (p, 0, 0))),
        scratch_shapes=[
            pltpu.VMEM((cols, PAIR), BF16),
            pltpu.VMEM((PAIR, cols), BF16),
            pltpu.VMEM((cols, PAIR), F32),
            pltpu.VMEM((cols, PAIR), F32),
        ],
        compiler_params=pltpu.CompilerParams(vmem_limit_bytes=56 * 2**20),
        cost_estimate=pl.CostEstimate(flops=30 * 10**9, bytes_accessed=40 * 10**6, transcendentals=13 * 10**6),
    )(q_pre, k_pre, value_all, o_low, grad_spre, attn_low, attn_low, gain_qk, bias_turned, lse)


START = 5


def gather_kernel(shards, attn_ref, ffn_ref, gains_ref, tokens_ref, bias_ref,
                  out, gains_out, h_out, qp_out, kp_out, v_out, o_out, lse_ref,
                  wide, low, mine, wide_sem, low_sem, mine_sem, line_send, line_recv, plane_send, beside_recv,
                  above_recv, across_recv, pair_send, pair_recv, gains_send, gains_recv, tokens_send,
                  tokens_recv, local_sem, gains_buf, before, h_buf, load_sem, store_sem,
                  weight_buf, gain_row, qp_buf, kp_buf, v_buf, o_buf, key_buf, query_buf, value_buf):
    core, chip, beside, above, across = place()
    line = lax.axis_index("shard")
    rep = 2 * chip + core
    sibling = 2 * chip + 1 - core
    to_beside, to_above = 2 * beside + core, 2 * above + core
    piece = attn_ref.shape[1]
    rows = tokens_ref.shape[0]
    heads = 2 * piece // HEAD_DIM
    others = shards - 1
    steps = 4 * others
    greet(shards)

    def rows_of(m, shard, rep, start=0, size=None):
        first = pl.multiple_of(rep * piece + start, 16)
        return out.at[m, shard, pl.ds(first, piece if size is None else size)]

    def source(n):
        low_side = 2 * line < shards
        edge = lax.select(low_side, line, shards - 1 - line)
        near = lax.select(lax.rem(n, 2) == 0, edge - 1 - n // 2, edge + 1 + n // 2)
        found = lax.select(n < 2 * edge, near, n + 1)
        return lax.select(low_side, found, shards - 1 - found)

    def own_send(m):
        @pl.when(line < shards - 1)
        def _():
            remote(mine.at[m], rows_of(m, line, rep), line_send, line_recv.at[m, line], rep, line + 1).start()

        @pl.when(line > 0)
        def _():
            remote(mine.at[m], rows_of(m, line, rep), line_send, line_recv.at[m, line], rep, line - 1).start()

    def fetch(index, slot):
        @pl.when(index < 8)
        def _():
            pltpu.make_async_copy(attn_ref.at[lax.rem(index, 8)], wide.at[slot], wide_sem.at[slot]).start()

        @pl.when(index >= 8)
        def _():
            pltpu.make_async_copy(
                ffn_ref.at[jnp.maximum(index // 8 - 1, 0), lax.rem(index, 8)], wide.at[slot], wide_sem.at[slot]
            ).start()

    def store(index, slot):
        return pltpu.make_async_copy(low.at[slot], rows_of(index // 8, line, lax.rem(index, 8)), low_sem.at[slot])

    def lower(src, dst):
        def step(i, _):
            part = pl.ds(pl.multiple_of(i * 32, 32), 32)
            dst[part, :] = src[part, :].astype(BF16)
            return 0

        lax.fori_loop(0, piece // 32, step, 0)

    for n in range(1, shards):
        other = lax.rem(line + n, shards)
        remote(gains_ref, gains_buf.at[line], gains_send, gains_recv.at[line], rep, other).start()
    pltpu.make_async_copy(gains_ref, gains_buf.at[line], local_sem).start()
    own = pl.ds(2 * rows, rows)
    pltpu.make_async_copy(tokens_ref, h_buf.at[own], load_sem.at[0, 0]).start()
    for m in range(4):
        origin = attn_ref.at[rep] if m == 0 else ffn_ref.at[m - 1, rep]
        pltpu.make_async_copy(origin, wide.at[m], mine_sem.at[m]).start()
    for m in range(4):
        arrived(wide.at[m], mine_sem.at[m])
        lower(wide.at[m], mine.at[m])
        if m == 0:
            own_send(0)

            @pl.when(line < shards - 1)
            def _():
                remote(tokens_ref, before.at[1], tokens_send, tokens_recv.at[1], rep, line + 1).start()

    for n in range(2):
        fetch(n, n)

    def norm_rows(source, first):
        def step(i, _):
            at = pl.multiple_of(first + i * 32, 32)
            value = source[pl.ds(pl.multiple_of(i * 32, 32), 32), :].astype(F32)
            h_buf[pl.ds(at, 32), :] = rownorm(value)[0].astype(BF16)
            return 0

        lax.fori_loop(0, rows // 32, step, 0)

    def clear_rows(first):
        h_buf[pl.ds(first, rows), :] = jnp.zeros((rows, D), BF16)

    arrived(h_buf.at[own], load_sem.at[0, 0])
    norm_rows(h_buf.at[own], 2 * rows)

    def loads(p, slot):
        copies = []
        for j in range(3):
            for second in range(2):
                head = 2 * p + second
                first = pl.multiple_of(2 * piece * j + HEAD_DIM * lax.rem(head, heads), HEAD_DIM)
                copies.append(
                    pltpu.make_async_copy(
                        out.at[0, head // heads, pl.ds(first, HEAD_DIM)], weight_buf.at[slot, 2 * j + second],
                        load_sem.at[slot, 2 * j + second],
                    )
                )
        return copies

    def stores(p, slot):
        lanes = pl.ds(pl.multiple_of(p * PAIR, PAIR), PAIR)
        return [
            pltpu.make_async_copy(buf.at[slot], ref.at[:, lanes], store_sem.at[slot, n])
            for n, (ref, buf) in enumerate(((qp_out, qp_buf), (kp_out, kp_buf), (v_out, v_buf), (o_out, o_buf)))
        ]

    def pair(p):
        slot = lax.rem(p, 2)

        @pl.when(p + 1 < PAIRS)
        def _():
            for copy in loads(p + 1, 1 - slot):
                copy.start()

        for copy in loads(p, slot):
            copy.wait()

        @pl.when(p >= 2)
        def _():
            for copy in stores(p - 2, slot):
                copy.wait()

        row = lax.broadcasted_iota(jnp.int32, (8, PAIR), 0)
        left, right = (
            jnp.sum(
                jnp.where(row == lax.rem(2 * p + n, heads), gains_buf[(2 * p + n) // heads, :8, :PAIR], 0.0),
                0, keepdims=True,
            )
            for n in range(2)
        )
        lane = lax.broadcasted_iota(jnp.int32, (1, PAIR), 1)
        gain_row[...] = jnp.where(lane < HEAD_DIM, left, right)
        attend_pair(
            h_buf, *(weight_buf.at[slot, n] for n in range(6)), gain_row, bias_ref, qp_buf.at[slot],
            kp_buf.at[slot], v_buf.at[slot], o_buf.at[slot], lse_ref.at[p], key_buf, query_buf, value_buf,
        )
        for copy in stores(p, slot):
            copy.start()

    def begin(c):
        m, origin = c // others, source(lax.rem(c, others))
        got = rows_of(m, origin, rep)
        arrived(got, line_recv.at[m, origin])

        @pl.when((origin < line) & (line < shards - 1))
        def _():
            remote(got, got, line_send, line_recv.at[m, origin], rep, line + 1).start()

        @pl.when((origin > line) & (line > 0))
        def _():
            remote(got, got, line_send, line_recv.at[m, origin], rep, line - 1).start()

        remote(got, got, plane_send, beside_recv.at[m, origin], to_beside, line).start()
        remote(got, got, plane_send, above_recv.at[m, origin], to_above, line).start()
        remote(got, got, pair_send, pair_recv.at[m], sibling, line).start()

    def middle(c):
        m, origin = c // others, source(lax.rem(c, others))
        got = rows_of(m, origin, to_beside)
        arrived(got, beside_recv.at[m, origin])
        part = rows_of(m, origin, to_beside, 0, HALF)
        remote(part, part, plane_send, across_recv.at[m, origin, 0], to_above, line).start()
        remote(got, got, pair_send, pair_recv.at[m], sibling, line).start()
        got = rows_of(m, origin, to_above)
        arrived(got, above_recv.at[m, origin])
        part = rows_of(m, origin, to_above, HALF, piece - HALF)
        remote(part, part, plane_send, across_recv.at[m, origin, 1], to_beside, line).start()
        remote(got, got, pair_send, pair_recv.at[m], sibling, line).start()

    def last(c):
        m, origin = c // others, source(lax.rem(c, others))
        got = rows_of(m, origin, 2 * across + core)
        arrived(rows_of(m, origin, 2 * across + core, 0, HALF), across_recv.at[m, origin, 0])
        arrived(rows_of(m, origin, 2 * across + core, HALF, piece - HALF), across_recv.at[m, origin, 1])
        remote(got, got, pair_send, pair_recv.at[m], sibling, line).start()

    def local(t):
        for n in range(2):
            index = 2 * t + n
            slot = 2 * lax.rem(t, 2) + n
            arrived(wide.at[slot], wide_sem.at[slot])

            @pl.when(index + 2 < 32)
            def _():
                fetch(index + 2, lax.rem(slot + 2, 4))

            @pl.when(t >= 2)
            def _():
                store(index - 4, slot).wait()

            lower(wide.at[slot], low.at[slot])
            store(index, slot).start()

    def turn(t, _):
        @pl.when((lax.rem(t, others) == 0) & (t // others < 3))
        def _():
            own_send(t // others + 1)

        @pl.when(t < steps)
        def _():
            begin(t)

        @pl.when((t == 1) & (line > 0))
        def _():
            arrived(before.at[1], tokens_recv.at[1])

            @pl.when(line < shards - 1)
            def _():
                remote(before.at[1], before.at[0], tokens_send, tokens_recv.at[0], rep, line + 1).start()

            norm_rows(before.at[1], rows)

        @pl.when((t == 1) & (line == 0))
        def _():
            clear_rows(rows)

        @pl.when((t == 3) & (line > 1))
        def _():
            arrived(before.at[0], tokens_recv.at[0])
            norm_rows(before.at[0], 0)

        @pl.when((t == 3) & (line <= 1))
        def _():
            clear_rows(0)

        @pl.when(t < 2)
        def _():
            local(2 * t)
            local(2 * t + 1)

        @pl.when(t >= 2)
        def _():
            local(t + 2)

        @pl.when(t == START)
        def _():
            pltpu.make_async_copy(gains_ref, gains_buf.at[line], local_sem).wait()
            for n in range(1, shards):
                other = lax.rem(line + n, shards)
                arrived(gains_buf.at[other], gains_recv.at[other])
            arrived(out.at[0, pl.ds(0, others), pl.ds(0, 4 * piece)], pair_recv.at[0])
            for copy in loads(0, 0):
                copy.start()

        early = (t > START + 3).astype(jnp.int32) + (t > START + 6).astype(jnp.int32)
        most = lax.select((t == START + 3) | (t == START + 6), 2, 1)

        def one(n, _):
            pair(t - START + early + n)
            return 0

        lax.fori_loop(0, lax.select((t >= START) & (t < START + PAIRS - 2), most, 0), one, 0)

        @pl.when((t >= 1) & (t < steps + 1))
        def _():
            middle(t - 1)

        @pl.when((t >= 2) & (t < steps + 2))
        def _():
            last(t - 2)

        return 0

    lax.fori_loop(0, 14, turn, 0)
    for n in range(4):
        store(28 + n, n).wait()
    gains_copy = pltpu.make_async_copy(gains_buf, gains_out, local_sem)
    h_copy = pltpu.make_async_copy(h_buf, h_out, load_sem.at[0, 0])
    gains_copy.start()
    h_copy.start()
    for p in (PAIRS - 2, PAIRS - 1):
        for copy in stores(p, p % 2):
            copy.wait()
    for m in range(1, 4):
        arrived(out.at[m, pl.ds(0, others), pl.ds(0, 4 * piece)], pair_recv.at[m])
    gains_copy.wait()
    h_copy.wait()

    @pl.when((line == 1) | (line == shards - 2))
    def _():
        arrived(before, tokens_send)

    @pl.when(line == 0)
    def _():
        arrived(before.at[0], tokens_send)

    @pl.when((line == 0) | (line == shards - 1))
    def _():
        arrived(out.at[:, 0, pl.ds(0, piece)], line_send)

    @pl.when((line > 0) & (line < shards - 1))
    def _():
        arrived(out.at[:, 0, pl.ds(0, 5 * piece)], line_send)

    arrived(out.at[:, pl.ds(0, others), pl.ds(0, 3 * piece)], plane_send)
    arrived(out.at[:, pl.ds(0, others), pl.ds(0, 4 * piece)], pair_send)
    arrived(gains_buf.at[pl.ds(0, others)], gains_send)


def gather_attend(attn_w, ffn_w, gains, tokens, bias, shards):
    piece = attn_w.shape[1]
    rows = tokens.shape[0]
    cols = rows + WINDOW
    any_space = pl.BlockSpec(memory_space=pl.ANY)
    vmem = pl.BlockSpec(memory_space=pltpu.VMEM)
    dma = pltpu.SemaphoreType.DMA
    return pl.pallas_call(
        functools.partial(gather_kernel, shards),
        out_shape=(
            jax.ShapeDtypeStruct((4, shards, 8 * piece, D), BF16),
            jax.ShapeDtypeStruct((shards,) + gains.shape, F32),
            jax.ShapeDtypeStruct((cols, D), BF16),
            jax.ShapeDtypeStruct((rows, D), F32),
            jax.ShapeDtypeStruct((cols, D), F32),
            jax.ShapeDtypeStruct((cols, D), BF16),
            jax.ShapeDtypeStruct((rows, D), BF16),
            jax.ShapeDtypeStruct((PAIRS, 8, rows), F32),
        ),
        in_specs=[any_space] * 4 + [vmem],
        out_specs=(any_space,) * 7 + (vmem,),
        scratch_shapes=[
            pltpu.VMEM((4, piece, D), F32),
            pltpu.VMEM((4, piece, D), BF16),
            pltpu.VMEM((4, piece, D), BF16),
            dma((4,)), dma((4,)), dma((4,)), dma(()), dma((4, shards)), dma(()), dma((4, shards)),
            dma((4, shards)), dma((4, shards, 2)), dma(()), dma((4,)), dma(()), dma((shards,)), dma(()),
            dma((2,)), dma(()),
            pltpu.VMEM((shards,) + gains.shape, F32),
            pltpu.VMEM((2, rows, D), BF16),
            pltpu.VMEM((cols, D), BF16),
            dma((2, 6)), dma((2, 4)),
            pltpu.VMEM((2, 6, HEAD_DIM, D), BF16),
            pltpu.VMEM((1, PAIR), F32),
            pltpu.VMEM((2, rows, PAIR), F32),
            pltpu.VMEM((2, cols, PAIR), F32),
            pltpu.VMEM((2, cols, PAIR), BF16),
            pltpu.VMEM((2, rows, PAIR), BF16),
            pltpu.VMEM((cols, PAIR), BF16),
            pltpu.VMEM((rows, PAIR), BF16),
            pltpu.VMEM((cols, 2 * PAIR), BF16),
        ],
        compiler_params=pltpu.CompilerParams(
            collective_id=3, has_side_effects=True, vmem_limit_bytes=60 * 2**20
        ),
        cost_estimate=pl.CostEstimate(flops=20 * 10**9, bytes_accessed=2 * 10**8, transcendentals=13 * 10**6),
    )(attn_w, ffn_w, gains, tokens, bias)


BACK_BLOCK = 256


def backward_kernel(shards, grads_ref, down_ref, qp_ref, kp_ref, v_ref, o_ref, weight_ref, gains_ref, da_ref, gain_ref,
                    bias_ref, lse_ref, h_ref, out, dq_ref, dk_ref, dv_ref, turned_ref, gains_out, sums_out, back_out,
                    own_out, sums, line_got, plane_got, line_sums, plane_sums, mine_gains, mine_sums, line_send, line_recv, plane_send,
                    plane_recv, back_send, back_recv, *scratch):
    rep, line = lax.axis_index("rep"), lax.axis_index("shard")
    grads = (grads_ref.at[0], grads_ref.at[1], down_ref, turned_ref)
    turns, lead, follow, finish, pair_send = reduction(grads, out, scratch)
    height = weight_ref.shape[2] // 4
    heads = height // HEAD_DIM
    rows, cols = da_ref.shape[0], h_ref.shape[0]
    reach = back_out.shape[0]
    per = rows // BACK_BLOCK
    attended = PAIRS + 1
    dma = pltpu.SemaphoreType.DMA
    greet(shards)

    def attention(qp_buf, kp_buf, v_buf, o_buf, wo_buf, dq_buf, dk_buf, dv_buf, turned_buf, load_sem, store_sem,
                  key_buf, key_turned, k_total, v_total):
        def loads(p, slot):
            lanes = pl.ds(pl.multiple_of(p * PAIR, PAIR), PAIR)
            copies = [
                pltpu.make_async_copy(ref.at[:, lanes], buf.at[slot], load_sem.at[slot, n])
                for n, (ref, buf) in enumerate(((qp_ref, qp_buf), (kp_ref, kp_buf), (v_ref, v_buf), (o_ref, o_buf)))
            ]
            for second in range(2):
                head = 2 * p + second
                first = pl.multiple_of(3 * height + HEAD_DIM * lax.rem(head, heads), HEAD_DIM)
                copies.append(
                    pltpu.make_async_copy(
                        weight_ref.at[0, head // heads, pl.ds(first, HEAD_DIM)], wo_buf.at[slot, second],
                        load_sem.at[slot, 4 + second],
                    )
                )
            return copies

        def lane_stores(p, slot):
            lanes = pl.ds(pl.multiple_of(p * PAIR, PAIR), PAIR)
            return [
                pltpu.make_async_copy(buf.at[slot], ref.at[:, lanes], store_sem.at[slot, n])
                for n, (ref, buf) in enumerate(((dq_ref, dq_buf), (dk_ref, dk_buf), (dv_ref, dv_buf)))
            ]

        def start_stores(p, slot):
            for copy in lane_stores(p, slot):
                copy.start()
            for second in range(2):
                head = 2 * p + second
                for n in range(HEAD_DIM // 32):
                    row = HEAD_DIM * lax.rem(head, heads) + 32 * n
                    place_of = pl.ds(pl.multiple_of(lax.rem(row, height // 2), 32), 32)
                    for j in range(4):
                        pltpu.make_async_copy(
                            turned_buf.at[slot, j, pl.ds(second * HEAD_DIM + 32 * n, 32)],
                            turned_ref.at[head // heads, j, row // (height // 2), place_of], store_sem.at[slot, 3],
                        ).start()

        def wait_stores(p, slot):
            for copy in lane_stores(p, slot):
                copy.wait()
            arrived(turned_buf.at[slot], store_sem.at[slot, 3])

        def pair(p):
            slot = lax.rem(p, 2)

            @pl.when(p + 1 < PAIRS)
            def _():
                for copy in loads(p + 1, 1 - slot):
                    copy.start()

            for copy in loads(p, slot):
                copy.wait()

            @pl.when(p >= 2)
            def _():
                wait_stores(p - 2, slot)

            back_pair(
                qp_buf.at[slot], kp_buf.at[slot], v_buf.at[slot], o_buf.at[slot], da_ref, wo_buf.at[slot, 0],
                wo_buf.at[slot, 1], gain_ref.at[p], bias_ref, lse_ref.at[p], dq_buf.at[slot], dk_buf.at[slot],
                dv_buf.at[slot], sums.at[p], key_buf, key_turned, k_total, v_total,
            )
            turned_buf[slot, 0] = dot_tn(dq_buf[slot], h_ref[pl.ds(cols - rows, rows), :]).astype(BF16)
            turned_buf[slot, 1] = dot_tn(dk_buf[slot], h_ref[...]).astype(BF16)
            turned_buf[slot, 2] = dot_tn(dv_buf[slot], h_ref[...]).astype(BF16)
            turned_buf[slot, 3] = dot_tn(o_buf[slot], da_ref[...]).astype(BF16)
            start_stores(p, slot)

        for copy in loads(0, 0):
            copy.start()

        def step(t, _):
            lead(t)

            @pl.when(t < PAIRS)
            def _():
                pair(t)

            follow(t)
            return 0

        lax.fori_loop(0, attended, step, 0)
        for p in (PAIRS - 2, PAIRS - 1):
            wait_stores(p, p % 2)

    pl.run_scoped(
        attention,
        pltpu.VMEM((2, rows, PAIR), F32),
        pltpu.VMEM((2, cols, PAIR), F32),
        pltpu.VMEM((2, cols, PAIR), BF16),
        pltpu.VMEM((2, rows, PAIR), BF16),
        pltpu.VMEM((2, 2, HEAD_DIM, D), BF16),
        pltpu.VMEM((2, rows, PAIR), BF16),
        pltpu.VMEM((2, cols, PAIR), BF16),
        pltpu.VMEM((2, cols, PAIR), BF16),
        pltpu.VMEM((2, 4, PAIR, D), BF16),
        dma((2, 6)), dma((2, 4)),
        pltpu.VMEM((cols, PAIR), BF16),
        pltpu.VMEM((PAIR, cols), BF16),
        pltpu.VMEM((cols, PAIR), F32),
        pltpu.VMEM((cols, PAIR), F32),
    )

    def inputs(weight_buf, left_buf, parts, weight_sem, left_sem):
        for j in range(3):
            for shard in range(shards):
                pltpu.make_async_copy(
                    weight_ref.at[0, shard, pl.ds(j * height, height)],
                    weight_buf.at[j, pl.ds(shard * height, height)], weight_sem,
                ).start()
        for n in range(1, shards):
            other = lax.rem(line + n, shards)
            remote(gains_ref.at[other], line_got.at[n - 1], line_send.at[0], line_recv.at[0, n - 1], rep, other).start()
            remote(sums, line_sums.at[n - 1], line_send.at[1], line_recv.at[1, n - 1], rep, other).start()

        def lefts(block):
            slot = lax.rem(block, 2)
            part = pl.ds(pl.multiple_of(block * BACK_BLOCK, BACK_BLOCK), BACK_BLOCK)
            return [
                pltpu.make_async_copy(ref.at[part], left_buf.at[slot, n], left_sem.at[slot, n])
                for n, ref in ((1, dk_ref), (2, dv_ref))
            ]

        def own_left(block):
            slot = lax.rem(block, 2)
            part = pl.ds(pl.multiple_of((block - reach * per) * BACK_BLOCK, BACK_BLOCK), BACK_BLOCK)
            return pltpu.make_async_copy(dq_ref.at[part], left_buf.at[slot, 0], left_sem.at[slot, 0])

        def fetch(block):
            for copy in lefts(block):
                copy.start()

            @pl.when(block >= reach * per)
            def _():
                own_left(block).start()

        def product(block):
            slot = lax.rem(block, 2)

            @pl.when(block + 1 < cols // BACK_BLOCK)
            def _():
                fetch(block + 1)

            for copy in lefts(block):
                copy.wait()
            total = dot(left_buf[slot, 1], weight_buf[1]) + dot(left_buf[slot, 2], weight_buf[2])

            @pl.when(block < reach * per)
            def _():
                parts[block] = total.astype(BF16)
                n = block // per
                part = pl.ds(pl.multiple_of(lax.rem(block, per) * BACK_BLOCK, BACK_BLOCK), BACK_BLOCK)

                @pl.when(line >= reach - n)
                def _():
                    remote(parts.at[block], back_out.at[n, part], back_send.at[n], back_recv.at[n], rep,
                           line - (reach - n)).start()

            @pl.when(block >= reach * per)
            def _():
                own_left(block).wait()
                part = pl.ds(pl.multiple_of((block - reach * per) * BACK_BLOCK, BACK_BLOCK), BACK_BLOCK)
                own_out[part, :] = total + dot(left_buf[slot, 0], weight_buf[0])

        fetch(0)

        def step(t, _):
            lead(t)

            @pl.when(t == attended + 1)
            def _():
                arrived(weight_buf, weight_sem)
                for pair_of, (whole, got, got_plane, mine) in enumerate(
                    ((gains_ref.at[line], line_got, plane_got, mine_gains), (sums, line_sums, plane_sums, mine_sums))
                ):
                    total = whole[...]
                    for n in range(shards - 1):
                        arrived(got.at[n], line_recv.at[pair_of, n])
                        total = total + got[n]
                    mine[...] = total
                    for n in range(1, 8):
                        remote(mine, got_plane.at[n - 1], plane_send.at[pair_of], plane_recv.at[pair_of, n - 1],
                               lax.rem(rep + n, 8), line).start()

            @pl.when(t == attended + 3)
            def _():
                for pair_of, (got_plane, mine, result) in enumerate(
                    ((plane_got, mine_gains, gains_out), (plane_sums, mine_sums, sums_out))
                ):
                    total = mine[...]
                    for n in range(7):
                        arrived(got_plane.at[n], plane_recv.at[pair_of, n])
                        total = total + got_plane[n]
                    result[...] = total

            @pl.when((t > attended + 1) & (t < attended + 2 + cols // BACK_BLOCK))
            def _():
                product(t - attended - 2)

            follow(t)
            return 0

        lax.fori_loop(attended, turns, step, 0)
        for n in range(reach):
            @pl.when(line >= reach - n)
            def _(n=n):
                arrived(parts.at[pl.ds(0, per)], back_send.at[n])

            @pl.when(line + reach - n < shards)
            def _(n=n):
                arrived(back_out.at[n], back_recv.at[n])

    pl.run_scoped(
        inputs,
        pltpu.VMEM((3, D, D), BF16),
        pltpu.VMEM((2, 3, BACK_BLOCK, D), BF16),
        pltpu.VMEM((reach * per, BACK_BLOCK, D), BF16),
        dma(()), dma((2, 3)),
    )
    finish()
    arrived(grads_ref, pair_send)
    arrived(line_got, line_send.at[0])
    arrived(line_sums, line_send.at[1])
    arrived(plane_got, plane_send.at[0])
    arrived(plane_sums, plane_send.at[1])


def backward_reduce(grads, down, q_pre, k_pre, value_all, o_low, gathered, gains, grad_spre, gain_qk, bias_turned, lse,
                    low_all):
    _, shards, _, _, rows, _ = grads.shape
    tokens, cols = q_pre.shape[0], k_pre.shape[0]
    reach = (cols - tokens) // tokens
    lines = gains.shape[1:]
    any_space = pl.BlockSpec(memory_space=pl.ANY)
    vmem = pl.BlockSpec(memory_space=pltpu.VMEM)
    dma = pltpu.SemaphoreType.DMA
    return pl.pallas_call(
        functools.partial(backward_kernel, shards),
        out_shape=(
            jax.ShapeDtypeStruct((4, 8, rows, D), BF16),
            jax.ShapeDtypeStruct((tokens, D), BF16),
            jax.ShapeDtypeStruct((cols, D), BF16),
            jax.ShapeDtypeStruct((cols, D), BF16),
            jax.ShapeDtypeStruct(grads.shape[1:], BF16),
            jax.ShapeDtypeStruct(lines, F32),
            jax.ShapeDtypeStruct((PAIRS, 8, PAIR), F32),
            jax.ShapeDtypeStruct((reach, tokens, D), BF16),
            jax.ShapeDtypeStruct((tokens, D), F32),
        ),
        in_specs=[any_space] * 7 + [vmem] * 6,
        out_specs=(any_space,) * 5 + (vmem, vmem, any_space, vmem),
        scratch_shapes=[
            pltpu.VMEM((PAIRS, 8, PAIR), F32),
            pltpu.VMEM((shards - 1,) + lines, F32),
            pltpu.VMEM((7,) + lines, F32),
            pltpu.VMEM((shards - 1, PAIRS, 8, PAIR), F32),
            pltpu.VMEM((7, PAIRS, 8, PAIR), F32),
            pltpu.VMEM(lines, F32),
            pltpu.VMEM((PAIRS, 8, PAIR), F32),
            dma((2,)), dma((2, shards - 1)), dma((2,)), dma((2, 7)), dma((reach,)), dma((reach,)),
        ] + reduction_scratch(4, shards, rows),
        compiler_params=pltpu.CompilerParams(
            collective_id=1, has_side_effects=True, vmem_limit_bytes=63 * 2**20
        ),
        cost_estimate=pl.CostEstimate(flops=55 * 10**9, bytes_accessed=4 * 10**8, transcendentals=13 * 10**6),
    )(grads, down, q_pre, k_pre, value_all, o_low, gathered, gains, grad_spre, gain_qk, bias_turned, lse, low_all)


def body(
    tokens,
    doc_lengths,
    cotangent,
    attn_w,
    ffn_w,
    attn_m,
    attn_v,
    ffn_m,
    ffn_v,
    gains_d,
    gains_ff,
    gd_m,
    gd_v,
    gf_m,
    gf_v,
):
    shards = lax.axis_size("shard")
    reps = lax.axis_size("rep")
    device_index = lax.axis_index("shard")
    rows = tokens.shape[0]
    reach = WINDOW // rows
    cols = (reach + 1) * rows
    attn_rows = attn_w.shape[1]
    ffn_rows = ffn_w.shape[1]
    ffn_all = shards * ffn_rows
    piece = ffn_rows // reps

    lengths_row = doc_lengths[0]
    starts = jnp.cumsum(lengths_row) - lengths_row
    positions = device_index * rows + jnp.arange(rows, dtype=jnp.int32)
    doc_start = jnp.max(
        jnp.where(starts[None, :] <= positions[:, None], starts[None, :], 0), axis=1
    )
    blocks = rows // QUERY_BLOCK
    span = WINDOW + QUERY_BLOCK
    query = jnp.arange(rows, dtype=jnp.int32).reshape(blocks, QUERY_BLOCK)
    lead = query[:, :1] - reach * rows + jnp.arange(span, dtype=jnp.int32)
    ahead = query[:, :, None] - lead[:, None, :]
    floor = (doc_start - device_index * rows).reshape(blocks, QUERY_BLOCK, 1)
    mask = (ahead >= 0) & (ahead < WINDOW) & (lead[:, None, :] >= floor)
    bias = jnp.where(mask, 0.0, NEGATIVE).astype(F32)
    bias_turned = bias.transpose(0, 2, 1)
    bias = bias.reshape(rows, span)
    cut = gains_d.size
    small = jnp.concatenate([gains_d.reshape(-1), gains_ff.reshape(-1)]).astype(BF16)
    normed_in, factor_in = rownorm(tokens.astype(F32))
    fast = reps == 8 and shards == 4 and attn_rows % HEAD_DIM == 0 and reach == 2
    if fast:
        small = small.astype(F32)
        qk_heads = small[:attn_rows].reshape(-1, HEAD_DIM)
        qk_heads = jnp.pad(
            jnp.concatenate([qk_heads, qk_heads], 1), ((0, 8 - qk_heads.shape[0]), (0, D - PAIR))
        )
        small = jnp.pad(small, (0, 8 * D - small.size)).reshape(8, D)
        gathered, small, low_all, q_pre, k_pre, value_all, o_low, lse = gather_attend(
            attn_w.reshape(8, piece, D),
            ffn_w.reshape(3, 8, piece, D),
            jnp.concatenate([qk_heads, small]),
            tokens,
            bias,
            shards,
        )
        small = small[:, 8:].reshape(shards, -1)[:, : cut + gains_ff.size]
        out_low = gathered[0, :, 3 * attn_rows :].reshape(D, D)
        ffn_low = [gathered.reshape(4, ffn_all, D)] * 3
        firsts = (1, 2, 3)
    else:
        attn_low = (
            gather_rows(attn_w.reshape(4 * attn_rows, D).astype(BF16))
            .reshape(shards, 4, attn_rows, D)
            .transpose(1, 0, 2, 3)
            .reshape(1, 4, HEADS, HEAD_DIM, D)
        )
        ffn_low = [gather_rows(ffn_w[m].astype(BF16)).reshape(1, ffn_all, D) for m in range(3)]
        firsts = (0, 0, 0)
        small = lax.all_gather(small, "shard", axis=0).astype(F32)
        query_low, key_low, value_low, out_low = (attn_low[0, j].reshape(D, D) for j in range(4))
    gd_all = small[:, :cut].reshape(shards, 3, -1).transpose(1, 0, 2).reshape(3, D)
    gf_all = small[:, cut:].reshape(shards, 2, ffn_rows).transpose(1, 0, 2).reshape(2, ffn_all)
    gain_qk = gd_all[0]
    alpha_attn = gd_all[1]
    alpha_ffn = gd_all[2]

    if not fast:
        earlier = [from_behind(tokens, "shard", offset) for offset in range(reach, 0, -1)]
        low_all = rownorm(jnp.concatenate(earlier + [tokens], 0).astype(F32))[0].astype(BF16)
        q_pre, k_pre, value_all, o_low, lse = attention_forward(
            low_all, attn_low, gain_qk[None], bias, rows
        )
    in_low = low_all[-rows:]
    side, side_factor = rownorm(dot(o_low, out_low))
    middle, mid_factor = rownorm(normed_in + alpha_attn * (side - normed_in))
    mid_low = middle.astype(BF16)
    output, grad_mid, ffn_grads, down_grads, grad_scale_up, grad_scale_gate, grad_alpha_ffn = feed_forward(
        mid_low, middle, cotangent, alpha_ffn[None], gf_all, ffn_low, firsts
    )
    grad_mixed = norm_back(middle, mid_factor, grad_mid)
    grad_in = grad_mixed * (1.0 - alpha_attn)
    grad_alpha_attn = jnp.sum(grad_mixed * (side - normed_in), 0)
    grad_spre = norm_back(side, side_factor, grad_mixed * alpha_attn).astype(BF16)
    pair_gain = gain_qk.reshape(PAIRS, 1, PAIR)
    grad_gf = jnp.concatenate([grad_scale_up, grad_scale_gate])
    gd_rows = D // shards
    if fast:
        units = (shards, 4, 2, piece, D)
        grad_gd = jnp.stack([grad_alpha_attn, grad_alpha_ffn[0]])
        small = jnp.concatenate(
            [
                grad_gd.reshape(2, shards, gd_rows).transpose(1, 0, 2).reshape(shards, -1),
                grad_gf.reshape(2, shards, ffn_rows).transpose(1, 0, 2).reshape(shards, -1),
            ],
            1,
        )
        small = jnp.pad(small, ((0, 0), (0, 8 * D - small.shape[1]))).reshape(shards, 8, D)
        summed, _, _, _, _, sum_small, sum_qk, back_got, back_own = backward_reduce(
            ffn_grads.reshape((2,) + units), down_grads.reshape(units), q_pre, k_pre, value_all, o_low, gathered,
            small, grad_spre, pair_gain, bias_turned, lse, low_all,
        )
        grad_in = grad_in + back_own
        for n in range(reach):
            sent = device_index + reach - n < shards
            grad_in = grad_in + jnp.where(sent, back_got[n], 0).astype(F32)
        sum_small = sum_small.reshape(-1)
        sum_qk = lax.dynamic_slice_in_dim(sum_qk[:, 0].reshape(D), device_index * gd_rows, gd_rows, 0)
        sum_gd = jnp.concatenate([sum_qk, sum_small[: 2 * gd_rows]]).reshape(3, gd_rows)
        sum_gf = sum_small[2 * gd_rows : 2 * gd_rows + 2 * ffn_rows].reshape(2, ffn_rows)
        attn_sums, ffn_sums = [(summed, 3)], [(summed, 0), (summed, 1), (summed, 2)]
    else:
        grad_qpre, grad_kpre, grad_vpre, gain_sums = attention_backward(
            q_pre, k_pre, value_all, o_low, grad_spre, attn_low, pair_gain, bias_turned, lse
        )
        grad_gain_qk = gain_sums[:, 0].reshape(D)
        back_all = dot(grad_kpre, key_low) + dot(grad_vpre, value_low)
        grad_in = grad_in + dot(grad_qpre, query_low) + back_all[reach * rows :]
        back_parts = back_all[: reach * rows].reshape(reach, rows, D).astype(BF16)
        for n in range(reach):
            grad_in = grad_in + from_behind(back_parts[n], "shard", n - reach).astype(F32)
        attn_grad = jnp.stack(
            [
                dot_tn(grad_qpre, in_low),
                dot_tn(grad_kpre, low_all),
                dot_tn(grad_vpre, low_all),
                dot_tn(o_low, grad_spre),
            ]
        ).astype(BF16)
        attn_grad = attn_grad.reshape(4, shards, attn_rows, D).transpose(1, 0, 2, 3)
        attn_grad = attn_grad.reshape(shards, reps, 4 * attn_rows // reps, D).transpose(1, 0, 2, 3)
        attn_sums = [(reduce_rows(attn_grad).reshape(1, 4, attn_rows, D), 0)]
        ready = (shards, reps, piece, D)
        ffn_sums = [
            (reduce_rows(part.reshape(ready).transpose(1, 0, 2, 3)).reshape(1, 1, ffn_rows, D), 0)
            for part in (ffn_grads[0], ffn_grads[1], down_grads)
        ]
        grad_small = jnp.concatenate(
            [grad_gain_qk, grad_alpha_attn, grad_alpha_ffn[0], grad_gf.reshape(-1)]
        )
        grad_small = lax.psum(grad_small, ("rep", "shard"))
        sum_gd = lax.dynamic_slice_in_dim(
            grad_small[: 3 * D].reshape(3, D), device_index * gd_rows, gd_rows, 1
        )
        sum_gf = lax.dynamic_slice_in_dim(
            grad_small[3 * D :].reshape(2, ffn_all), device_index * ffn_rows, ffn_rows, 1
        )
    grad_tokens = norm_back(normed_in, factor_in, grad_in)

    attn_unit, attn_m_new, attn_v_new = adam_rows(attn_w, attn_sums, attn_m, attn_v)
    ffn_unit, ffn_m_new, ffn_v_new = adam_rows(ffn_w, ffn_sums, ffn_m, ffn_v)
    gd_new, gd_m_new, gd_v_new = adam(gains_d, sum_gd, gd_m, gd_v, GAIN_RATE, 0.0)
    gf_new, gf_m_new, gf_v_new = adam(gains_ff, sum_gf, gf_m, gf_v, GAIN_RATE, 0.0)
    return (
        output,
        grad_tokens,
        attn_unit,
        attn_m_new,
        attn_v_new,
        ffn_unit,
        ffn_m_new,
        ffn_v_new,
        gd_new,
        gd_m_new,
        gd_v_new,
        gf_new,
        gf_m_new,
        gf_v_new,
    )

def solution(mesh):
    return jax.shard_map(
        body,
        mesh=mesh,
        in_specs=(
            P(("rep", "shard"), None),
            P("rep", None),
            P(("rep", "shard"), None),
            P(None, "shard", None),
            P(None, "shard", None),
            P(None, "shard", None),
            P(None, "shard", None),
            P(None, "shard", None),
            P(None, "shard", None),
            P(None, "shard"),
            P(None, "shard"),
            P(None, "shard"),
            P(None, "shard"),
            P(None, "shard"),
            P(None, "shard"),
        ),
        out_specs=(
            P(("rep", "shard"), None),
            P(("rep", "shard"), None),
            P(None, "shard", None),
            P(None, "shard", None),
            P(None, "shard", None),
            P(None, "shard", None),
            P(None, "shard", None),
            P(None, "shard", None),
            P(None, "shard"),
            P(None, "shard"),
            P(None, "shard"),
            P(None, "shard"),
            P(None, "shard"),
            P(None, "shard"),
        ),
        check_vma=False,
    )
```

```python
import functools
import math

import jax
import jax.numpy as jnp
from jax import lax
from jax.experimental import pallas as pl
from jax.experimental.pallas import tpu as pltpu
from jax.sharding import PartitionSpec as P

D = 1280
HEADS = 20
HEAD_DIM = 64
WINDOW = 1024
STEP = 10


SMALL = 1e-06
NEGATIVE = -1e30
BETA_ONE = 0.9
BETA_TWO = 0.95
RATE = 0.02
GAIN_RATE = 1.0
DECAY = 0.1
TINY = 1e-08
F32 = jnp.float32
BF16 = jnp.bfloat16


def from_behind(block, axis, distance):
    devices = range(lax.axis_size(axis))
    route = [(i - distance, i) for i in devices if i - distance in devices]
    return lax.ppermute(block, axis, route)


def rownorm(value):
    factor = lax.rsqrt(jnp.sum(value * value, -1, keepdims=True) + SMALL)
    return (value * factor, factor)


def norm_back(normed, factor, grad):
    return factor * (grad - normed * jnp.sum(normed * grad, -1, keepdims=True))


def adam(weight, grad, first, second, rate, decay):
    first = BETA_ONE * first + (1.0 - BETA_ONE) * grad
    second = BETA_TWO * second + (1.0 - BETA_TWO) * grad * grad
    fix_one = 1.0 - BETA_ONE**STEP
    fix_two = 1.0 - BETA_TWO**STEP
    change = first / fix_one / (jnp.sqrt(second / fix_two) + TINY) + decay * weight
    return (weight - rate * change, first, second)


def dot(a, b):
    return jnp.dot(a, b, preferred_element_type=F32)


def dot_nt(a, b):
    return lax.dot_general(a, b, (((1,), (1,)), ((), ())), preferred_element_type=F32)


def dot_tn(a, b):
    return lax.dot_general(a, b, (((0,), (0,)), ((), ())), preferred_element_type=F32)


def gather_rows(shard_rows):
    reps = lax.axis_size("rep")
    piece = shard_rows.shape[0] // reps
    mine = lax.dynamic_slice_in_dim(shard_rows, lax.axis_index("rep") * piece, piece, 0)
    column = lax.all_gather(mine, "shard", axis=0)
    return lax.all_gather(column, "rep", axis=1)


def reduce_rows(grad):
    part = lax.psum_scatter(grad, "rep", scatter_dimension=0)
    part = lax.psum_scatter(part, "shard", scatter_dimension=0)
    return lax.all_gather(part, "rep", axis=0, tiled=True)


MESH = pl.DeviceIdType.MESH
HALF = 80
RING = 8
HALF_RING = 4


def place():
    rep = lax.axis_index("rep")
    core, chip = lax.rem(rep, 2), rep // 2
    beside, above = chip + 1 - 2 * lax.rem(chip, 2), chip + 2 - 4 * (chip // 2)
    return core, chip, beside, above, 3 - chip


def remote(src, dst, send, recv, rep, shard):
    return pltpu.make_async_remote_copy(
        src_ref=src, dst_ref=dst, send_sem=send, recv_sem=recv,
        device_id=(rep, shard), device_id_type=MESH,
    )


def arrived(ref, sem):
    pltpu.make_async_copy(ref, ref, sem).wait()


def greet(shards):
    rep, line = lax.axis_index("rep"), lax.axis_index("shard")
    barrier = pltpu.get_barrier_semaphore()
    for n in range(1, 8):
        pl.semaphore_signal(barrier, inc=1, device_id=(lax.rem(rep + n, 8), line), device_id_type=MESH)
    for n in range(1, shards):
        pl.semaphore_signal(barrier, inc=1, device_id=(rep, lax.rem(line + n, shards)), device_id_type=MESH)
    pl.semaphore_wait(barrier, 6 + shards)


def add_into(target, sources, rows):
    def step(i, _):
        part = pl.ds(pl.multiple_of(i * 16, 16), 16)
        if len(sources) == 1:
            target[part, :] = target[part, :] + sources[0][part, :]
        else:
            value = target[part, :].astype(F32)
            for source in sources:
                value = value + source[part, :].astype(F32)
            target[part, :] = value.astype(BF16)
        return 0

    lax.fori_loop(0, rows // 16, step, 0, unroll=min(5, rows // 16))


def reduction_scratch(count, shards, rows):
    steps = count * shards
    dma = pltpu.SemaphoreType.DMA
    return [
        pltpu.VMEM((RING, 4, rows, D), BF16),
        pltpu.VMEM((2, 4, rows, D), BF16),
        pltpu.VMEM((HALF_RING, rows, D), BF16),
        pltpu.VMEM((HALF_RING, 2, rows, D), BF16),
        pltpu.VMEM((count, shards + 1, rows, D), BF16),
        dma((2,)), dma(()), dma((steps,)), dma((steps,)), dma((steps, 2)),
        dma((steps,)), dma((steps, 2)), dma((steps,)), dma((count, shards + 1)),
        dma((count,)), dma((count, 8)), dma((count,)), dma(()), pltpu.SemaphoreType.REGULAR,
    ]


def reduction(grads, out, scratch):
    (acc, own, half, piece, below, own_sem, pair_send, pair_recv, half_send, half_recv,
     piece_send, piece_recv, line_send, line_recv, out_send, out_recv, out_local, on_send, credit) = scratch
    count = len(grads)
    rows = own.shape[2]
    shards = below.shape[1] - 1
    core, chip, beside, above, across = place()
    line = lax.axis_index("shard")
    steps = count * shards
    mine, sibling = 2 * chip + core, 2 * chip + 1 - core
    one = piece.at[0, 0]

    def owner(step):
        i = lax.rem(step, shards)
        back = lax.select(i < shards - 1 - line, shards - 1 - i, i - (shards - 1 - line))
        ahead = lax.select(i < line, i, shards - 1 - (i - line))
        other = lax.select(2 * line < shards, back, ahead)
        return lax.select(i == shards - 1, line, other)

    def room(step):
        return acc.at[lax.rem(step, RING)]

    def begin(step):
        slot = lax.rem(step, 2)

        @pl.when(step >= RING)
        def _():
            pl.semaphore_wait(credit, 1)

        for n, grad in enumerate(grads):
            @pl.when(step // shards == n)
            def _(grad=grad):
                remote(grad.at[owner(step), :, 1 - core], room(step), pair_send, pair_recv.at[step], sibling, line).start()
                pltpu.make_async_copy(grad.at[owner(step), :, core], own.at[slot], own_sem.at[slot]).start()

    def first(step):
        slot, part = lax.rem(step, 2), lax.rem(step, HALF_RING)
        total = room(step)
        arrived(own.at[slot], own_sem.at[slot])
        arrived(total, pair_recv.at[step])
        for q in range(4):
            add_into(total.at[q], (own.at[slot, q],), rows)
        remote(total.at[across, pl.ds(0, HALF)], half.at[part, pl.ds(0, HALF)],
               half_send.at[step], half_recv.at[step, 0], 2 * beside + core, line).start()
        remote(total.at[across, pl.ds(HALF, rows - HALF)], half.at[part, pl.ds(HALF, rows - HALF)],
               half_send.at[step], half_recv.at[step, 1], 2 * above + core, line).start()

    def second(step):
        part = lax.rem(step, HALF_RING)
        total = room(step)
        low, high = half.at[part, pl.ds(0, HALF)], half.at[part, pl.ds(HALF, rows - HALF)]
        arrived(low, half_recv.at[step, 0])
        arrived(high, half_recv.at[step, 1])
        add_into(total.at[above, pl.ds(0, HALF)], (low,), HALF)
        add_into(total.at[beside, pl.ds(HALF, rows - HALF)], (high,), rows - HALF)
        remote(total.at[beside], piece.at[part, 0], piece_send.at[step], piece_recv.at[step, 0],
               2 * beside + core, line).start()
        remote(total.at[above], piece.at[part, 1], piece_send.at[step], piece_recv.at[step, 1],
               2 * above + core, line).start()

    def pass_on(step):
        m, target = step // shards, owner(step)

        @pl.when(target > line)
        def _():
            remote(room(step).at[chip], below.at[m, target], line_send.at[step], line_recv.at[m, target],
                   mine, line + 1).start()

        @pl.when(target < line)
        def _():
            slot = lax.select(target == line - 1, shards, target)
            remote(room(step).at[chip], below.at[m, slot], line_send.at[step], line_recv.at[m, slot],
                   mine, line - 1).start()

    def outermost(step):
        target = owner(step)
        return ((target > line) & (line == 0)) | ((target < line) & (line == shards - 1))

    def third(step):
        part = lax.rem(step, HALF_RING)
        for n in range(2):
            arrived(piece.at[part, n], piece_recv.at[step, n])
        add_into(room(step).at[chip], (piece.at[part, 0], piece.at[part, 1]), rows)

        @pl.when(outermost(step))
        def _():
            pass_on(step)

    def along(step):
        m, target = step // shards, owner(step)

        def add_line(slot):
            arrived(below.at[m, slot], line_recv.at[m, slot])
            add_into(room(step).at[chip], (below.at[m, slot],), rows)

        @pl.when(((target >= line) & (line > 0)) | ((target < line) & (line < shards - 1)))
        def _():
            add_line(target)

        @pl.when((target == line) & (line < shards - 1))
        def _():
            add_line(shards)

        @pl.when(jnp.logical_not(outermost(step)))
        def _():
            pass_on(step)

        @pl.when(target == line)
        def _():
            total = room(step).at[chip]
            pltpu.make_async_copy(total, out.at[m, mine], out_local.at[m]).start()
            for n, other in enumerate((2 * beside + core, 2 * above + core, sibling)):
                remote(total, out.at[m, mine], out_send.at[m], out_recv.at[m, n], other, line).start()

    def fourth(step):
        m = step // shards
        for n, (origin, other, part) in enumerate(
            (
                (2 * beside + core, 2 * above + core, pl.ds(0, HALF)),
                (2 * above + core, 2 * beside + core, pl.ds(HALF, rows - HALF)),
            )
        ):
            arrived(out.at[m, origin], out_recv.at[m, n])
            share = out.at[m, origin, part]
            remote(share, share, on_send, out_recv.at[m, 3 + n], other, line).start()
            remote(out.at[m, origin], out.at[m, origin], on_send, out_recv.at[m, 5 + n], sibling, line).start()

    def fifth(step):
        m, origin = step // shards, 2 * across + core
        arrived(out.at[m, origin, pl.ds(0, HALF)], out_recv.at[m, 3])
        arrived(out.at[m, origin, pl.ds(HALF, rows - HALF)], out_recv.at[m, 4])
        remote(out.at[m, origin], out.at[m, origin], on_send, out_recv.at[m, 7], sibling, line).start()

    def retire(step):
        m, target = step // shards, owner(step)
        arrived(one, half_send.at[step])
        arrived(piece.at[0], piece_send.at[step])

        @pl.when(target != line)
        def _():
            arrived(one, line_send.at[step])

        @pl.when(target == line)
        def _():
            arrived(acc.at[0, pl.ds(0, 3)], out_send.at[m])
            arrived(one, out_local.at[m])

        @pl.when(step + RING < steps)
        def _():
            pl.semaphore_signal(credit, inc=1, device_id=(sibling, line), device_id_type=MESH)

    def lead(t):
        @pl.when((t >= 6) & (t < steps + 6))
        def _():
            retire(t - 6)

        @pl.when(t == 0)
        def _():
            begin(0)

        @pl.when(t + 1 < steps)
        def _():
            begin(t + 1)

        @pl.when(t < steps)
        def _():
            first(t)

    def follow(t):
        @pl.when((t >= 1) & (t < steps + 1))
        def _():
            second(t - 1)

        @pl.when((t >= 3) & (t < steps + 3))
        def _():
            third(t - 3)

        @pl.when((t >= 4) & (t < steps + 4))
        def _():
            along(t - 4)

        @pl.when((t >= 5) & (t < steps + 5) & (lax.rem(t - 5, shards) == shards - 1))
        def _():
            fourth(t - 5)

        @pl.when((t >= 6) & (t < steps + 6) & (lax.rem(t - 6, shards) == shards - 1))
        def _():
            fifth(t - 6)

    def finish():
        for m in range(count):
            for n in (2, 5, 6, 7):
                arrived(out.at[m, 0], out_recv.at[m, n])
        arrived(out.at[:, pl.ds(0, 4)], on_send)

    return steps + 6, lead, follow, finish, pair_send


UNITS = 256


def feed_kernel(blocks, tokens_ref, o_ref, wo_ref, cot_ref, alpha_attn_ref, alpha_ref, up_scale_ref, gate_scale_ref,
                wu_ref, wg_ref, wd_ref, out_ref, grad_side_ref, grad_in_ref, grad_ref, down_ref, up_sum_ref,
                gate_sum_ref, alpha_sum_ref, alpha_attn_sum_ref, up_buf, gate_buf, hidden_buf, total, back,
                grad_hidden_buf, grad_u_buf, grad_g_buf, up_now, gate_now, side_pre, middle_ref, mid_ref, grad_mid_ref):
    turn = pl.program_id(0)
    after = turn - blocks - 2
    rows = tokens_ref.shape[0]

    def inputs(part):
        normed = rownorm(tokens_ref[part, :].astype(F32))[0]
        side, side_factor = rownorm(side_pre[part, :])
        middle, mid_factor = rownorm(normed + alpha_attn_ref[...] * (side - normed))
        return normed, side, side_factor, middle, mid_factor

    def start_step():
        side_pre[...] = dot(o_ref[...], wo_ref[...].reshape(D, D))

        def step(i, _):
            part = pl.ds(pl.multiple_of(i * 32, 32), 32)
            middle = inputs(part)[3]
            middle_ref[part, :] = middle
            mid_ref[part, :] = middle.astype(BF16)
            return 0

        lax.fori_loop(0, rows // 32, step, 0)

    def end_step():
        alpha = alpha_attn_ref[...]

        def step(i, sums):
            part = pl.ds(pl.multiple_of(i * 32, 32), 32)
            normed, side, side_factor, middle, mid_factor = inputs(part)
            grad = norm_back(middle, mid_factor, grad_mid_ref[part, :])
            grad_in_ref[part, :] = grad * (1.0 - alpha)
            grad_side_ref[part, :] = norm_back(side, side_factor, grad * alpha).astype(BF16)
            return sums + jnp.sum(grad * (side - normed), 0, keepdims=True)

        alpha_attn_sum_ref[...] = lax.fori_loop(0, rows // 32, step, jnp.zeros((1, D), F32))

    def raw(block):
        up_raw, gate_raw = dot_nt(mid_ref[...], wu_ref[...]), dot_nt(mid_ref[...], wg_ref[...])
        up_now[...] = up_raw
        gate_now[...] = gate_raw
        up_buf[block] = up_raw.astype(BF16)
        gate_buf[block] = gate_raw.astype(BF16)

    def activate(block):
        gate = gate_now[...] * (gate_scale_ref[...] * math.sqrt(D))
        hidden = gate * jax.nn.sigmoid(gate) * (up_now[...] * up_scale_ref[...])
        hidden_buf[block] = hidden.astype(BF16)

    def project(block, first):
        part = dot(hidden_buf[block], wd_ref[...])
        total[...] = part if first else total[...] + part

    def middle_step():
        alpha = alpha_ref[...]

        def step(i, sums):
            part = pl.ds(pl.multiple_of(i * 32, 32), 32)
            branch, factor = rownorm(total[part, :])
            middle = middle_ref[part, :]
            final, final_factor = rownorm(middle + alpha * (branch - middle))
            out_ref[part, :] = final.astype(BF16)
            grad = norm_back(final, final_factor, cot_ref[part, :].astype(F32))
            grad_mid_ref[part, :] = grad * (1.0 - alpha)
            back[part, :] = norm_back(branch, factor, grad * alpha).astype(BF16)
            return sums + jnp.sum(grad * (branch - middle), 0, keepdims=True)

        alpha_sum_ref[...] = lax.fori_loop(0, rows // 32, step, jnp.zeros((1, D), F32))

    def back_raw():
        grad_hidden_buf[...] = dot_nt(back[...], wd_ref[...])

    def back_activate(block):
        up_scale, gate_scale = up_scale_ref[...], gate_scale_ref[...] * math.sqrt(D)
        grad_hidden = grad_hidden_buf[...]
        up_raw, gate_raw = up_buf[block].astype(F32), gate_buf[block].astype(F32)
        gate = gate_raw * gate_scale
        sigma = jax.nn.sigmoid(gate)
        active = gate * sigma
        upward = up_raw * up_scale
        grad_upward = grad_hidden * active
        grad_gate = grad_hidden * upward * (sigma * (1.0 + gate * (1.0 - sigma)))
        up_sum_ref[...] = jnp.sum(grad_upward * up_raw, 0, keepdims=True)
        gate_sum_ref[...] = jnp.sum(grad_gate * gate_raw, 0, keepdims=True) * math.sqrt(D)
        grad_u_buf[...] = (grad_upward * up_scale).astype(BF16)
        grad_g_buf[...] = (grad_gate * gate_scale).astype(BF16)

    def back_project(block):
        grad_u, grad_g = grad_u_buf[...], grad_g_buf[...]
        grad_ref[0] = dot_tn(grad_u, mid_ref[...]).astype(BF16)
        grad_ref[1] = dot_tn(grad_g, mid_ref[...]).astype(BF16)
        down_ref[...] = dot_tn(hidden_buf[block], back[...]).astype(BF16)
        grad_mid_ref[...] += dot(grad_u, wu_ref[...]) + dot(grad_g, wg_ref[...])

    @pl.when(turn == 0)
    def _():
        start_step()
        raw(0)

    @pl.when(turn == 1)
    def _():
        activate(0)
        raw(1)

    @pl.when(turn == 2)
    def _():
        project(0, True)
        activate(1)
        raw(2)

    @pl.when((turn > 2) & (turn < blocks))
    def _():
        project(turn - 2, False)
        activate(turn - 1)
        raw(turn)

    @pl.when(turn == blocks)
    def _():
        project(turn - 2, False)
        activate(turn - 1)

    @pl.when(turn == blocks + 1)
    def _():
        project(turn - 2, False)
        middle_step()

    @pl.when(after == 0)
    def _():
        back_raw()

    @pl.when(after == 1)
    def _():
        back_activate(0)
        back_raw()

    @pl.when((after > 1) & (after < blocks))
    def _():
        back_project(after - 2)
        back_activate(after - 1)
        back_raw()

    @pl.when(after == blocks)
    def _():
        back_project(after - 2)
        back_activate(after - 1)

    @pl.when(after == blocks + 1)
    def _():
        back_project(after - 2)
        end_step()


def feed_forward(tokens, o_low, projection, cotangent, alphas, scales, weights, firsts):
    rows = tokens.shape[0]
    out_low, place_of = projection
    _, parts, _, _ = out_low.shape
    blocks = scales.shape[1] // UNITS
    whole = lambda *shape: pl.BlockSpec(shape, lambda t: (0,) * len(shape))
    held = lambda *shape: pl.BlockSpec(shape, lambda t: (0,) * len(shape), pipeline_mode=pl.Buffered(1))
    half = blocks + 2

    def stage(t, early, late):
        return jnp.clip(lax.select(t < half, t - early, t - half - late), 0, blocks - 1)

    weight = lambda m, early, late: pl.BlockSpec((None, UNITS, D), lambda t: (m, stage(t, early, late), 0))
    done = lambda t, lag: jnp.clip(t - half - lag, 0, blocks - 1)
    units = pl.BlockSpec((1, UNITS), lambda t: (0, done(t, 1)))
    scale = pl.BlockSpec((1, UNITS), lambda t: (0, stage(t, 1, 1)))
    return pl.pallas_call(
        functools.partial(feed_kernel, blocks),
        grid=(2 * half,),
        out_shape=(
            jax.ShapeDtypeStruct((rows, D), BF16),
            jax.ShapeDtypeStruct((rows, D), BF16),
            jax.ShapeDtypeStruct((rows, D), F32),
            jax.ShapeDtypeStruct((2, blocks * UNITS, D), BF16),
            jax.ShapeDtypeStruct((blocks * UNITS, D), BF16),
            jax.ShapeDtypeStruct((1, blocks * UNITS), F32),
            jax.ShapeDtypeStruct((1, blocks * UNITS), F32),
            jax.ShapeDtypeStruct((1, D), F32),
            jax.ShapeDtypeStruct((1, D), F32),
        ),
        in_specs=[
            held(rows, D),
            held(rows, D),
            pl.BlockSpec((None, parts, D // parts, D), lambda t: (0, 0, place_of, 0), pipeline_mode=pl.Buffered(1)),
            held(rows, D),
            whole(1, D), whole(1, D), scale, scale,
        ]
        + [weight(firsts[0], 0, 2), weight(firsts[1], 0, 2), weight(firsts[2], 2, 0)],
        out_specs=(
            whole(rows, D), whole(rows, D), whole(rows, D),
            pl.BlockSpec((2, UNITS, D), lambda t: (0, done(t, 2), 0)),
            pl.BlockSpec((UNITS, D), lambda t: (done(t, 2), 0)),
            units, units, whole(1, D), whole(1, D),
        ),
        scratch_shapes=[
            pltpu.VMEM((blocks, rows, UNITS), BF16),
            pltpu.VMEM((blocks, rows, UNITS), BF16),
            pltpu.VMEM((blocks, rows, UNITS), BF16),
            pltpu.VMEM((rows, D), F32),
            pltpu.VMEM((rows, D), BF16),
            pltpu.VMEM((rows, UNITS), F32),
            pltpu.VMEM((rows, UNITS), BF16),
            pltpu.VMEM((rows, UNITS), BF16),
            pltpu.VMEM((rows, UNITS), F32),
            pltpu.VMEM((rows, UNITS), F32),
            pltpu.VMEM((rows, D), F32),
            pltpu.VMEM((rows, D), F32),
            pltpu.VMEM((rows, D), BF16),
            pltpu.VMEM((rows, D), F32),
        ],
        compiler_params=pltpu.CompilerParams(vmem_limit_bytes=62 * 2**20),
        cost_estimate=pl.CostEstimate(flops=60 * 10**9, bytes_accessed=120 * 10**6, transcendentals=5 * 10**6),
    )(tokens, o_low, out_low, cotangent, alphas[:1], alphas[1:], scales[:1], scales[1:], *weights)


def adam_kernel(places, per, *refs):
    grads = refs[:places]
    w_ref, m_ref, v_ref, w_out, m_out, v_out = refs[places:]
    group, piece, _ = w_ref.shape

    def update(g_ref):
        for n in range(group):
            def step(i, _, n=n):
                part = (n, pl.ds(pl.multiple_of(i * 16, 16), 16), slice(None))
                new, first, second = adam(
                    w_ref[part], g_ref[part].astype(F32), m_ref[part], v_ref[part], RATE, DECAY
                )
                w_out[part] = rownorm(new)[0]
                m_out[part] = first
                v_out[part] = second
                return 0

            lax.fori_loop(0, piece // 16, step, 0, unroll=5)

    for n in range(places):
        @pl.when(pl.program_id(0) // per == n)
        def _(n=n):
            update(grads[n])


def adam_rows(weight, grads, first, second):
    places = len(grads)
    _, per, piece, _ = grads[0][0].shape
    group = 2 if per % 2 == 0 else 1
    steps = per // group
    spec = pl.BlockSpec((group, piece, D), lambda p: (p, 0, 0))

    def grad_spec(n, index):
        return pl.BlockSpec(
            (None, group, piece, D), lambda p: (index, jnp.clip(p - n * steps, 0, steps - 1), 0, 0)
        )

    shape = jax.ShapeDtypeStruct((places * per, piece, D), F32)
    news = pl.pallas_call(
        functools.partial(adam_kernel, places, steps),
        grid=(places * steps,),
        out_shape=(shape,) * 3,
        in_specs=[grad_spec(n, index) for n, (_, index) in enumerate(grads)] + [spec] * 3,
        out_specs=(spec,) * 3,
        compiler_params=pltpu.CompilerParams(vmem_limit_bytes=60 * 2**20),
        cost_estimate=pl.CostEstimate(flops=20 * weight.size, bytes_accessed=26 * weight.size, transcendentals=0),
    )(*(array for array, _ in grads), *(old.reshape(shape.shape) for old in (weight, first, second)))
    return tuple(new.reshape(weight.shape) for new in news)


QUERY_BLOCK = 256
PAIR = 2 * HEAD_DIM
PAIRS = HEADS // 2


def head_ones():
    row = lax.broadcasted_iota(jnp.int32, (PAIR, PAIR), 0) // HEAD_DIM
    col = lax.broadcasted_iota(jnp.int32, (PAIR, PAIR), 1) // HEAD_DIM
    return (row == col).astype(F32).astype(BF16)


def head_sum(value, ones):
    high = value.astype(BF16)
    rest = (value - high.astype(F32)).astype(BF16)
    return dot(high, ones) + dot(rest, ones)


def of_head(value, head):
    lane = lax.broadcasted_iota(jnp.int32, value.shape, 1) // HEAD_DIM
    return jnp.where(lane == head, value, jnp.zeros_like(value))


def attend_pair(h_ref, wq_ref, wq2_ref, wk_ref, wk2_ref, wv_ref, wv2_ref, gain_ref, bias_ref, qp_ref, kp_ref, v_ref, o_ref, lse_ref,
                key_buf, query_buf, value_buf):
    cols = h_ref.shape[0]
    rows = qp_ref.shape[0]
    span = bias_ref.shape[1]
    ones = head_ones()
    gain = gain_ref[...]
    weights = jnp.concatenate([wk_ref[...], wk2_ref[...], wv_ref[...], wv2_ref[...]], 0)
    query_weights = jnp.concatenate([wq_ref[...], wq2_ref[...]], 0)

    def project(i, _):
        part = pl.ds(pl.multiple_of(i * QUERY_BLOCK, QUERY_BLOCK), QUERY_BLOCK)
        both = dot_nt(h_ref[part, :], weights)
        keys = both[:, :PAIR]
        kp_ref[part, :] = keys
        factor = lax.rsqrt(head_sum(keys * keys, ones) + SMALL)
        key_buf[part, :] = (keys * factor * gain).astype(BF16)
        values = both[:, PAIR:].astype(BF16)
        v_ref[part, :] = values
        value_buf[part, :PAIR] = values
        value_buf[part, PAIR:] = jnp.ones_like(values)
        return 0

    lax.fori_loop(0, cols // QUERY_BLOCK, project, 0)

    def project_queries(i, _):
        part = pl.ds(pl.multiple_of(i * QUERY_BLOCK, QUERY_BLOCK), QUERY_BLOCK)
        own = pl.ds(pl.multiple_of(cols - rows + i * QUERY_BLOCK, QUERY_BLOCK), QUERY_BLOCK)
        queries = dot_nt(h_ref[own, :], query_weights)
        qp_ref[part, :] = queries
        factor = lax.rsqrt(head_sum(queries * queries, ones) + SMALL)
        scaled = (queries * factor * gain).astype(BF16).astype(F32) * math.sqrt(HEAD_DIM)
        query_buf[part, :] = scaled.astype(BF16)
        return 0

    lax.fori_loop(0, rows // QUERY_BLOCK, project_queries, 0)
    for i in range(rows // QUERY_BLOCK):
        part = pl.ds(i * QUERY_BLOCK, QUERY_BLOCK)
        reach = pl.ds(i * QUERY_BLOCK, span)
        sides = []
        for head in range(2):
            scores = dot_nt(of_head(query_buf[part, :], head), key_buf[reach, :])
            probs = jnp.exp(scores + bias_ref[part, :]).astype(BF16)
            both = dot(probs, value_buf[reach, :])
            total = both[:, PAIR:]
            sides.append(both[:, :PAIR] / total)
            lse_ref[head : head + 1, part] = jnp.log(total).T[:1, :]
        lane = lax.broadcasted_iota(jnp.int32, sides[0].shape, 1)
        o_ref[part, :] = jnp.where(lane < HEAD_DIM, sides[0], sides[1]).astype(BF16)


def back_pair(*refs):
    start, block, finish = back_parts(*refs)
    start()
    for i in range(refs[0].shape[0] // QUERY_BLOCK):
        block(i)
    finish()


def back_parts(qp_ref, kp_ref, v_ref, o_ref, da_ref, wo_ref, wo2_ref, gain_ref, bias_ref, lse_ref,
               dq_ref, dk_ref, dv_ref, sum_ref, key_buf, key_turned, k_total, v_total):
    cols = kp_ref.shape[0]
    rows = qp_ref.shape[0]
    span = bias_ref.shape[1]

    def keys_of(i, _):
        ones, gain = head_ones(), gain_ref[...]
        part = pl.ds(pl.multiple_of(i * QUERY_BLOCK, QUERY_BLOCK), QUERY_BLOCK)
        keys = kp_ref[part, :]
        factor = lax.rsqrt(head_sum(keys * keys, ones) + SMALL)
        low = keys * factor * gain
        key_buf[part, :] = low.astype(BF16)
        key_turned[:, part] = low.T.astype(BF16)
        k_total[part, :] = jnp.zeros_like(keys)
        v_total[part, :] = jnp.zeros_like(keys)
        return 0

    def start():
        lax.fori_loop(0, cols // QUERY_BLOCK, keys_of, 0)

    def block(i):
        ones, gain = head_ones(), gain_ref[...]
        weights = jnp.concatenate([wo_ref[...], wo2_ref[...]], 0)
        part = pl.ds(i * QUERY_BLOCK, QUERY_BLOCK)
        reach = pl.ds(i * QUERY_BLOCK, span)
        queries = qp_ref[part, :]
        factor = lax.rsqrt(head_sum(queries * queries, ones) + SMALL)
        hat = queries * factor
        scaled = ((hat * gain).astype(BF16).astype(F32) * math.sqrt(HEAD_DIM)).astype(BF16)
        back = dot_nt(da_ref[part, :], weights).astype(BF16)
        inner = (back.astype(F32) * o_ref[part, :].astype(F32)).T
        sides = []
        for head in range(2):
            mine = slice(head * HEAD_DIM, (head + 1) * HEAD_DIM)
            query, grad = of_head(scaled, head), of_head(back, head)
            scores = dot_nt(key_buf[reach, :], query)
            probs = jnp.exp(scores + bias_ref[i] - lse_ref[head : head + 1, part])
            v_total[reach, :] += dot(probs.astype(BF16), grad)
            delta = jnp.sum(inner[mine, :], 0, keepdims=True)
            grad_scores = (probs * (dot_nt(v_ref[reach, :], grad) - delta)).astype(BF16)
            k_total[reach, :] += dot(grad_scores, query)
            sides.append(dot(key_turned[mine, reach], grad_scores))
        grad_q = jnp.concatenate(sides, 0).T * math.sqrt(HEAD_DIM)
        sums = jnp.sum(grad_q * hat, 0, keepdims=True)
        if i == 0:
            sum_ref[...] = jnp.broadcast_to(sums, sum_ref.shape)
        else:
            sum_ref[...] += jnp.broadcast_to(sums, sum_ref.shape)
        grad_q = grad_q * gain
        dq_ref[part, :] = (factor * (grad_q - hat * head_sum(hat * grad_q, ones))).astype(BF16)

    def close(i, _):
        ones, gain = head_ones(), gain_ref[...]
        part = pl.ds(pl.multiple_of(i * QUERY_BLOCK, QUERY_BLOCK), QUERY_BLOCK)
        keys = kp_ref[part, :]
        factor = lax.rsqrt(head_sum(keys * keys, ones) + SMALL)
        hat = keys * factor
        grad_k = k_total[part, :]
        sum_ref[...] += jnp.broadcast_to(jnp.sum(grad_k * hat, 0, keepdims=True), sum_ref.shape)
        grad_k = grad_k * gain
        dk_ref[part, :] = (factor * (grad_k - hat * head_sum(hat * grad_k, ones))).astype(BF16)
        dv_ref[part, :] = v_total[part, :].astype(BF16)
        return 0

    def finish():
        lax.fori_loop(0, cols // QUERY_BLOCK, close, 0)

    return start, block, finish


def head_rows(attn_low, matrix, second):
    heads = attn_low.shape[2]

    def index(p):
        head = 2 * p + second
        return (head // heads, matrix, lax.rem(head, heads), 0, 0)

    return pl.BlockSpec((None, None, None, HEAD_DIM, D), index)


def attention_forward(low_all, attn_low, gain_qk, bias, rows):
    cols = low_all.shape[0]
    span = bias.shape[1]
    side = lambda n: pl.BlockSpec((n, PAIR), lambda p: (0, p))
    whole = lambda *shape: pl.BlockSpec(shape, lambda p: (0,) * len(shape))
    return pl.pallas_call(
        attend_pair,
        grid=(PAIRS,),
        out_shape=(
            jax.ShapeDtypeStruct((rows, D), F32),
            jax.ShapeDtypeStruct((cols, D), F32),
            jax.ShapeDtypeStruct((cols, D), BF16),
            jax.ShapeDtypeStruct((rows, D), BF16),
            jax.ShapeDtypeStruct((PAIRS, 8, rows), F32),
        ),
        in_specs=[whole(cols, D)]
        + [head_rows(attn_low, j, second) for j in range(3) for second in range(2)]
        + [side(1), whole(rows, span)],
        out_specs=(side(rows), side(cols), side(cols), side(rows),
                   pl.BlockSpec((None, 8, rows), lambda p: (p, 0, 0))),
        scratch_shapes=[
            pltpu.VMEM((cols, PAIR), BF16),
            pltpu.VMEM((rows, PAIR), BF16),
            pltpu.VMEM((cols, 2 * PAIR), BF16),
        ],
        compiler_params=pltpu.CompilerParams(vmem_limit_bytes=56 * 2**20),
        cost_estimate=pl.CostEstimate(flops=20 * 10**9, bytes_accessed=30 * 10**6, transcendentals=13 * 10**6),
    )(low_all, *[attn_low] * 6, gain_qk, bias)


def attention_backward(q_pre, k_pre, value_all, o_low, grad_spre, attn_low, gain_qk, bias_turned, lse):
    rows, cols = q_pre.shape[0], k_pre.shape[0]
    side = lambda n: pl.BlockSpec((n, PAIR), lambda p: (0, p))
    whole = lambda *shape: pl.BlockSpec(shape, lambda p: (0,) * len(shape))
    stat = pl.BlockSpec((None, 8, rows), lambda p: (p, 0, 0))
    return pl.pallas_call(
        back_pair,
        grid=(PAIRS,),
        out_shape=(
            jax.ShapeDtypeStruct((rows, D), BF16),
            jax.ShapeDtypeStruct((cols, D), BF16),
            jax.ShapeDtypeStruct((cols, D), BF16),
            jax.ShapeDtypeStruct((PAIRS, 8, PAIR), F32),
        ),
        in_specs=[
            side(rows), side(cols), side(cols), side(rows), whole(rows, D),
            head_rows(attn_low, 3, 0), head_rows(attn_low, 3, 1),
            pl.BlockSpec((None, 1, PAIR), lambda p: (p, 0, 0)), whole(*bias_turned.shape), stat,
        ],
        out_specs=(side(rows), side(cols), side(cols), pl.BlockSpec((None, 8, PAIR), lambda p: (p, 0, 0))),
        scratch_shapes=[
            pltpu.VMEM((cols, PAIR), BF16),
            pltpu.VMEM((PAIR, cols), BF16),
            pltpu.VMEM((cols, PAIR), F32),
            pltpu.VMEM((cols, PAIR), F32),
        ],
        compiler_params=pltpu.CompilerParams(vmem_limit_bytes=56 * 2**20),
        cost_estimate=pl.CostEstimate(flops=30 * 10**9, bytes_accessed=40 * 10**6, transcendentals=13 * 10**6),
    )(q_pre, k_pre, value_all, o_low, grad_spre, attn_low, attn_low, gain_qk, bias_turned, lse)


START = 5


def gather_kernel(shards, attn_ref, ffn_ref, gains_ref, tokens_ref, bias_ref,
                  out, gains_out, h_out, qp_out, kp_out, v_out, o_out, lse_ref,
                  wide, low, mine, wide_sem, low_sem, mine_sem, line_send, line_recv, plane_send, beside_recv,
                  above_recv, across_recv, pair_send, pair_recv, gains_send, gains_recv, tokens_send,
                  tokens_recv, local_sem, gains_buf, before, h_buf, load_sem, store_sem,
                  weight_buf, gain_row, qp_buf, kp_buf, v_buf, o_buf, key_buf, query_buf, value_buf):
    core, chip, beside, above, across = place()
    line = lax.axis_index("shard")
    rep = 2 * chip + core
    sibling = 2 * chip + 1 - core
    to_beside, to_above = 2 * beside + core, 2 * above + core
    piece = attn_ref.shape[1]
    rows = tokens_ref.shape[0]
    heads = 2 * piece // HEAD_DIM
    others = shards - 1
    steps = 4 * others
    greet(shards)

    def rows_of(m, shard, rep, start=0, size=None):
        first = pl.multiple_of(rep * piece + start, 16)
        return out.at[m, shard, pl.ds(first, piece if size is None else size)]

    def source(n):
        low_side = 2 * line < shards
        edge = lax.select(low_side, line, shards - 1 - line)
        near = lax.select(lax.rem(n, 2) == 0, edge - 1 - n // 2, edge + 1 + n // 2)
        found = lax.select(n < 2 * edge, near, n + 1)
        return lax.select(low_side, found, shards - 1 - found)

    def own_send(m):
        @pl.when(line < shards - 1)
        def _():
            remote(mine.at[m], rows_of(m, line, rep), line_send, line_recv.at[m, line], rep, line + 1).start()

        @pl.when(line > 0)
        def _():
            remote(mine.at[m], rows_of(m, line, rep), line_send, line_recv.at[m, line], rep, line - 1).start()

    def fetch(index, slot):
        @pl.when(index < 8)
        def _():
            pltpu.make_async_copy(attn_ref.at[lax.rem(index, 8)], wide.at[slot], wide_sem.at[slot]).start()

        @pl.when(index >= 8)
        def _():
            pltpu.make_async_copy(
                ffn_ref.at[jnp.maximum(index // 8 - 1, 0), lax.rem(index, 8)], wide.at[slot], wide_sem.at[slot]
            ).start()

    def store(index, slot):
        return pltpu.make_async_copy(low.at[slot], rows_of(index // 8, line, lax.rem(index, 8)), low_sem.at[slot])

    def lower(src, dst):
        def step(i, _):
            part = pl.ds(pl.multiple_of(i * 32, 32), 32)
            dst[part, :] = src[part, :].astype(BF16)
            return 0

        lax.fori_loop(0, piece // 32, step, 0)

    for n in range(1, shards):
        other = lax.rem(line + n, shards)
        remote(gains_ref, gains_buf.at[line], gains_send, gains_recv.at[line], rep, other).start()
    pltpu.make_async_copy(gains_ref, gains_buf.at[line], local_sem).start()
    own = pl.ds(2 * rows, rows)
    pltpu.make_async_copy(tokens_ref, h_buf.at[own], load_sem.at[0, 0]).start()
    for m in range(4):
        origin = attn_ref.at[rep] if m == 0 else ffn_ref.at[m - 1, rep]
        pltpu.make_async_copy(origin, wide.at[m], mine_sem.at[m]).start()
    for m in range(4):
        arrived(wide.at[m], mine_sem.at[m])
        lower(wide.at[m], mine.at[m])
        if m == 0:
            own_send(0)

            @pl.when(line < shards - 1)
            def _():
                remote(tokens_ref, before.at[1], tokens_send, tokens_recv.at[1], rep, line + 1).start()

    for n in range(2):
        fetch(n, n)

    def norm_rows(source, first):
        def step(i, _):
            at = pl.multiple_of(first + i * 32, 32)
            value = source[pl.ds(pl.multiple_of(i * 32, 32), 32), :].astype(F32)
            h_buf[pl.ds(at, 32), :] = rownorm(value)[0].astype(BF16)
            return 0

        lax.fori_loop(0, rows // 32, step, 0)

    def clear_rows(first):
        h_buf[pl.ds(first, rows), :] = jnp.zeros((rows, D), BF16)

    arrived(h_buf.at[own], load_sem.at[0, 0])
    norm_rows(h_buf.at[own], 2 * rows)

    def loads(p, slot):
        copies = []
        for j in range(3):
            for second in range(2):
                head = 2 * p + second
                first = pl.multiple_of(2 * piece * j + HEAD_DIM * lax.rem(head, heads), HEAD_DIM)
                copies.append(
                    pltpu.make_async_copy(
                        out.at[0, head // heads, pl.ds(first, HEAD_DIM)], weight_buf.at[slot, 2 * j + second],
                        load_sem.at[slot, 2 * j + second],
                    )
                )
        return copies

    def stores(p, slot):
        lanes = pl.ds(pl.multiple_of(p * PAIR, PAIR), PAIR)
        return [
            pltpu.make_async_copy(buf.at[slot], ref.at[:, lanes], store_sem.at[slot, n])
            for n, (ref, buf) in enumerate(((qp_out, qp_buf), (kp_out, kp_buf), (v_out, v_buf), (o_out, o_buf)))
        ]

    def pair(p):
        slot = lax.rem(p, 2)

        @pl.when(p + 1 < PAIRS)
        def _():
            for copy in loads(p + 1, 1 - slot):
                copy.start()

        for copy in loads(p, slot):
            copy.wait()

        @pl.when(p >= 2)
        def _():
            for copy in stores(p - 2, slot):
                copy.wait()

        row = lax.broadcasted_iota(jnp.int32, (8, PAIR), 0)
        left, right = (
            jnp.sum(
                jnp.where(row == lax.rem(2 * p + n, heads), gains_buf[(2 * p + n) // heads, :8, :PAIR], 0.0),
                0, keepdims=True,
            )
            for n in range(2)
        )
        lane = lax.broadcasted_iota(jnp.int32, (1, PAIR), 1)
        gain_row[...] = jnp.where(lane < HEAD_DIM, left, right)
        attend_pair(
            h_buf, *(weight_buf.at[slot, n] for n in range(6)), gain_row, bias_ref, qp_buf.at[slot],
            kp_buf.at[slot], v_buf.at[slot], o_buf.at[slot], lse_ref.at[p], key_buf, query_buf, value_buf,
        )
        for copy in stores(p, slot):
            copy.start()

    def begin(c):
        m, origin = c // others, source(lax.rem(c, others))
        got = rows_of(m, origin, rep)
        arrived(got, line_recv.at[m, origin])

        @pl.when((origin < line) & (line < shards - 1))
        def _():
            remote(got, got, line_send, line_recv.at[m, origin], rep, line + 1).start()

        @pl.when((origin > line) & (line > 0))
        def _():
            remote(got, got, line_send, line_recv.at[m, origin], rep, line - 1).start()

        remote(got, got, plane_send, beside_recv.at[m, origin], to_beside, line).start()
        remote(got, got, plane_send, above_recv.at[m, origin], to_above, line).start()
        remote(got, got, pair_send, pair_recv.at[m], sibling, line).start()

    def middle(c):
        m, origin = c // others, source(lax.rem(c, others))
        got = rows_of(m, origin, to_beside)
        arrived(got, beside_recv.at[m, origin])
        part = rows_of(m, origin, to_beside, 0, HALF)
        remote(part, part, plane_send, across_recv.at[m, origin, 0], to_above, line).start()
        remote(got, got, pair_send, pair_recv.at[m], sibling, line).start()
        got = rows_of(m, origin, to_above)
        arrived(got, above_recv.at[m, origin])
        part = rows_of(m, origin, to_above, HALF, piece - HALF)
        remote(part, part, plane_send, across_recv.at[m, origin, 1], to_beside, line).start()
        remote(got, got, pair_send, pair_recv.at[m], sibling, line).start()

    def last(c):
        m, origin = c // others, source(lax.rem(c, others))
        got = rows_of(m, origin, 2 * across + core)
        arrived(rows_of(m, origin, 2 * across + core, 0, HALF), across_recv.at[m, origin, 0])
        arrived(rows_of(m, origin, 2 * across + core, HALF, piece - HALF), across_recv.at[m, origin, 1])
        remote(got, got, pair_send, pair_recv.at[m], sibling, line).start()

    def local(t):
        for n in range(2):
            index = 2 * t + n
            slot = 2 * lax.rem(t, 2) + n
            arrived(wide.at[slot], wide_sem.at[slot])

            @pl.when(index + 2 < 32)
            def _():
                fetch(index + 2, lax.rem(slot + 2, 4))

            @pl.when(t >= 2)
            def _():
                store(index - 4, slot).wait()

            lower(wide.at[slot], low.at[slot])
            store(index, slot).start()

    def turn(t, _):
        @pl.when((lax.rem(t, others) == 0) & (t // others < 3))
        def _():
            own_send(t // others + 1)

        @pl.when(t < steps)
        def _():
            begin(t)

        @pl.when((t == 1) & (line > 0))
        def _():
            arrived(before.at[1], tokens_recv.at[1])

            @pl.when(line < shards - 1)
            def _():
                remote(before.at[1], before.at[0], tokens_send, tokens_recv.at[0], rep, line + 1).start()

            norm_rows(before.at[1], rows)

        @pl.when((t == 1) & (line == 0))
        def _():
            clear_rows(rows)

        @pl.when((t == 3) & (line > 1))
        def _():
            arrived(before.at[0], tokens_recv.at[0])
            norm_rows(before.at[0], 0)

        @pl.when((t == 3) & (line <= 1))
        def _():
            clear_rows(0)

        @pl.when(t < 2)
        def _():
            local(2 * t)
            local(2 * t + 1)

        @pl.when(t >= 2)
        def _():
            local(t + 2)

        @pl.when(t == START)
        def _():
            pltpu.make_async_copy(gains_ref, gains_buf.at[line], local_sem).wait()
            for n in range(1, shards):
                other = lax.rem(line + n, shards)
                arrived(gains_buf.at[other], gains_recv.at[other])
            arrived(out.at[0, pl.ds(0, others), pl.ds(0, 4 * piece)], pair_recv.at[0])
            for copy in loads(0, 0):
                copy.start()

        early = (t > START + 3).astype(jnp.int32) + (t > START + 6).astype(jnp.int32)
        most = lax.select((t == START + 3) | (t == START + 6), 2, 1)

        def one(n, _):
            pair(t - START + early + n)
            return 0

        lax.fori_loop(0, lax.select((t >= START) & (t < START + PAIRS - 2), most, 0), one, 0)

        @pl.when((t >= 1) & (t < steps + 1))
        def _():
            middle(t - 1)

        @pl.when((t >= 2) & (t < steps + 2))
        def _():
            last(t - 2)

        return 0

    lax.fori_loop(0, 14, turn, 0)
    for n in range(4):
        store(28 + n, n).wait()
    gains_copy = pltpu.make_async_copy(gains_buf, gains_out, local_sem)
    h_copy = pltpu.make_async_copy(h_buf, h_out, load_sem.at[0, 0])
    gains_copy.start()
    h_copy.start()
    for p in (PAIRS - 2, PAIRS - 1):
        for copy in stores(p, p % 2):
            copy.wait()
    for m in range(1, 4):
        arrived(out.at[m, pl.ds(0, others), pl.ds(0, 4 * piece)], pair_recv.at[m])
    gains_copy.wait()
    h_copy.wait()

    @pl.when((line == 1) | (line == shards - 2))
    def _():
        arrived(before, tokens_send)

    @pl.when(line == 0)
    def _():
        arrived(before.at[0], tokens_send)

    @pl.when((line == 0) | (line == shards - 1))
    def _():
        arrived(out.at[:, 0, pl.ds(0, piece)], line_send)

    @pl.when((line > 0) & (line < shards - 1))
    def _():
        arrived(out.at[:, 0, pl.ds(0, 5 * piece)], line_send)

    arrived(out.at[:, pl.ds(0, others), pl.ds(0, 3 * piece)], plane_send)
    arrived(out.at[:, pl.ds(0, others), pl.ds(0, 4 * piece)], pair_send)
    arrived(gains_buf.at[pl.ds(0, others)], gains_send)


def gather_attend(attn_w, ffn_w, gains, tokens, bias, shards):
    piece = attn_w.shape[1]
    rows = tokens.shape[0]
    cols = rows + WINDOW
    any_space = pl.BlockSpec(memory_space=pl.ANY)
    vmem = pl.BlockSpec(memory_space=pltpu.VMEM)
    dma = pltpu.SemaphoreType.DMA
    return pl.pallas_call(
        functools.partial(gather_kernel, shards),
        out_shape=(
            jax.ShapeDtypeStruct((4, shards, 8 * piece, D), BF16),
            jax.ShapeDtypeStruct((shards,) + gains.shape, F32),
            jax.ShapeDtypeStruct((cols, D), BF16),
            jax.ShapeDtypeStruct((rows, D), F32),
            jax.ShapeDtypeStruct((cols, D), F32),
            jax.ShapeDtypeStruct((cols, D), BF16),
            jax.ShapeDtypeStruct((rows, D), BF16),
            jax.ShapeDtypeStruct((PAIRS, 8, rows), F32),
        ),
        in_specs=[any_space] * 4 + [vmem],
        out_specs=(any_space,) * 7 + (vmem,),
        scratch_shapes=[
            pltpu.VMEM((4, piece, D), F32),
            pltpu.VMEM((4, piece, D), BF16),
            pltpu.VMEM((4, piece, D), BF16),
            dma((4,)), dma((4,)), dma((4,)), dma(()), dma((4, shards)), dma(()), dma((4, shards)),
            dma((4, shards)), dma((4, shards, 2)), dma(()), dma((4,)), dma(()), dma((shards,)), dma(()),
            dma((2,)), dma(()),
            pltpu.VMEM((shards,) + gains.shape, F32),
            pltpu.VMEM((2, rows, D), BF16),
            pltpu.VMEM((cols, D), BF16),
            dma((2, 6)), dma((2, 4)),
            pltpu.VMEM((2, 6, HEAD_DIM, D), BF16),
            pltpu.VMEM((1, PAIR), F32),
            pltpu.VMEM((2, rows, PAIR), F32),
            pltpu.VMEM((2, cols, PAIR), F32),
            pltpu.VMEM((2, cols, PAIR), BF16),
            pltpu.VMEM((2, rows, PAIR), BF16),
            pltpu.VMEM((cols, PAIR), BF16),
            pltpu.VMEM((rows, PAIR), BF16),
            pltpu.VMEM((cols, 2 * PAIR), BF16),
        ],
        compiler_params=pltpu.CompilerParams(
            collective_id=3, has_side_effects=True, vmem_limit_bytes=60 * 2**20
        ),
        cost_estimate=pl.CostEstimate(flops=20 * 10**9, bytes_accessed=2 * 10**8, transcendentals=13 * 10**6),
    )(attn_w, ffn_w, gains, tokens, bias)


BACK_BLOCK = 256


def backward_kernel(shards, grads_ref, down_ref, qp_ref, kp_ref, v_ref, o_ref, weight_ref, gains_ref, da_ref, gain_ref,
                    bias_ref, lse_ref, h_ref, out, dq_ref, dk_ref, dv_ref, turned_ref, gains_out, sums_out, back_out,
                    own_out, sums, line_got, plane_got, line_sums, plane_sums, mine_gains, mine_sums, line_send, line_recv, plane_send,
                    plane_recv, back_send, back_recv, *scratch):
    rep, line = lax.axis_index("rep"), lax.axis_index("shard")
    grads = (grads_ref.at[0], grads_ref.at[1], down_ref, turned_ref)
    turns, lead, follow, finish, pair_send = reduction(grads, out, scratch)
    height = weight_ref.shape[2] // 4
    heads = height // HEAD_DIM
    rows, cols = da_ref.shape[0], h_ref.shape[0]
    reach = back_out.shape[0]
    per = rows // BACK_BLOCK
    attended = PAIRS + 1
    dma = pltpu.SemaphoreType.DMA
    greet(shards)

    def attention(qp_buf, kp_buf, v_buf, o_buf, wo_buf, dq_buf, dk_buf, dv_buf, turned_buf, load_sem, store_sem,
                  key_buf, key_turned, k_total, v_total):
        def loads(p, slot):
            lanes = pl.ds(pl.multiple_of(p * PAIR, PAIR), PAIR)
            copies = [
                pltpu.make_async_copy(ref.at[:, lanes], buf.at[slot], load_sem.at[slot, n])
                for n, (ref, buf) in enumerate(((qp_ref, qp_buf), (kp_ref, kp_buf), (v_ref, v_buf), (o_ref, o_buf)))
            ]
            for second in range(2):
                head = 2 * p + second
                first = pl.multiple_of(3 * height + HEAD_DIM * lax.rem(head, heads), HEAD_DIM)
                copies.append(
                    pltpu.make_async_copy(
                        weight_ref.at[0, head // heads, pl.ds(first, HEAD_DIM)], wo_buf.at[slot, second],
                        load_sem.at[slot, 4 + second],
                    )
                )
            return copies

        def lane_stores(p, slot):
            lanes = pl.ds(pl.multiple_of(p * PAIR, PAIR), PAIR)
            return [
                pltpu.make_async_copy(buf.at[slot], ref.at[:, lanes], store_sem.at[slot, n])
                for n, (ref, buf) in enumerate(((dq_ref, dq_buf), (dk_ref, dk_buf), (dv_ref, dv_buf)))
            ]

        def start_stores(p, slot):
            for copy in lane_stores(p, slot):
                copy.start()
            for second in range(2):
                head = 2 * p + second
                for n in range(HEAD_DIM // 32):
                    row = HEAD_DIM * lax.rem(head, heads) + 32 * n
                    place_of = pl.ds(pl.multiple_of(lax.rem(row, height // 2), 32), 32)
                    for j in range(4):
                        pltpu.make_async_copy(
                            turned_buf.at[slot, j, pl.ds(second * HEAD_DIM + 32 * n, 32)],
                            turned_ref.at[head // heads, j, row // (height // 2), place_of], store_sem.at[slot, 3],
                        ).start()

        def wait_stores(p, slot):
            for copy in lane_stores(p, slot):
                copy.wait()
            arrived(turned_buf.at[slot], store_sem.at[slot, 3])

        def pair(p):
            slot = lax.rem(p, 2)

            @pl.when(p + 1 < PAIRS)
            def _():
                for copy in loads(p + 1, 1 - slot):
                    copy.start()

            for copy in loads(p, slot):
                copy.wait()

            @pl.when(p >= 2)
            def _():
                wait_stores(p - 2, slot)

            back_pair(
                qp_buf.at[slot], kp_buf.at[slot], v_buf.at[slot], o_buf.at[slot], da_ref, wo_buf.at[slot, 0],
                wo_buf.at[slot, 1], gain_ref.at[p], bias_ref, lse_ref.at[p], dq_buf.at[slot], dk_buf.at[slot],
                dv_buf.at[slot], sums.at[p], key_buf, key_turned, k_total, v_total,
            )
            turned_buf[slot, 0] = dot_tn(dq_buf[slot], h_ref[pl.ds(cols - rows, rows), :]).astype(BF16)
            turned_buf[slot, 1] = dot_tn(dk_buf[slot], h_ref[...]).astype(BF16)
            turned_buf[slot, 2] = dot_tn(dv_buf[slot], h_ref[...]).astype(BF16)
            turned_buf[slot, 3] = dot_tn(o_buf[slot], da_ref[...]).astype(BF16)
            start_stores(p, slot)

        for copy in loads(0, 0):
            copy.start()

        def step(t, _):
            lead(t)

            @pl.when(t < PAIRS)
            def _():
                pair(t)

            follow(t)
            return 0

        lax.fori_loop(0, attended, step, 0)
        for p in (PAIRS - 2, PAIRS - 1):
            wait_stores(p, p % 2)

    pl.run_scoped(
        attention,
        pltpu.VMEM((2, rows, PAIR), F32),
        pltpu.VMEM((2, cols, PAIR), F32),
        pltpu.VMEM((2, cols, PAIR), BF16),
        pltpu.VMEM((2, rows, PAIR), BF16),
        pltpu.VMEM((2, 2, HEAD_DIM, D), BF16),
        pltpu.VMEM((2, rows, PAIR), BF16),
        pltpu.VMEM((2, cols, PAIR), BF16),
        pltpu.VMEM((2, cols, PAIR), BF16),
        pltpu.VMEM((2, 4, PAIR, D), BF16),
        dma((2, 6)), dma((2, 4)),
        pltpu.VMEM((cols, PAIR), BF16),
        pltpu.VMEM((PAIR, cols), BF16),
        pltpu.VMEM((cols, PAIR), F32),
        pltpu.VMEM((cols, PAIR), F32),
    )

    def inputs(weight_buf, left_buf, parts, weight_sem, left_sem):
        for j in range(3):
            for shard in range(shards):
                pltpu.make_async_copy(
                    weight_ref.at[0, shard, pl.ds(j * height, height)],
                    weight_buf.at[j, pl.ds(shard * height, height)], weight_sem,
                ).start()
        for n in range(1, shards):
            other = lax.rem(line + n, shards)
            remote(gains_ref.at[other], line_got.at[n - 1], line_send.at[0], line_recv.at[0, n - 1], rep, other).start()
            remote(sums, line_sums.at[n - 1], line_send.at[1], line_recv.at[1, n - 1], rep, other).start()

        def lefts(block):
            slot = lax.rem(block, 2)
            part = pl.ds(pl.multiple_of(block * BACK_BLOCK, BACK_BLOCK), BACK_BLOCK)
            return [
                pltpu.make_async_copy(ref.at[part], left_buf.at[slot, n], left_sem.at[slot, n])
                for n, ref in ((1, dk_ref), (2, dv_ref))
            ]

        def own_left(block):
            slot = lax.rem(block, 2)
            part = pl.ds(pl.multiple_of((block - reach * per) * BACK_BLOCK, BACK_BLOCK), BACK_BLOCK)
            return pltpu.make_async_copy(dq_ref.at[part], left_buf.at[slot, 0], left_sem.at[slot, 0])

        def fetch(block):
            for copy in lefts(block):
                copy.start()

            @pl.when(block >= reach * per)
            def _():
                own_left(block).start()

        def product(block):
            slot = lax.rem(block, 2)

            @pl.when(block + 1 < cols // BACK_BLOCK)
            def _():
                fetch(block + 1)

            for copy in lefts(block):
                copy.wait()
            total = dot(left_buf[slot, 1], weight_buf[1]) + dot(left_buf[slot, 2], weight_buf[2])

            @pl.when(block < reach * per)
            def _():
                parts[block] = total.astype(BF16)
                n = block // per
                part = pl.ds(pl.multiple_of(lax.rem(block, per) * BACK_BLOCK, BACK_BLOCK), BACK_BLOCK)

                @pl.when(line >= reach - n)
                def _():
                    remote(parts.at[block], back_out.at[n, part], back_send.at[n], back_recv.at[n], rep,
                           line - (reach - n)).start()

            @pl.when(block >= reach * per)
            def _():
                own_left(block).wait()
                part = pl.ds(pl.multiple_of((block - reach * per) * BACK_BLOCK, BACK_BLOCK), BACK_BLOCK)
                own_out[part, :] = total + dot(left_buf[slot, 0], weight_buf[0])

        fetch(0)

        def step(t, _):
            lead(t)

            @pl.when(t == attended + 1)
            def _():
                arrived(weight_buf, weight_sem)
                for pair_of, (whole, got, got_plane, mine) in enumerate(
                    ((gains_ref.at[line], line_got, plane_got, mine_gains), (sums, line_sums, plane_sums, mine_sums))
                ):
                    total = whole[...]
                    for n in range(shards - 1):
                        arrived(got.at[n], line_recv.at[pair_of, n])
                        total = total + got[n]
                    mine[...] = total
                    for n in range(1, 8):
                        remote(mine, got_plane.at[n - 1], plane_send.at[pair_of], plane_recv.at[pair_of, n - 1],
                               lax.rem(rep + n, 8), line).start()

            @pl.when(t == attended + 3)
            def _():
                for pair_of, (got_plane, mine, result) in enumerate(
                    ((plane_got, mine_gains, gains_out), (plane_sums, mine_sums, sums_out))
                ):
                    total = mine[...]
                    for n in range(7):
                        arrived(got_plane.at[n], plane_recv.at[pair_of, n])
                        total = total + got_plane[n]
                    result[...] = total

            @pl.when((t > attended + 1) & (t < attended + 2 + cols // BACK_BLOCK))
            def _():
                product(t - attended - 2)

            follow(t)
            return 0

        lax.fori_loop(attended, turns, step, 0)
        for n in range(reach):
            @pl.when(line >= reach - n)
            def _(n=n):
                arrived(parts.at[pl.ds(0, per)], back_send.at[n])

            @pl.when(line + reach - n < shards)
            def _(n=n):
                arrived(back_out.at[n], back_recv.at[n])

    pl.run_scoped(
        inputs,
        pltpu.VMEM((3, D, D), BF16),
        pltpu.VMEM((2, 3, BACK_BLOCK, D), BF16),
        pltpu.VMEM((reach * per, BACK_BLOCK, D), BF16),
        dma(()), dma((2, 3)),
    )
    finish()
    arrived(grads_ref, pair_send)
    arrived(line_got, line_send.at[0])
    arrived(line_sums, line_send.at[1])
    arrived(plane_got, plane_send.at[0])
    arrived(plane_sums, plane_send.at[1])


def backward_reduce(grads, down, q_pre, k_pre, value_all, o_low, gathered, gains, grad_spre, gain_qk, bias_turned, lse,
                    low_all):
    _, shards, _, _, rows, _ = grads.shape
    tokens, cols = q_pre.shape[0], k_pre.shape[0]
    reach = (cols - tokens) // tokens
    lines = gains.shape[1:]
    any_space = pl.BlockSpec(memory_space=pl.ANY)
    vmem = pl.BlockSpec(memory_space=pltpu.VMEM)
    dma = pltpu.SemaphoreType.DMA
    return pl.pallas_call(
        functools.partial(backward_kernel, shards),
        out_shape=(
            jax.ShapeDtypeStruct((4, 8, rows, D), BF16),
            jax.ShapeDtypeStruct((tokens, D), BF16),
            jax.ShapeDtypeStruct((cols, D), BF16),
            jax.ShapeDtypeStruct((cols, D), BF16),
            jax.ShapeDtypeStruct(grads.shape[1:], BF16),
            jax.ShapeDtypeStruct(lines, F32),
            jax.ShapeDtypeStruct((PAIRS, 8, PAIR), F32),
            jax.ShapeDtypeStruct((reach, tokens, D), BF16),
            jax.ShapeDtypeStruct((tokens, D), F32),
        ),
        in_specs=[any_space] * 7 + [vmem] * 6,
        out_specs=(any_space,) * 5 + (vmem, vmem, any_space, vmem),
        scratch_shapes=[
            pltpu.VMEM((PAIRS, 8, PAIR), F32),
            pltpu.VMEM((shards - 1,) + lines, F32),
            pltpu.VMEM((7,) + lines, F32),
            pltpu.VMEM((shards - 1, PAIRS, 8, PAIR), F32),
            pltpu.VMEM((7, PAIRS, 8, PAIR), F32),
            pltpu.VMEM(lines, F32),
            pltpu.VMEM((PAIRS, 8, PAIR), F32),
            dma((2,)), dma((2, shards - 1)), dma((2,)), dma((2, 7)), dma((reach,)), dma((reach,)),
        ] + reduction_scratch(4, shards, rows),
        compiler_params=pltpu.CompilerParams(
            collective_id=1, has_side_effects=True, vmem_limit_bytes=63 * 2**20
        ),
        cost_estimate=pl.CostEstimate(flops=55 * 10**9, bytes_accessed=4 * 10**8, transcendentals=13 * 10**6),
    )(grads, down, q_pre, k_pre, value_all, o_low, gathered, gains, grad_spre, gain_qk, bias_turned, lse, low_all)


def body(
    tokens,
    doc_lengths,
    cotangent,
    attn_w,
    ffn_w,
    attn_m,
    attn_v,
    ffn_m,
    ffn_v,
    gains_d,
    gains_ff,
    gd_m,
    gd_v,
    gf_m,
    gf_v,
):
    shards = lax.axis_size("shard")
    reps = lax.axis_size("rep")
    device_index = lax.axis_index("shard")
    rows = tokens.shape[0]
    reach = WINDOW // rows
    cols = (reach + 1) * rows
    attn_rows = attn_w.shape[1]
    ffn_rows = ffn_w.shape[1]
    ffn_all = shards * ffn_rows
    piece = ffn_rows // reps

    lengths_row = doc_lengths[0]
    starts = jnp.cumsum(lengths_row) - lengths_row
    positions = device_index * rows + jnp.arange(rows, dtype=jnp.int32)
    doc_start = jnp.max(
        jnp.where(starts[None, :] <= positions[:, None], starts[None, :], 0), axis=1
    )
    blocks = rows // QUERY_BLOCK
    span = WINDOW + QUERY_BLOCK
    query = jnp.arange(rows, dtype=jnp.int32).reshape(blocks, QUERY_BLOCK)
    lead = query[:, :1] - reach * rows + jnp.arange(span, dtype=jnp.int32)
    ahead = query[:, :, None] - lead[:, None, :]
    floor = (doc_start - device_index * rows).reshape(blocks, QUERY_BLOCK, 1)
    mask = (ahead >= 0) & (ahead < WINDOW) & (lead[:, None, :] >= floor)
    bias = jnp.where(mask, 0.0, NEGATIVE).astype(F32)
    bias_turned = bias.transpose(0, 2, 1)
    bias = bias.reshape(rows, span)
    cut = gains_d.size
    small = jnp.concatenate([gains_d.reshape(-1), gains_ff.reshape(-1)]).astype(BF16)
    normed_in, factor_in = rownorm(tokens.astype(F32))
    fast = reps == 8 and shards == 4 and attn_rows % HEAD_DIM == 0 and reach == 2
    if fast:
        small = small.astype(F32)
        qk_heads = small[:attn_rows].reshape(-1, HEAD_DIM)
        qk_heads = jnp.pad(
            jnp.concatenate([qk_heads, qk_heads], 1), ((0, 8 - qk_heads.shape[0]), (0, D - PAIR))
        )
        small = jnp.pad(small, (0, 8 * D - small.size)).reshape(8, D)
        gathered, small, low_all, q_pre, k_pre, value_all, o_low, lse = gather_attend(
            attn_w.reshape(8, piece, D),
            ffn_w.reshape(3, 8, piece, D),
            jnp.concatenate([qk_heads, small]),
            tokens,
            bias,
            shards,
        )
        small = small[:, 8:].reshape(shards, -1)[:, : cut + gains_ff.size]
        projection = (gathered, 3)
        ffn_low = [gathered.reshape(4, ffn_all, D)] * 3
        firsts = (1, 2, 3)
    else:
        attn_low = (
            gather_rows(attn_w.reshape(4 * attn_rows, D).astype(BF16))
            .reshape(shards, 4, attn_rows, D)
            .transpose(1, 0, 2, 3)
            .reshape(1, 4, HEADS, HEAD_DIM, D)
        )
        ffn_low = [gather_rows(ffn_w[m].astype(BF16)).reshape(1, ffn_all, D) for m in range(3)]
        firsts = (0, 0, 0)
        small = lax.all_gather(small, "shard", axis=0).astype(F32)
        query_low, key_low, value_low, out_low = (attn_low[0, j].reshape(D, D) for j in range(4))
        projection = (out_low.reshape(1, 1, D, D), 0)
    gd_all = small[:, :cut].reshape(shards, 3, -1).transpose(1, 0, 2).reshape(3, D)
    gf_all = small[:, cut:].reshape(shards, 2, ffn_rows).transpose(1, 0, 2).reshape(2, ffn_all)
    gain_qk = gd_all[0]

    if not fast:
        earlier = [from_behind(tokens, "shard", offset) for offset in range(reach, 0, -1)]
        low_all = rownorm(jnp.concatenate(earlier + [tokens], 0).astype(F32))[0].astype(BF16)
        q_pre, k_pre, value_all, o_low, lse = attention_forward(
            low_all, attn_low, gain_qk[None], bias, rows
        )
    in_low = low_all[-rows:]
    output, grad_spre, grad_in, ffn_grads, down_grads, grad_scale_up, grad_scale_gate, grad_alpha_ffn, grad_alpha_attn = (
        feed_forward(tokens, o_low, projection, cotangent, gd_all[1:], gf_all, ffn_low, firsts)
    )
    pair_gain = gain_qk.reshape(PAIRS, 1, PAIR)
    grad_gf = jnp.concatenate([grad_scale_up, grad_scale_gate])
    gd_rows = D // shards
    if fast:
        units = (shards, 4, 2, piece, D)
        grad_gd = jnp.concatenate([grad_alpha_attn, grad_alpha_ffn])
        small = jnp.concatenate(
            [
                grad_gd.reshape(2, shards, gd_rows).transpose(1, 0, 2).reshape(shards, -1),
                grad_gf.reshape(2, shards, ffn_rows).transpose(1, 0, 2).reshape(shards, -1),
            ],
            1,
        )
        small = jnp.pad(small, ((0, 0), (0, 8 * D - small.shape[1]))).reshape(shards, 8, D)
        summed, _, _, _, _, sum_small, sum_qk, back_got, back_own = backward_reduce(
            ffn_grads.reshape((2,) + units), down_grads.reshape(units), q_pre, k_pre, value_all, o_low, gathered,
            small, grad_spre, pair_gain, bias_turned, lse, low_all,
        )
        grad_in = grad_in + back_own
        for n in range(reach):
            sent = device_index + reach - n < shards
            grad_in = grad_in + jnp.where(sent, back_got[n], 0).astype(F32)
        sum_small = sum_small.reshape(-1)
        sum_qk = lax.dynamic_slice_in_dim(sum_qk[:, 0].reshape(D), device_index * gd_rows, gd_rows, 0)
        sum_gd = jnp.concatenate([sum_qk, sum_small[: 2 * gd_rows]]).reshape(3, gd_rows)
        sum_gf = sum_small[2 * gd_rows : 2 * gd_rows + 2 * ffn_rows].reshape(2, ffn_rows)
        attn_sums, ffn_sums = [(summed, 3)], [(summed, 0), (summed, 1), (summed, 2)]
    else:
        grad_qpre, grad_kpre, grad_vpre, gain_sums = attention_backward(
            q_pre, k_pre, value_all, o_low, grad_spre, attn_low, pair_gain, bias_turned, lse
        )
        grad_gain_qk = gain_sums[:, 0].reshape(D)
        back_all = dot(grad_kpre, key_low) + dot(grad_vpre, value_low)
        grad_in = grad_in + dot(grad_qpre, query_low) + back_all[reach * rows :]
        back_parts = back_all[: reach * rows].reshape(reach, rows, D).astype(BF16)
        for n in range(reach):
            grad_in = grad_in + from_behind(back_parts[n], "shard", n - reach).astype(F32)
        attn_grad = jnp.stack(
            [
                dot_tn(grad_qpre, in_low),
                dot_tn(grad_kpre, low_all),
                dot_tn(grad_vpre, low_all),
                dot_tn(o_low, grad_spre),
            ]
        ).astype(BF16)
        attn_grad = attn_grad.reshape(4, shards, attn_rows, D).transpose(1, 0, 2, 3)
        attn_grad = attn_grad.reshape(shards, reps, 4 * attn_rows // reps, D).transpose(1, 0, 2, 3)
        attn_sums = [(reduce_rows(attn_grad).reshape(1, 4, attn_rows, D), 0)]
        ready = (shards, reps, piece, D)
        ffn_sums = [
            (reduce_rows(part.reshape(ready).transpose(1, 0, 2, 3)).reshape(1, 1, ffn_rows, D), 0)
            for part in (ffn_grads[0], ffn_grads[1], down_grads)
        ]
        grad_small = jnp.concatenate(
            [grad_gain_qk, grad_alpha_attn[0], grad_alpha_ffn[0], grad_gf.reshape(-1)]
        )
        grad_small = lax.psum(grad_small, ("rep", "shard"))
        sum_gd = lax.dynamic_slice_in_dim(
            grad_small[: 3 * D].reshape(3, D), device_index * gd_rows, gd_rows, 1
        )
        sum_gf = lax.dynamic_slice_in_dim(
            grad_small[3 * D :].reshape(2, ffn_all), device_index * ffn_rows, ffn_rows, 1
        )
    grad_tokens = norm_back(normed_in, factor_in, grad_in)

    attn_unit, attn_m_new, attn_v_new = adam_rows(attn_w, attn_sums, attn_m, attn_v)
    ffn_unit, ffn_m_new, ffn_v_new = adam_rows(ffn_w, ffn_sums, ffn_m, ffn_v)
    gd_new, gd_m_new, gd_v_new = adam(gains_d, sum_gd, gd_m, gd_v, GAIN_RATE, 0.0)
    gf_new, gf_m_new, gf_v_new = adam(gains_ff, sum_gf, gf_m, gf_v, GAIN_RATE, 0.0)
    return (
        output,
        grad_tokens,
        attn_unit,
        attn_m_new,
        attn_v_new,
        ffn_unit,
        ffn_m_new,
        ffn_v_new,
        gd_new,
        gd_m_new,
        gd_v_new,
        gf_new,
        gf_m_new,
        gf_v_new,
    )

def solution(mesh):
    return jax.shard_map(
        body,
        mesh=mesh,
        in_specs=(
            P(("rep", "shard"), None),
            P("rep", None),
            P(("rep", "shard"), None),
            P(None, "shard", None),
            P(None, "shard", None),
            P(None, "shard", None),
            P(None, "shard", None),
            P(None, "shard", None),
            P(None, "shard", None),
            P(None, "shard"),
            P(None, "shard"),
            P(None, "shard"),
            P(None, "shard"),
            P(None, "shard"),
            P(None, "shard"),
        ),
        out_specs=(
            P(("rep", "shard"), None),
            P(("rep", "shard"), None),
            P(None, "shard", None),
            P(None, "shard", None),
            P(None, "shard", None),
            P(None, "shard", None),
            P(None, "shard", None),
            P(None, "shard", None),
            P(None, "shard"),
            P(None, "shard"),
            P(None, "shard"),
            P(None, "shard"),
            P(None, "shard"),
            P(None, "shard"),
        ),
        check_vma=False,
    )
```

```python
import functools
import math

import jax
import jax.numpy as jnp
from jax import lax
from jax.experimental import pallas as pl
from jax.experimental.pallas import tpu as pltpu
from jax.sharding import PartitionSpec as P

D = 1280
HEADS = 20
HEAD_DIM = 64
WINDOW = 1024
STEP = 10


SMALL = 1e-06
NEGATIVE = -1e30
BETA_ONE = 0.9
BETA_TWO = 0.95
RATE = 0.02
GAIN_RATE = 1.0
DECAY = 0.1
TINY = 1e-08
F32 = jnp.float32
BF16 = jnp.bfloat16


def from_behind(block, axis, distance):
    devices = range(lax.axis_size(axis))
    route = [(i - distance, i) for i in devices if i - distance in devices]
    return lax.ppermute(block, axis, route)


def rownorm(value):
    factor = lax.rsqrt(jnp.sum(value * value, -1, keepdims=True) + SMALL)
    return (value * factor, factor)


def norm_back(normed, factor, grad):
    return factor * (grad - normed * jnp.sum(normed * grad, -1, keepdims=True))


def adam(weight, grad, first, second, rate, decay):
    first = BETA_ONE * first + (1.0 - BETA_ONE) * grad
    second = BETA_TWO * second + (1.0 - BETA_TWO) * grad * grad
    fix_one = 1.0 - BETA_ONE**STEP
    fix_two = 1.0 - BETA_TWO**STEP
    change = first / fix_one / (jnp.sqrt(second / fix_two) + TINY) + decay * weight
    return (weight - rate * change, first, second)


def dot(a, b):
    return jnp.dot(a, b, preferred_element_type=F32)


def dot_nt(a, b):
    return lax.dot_general(a, b, (((1,), (1,)), ((), ())), preferred_element_type=F32)


def dot_tn(a, b):
    return lax.dot_general(a, b, (((0,), (0,)), ((), ())), preferred_element_type=F32)


def gather_rows(shard_rows):
    reps = lax.axis_size("rep")
    piece = shard_rows.shape[0] // reps
    mine = lax.dynamic_slice_in_dim(shard_rows, lax.axis_index("rep") * piece, piece, 0)
    column = lax.all_gather(mine, "shard", axis=0)
    return lax.all_gather(column, "rep", axis=1)


def reduce_rows(grad):
    part = lax.psum_scatter(grad, "rep", scatter_dimension=0)
    part = lax.psum_scatter(part, "shard", scatter_dimension=0)
    return lax.all_gather(part, "rep", axis=0, tiled=True)


MESH = pl.DeviceIdType.MESH
HALF = 80
RING = 8
HALF_RING = 4


def place():
    rep = lax.axis_index("rep")
    core, chip = lax.rem(rep, 2), rep // 2
    beside, above = chip + 1 - 2 * lax.rem(chip, 2), chip + 2 - 4 * (chip // 2)
    return core, chip, beside, above, 3 - chip


def remote(src, dst, send, recv, rep, shard):
    return pltpu.make_async_remote_copy(
        src_ref=src, dst_ref=dst, send_sem=send, recv_sem=recv,
        device_id=(rep, shard), device_id_type=MESH,
    )


def arrived(ref, sem):
    pltpu.make_async_copy(ref, ref, sem).wait()


def greet(shards):
    rep, line = lax.axis_index("rep"), lax.axis_index("shard")
    barrier = pltpu.get_barrier_semaphore()
    for n in range(1, 8):
        pl.semaphore_signal(barrier, inc=1, device_id=(lax.rem(rep + n, 8), line), device_id_type=MESH)
    for n in range(1, shards):
        pl.semaphore_signal(barrier, inc=1, device_id=(rep, lax.rem(line + n, shards)), device_id_type=MESH)
    pl.semaphore_wait(barrier, 6 + shards)


def add_into(target, sources, rows):
    def step(i, _):
        part = pl.ds(pl.multiple_of(i * 16, 16), 16)
        if len(sources) == 1:
            target[part, :] = target[part, :] + sources[0][part, :]
        else:
            value = target[part, :].astype(F32)
            for source in sources:
                value = value + source[part, :].astype(F32)
            target[part, :] = value.astype(BF16)
        return 0

    lax.fori_loop(0, rows // 16, step, 0, unroll=min(5, rows // 16))


def reduction_scratch(count, shards, rows):
    steps = count * shards
    dma = pltpu.SemaphoreType.DMA
    return [
        pltpu.VMEM((RING, 4, rows, D), BF16),
        pltpu.VMEM((2, 4, rows, D), BF16),
        pltpu.VMEM((HALF_RING, rows, D), BF16),
        pltpu.VMEM((HALF_RING, 2, rows, D), BF16),
        pltpu.VMEM((count, shards + 1, rows, D), BF16),
        dma((2,)), dma(()), dma((steps,)), dma((steps,)), dma((steps, 2)),
        dma((steps,)), dma((steps, 2)), dma((steps,)), dma((count, shards + 1)),
        dma((count,)), dma((count, 8)), dma((count,)), dma(()), pltpu.SemaphoreType.REGULAR,
    ]


def reduction(grads, out, scratch):
    (acc, own, half, piece, below, own_sem, pair_send, pair_recv, half_send, half_recv,
     piece_send, piece_recv, line_send, line_recv, out_send, out_recv, out_local, on_send, credit) = scratch
    count = len(grads)
    rows = own.shape[2]
    shards = below.shape[1] - 1
    core, chip, beside, above, across = place()
    line = lax.axis_index("shard")
    steps = count * shards
    mine, sibling = 2 * chip + core, 2 * chip + 1 - core
    one = piece.at[0, 0]

    def owner(step):
        i = lax.rem(step, shards)
        back = lax.select(i < shards - 1 - line, shards - 1 - i, i - (shards - 1 - line))
        ahead = lax.select(i < line, i, shards - 1 - (i - line))
        other = lax.select(2 * line < shards, back, ahead)
        return lax.select(i == shards - 1, line, other)

    def room(step):
        return acc.at[lax.rem(step, RING)]

    def begin(step):
        slot = lax.rem(step, 2)

        @pl.when(step >= RING)
        def _():
            pl.semaphore_wait(credit, 1)

        for n, grad in enumerate(grads):
            @pl.when(step // shards == n)
            def _(grad=grad):
                remote(grad.at[owner(step), :, 1 - core], room(step), pair_send, pair_recv.at[step], sibling, line).start()
                pltpu.make_async_copy(grad.at[owner(step), :, core], own.at[slot], own_sem.at[slot]).start()

    def first(step):
        slot, part = lax.rem(step, 2), lax.rem(step, HALF_RING)
        total = room(step)
        arrived(own.at[slot], own_sem.at[slot])
        arrived(total, pair_recv.at[step])
        for q in range(4):
            add_into(total.at[q], (own.at[slot, q],), rows)
        remote(total.at[across, pl.ds(0, HALF)], half.at[part, pl.ds(0, HALF)],
               half_send.at[step], half_recv.at[step, 0], 2 * beside + core, line).start()
        remote(total.at[across, pl.ds(HALF, rows - HALF)], half.at[part, pl.ds(HALF, rows - HALF)],
               half_send.at[step], half_recv.at[step, 1], 2 * above + core, line).start()

    def second(step):
        part = lax.rem(step, HALF_RING)
        total = room(step)
        low, high = half.at[part, pl.ds(0, HALF)], half.at[part, pl.ds(HALF, rows - HALF)]
        arrived(low, half_recv.at[step, 0])
        arrived(high, half_recv.at[step, 1])
        add_into(total.at[above, pl.ds(0, HALF)], (low,), HALF)
        add_into(total.at[beside, pl.ds(HALF, rows - HALF)], (high,), rows - HALF)
        remote(total.at[beside], piece.at[part, 0], piece_send.at[step], piece_recv.at[step, 0],
               2 * beside + core, line).start()
        remote(total.at[above], piece.at[part, 1], piece_send.at[step], piece_recv.at[step, 1],
               2 * above + core, line).start()

    def pass_on(step):
        m, target = step // shards, owner(step)

        @pl.when(target > line)
        def _():
            remote(room(step).at[chip], below.at[m, target], line_send.at[step], line_recv.at[m, target],
                   mine, line + 1).start()

        @pl.when(target < line)
        def _():
            slot = lax.select(target == line - 1, shards, target)
            remote(room(step).at[chip], below.at[m, slot], line_send.at[step], line_recv.at[m, slot],
                   mine, line - 1).start()

    def outermost(step):
        target = owner(step)
        return ((target > line) & (line == 0)) | ((target < line) & (line == shards - 1))

    def third(step):
        part = lax.rem(step, HALF_RING)
        for n in range(2):
            arrived(piece.at[part, n], piece_recv.at[step, n])
        add_into(room(step).at[chip], (piece.at[part, 0], piece.at[part, 1]), rows)

        @pl.when(outermost(step))
        def _():
            pass_on(step)

    def along(step):
        m, target = step // shards, owner(step)

        def add_line(slot):
            arrived(below.at[m, slot], line_recv.at[m, slot])
            add_into(room(step).at[chip], (below.at[m, slot],), rows)

        @pl.when(((target >= line) & (line > 0)) | ((target < line) & (line < shards - 1)))
        def _():
            add_line(target)

        @pl.when((target == line) & (line < shards - 1))
        def _():
            add_line(shards)

        @pl.when(jnp.logical_not(outermost(step)))
        def _():
            pass_on(step)

        @pl.when(target == line)
        def _():
            total = room(step).at[chip]
            pltpu.make_async_copy(total, out.at[m, mine], out_local.at[m]).start()
            for n, other in enumerate((2 * beside + core, 2 * above + core, sibling)):
                remote(total, out.at[m, mine], out_send.at[m], out_recv.at[m, n], other, line).start()

    def fourth(step):
        m = step // shards
        for n, (origin, other, part) in enumerate(
            (
                (2 * beside + core, 2 * above + core, pl.ds(0, HALF)),
                (2 * above + core, 2 * beside + core, pl.ds(HALF, rows - HALF)),
            )
        ):
            arrived(out.at[m, origin], out_recv.at[m, n])
            share = out.at[m, origin, part]
            remote(share, share, on_send, out_recv.at[m, 3 + n], other, line).start()
            remote(out.at[m, origin], out.at[m, origin], on_send, out_recv.at[m, 5 + n], sibling, line).start()

    def fifth(step):
        m, origin = step // shards, 2 * across + core
        arrived(out.at[m, origin, pl.ds(0, HALF)], out_recv.at[m, 3])
        arrived(out.at[m, origin, pl.ds(HALF, rows - HALF)], out_recv.at[m, 4])
        remote(out.at[m, origin], out.at[m, origin], on_send, out_recv.at[m, 7], sibling, line).start()

    def retire(step):
        m, target = step // shards, owner(step)
        arrived(one, half_send.at[step])
        arrived(piece.at[0], piece_send.at[step])

        @pl.when(target != line)
        def _():
            arrived(one, line_send.at[step])

        @pl.when(target == line)
        def _():
            arrived(acc.at[0, pl.ds(0, 3)], out_send.at[m])
            arrived(one, out_local.at[m])

        @pl.when(step + RING < steps)
        def _():
            pl.semaphore_signal(credit, inc=1, device_id=(sibling, line), device_id_type=MESH)

    def lead(t):
        @pl.when((t >= 6) & (t < steps + 6))
        def _():
            retire(t - 6)

        @pl.when(t == 0)
        def _():
            begin(0)

        @pl.when(t + 1 < steps)
        def _():
            begin(t + 1)

        @pl.when(t < steps)
        def _():
            first(t)

    def follow(t):
        @pl.when((t >= 1) & (t < steps + 1))
        def _():
            second(t - 1)

        @pl.when((t >= 3) & (t < steps + 3))
        def _():
            third(t - 3)

    def settle(t):
        @pl.when((t >= 4) & (t < steps + 4))
        def _():
            along(t - 4)

        @pl.when((t >= 5) & (t < steps + 5) & (lax.rem(t - 5, shards) == shards - 1))
        def _():
            fourth(t - 5)

        @pl.when((t >= 6) & (t < steps + 6) & (lax.rem(t - 6, shards) == shards - 1))
        def _():
            fifth(t - 6)

    def finish():
        for m in range(count):
            for n in (2, 5, 6, 7):
                arrived(out.at[m, 0], out_recv.at[m, n])
        arrived(out.at[:, pl.ds(0, 4)], on_send)

    return steps + 6, lead, follow, settle, finish, pair_send


UNITS = 256


def feed_kernel(blocks, tokens_ref, o_ref, wo_ref, cot_ref, alpha_attn_ref, alpha_ref, up_scale_ref, gate_scale_ref,
                wu_ref, wg_ref, wd_ref, out_ref, grad_side_ref, grad_in_ref, grad_ref, down_ref, up_sum_ref,
                gate_sum_ref, alpha_sum_ref, alpha_attn_sum_ref, up_buf, gate_buf, hidden_buf, total, back,
                grad_hidden_buf, grad_u_buf, grad_g_buf, up_now, gate_now, side_pre, middle_ref, mid_ref, grad_mid_ref):
    turn = pl.program_id(0)
    after = turn - blocks - 2
    rows = tokens_ref.shape[0]

    def inputs(part):
        normed = rownorm(tokens_ref[part, :].astype(F32))[0]
        side, side_factor = rownorm(side_pre[part, :])
        middle, mid_factor = rownorm(normed + alpha_attn_ref[...] * (side - normed))
        return normed, side, side_factor, middle, mid_factor

    def start_step():
        side_pre[...] = dot(o_ref[...], wo_ref[...].reshape(D, D))

        def step(i, _):
            part = pl.ds(pl.multiple_of(i * 32, 32), 32)
            middle = inputs(part)[3]
            middle_ref[part, :] = middle
            mid_ref[part, :] = middle.astype(BF16)
            return 0

        lax.fori_loop(0, rows // 32, step, 0, unroll=2)

    def end_step():
        alpha = alpha_attn_ref[...]

        def step(i, sums):
            part = pl.ds(pl.multiple_of(i * 32, 32), 32)
            normed, side, side_factor, middle, mid_factor = inputs(part)
            grad = norm_back(middle, mid_factor, grad_mid_ref[part, :])
            grad_in_ref[part, :] = grad * (1.0 - alpha)
            grad_side_ref[part, :] = norm_back(side, side_factor, grad * alpha).astype(BF16)
            return sums + jnp.sum(grad * (side - normed), 0, keepdims=True)

        alpha_attn_sum_ref[...] = lax.fori_loop(0, rows // 32, step, jnp.zeros((1, D), F32), unroll=2)

    def raw(block):
        up_raw, gate_raw = dot_nt(mid_ref[...], wu_ref[...]), dot_nt(mid_ref[...], wg_ref[...])
        up_now[...] = up_raw
        gate_now[...] = gate_raw
        up_buf[block] = up_raw.astype(BF16)
        gate_buf[block] = gate_raw.astype(BF16)

    def activate(block):
        gate = gate_now[...] * (gate_scale_ref[...] * math.sqrt(D))
        hidden = gate * jax.nn.sigmoid(gate) * (up_now[...] * up_scale_ref[...])
        hidden_buf[block] = hidden.astype(BF16)

    def project(block, first):
        part = dot(hidden_buf[block], wd_ref[...])
        total[...] = part if first else total[...] + part

    def middle_step():
        alpha = alpha_ref[...]

        def step(i, sums):
            part = pl.ds(pl.multiple_of(i * 32, 32), 32)
            branch, factor = rownorm(total[part, :])
            middle = middle_ref[part, :]
            final, final_factor = rownorm(middle + alpha * (branch - middle))
            out_ref[part, :] = final.astype(BF16)
            grad = norm_back(final, final_factor, cot_ref[part, :].astype(F32))
            grad_mid_ref[part, :] = grad * (1.0 - alpha)
            back[part, :] = norm_back(branch, factor, grad * alpha).astype(BF16)
            return sums + jnp.sum(grad * (branch - middle), 0, keepdims=True)

        alpha_sum_ref[...] = lax.fori_loop(0, rows // 32, step, jnp.zeros((1, D), F32), unroll=2)

    def back_raw():
        grad_hidden_buf[...] = dot_nt(back[...], wd_ref[...])

    def back_activate(block):
        up_scale, gate_scale = up_scale_ref[...], gate_scale_ref[...] * math.sqrt(D)
        grad_hidden = grad_hidden_buf[...]
        up_raw, gate_raw = up_buf[block].astype(F32), gate_buf[block].astype(F32)
        gate = gate_raw * gate_scale
        sigma = jax.nn.sigmoid(gate)
        active = gate * sigma
        upward = up_raw * up_scale
        grad_upward = grad_hidden * active
        grad_gate = grad_hidden * upward * (sigma * (1.0 + gate * (1.0 - sigma)))
        up_sum_ref[...] = jnp.sum(grad_upward * up_raw, 0, keepdims=True)
        gate_sum_ref[...] = jnp.sum(grad_gate * gate_raw, 0, keepdims=True) * math.sqrt(D)
        grad_u_buf[...] = (grad_upward * up_scale).astype(BF16)
        grad_g_buf[...] = (grad_gate * gate_scale).astype(BF16)

    def back_project(block):
        grad_u, grad_g = grad_u_buf[...], grad_g_buf[...]
        grad_ref[0] = dot_tn(grad_u, mid_ref[...]).astype(BF16)
        grad_ref[1] = dot_tn(grad_g, mid_ref[...]).astype(BF16)
        down_ref[...] = dot_tn(hidden_buf[block], back[...]).astype(BF16)
        grad_mid_ref[...] += dot(grad_u, wu_ref[...]) + dot(grad_g, wg_ref[...])

    @pl.when(turn == 0)
    def _():
        start_step()
        raw(0)

    @pl.when(turn == 1)
    def _():
        activate(0)
        raw(1)

    @pl.when(turn == 2)
    def _():
        project(0, True)
        activate(1)
        raw(2)

    @pl.when((turn > 2) & (turn < blocks))
    def _():
        project(turn - 2, False)
        activate(turn - 1)
        raw(turn)

    @pl.when(turn == blocks)
    def _():
        project(turn - 2, False)
        activate(turn - 1)

    @pl.when(turn == blocks + 1)
    def _():
        project(turn - 2, False)
        middle_step()

    @pl.when(after == 0)
    def _():
        back_raw()

    @pl.when(after == 1)
    def _():
        back_activate(0)
        back_raw()

    @pl.when((after > 1) & (after < blocks))
    def _():
        back_project(after - 2)
        back_activate(after - 1)
        back_raw()

    @pl.when(after == blocks)
    def _():
        back_project(after - 2)
        back_activate(after - 1)

    @pl.when(after == blocks + 1)
    def _():
        back_project(after - 2)
        end_step()


def feed_forward(tokens, o_low, projection, cotangent, alphas, scales, weights, firsts):
    rows = tokens.shape[0]
    out_low, place_of = projection
    _, parts, _, _ = out_low.shape
    blocks = scales.shape[1] // UNITS
    whole = lambda *shape: pl.BlockSpec(shape, lambda t: (0,) * len(shape))
    held = lambda *shape: pl.BlockSpec(shape, lambda t: (0,) * len(shape), pipeline_mode=pl.Buffered(1))
    half = blocks + 2

    def stage(t, early, late):
        return jnp.clip(lax.select(t < half, t - early, t - half - late), 0, blocks - 1)

    weight = lambda m, early, late: pl.BlockSpec((None, UNITS, D), lambda t: (m, stage(t, early, late), 0))
    done = lambda t, lag: jnp.clip(t - half - lag, 0, blocks - 1)
    units = pl.BlockSpec((1, UNITS), lambda t: (0, done(t, 1)))
    scale = pl.BlockSpec((1, UNITS), lambda t: (0, stage(t, 1, 1)))
    return pl.pallas_call(
        functools.partial(feed_kernel, blocks),
        grid=(2 * half,),
        out_shape=(
            jax.ShapeDtypeStruct((rows, D), BF16),
            jax.ShapeDtypeStruct((rows, D), BF16),
            jax.ShapeDtypeStruct((rows, D), F32),
            jax.ShapeDtypeStruct((2, blocks * UNITS, D), BF16),
            jax.ShapeDtypeStruct((blocks * UNITS, D), BF16),
            jax.ShapeDtypeStruct((1, blocks * UNITS), F32),
            jax.ShapeDtypeStruct((1, blocks * UNITS), F32),
            jax.ShapeDtypeStruct((1, D), F32),
            jax.ShapeDtypeStruct((1, D), F32),
        ),
        in_specs=[
            held(rows, D),
            held(rows, D),
            pl.BlockSpec((None, parts, D // parts, D), lambda t: (0, 0, place_of, 0), pipeline_mode=pl.Buffered(1)),
            held(rows, D),
            whole(1, D), whole(1, D), scale, scale,
        ]
        + [weight(firsts[0], 0, 2), weight(firsts[1], 0, 2), weight(firsts[2], 2, 0)],
        out_specs=(
            whole(rows, D), whole(rows, D), whole(rows, D),
            pl.BlockSpec((2, UNITS, D), lambda t: (0, done(t, 2), 0)),
            pl.BlockSpec((UNITS, D), lambda t: (done(t, 2), 0)),
            units, units, whole(1, D), whole(1, D),
        ),
        scratch_shapes=[
            pltpu.VMEM((blocks, rows, UNITS), BF16),
            pltpu.VMEM((blocks, rows, UNITS), BF16),
            pltpu.VMEM((blocks, rows, UNITS), BF16),
            pltpu.VMEM((rows, D), F32),
            pltpu.VMEM((rows, D), BF16),
            pltpu.VMEM((rows, UNITS), F32),
            pltpu.VMEM((rows, UNITS), BF16),
            pltpu.VMEM((rows, UNITS), BF16),
            pltpu.VMEM((rows, UNITS), F32),
            pltpu.VMEM((rows, UNITS), F32),
            pltpu.VMEM((rows, D), F32),
            pltpu.VMEM((rows, D), F32),
            pltpu.VMEM((rows, D), BF16),
            pltpu.VMEM((rows, D), F32),
        ],
        compiler_params=pltpu.CompilerParams(vmem_limit_bytes=62 * 2**20),
        cost_estimate=pl.CostEstimate(flops=60 * 10**9, bytes_accessed=120 * 10**6, transcendentals=5 * 10**6),
    )(tokens, o_low, out_low, cotangent, alphas[:1], alphas[1:], scales[:1], scales[1:], *weights)


def adam_kernel(places, per, *refs):
    grads = refs[:places]
    w_ref, m_ref, v_ref, w_out, m_out, v_out = refs[places:]
    group, piece, _ = w_ref.shape

    def update(g_ref):
        for n in range(group):
            def step(i, _, n=n):
                part = (n, pl.ds(pl.multiple_of(i * 16, 16), 16), slice(None))
                new, first, second = adam(
                    w_ref[part], g_ref[part].astype(F32), m_ref[part], v_ref[part], RATE, DECAY
                )
                w_out[part] = rownorm(new)[0]
                m_out[part] = first
                v_out[part] = second
                return 0

            lax.fori_loop(0, piece // 16, step, 0, unroll=5)

    for n in range(places):
        @pl.when(pl.program_id(0) // per == n)
        def _(n=n):
            update(grads[n])


def adam_rows(weight, grads, first, second):
    places = len(grads)
    _, per, piece, _ = grads[0][0].shape
    group = 2 if per % 2 == 0 else 1
    steps = per // group
    spec = pl.BlockSpec((group, piece, D), lambda p: (p, 0, 0))

    def grad_spec(n, index):
        return pl.BlockSpec(
            (None, group, piece, D), lambda p: (index, jnp.clip(p - n * steps, 0, steps - 1), 0, 0)
        )

    shape = jax.ShapeDtypeStruct((places * per, piece, D), F32)
    news = pl.pallas_call(
        functools.partial(adam_kernel, places, steps),
        grid=(places * steps,),
        out_shape=(shape,) * 3,
        in_specs=[grad_spec(n, index) for n, (_, index) in enumerate(grads)] + [spec] * 3,
        out_specs=(spec,) * 3,
        compiler_params=pltpu.CompilerParams(vmem_limit_bytes=60 * 2**20),
        cost_estimate=pl.CostEstimate(flops=20 * weight.size, bytes_accessed=26 * weight.size, transcendentals=0),
    )(*(array for array, _ in grads), *(old.reshape(shape.shape) for old in (weight, first, second)))
    return tuple(new.reshape(weight.shape) for new in news)


QUERY_BLOCK = 256
PAIR = 2 * HEAD_DIM
PAIRS = HEADS // 2


def head_ones():
    row = lax.broadcasted_iota(jnp.int32, (PAIR, PAIR), 0) // HEAD_DIM
    col = lax.broadcasted_iota(jnp.int32, (PAIR, PAIR), 1) // HEAD_DIM
    return (row == col).astype(F32).astype(BF16)


def head_sum(value, ones):
    high = value.astype(BF16)
    rest = (value - high.astype(F32)).astype(BF16)
    return dot(high, ones) + dot(rest, ones)


def of_head(value, head):
    lane = lax.broadcasted_iota(jnp.int32, value.shape, 1) // HEAD_DIM
    return jnp.where(lane == head, value, jnp.zeros_like(value))


def attend_pair(h_ref, wq_ref, wq2_ref, wk_ref, wk2_ref, wv_ref, wv2_ref, gain_ref, bias_ref, qp_ref, kp_ref, v_ref, o_ref, lse_ref,
                key_buf, query_buf, value_buf):
    cols = h_ref.shape[0]
    rows = qp_ref.shape[0]
    span = bias_ref.shape[1]
    ones = head_ones()
    gain = gain_ref[...]
    weights = jnp.concatenate([wk_ref[...], wk2_ref[...], wv_ref[...], wv2_ref[...]], 0)
    query_weights = jnp.concatenate([wq_ref[...], wq2_ref[...]], 0)

    def project(i, _):
        part = pl.ds(pl.multiple_of(i * QUERY_BLOCK, QUERY_BLOCK), QUERY_BLOCK)
        both = dot_nt(h_ref[part, :], weights)
        keys = both[:, :PAIR]
        kp_ref[part, :] = keys
        factor = lax.rsqrt(head_sum(keys * keys, ones) + SMALL)
        key_buf[part, :] = (keys * factor * gain).astype(BF16)
        values = both[:, PAIR:].astype(BF16)
        v_ref[part, :] = values
        value_buf[part, :PAIR] = values
        value_buf[part, PAIR:] = jnp.ones_like(values)
        return 0

    lax.fori_loop(0, cols // QUERY_BLOCK, project, 0)

    def project_queries(i, _):
        part = pl.ds(pl.multiple_of(i * QUERY_BLOCK, QUERY_BLOCK), QUERY_BLOCK)
        own = pl.ds(pl.multiple_of(cols - rows + i * QUERY_BLOCK, QUERY_BLOCK), QUERY_BLOCK)
        queries = dot_nt(h_ref[own, :], query_weights)
        qp_ref[part, :] = queries
        factor = lax.rsqrt(head_sum(queries * queries, ones) + SMALL)
        scaled = (queries * factor * gain).astype(BF16).astype(F32) * math.sqrt(HEAD_DIM)
        query_buf[part, :] = scaled.astype(BF16)
        return 0

    lax.fori_loop(0, rows // QUERY_BLOCK, project_queries, 0)
    for i in range(rows // QUERY_BLOCK):
        part = pl.ds(i * QUERY_BLOCK, QUERY_BLOCK)
        reach = pl.ds(i * QUERY_BLOCK, span)
        sides = []
        for head in range(2):
            scores = dot_nt(of_head(query_buf[part, :], head), key_buf[reach, :])
            probs = jnp.exp(scores + bias_ref[part, :]).astype(BF16)
            both = dot(probs, value_buf[reach, :])
            total = both[:, PAIR:]
            sides.append(both[:, :PAIR] / total)
            lse_ref[head : head + 1, part] = jnp.log(total).T[:1, :]
        lane = lax.broadcasted_iota(jnp.int32, sides[0].shape, 1)
        o_ref[part, :] = jnp.where(lane < HEAD_DIM, sides[0], sides[1]).astype(BF16)


def back_pair(*refs):
    start, block, finish = back_parts(*refs)
    start()
    for i in range(refs[0].shape[0] // QUERY_BLOCK):
        block(i)
    finish()


def back_parts(qp_ref, kp_ref, v_ref, o_ref, da_ref, wo_ref, wo2_ref, gain_ref, bias_ref, lse_ref,
               dq_ref, dk_ref, dv_ref, sum_ref, key_buf, key_turned, k_total, v_total):
    cols = kp_ref.shape[0]
    rows = qp_ref.shape[0]
    span = bias_ref.shape[1]

    def keys_of(i, _):
        ones, gain = head_ones(), gain_ref[...]
        part = pl.ds(pl.multiple_of(i * QUERY_BLOCK, QUERY_BLOCK), QUERY_BLOCK)
        keys = kp_ref[part, :]
        factor = lax.rsqrt(head_sum(keys * keys, ones) + SMALL)
        low = keys * factor * gain
        key_buf[part, :] = low.astype(BF16)
        key_turned[:, part] = low.T.astype(BF16)
        k_total[part, :] = jnp.zeros_like(keys)
        v_total[part, :] = jnp.zeros_like(keys)
        return 0

    def start():
        lax.fori_loop(0, cols // QUERY_BLOCK, keys_of, 0)

    def block(i):
        ones, gain = head_ones(), gain_ref[...]
        weights = jnp.concatenate([wo_ref[...], wo2_ref[...]], 0)
        part = pl.ds(i * QUERY_BLOCK, QUERY_BLOCK)
        reach = pl.ds(i * QUERY_BLOCK, span)
        queries = qp_ref[part, :]
        factor = lax.rsqrt(head_sum(queries * queries, ones) + SMALL)
        hat = queries * factor
        scaled = ((hat * gain).astype(BF16).astype(F32) * math.sqrt(HEAD_DIM)).astype(BF16)
        back = dot_nt(da_ref[part, :], weights).astype(BF16)
        inner = (back.astype(F32) * o_ref[part, :].astype(F32)).T
        sides = []
        for head in range(2):
            mine = slice(head * HEAD_DIM, (head + 1) * HEAD_DIM)
            query, grad = of_head(scaled, head), of_head(back, head)
            scores = dot_nt(key_buf[reach, :], query)
            probs = jnp.exp(scores + bias_ref[i] - lse_ref[head : head + 1, part])
            v_total[reach, :] += dot(probs.astype(BF16), grad)
            delta = jnp.sum(inner[mine, :], 0, keepdims=True)
            grad_scores = (probs * (dot_nt(v_ref[reach, :], grad) - delta)).astype(BF16)
            k_total[reach, :] += dot(grad_scores, query)
            sides.append(dot(key_turned[mine, reach], grad_scores))
        grad_q = jnp.concatenate(sides, 0).T * math.sqrt(HEAD_DIM)
        sums = jnp.sum(grad_q * hat, 0, keepdims=True)
        if i == 0:
            sum_ref[...] = jnp.broadcast_to(sums, sum_ref.shape)
        else:
            sum_ref[...] += jnp.broadcast_to(sums, sum_ref.shape)
        grad_q = grad_q * gain
        dq_ref[part, :] = (factor * (grad_q - hat * head_sum(hat * grad_q, ones))).astype(BF16)

    def close(i, _):
        ones, gain = head_ones(), gain_ref[...]
        part = pl.ds(pl.multiple_of(i * QUERY_BLOCK, QUERY_BLOCK), QUERY_BLOCK)
        keys = kp_ref[part, :]
        factor = lax.rsqrt(head_sum(keys * keys, ones) + SMALL)
        hat = keys * factor
        grad_k = k_total[part, :]
        sum_ref[...] += jnp.broadcast_to(jnp.sum(grad_k * hat, 0, keepdims=True), sum_ref.shape)
        grad_k = grad_k * gain
        dk_ref[part, :] = (factor * (grad_k - hat * head_sum(hat * grad_k, ones))).astype(BF16)
        dv_ref[part, :] = v_total[part, :].astype(BF16)
        return 0

    def finish():
        lax.fori_loop(0, cols // QUERY_BLOCK, close, 0)

    return start, block, finish


def head_rows(attn_low, matrix, second):
    heads = attn_low.shape[2]

    def index(p):
        head = 2 * p + second
        return (head // heads, matrix, lax.rem(head, heads), 0, 0)

    return pl.BlockSpec((None, None, None, HEAD_DIM, D), index)


def attention_forward(low_all, attn_low, gain_qk, bias, rows):
    cols = low_all.shape[0]
    span = bias.shape[1]
    side = lambda n: pl.BlockSpec((n, PAIR), lambda p: (0, p))
    whole = lambda *shape: pl.BlockSpec(shape, lambda p: (0,) * len(shape))
    return pl.pallas_call(
        attend_pair,
        grid=(PAIRS,),
        out_shape=(
            jax.ShapeDtypeStruct((rows, D), F32),
            jax.ShapeDtypeStruct((cols, D), F32),
            jax.ShapeDtypeStruct((cols, D), BF16),
            jax.ShapeDtypeStruct((rows, D), BF16),
            jax.ShapeDtypeStruct((PAIRS, 8, rows), F32),
        ),
        in_specs=[whole(cols, D)]
        + [head_rows(attn_low, j, second) for j in range(3) for second in range(2)]
        + [side(1), whole(rows, span)],
        out_specs=(side(rows), side(cols), side(cols), side(rows),
                   pl.BlockSpec((None, 8, rows), lambda p: (p, 0, 0))),
        scratch_shapes=[
            pltpu.VMEM((cols, PAIR), BF16),
            pltpu.VMEM((rows, PAIR), BF16),
            pltpu.VMEM((cols, 2 * PAIR), BF16),
        ],
        compiler_params=pltpu.CompilerParams(vmem_limit_bytes=56 * 2**20),
        cost_estimate=pl.CostEstimate(flops=20 * 10**9, bytes_accessed=30 * 10**6, transcendentals=13 * 10**6),
    )(low_all, *[attn_low] * 6, gain_qk, bias)


def attention_backward(q_pre, k_pre, value_all, o_low, grad_spre, attn_low, gain_qk, bias_turned, lse):
    rows, cols = q_pre.shape[0], k_pre.shape[0]
    side = lambda n: pl.BlockSpec((n, PAIR), lambda p: (0, p))
    whole = lambda *shape: pl.BlockSpec(shape, lambda p: (0,) * len(shape))
    stat = pl.BlockSpec((None, 8, rows), lambda p: (p, 0, 0))
    return pl.pallas_call(
        back_pair,
        grid=(PAIRS,),
        out_shape=(
            jax.ShapeDtypeStruct((rows, D), BF16),
            jax.ShapeDtypeStruct((cols, D), BF16),
            jax.ShapeDtypeStruct((cols, D), BF16),
            jax.ShapeDtypeStruct((PAIRS, 8, PAIR), F32),
        ),
        in_specs=[
            side(rows), side(cols), side(cols), side(rows), whole(rows, D),
            head_rows(attn_low, 3, 0), head_rows(attn_low, 3, 1),
            pl.BlockSpec((None, 1, PAIR), lambda p: (p, 0, 0)), whole(*bias_turned.shape), stat,
        ],
        out_specs=(side(rows), side(cols), side(cols), pl.BlockSpec((None, 8, PAIR), lambda p: (p, 0, 0))),
        scratch_shapes=[
            pltpu.VMEM((cols, PAIR), BF16),
            pltpu.VMEM((PAIR, cols), BF16),
            pltpu.VMEM((cols, PAIR), F32),
            pltpu.VMEM((cols, PAIR), F32),
        ],
        compiler_params=pltpu.CompilerParams(vmem_limit_bytes=56 * 2**20),
        cost_estimate=pl.CostEstimate(flops=30 * 10**9, bytes_accessed=40 * 10**6, transcendentals=13 * 10**6),
    )(q_pre, k_pre, value_all, o_low, grad_spre, attn_low, attn_low, gain_qk, bias_turned, lse)


START = 5


def gather_kernel(shards, attn_ref, ffn_ref, gains_ref, tokens_ref, bias_ref,
                  out, gains_out, h_out, qp_out, kp_out, v_out, o_out, lse_ref,
                  wide, low, mine, wide_sem, low_sem, mine_sem, line_send, line_recv, plane_send, beside_recv,
                  above_recv, across_recv, pair_send, pair_recv, gains_send, gains_recv, tokens_send,
                  tokens_recv, local_sem, gains_buf, before, h_buf, load_sem, store_sem,
                  weight_buf, gain_row, qp_buf, kp_buf, v_buf, o_buf, key_buf, query_buf, value_buf):
    core, chip, beside, above, across = place()
    line = lax.axis_index("shard")
    rep = 2 * chip + core
    sibling = 2 * chip + 1 - core
    to_beside, to_above = 2 * beside + core, 2 * above + core
    piece = attn_ref.shape[1]
    rows = tokens_ref.shape[0]
    heads = 2 * piece // HEAD_DIM
    others = shards - 1
    steps = 4 * others
    greet(shards)

    def rows_of(m, shard, rep, start=0, size=None):
        first = pl.multiple_of(rep * piece + start, 16)
        return out.at[m, shard, pl.ds(first, piece if size is None else size)]

    def source(n):
        low_side = 2 * line < shards
        edge = lax.select(low_side, line, shards - 1 - line)
        near = lax.select(lax.rem(n, 2) == 0, edge - 1 - n // 2, edge + 1 + n // 2)
        found = lax.select(n < 2 * edge, near, n + 1)
        return lax.select(low_side, found, shards - 1 - found)

    def own_send(m):
        @pl.when(line < shards - 1)
        def _():
            remote(mine.at[m], rows_of(m, line, rep), line_send, line_recv.at[m, line], rep, line + 1).start()

        @pl.when(line > 0)
        def _():
            remote(mine.at[m], rows_of(m, line, rep), line_send, line_recv.at[m, line], rep, line - 1).start()

    def fetch(index, slot):
        @pl.when(index < 8)
        def _():
            pltpu.make_async_copy(attn_ref.at[lax.rem(index, 8)], wide.at[slot], wide_sem.at[slot]).start()

        @pl.when(index >= 8)
        def _():
            pltpu.make_async_copy(
                ffn_ref.at[jnp.maximum(index // 8 - 1, 0), lax.rem(index, 8)], wide.at[slot], wide_sem.at[slot]
            ).start()

    def store(index, slot):
        return pltpu.make_async_copy(low.at[slot], rows_of(index // 8, line, lax.rem(index, 8)), low_sem.at[slot])

    def lower(src, dst):
        def step(i, _):
            part = pl.ds(pl.multiple_of(i * 32, 32), 32)
            dst[part, :] = src[part, :].astype(BF16)
            return 0

        lax.fori_loop(0, piece // 32, step, 0)

    for n in range(1, shards):
        other = lax.rem(line + n, shards)
        remote(gains_ref, gains_buf.at[line], gains_send, gains_recv.at[line], rep, other).start()
    pltpu.make_async_copy(gains_ref, gains_buf.at[line], local_sem).start()
    own = pl.ds(2 * rows, rows)
    pltpu.make_async_copy(tokens_ref, h_buf.at[own], load_sem.at[0, 0]).start()
    for m in range(4):
        origin = attn_ref.at[rep] if m == 0 else ffn_ref.at[m - 1, rep]
        pltpu.make_async_copy(origin, wide.at[m], mine_sem.at[m]).start()
    for m in range(4):
        arrived(wide.at[m], mine_sem.at[m])
        lower(wide.at[m], mine.at[m])
        if m == 0:
            own_send(0)

            @pl.when(line < shards - 1)
            def _():
                remote(tokens_ref, before.at[1], tokens_send, tokens_recv.at[1], rep, line + 1).start()

    for n in range(2):
        fetch(n, n)

    def norm_rows(source, first):
        def step(i, _):
            at = pl.multiple_of(first + i * 32, 32)
            value = source[pl.ds(pl.multiple_of(i * 32, 32), 32), :].astype(F32)
            h_buf[pl.ds(at, 32), :] = rownorm(value)[0].astype(BF16)
            return 0

        lax.fori_loop(0, rows // 32, step, 0)

    def clear_rows(first):
        h_buf[pl.ds(first, rows), :] = jnp.zeros((rows, D), BF16)

    arrived(h_buf.at[own], load_sem.at[0, 0])
    norm_rows(h_buf.at[own], 2 * rows)

    def loads(p, slot):
        copies = []
        for j in range(3):
            for second in range(2):
                head = 2 * p + second
                first = pl.multiple_of(2 * piece * j + HEAD_DIM * lax.rem(head, heads), HEAD_DIM)
                copies.append(
                    pltpu.make_async_copy(
                        out.at[0, head // heads, pl.ds(first, HEAD_DIM)], weight_buf.at[slot, 2 * j + second],
                        load_sem.at[slot, 2 * j + second],
                    )
                )
        return copies

    def stores(p, slot):
        lanes = pl.ds(pl.multiple_of(p * PAIR, PAIR), PAIR)
        return [
            pltpu.make_async_copy(buf.at[slot], ref.at[:, lanes], store_sem.at[slot, n])
            for n, (ref, buf) in enumerate(((qp_out, qp_buf), (kp_out, kp_buf), (v_out, v_buf), (o_out, o_buf)))
        ]

    def pair(p):
        slot = lax.rem(p, 2)

        @pl.when(p + 1 < PAIRS)
        def _():
            for copy in loads(p + 1, 1 - slot):
                copy.start()

        for copy in loads(p, slot):
            copy.wait()

        @pl.when(p >= 2)
        def _():
            for copy in stores(p - 2, slot):
                copy.wait()

        row = lax.broadcasted_iota(jnp.int32, (8, PAIR), 0)
        left, right = (
            jnp.sum(
                jnp.where(row == lax.rem(2 * p + n, heads), gains_buf[(2 * p + n) // heads, :8, :PAIR], 0.0),
                0, keepdims=True,
            )
            for n in range(2)
        )
        lane = lax.broadcasted_iota(jnp.int32, (1, PAIR), 1)
        gain_row[...] = jnp.where(lane < HEAD_DIM, left, right)
        attend_pair(
            h_buf, *(weight_buf.at[slot, n] for n in range(6)), gain_row, bias_ref, qp_buf.at[slot],
            kp_buf.at[slot], v_buf.at[slot], o_buf.at[slot], lse_ref.at[p], key_buf, query_buf, value_buf,
        )
        for copy in stores(p, slot):
            copy.start()

    def begin(c):
        m, origin = c // others, source(lax.rem(c, others))
        got = rows_of(m, origin, rep)
        arrived(got, line_recv.at[m, origin])

        @pl.when((origin < line) & (line < shards - 1))
        def _():
            remote(got, got, line_send, line_recv.at[m, origin], rep, line + 1).start()

        @pl.when((origin > line) & (line > 0))
        def _():
            remote(got, got, line_send, line_recv.at[m, origin], rep, line - 1).start()

        remote(got, got, plane_send, beside_recv.at[m, origin], to_beside, line).start()
        remote(got, got, plane_send, above_recv.at[m, origin], to_above, line).start()
        remote(got, got, pair_send, pair_recv.at[m], sibling, line).start()

    def middle(c):
        m, origin = c // others, source(lax.rem(c, others))
        got = rows_of(m, origin, to_beside)
        arrived(got, beside_recv.at[m, origin])
        part = rows_of(m, origin, to_beside, 0, HALF)
        remote(part, part, plane_send, across_recv.at[m, origin, 0], to_above, line).start()
        remote(got, got, pair_send, pair_recv.at[m], sibling, line).start()
        got = rows_of(m, origin, to_above)
        arrived(got, above_recv.at[m, origin])
        part = rows_of(m, origin, to_above, HALF, piece - HALF)
        remote(part, part, plane_send, across_recv.at[m, origin, 1], to_beside, line).start()
        remote(got, got, pair_send, pair_recv.at[m], sibling, line).start()

    def last(c):
        m, origin = c // others, source(lax.rem(c, others))
        got = rows_of(m, origin, 2 * across + core)
        arrived(rows_of(m, origin, 2 * across + core, 0, HALF), across_recv.at[m, origin, 0])
        arrived(rows_of(m, origin, 2 * across + core, HALF, piece - HALF), across_recv.at[m, origin, 1])
        remote(got, got, pair_send, pair_recv.at[m], sibling, line).start()

    def local(t):
        for n in range(2):
            index = 2 * t + n
            slot = 2 * lax.rem(t, 2) + n
            arrived(wide.at[slot], wide_sem.at[slot])

            @pl.when(index + 2 < 32)
            def _():
                fetch(index + 2, lax.rem(slot + 2, 4))

            @pl.when(t >= 2)
            def _():
                store(index - 4, slot).wait()

            lower(wide.at[slot], low.at[slot])
            store(index, slot).start()

    def turn(t, _):
        @pl.when((lax.rem(t, others) == 0) & (t // others < 3))
        def _():
            own_send(t // others + 1)

        @pl.when(t < steps)
        def _():
            begin(t)

        @pl.when((t == 1) & (line > 0))
        def _():
            arrived(before.at[1], tokens_recv.at[1])

            @pl.when(line < shards - 1)
            def _():
                remote(before.at[1], before.at[0], tokens_send, tokens_recv.at[0], rep, line + 1).start()

            norm_rows(before.at[1], rows)

        @pl.when((t == 1) & (line == 0))
        def _():
            clear_rows(rows)

        @pl.when((t == 3) & (line > 1))
        def _():
            arrived(before.at[0], tokens_recv.at[0])
            norm_rows(before.at[0], 0)

        @pl.when((t == 3) & (line <= 1))
        def _():
            clear_rows(0)

        @pl.when(t < 2)
        def _():
            local(2 * t)
            local(2 * t + 1)

        @pl.when(t >= 2)
        def _():
            local(t + 2)

        @pl.when(t == START)
        def _():
            pltpu.make_async_copy(gains_ref, gains_buf.at[line], local_sem).wait()
            for n in range(1, shards):
                other = lax.rem(line + n, shards)
                arrived(gains_buf.at[other], gains_recv.at[other])
            arrived(out.at[0, pl.ds(0, others), pl.ds(0, 4 * piece)], pair_recv.at[0])
            for copy in loads(0, 0):
                copy.start()

        early = (t > START + 3).astype(jnp.int32) + (t > START + 6).astype(jnp.int32)
        most = lax.select((t == START + 3) | (t == START + 6), 2, 1)

        def one(n, _):
            pair(t - START + early + n)
            return 0

        lax.fori_loop(0, lax.select((t >= START) & (t < START + PAIRS - 2), most, 0), one, 0)

        @pl.when((t >= 1) & (t < steps + 1))
        def _():
            middle(t - 1)

        @pl.when((t >= 2) & (t < steps + 2))
        def _():
            last(t - 2)

        return 0

    lax.fori_loop(0, 14, turn, 0)
    for n in range(4):
        store(28 + n, n).wait()
    gains_copy = pltpu.make_async_copy(gains_buf, gains_out, local_sem)
    h_copy = pltpu.make_async_copy(h_buf, h_out, load_sem.at[0, 0])
    gains_copy.start()
    h_copy.start()
    for p in (PAIRS - 2, PAIRS - 1):
        for copy in stores(p, p % 2):
            copy.wait()
    for m in range(1, 4):
        arrived(out.at[m, pl.ds(0, others), pl.ds(0, 4 * piece)], pair_recv.at[m])
    gains_copy.wait()
    h_copy.wait()

    @pl.when((line == 1) | (line == shards - 2))
    def _():
        arrived(before, tokens_send)

    @pl.when(line == 0)
    def _():
        arrived(before.at[0], tokens_send)

    @pl.when((line == 0) | (line == shards - 1))
    def _():
        arrived(out.at[:, 0, pl.ds(0, piece)], line_send)

    @pl.when((line > 0) & (line < shards - 1))
    def _():
        arrived(out.at[:, 0, pl.ds(0, 5 * piece)], line_send)

    arrived(out.at[:, pl.ds(0, others), pl.ds(0, 3 * piece)], plane_send)
    arrived(out.at[:, pl.ds(0, others), pl.ds(0, 4 * piece)], pair_send)
    arrived(gains_buf.at[pl.ds(0, others)], gains_send)


def gather_attend(attn_w, ffn_w, gains, tokens, bias, shards):
    piece = attn_w.shape[1]
    rows = tokens.shape[0]
    cols = rows + WINDOW
    any_space = pl.BlockSpec(memory_space=pl.ANY)
    vmem = pl.BlockSpec(memory_space=pltpu.VMEM)
    dma = pltpu.SemaphoreType.DMA
    return pl.pallas_call(
        functools.partial(gather_kernel, shards),
        out_shape=(
            jax.ShapeDtypeStruct((4, shards, 8 * piece, D), BF16),
            jax.ShapeDtypeStruct((shards,) + gains.shape, F32),
            jax.ShapeDtypeStruct((cols, D), BF16),
            jax.ShapeDtypeStruct((rows, D), F32),
            jax.ShapeDtypeStruct((cols, D), F32),
            jax.ShapeDtypeStruct((cols, D), BF16),
            jax.ShapeDtypeStruct((rows, D), BF16),
            jax.ShapeDtypeStruct((PAIRS, 8, rows), F32),
        ),
        in_specs=[any_space] * 4 + [vmem],
        out_specs=(any_space,) * 7 + (vmem,),
        scratch_shapes=[
            pltpu.VMEM((4, piece, D), F32),
            pltpu.VMEM((4, piece, D), BF16),
            pltpu.VMEM((4, piece, D), BF16),
            dma((4,)), dma((4,)), dma((4,)), dma(()), dma((4, shards)), dma(()), dma((4, shards)),
            dma((4, shards)), dma((4, shards, 2)), dma(()), dma((4,)), dma(()), dma((shards,)), dma(()),
            dma((2,)), dma(()),
            pltpu.VMEM((shards,) + gains.shape, F32),
            pltpu.VMEM((2, rows, D), BF16),
            pltpu.VMEM((cols, D), BF16),
            dma((2, 6)), dma((2, 4)),
            pltpu.VMEM((2, 6, HEAD_DIM, D), BF16),
            pltpu.VMEM((1, PAIR), F32),
            pltpu.VMEM((2, rows, PAIR), F32),
            pltpu.VMEM((2, cols, PAIR), F32),
            pltpu.VMEM((2, cols, PAIR), BF16),
            pltpu.VMEM((2, rows, PAIR), BF16),
            pltpu.VMEM((cols, PAIR), BF16),
            pltpu.VMEM((rows, PAIR), BF16),
            pltpu.VMEM((cols, 2 * PAIR), BF16),
        ],
        compiler_params=pltpu.CompilerParams(
            collective_id=3, has_side_effects=True, vmem_limit_bytes=60 * 2**20
        ),
        cost_estimate=pl.CostEstimate(flops=20 * 10**9, bytes_accessed=2 * 10**8, transcendentals=13 * 10**6),
    )(attn_w, ffn_w, gains, tokens, bias)


BACK_BLOCK = 256


def backward_kernel(shards, grads_ref, down_ref, qp_ref, kp_ref, v_ref, o_ref, weight_ref, gains_ref, da_ref, gain_ref,
                    bias_ref, lse_ref, h_ref, out, dq_ref, dk_ref, dv_ref, turned_ref, gains_out, sums_out, back_out,
                    own_out, sums, line_got, plane_got, line_sums, plane_sums, mine_gains, mine_sums, line_send, line_recv, plane_send,
                    plane_recv, back_send, back_recv, *scratch):
    rep, line = lax.axis_index("rep"), lax.axis_index("shard")
    grads = (grads_ref.at[0], grads_ref.at[1], down_ref, turned_ref)
    turns, lead, follow, settle, finish, pair_send = reduction(grads, out, scratch)
    height = weight_ref.shape[2] // 4
    heads = height // HEAD_DIM
    rows, cols = da_ref.shape[0], h_ref.shape[0]
    reach = back_out.shape[0]
    per = rows // BACK_BLOCK
    attended = PAIRS + 1
    dma = pltpu.SemaphoreType.DMA
    greet(shards)

    def attention(qp_buf, kp_buf, v_buf, o_buf, wo_buf, dq_buf, dk_buf, dv_buf, turned_buf, load_sem, store_sem,
                  key_buf, key_turned, k_total, v_total):
        def loads(p, slot):
            lanes = pl.ds(pl.multiple_of(p * PAIR, PAIR), PAIR)
            copies = [
                pltpu.make_async_copy(ref.at[:, lanes], buf.at[slot], load_sem.at[slot, n])
                for n, (ref, buf) in enumerate(((qp_ref, qp_buf), (kp_ref, kp_buf), (v_ref, v_buf), (o_ref, o_buf)))
            ]
            for second in range(2):
                head = 2 * p + second
                first = pl.multiple_of(3 * height + HEAD_DIM * lax.rem(head, heads), HEAD_DIM)
                copies.append(
                    pltpu.make_async_copy(
                        weight_ref.at[0, head // heads, pl.ds(first, HEAD_DIM)], wo_buf.at[slot, second],
                        load_sem.at[slot, 4 + second],
                    )
                )
            return copies

        def lane_stores(p, slot):
            lanes = pl.ds(pl.multiple_of(p * PAIR, PAIR), PAIR)
            return [
                pltpu.make_async_copy(buf.at[slot], ref.at[:, lanes], store_sem.at[slot, n])
                for n, (ref, buf) in enumerate(((dq_ref, dq_buf), (dk_ref, dk_buf), (dv_ref, dv_buf)))
            ]

        def start_stores(p, slot):
            for copy in lane_stores(p, slot):
                copy.start()
            for second in range(2):
                head = 2 * p + second
                for n in range(HEAD_DIM // 32):
                    row = HEAD_DIM * lax.rem(head, heads) + 32 * n
                    place_of = pl.ds(pl.multiple_of(lax.rem(row, height // 2), 32), 32)
                    for j in range(4):
                        pltpu.make_async_copy(
                            turned_buf.at[slot, j, pl.ds(second * HEAD_DIM + 32 * n, 32)],
                            turned_ref.at[head // heads, j, row // (height // 2), place_of], store_sem.at[slot, 3],
                        ).start()

        def wait_stores(p, slot):
            for copy in lane_stores(p, slot):
                copy.wait()
            arrived(turned_buf.at[slot], store_sem.at[slot, 3])

        def stages(p):
            slot = lax.rem(p, 2)
            return back_parts(
                qp_buf.at[slot], kp_buf.at[slot], v_buf.at[slot], o_buf.at[slot], da_ref, wo_buf.at[slot, 0],
                wo_buf.at[slot, 1], gain_ref.at[p], bias_ref, lse_ref.at[p], dq_buf.at[slot], dk_buf.at[slot],
                dv_buf.at[slot], sums.at[p], key_buf, key_turned, k_total, v_total,
            )

        def early(p):
            slot = lax.rem(p, 2)

            @pl.when(p + 1 < PAIRS)
            def _():
                for copy in loads(p + 1, 1 - slot):
                    copy.start()

            for copy in loads(p, slot):
                copy.wait()

            @pl.when(p >= 2)
            def _():
                wait_stores(p - 2, slot)

            begin, block, _ = stages(p)
            begin()
            block(0)

        def late(p):
            slot = lax.rem(p, 2)
            _, block, close = stages(p)
            for i in range(1, rows // QUERY_BLOCK):
                block(i)
            close()
            turned_buf[slot, 0] = dot_tn(dq_buf[slot], h_ref[pl.ds(cols - rows, rows), :]).astype(BF16)
            turned_buf[slot, 1] = dot_tn(dk_buf[slot], h_ref[...]).astype(BF16)
            turned_buf[slot, 2] = dot_tn(dv_buf[slot], h_ref[...]).astype(BF16)
            turned_buf[slot, 3] = dot_tn(o_buf[slot], da_ref[...]).astype(BF16)
            start_stores(p, slot)

        for copy in loads(0, 0):
            copy.start()

        def step(t, _):
            lead(t)

            @pl.when(t < PAIRS)
            def _():
                early(t)

            follow(t)

            @pl.when(t < PAIRS)
            def _():
                late(t)

            settle(t)
            return 0

        lax.fori_loop(0, attended, step, 0)
        for p in (PAIRS - 2, PAIRS - 1):
            wait_stores(p, p % 2)

    pl.run_scoped(
        attention,
        pltpu.VMEM((2, rows, PAIR), F32),
        pltpu.VMEM((2, cols, PAIR), F32),
        pltpu.VMEM((2, cols, PAIR), BF16),
        pltpu.VMEM((2, rows, PAIR), BF16),
        pltpu.VMEM((2, 2, HEAD_DIM, D), BF16),
        pltpu.VMEM((2, rows, PAIR), BF16),
        pltpu.VMEM((2, cols, PAIR), BF16),
        pltpu.VMEM((2, cols, PAIR), BF16),
        pltpu.VMEM((2, 4, PAIR, D), BF16),
        dma((2, 6)), dma((2, 4)),
        pltpu.VMEM((cols, PAIR), BF16),
        pltpu.VMEM((PAIR, cols), BF16),
        pltpu.VMEM((cols, PAIR), F32),
        pltpu.VMEM((cols, PAIR), F32),
    )

    def inputs(weight_buf, left_buf, parts, weight_sem, left_sem):
        for j in range(3):
            for shard in range(shards):
                pltpu.make_async_copy(
                    weight_ref.at[0, shard, pl.ds(j * height, height)],
                    weight_buf.at[j, pl.ds(shard * height, height)], weight_sem,
                ).start()
        for n in range(1, shards):
            other = lax.rem(line + n, shards)
            remote(gains_ref.at[other], line_got.at[n - 1], line_send.at[0], line_recv.at[0, n - 1], rep, other).start()
            remote(sums, line_sums.at[n - 1], line_send.at[1], line_recv.at[1, n - 1], rep, other).start()

        def lefts(block):
            slot = lax.rem(block, 2)
            part = pl.ds(pl.multiple_of(block * BACK_BLOCK, BACK_BLOCK), BACK_BLOCK)
            return [
                pltpu.make_async_copy(ref.at[part], left_buf.at[slot, n], left_sem.at[slot, n])
                for n, ref in ((1, dk_ref), (2, dv_ref))
            ]

        def own_left(block):
            slot = lax.rem(block, 2)
            part = pl.ds(pl.multiple_of((block - reach * per) * BACK_BLOCK, BACK_BLOCK), BACK_BLOCK)
            return pltpu.make_async_copy(dq_ref.at[part], left_buf.at[slot, 0], left_sem.at[slot, 0])

        def fetch(block):
            for copy in lefts(block):
                copy.start()

            @pl.when(block >= reach * per)
            def _():
                own_left(block).start()

        def product(block):
            slot = lax.rem(block, 2)

            @pl.when(block + 1 < cols // BACK_BLOCK)
            def _():
                fetch(block + 1)

            for copy in lefts(block):
                copy.wait()
            total = dot(left_buf[slot, 1], weight_buf[1]) + dot(left_buf[slot, 2], weight_buf[2])

            @pl.when(block < reach * per)
            def _():
                parts[block] = total.astype(BF16)
                n = block // per
                part = pl.ds(pl.multiple_of(lax.rem(block, per) * BACK_BLOCK, BACK_BLOCK), BACK_BLOCK)

                @pl.when(line >= reach - n)
                def _():
                    remote(parts.at[block], back_out.at[n, part], back_send.at[n], back_recv.at[n], rep,
                           line - (reach - n)).start()

            @pl.when(block >= reach * per)
            def _():
                own_left(block).wait()
                part = pl.ds(pl.multiple_of((block - reach * per) * BACK_BLOCK, BACK_BLOCK), BACK_BLOCK)
                own_out[part, :] = total + dot(left_buf[slot, 0], weight_buf[0])

        fetch(0)

        def step(t, _):
            lead(t)

            @pl.when(t == attended + 1)
            def _():
                arrived(weight_buf, weight_sem)
                for pair_of, (whole, got, got_plane, mine) in enumerate(
                    ((gains_ref.at[line], line_got, plane_got, mine_gains), (sums, line_sums, plane_sums, mine_sums))
                ):
                    total = whole[...]
                    for n in range(shards - 1):
                        arrived(got.at[n], line_recv.at[pair_of, n])
                        total = total + got[n]
                    mine[...] = total
                    for n in range(1, 8):
                        remote(mine, got_plane.at[n - 1], plane_send.at[pair_of], plane_recv.at[pair_of, n - 1],
                               lax.rem(rep + n, 8), line).start()

            @pl.when(t == attended + 3)
            def _():
                for pair_of, (got_plane, mine, result) in enumerate(
                    ((plane_got, mine_gains, gains_out), (plane_sums, mine_sums, sums_out))
                ):
                    total = mine[...]
                    for n in range(7):
                        arrived(got_plane.at[n], plane_recv.at[pair_of, n])
                        total = total + got_plane[n]
                    result[...] = total

            @pl.when((t > attended + 1) & (t < attended + 2 + cols // BACK_BLOCK))
            def _():
                product(t - attended - 2)

            follow(t)
            settle(t)
            return 0

        lax.fori_loop(attended, turns, step, 0)
        for n in range(reach):
            @pl.when(line >= reach - n)
            def _(n=n):
                arrived(parts.at[pl.ds(0, per)], back_send.at[n])

            @pl.when(line + reach - n < shards)
            def _(n=n):
                arrived(back_out.at[n], back_recv.at[n])

    pl.run_scoped(
        inputs,
        pltpu.VMEM((3, D, D), BF16),
        pltpu.VMEM((2, 3, BACK_BLOCK, D), BF16),
        pltpu.VMEM((reach * per, BACK_BLOCK, D), BF16),
        dma(()), dma((2, 3)),
    )
    finish()
    arrived(grads_ref, pair_send)
    arrived(line_got, line_send.at[0])
    arrived(line_sums, line_send.at[1])
    arrived(plane_got, plane_send.at[0])
    arrived(plane_sums, plane_send.at[1])


def backward_reduce(grads, down, q_pre, k_pre, value_all, o_low, gathered, gains, grad_spre, gain_qk, bias_turned, lse,
                    low_all):
    _, shards, _, _, rows, _ = grads.shape
    tokens, cols = q_pre.shape[0], k_pre.shape[0]
    reach = (cols - tokens) // tokens
    lines = gains.shape[1:]
    any_space = pl.BlockSpec(memory_space=pl.ANY)
    vmem = pl.BlockSpec(memory_space=pltpu.VMEM)
    dma = pltpu.SemaphoreType.DMA
    return pl.pallas_call(
        functools.partial(backward_kernel, shards),
        out_shape=(
            jax.ShapeDtypeStruct((4, 8, rows, D), BF16),
            jax.ShapeDtypeStruct((tokens, D), BF16),
            jax.ShapeDtypeStruct((cols, D), BF16),
            jax.ShapeDtypeStruct((cols, D), BF16),
            jax.ShapeDtypeStruct(grads.shape[1:], BF16),
            jax.ShapeDtypeStruct(lines, F32),
            jax.ShapeDtypeStruct((PAIRS, 8, PAIR), F32),
            jax.ShapeDtypeStruct((reach, tokens, D), BF16),
            jax.ShapeDtypeStruct((tokens, D), F32),
        ),
        in_specs=[any_space] * 7 + [vmem] * 6,
        out_specs=(any_space,) * 5 + (vmem, vmem, any_space, vmem),
        scratch_shapes=[
            pltpu.VMEM((PAIRS, 8, PAIR), F32),
            pltpu.VMEM((shards - 1,) + lines, F32),
            pltpu.VMEM((7,) + lines, F32),
            pltpu.VMEM((shards - 1, PAIRS, 8, PAIR), F32),
            pltpu.VMEM((7, PAIRS, 8, PAIR), F32),
            pltpu.VMEM(lines, F32),
            pltpu.VMEM((PAIRS, 8, PAIR), F32),
            dma((2,)), dma((2, shards - 1)), dma((2,)), dma((2, 7)), dma((reach,)), dma((reach,)),
        ] + reduction_scratch(4, shards, rows),
        compiler_params=pltpu.CompilerParams(
            collective_id=1, has_side_effects=True, vmem_limit_bytes=63 * 2**20
        ),
        cost_estimate=pl.CostEstimate(flops=55 * 10**9, bytes_accessed=4 * 10**8, transcendentals=13 * 10**6),
    )(grads, down, q_pre, k_pre, value_all, o_low, gathered, gains, grad_spre, gain_qk, bias_turned, lse, low_all)


def body(
    tokens,
    doc_lengths,
    cotangent,
    attn_w,
    ffn_w,
    attn_m,
    attn_v,
    ffn_m,
    ffn_v,
    gains_d,
    gains_ff,
    gd_m,
    gd_v,
    gf_m,
    gf_v,
):
    shards = lax.axis_size("shard")
    reps = lax.axis_size("rep")
    device_index = lax.axis_index("shard")
    rows = tokens.shape[0]
    reach = WINDOW // rows
    cols = (reach + 1) * rows
    attn_rows = attn_w.shape[1]
    ffn_rows = ffn_w.shape[1]
    ffn_all = shards * ffn_rows
    piece = ffn_rows // reps

    lengths_row = doc_lengths[0]
    order = jnp.arange(lengths_row.shape[0])
    starts = jnp.sum(jnp.where(order[None, :] < order[:, None], lengths_row[None, :], 0), 1)
    positions = device_index * rows + jnp.arange(rows, dtype=jnp.int32)
    doc_start = jnp.max(
        jnp.where(starts[None, :] <= positions[:, None], starts[None, :], 0), axis=1
    )
    blocks = rows // QUERY_BLOCK
    span = WINDOW + QUERY_BLOCK
    query = jnp.arange(rows, dtype=jnp.int32).reshape(blocks, QUERY_BLOCK)
    lead = query[:, :1] - reach * rows + jnp.arange(span, dtype=jnp.int32)
    ahead = query[:, :, None] - lead[:, None, :]
    floor = (doc_start - device_index * rows).reshape(blocks, QUERY_BLOCK, 1)
    mask = (ahead >= 0) & (ahead < WINDOW) & (lead[:, None, :] >= floor)
    bias = jnp.where(mask, 0.0, NEGATIVE).astype(F32)
    bias_turned = bias.transpose(0, 2, 1)
    bias = bias.reshape(rows, span)
    cut = gains_d.size
    small = jnp.concatenate([gains_d.reshape(-1), gains_ff.reshape(-1)]).astype(BF16)
    normed_in, factor_in = rownorm(tokens.astype(F32))
    fast = reps == 8 and shards == 4 and attn_rows % HEAD_DIM == 0 and reach == 2
    if fast:
        small = small.astype(F32)
        qk_heads = small[:attn_rows].reshape(-1, HEAD_DIM)
        qk_heads = jnp.pad(
            jnp.concatenate([qk_heads, qk_heads], 1), ((0, 8 - qk_heads.shape[0]), (0, D - PAIR))
        )
        small = jnp.pad(small, (0, 8 * D - small.size)).reshape(8, D)
        gathered, small, low_all, q_pre, k_pre, value_all, o_low, lse = gather_attend(
            attn_w.reshape(8, piece, D),
            ffn_w.reshape(3, 8, piece, D),
            jnp.concatenate([qk_heads, small]),
            tokens,
            bias,
            shards,
        )
        small = small[:, 8:].reshape(shards, -1)[:, : cut + gains_ff.size]
        projection = (gathered, 3)
        ffn_low = [gathered.reshape(4, ffn_all, D)] * 3
        firsts = (1, 2, 3)
    else:
        attn_low = (
            gather_rows(attn_w.reshape(4 * attn_rows, D).astype(BF16))
            .reshape(shards, 4, attn_rows, D)
            .transpose(1, 0, 2, 3)
            .reshape(1, 4, HEADS, HEAD_DIM, D)
        )
        ffn_low = [gather_rows(ffn_w[m].astype(BF16)).reshape(1, ffn_all, D) for m in range(3)]
        firsts = (0, 0, 0)
        small = lax.all_gather(small, "shard", axis=0).astype(F32)
        query_low, key_low, value_low, out_low = (attn_low[0, j].reshape(D, D) for j in range(4))
        projection = (out_low.reshape(1, 1, D, D), 0)
    gd_all = small[:, :cut].reshape(shards, 3, -1).transpose(1, 0, 2).reshape(3, D)
    gf_all = small[:, cut:].reshape(shards, 2, ffn_rows).transpose(1, 0, 2).reshape(2, ffn_all)
    gain_qk = gd_all[0]

    if not fast:
        earlier = [from_behind(tokens, "shard", offset) for offset in range(reach, 0, -1)]
        low_all = rownorm(jnp.concatenate(earlier + [tokens], 0).astype(F32))[0].astype(BF16)
        q_pre, k_pre, value_all, o_low, lse = attention_forward(
            low_all, attn_low, gain_qk[None], bias, rows
        )
    in_low = low_all[-rows:]
    output, grad_spre, grad_in, ffn_grads, down_grads, grad_scale_up, grad_scale_gate, grad_alpha_ffn, grad_alpha_attn = (
        feed_forward(tokens, o_low, projection, cotangent, gd_all[1:], gf_all, ffn_low, firsts)
    )
    pair_gain = gain_qk.reshape(PAIRS, 1, PAIR)
    grad_gf = jnp.concatenate([grad_scale_up, grad_scale_gate])
    gd_rows = D // shards
    if fast:
        units = (shards, 4, 2, piece, D)
        grad_gd = jnp.concatenate([grad_alpha_attn, grad_alpha_ffn])
        small = jnp.concatenate(
            [
                grad_gd.reshape(2, shards, gd_rows).transpose(1, 0, 2).reshape(shards, -1),
                grad_gf.reshape(2, shards, ffn_rows).transpose(1, 0, 2).reshape(shards, -1),
            ],
            1,
        )
        small = jnp.pad(small, ((0, 0), (0, 8 * D - small.shape[1]))).reshape(shards, 8, D)
        summed, _, _, _, _, sum_small, sum_qk, back_got, back_own = backward_reduce(
            ffn_grads.reshape((2,) + units), down_grads.reshape(units), q_pre, k_pre, value_all, o_low, gathered,
            small, grad_spre, pair_gain, bias_turned, lse, low_all,
        )
        grad_in = grad_in + back_own
        for n in range(reach):
            sent = device_index + reach - n < shards
            grad_in = grad_in + jnp.where(sent, back_got[n], 0).astype(F32)
        sum_small = sum_small.reshape(-1)
        sum_qk = lax.dynamic_slice_in_dim(sum_qk[:, 0].reshape(D), device_index * gd_rows, gd_rows, 0)
        sum_gd = jnp.concatenate([sum_qk, sum_small[: 2 * gd_rows]]).reshape(3, gd_rows)
        sum_gf = sum_small[2 * gd_rows : 2 * gd_rows + 2 * ffn_rows].reshape(2, ffn_rows)
        attn_sums, ffn_sums = [(summed, 3)], [(summed, 0), (summed, 1), (summed, 2)]
    else:
        grad_qpre, grad_kpre, grad_vpre, gain_sums = attention_backward(
            q_pre, k_pre, value_all, o_low, grad_spre, attn_low, pair_gain, bias_turned, lse
        )
        grad_gain_qk = gain_sums[:, 0].reshape(D)
        back_all = dot(grad_kpre, key_low) + dot(grad_vpre, value_low)
        grad_in = grad_in + dot(grad_qpre, query_low) + back_all[reach * rows :]
        back_parts = back_all[: reach * rows].reshape(reach, rows, D).astype(BF16)
        for n in range(reach):
            grad_in = grad_in + from_behind(back_parts[n], "shard", n - reach).astype(F32)
        attn_grad = jnp.stack(
            [
                dot_tn(grad_qpre, in_low),
                dot_tn(grad_kpre, low_all),
                dot_tn(grad_vpre, low_all),
                dot_tn(o_low, grad_spre),
            ]
        ).astype(BF16)
        attn_grad = attn_grad.reshape(4, shards, attn_rows, D).transpose(1, 0, 2, 3)
        attn_grad = attn_grad.reshape(shards, reps, 4 * attn_rows // reps, D).transpose(1, 0, 2, 3)
        attn_sums = [(reduce_rows(attn_grad).reshape(1, 4, attn_rows, D), 0)]
        ready = (shards, reps, piece, D)
        ffn_sums = [
            (reduce_rows(part.reshape(ready).transpose(1, 0, 2, 3)).reshape(1, 1, ffn_rows, D), 0)
            for part in (ffn_grads[0], ffn_grads[1], down_grads)
        ]
        grad_small = jnp.concatenate(
            [grad_gain_qk, grad_alpha_attn[0], grad_alpha_ffn[0], grad_gf.reshape(-1)]
        )
        grad_small = lax.psum(grad_small, ("rep", "shard"))
        sum_gd = lax.dynamic_slice_in_dim(
            grad_small[: 3 * D].reshape(3, D), device_index * gd_rows, gd_rows, 1
        )
        sum_gf = lax.dynamic_slice_in_dim(
            grad_small[3 * D :].reshape(2, ffn_all), device_index * ffn_rows, ffn_rows, 1
        )
    grad_tokens = norm_back(normed_in, factor_in, grad_in)

    attn_unit, attn_m_new, attn_v_new = adam_rows(attn_w, attn_sums, attn_m, attn_v)
    ffn_unit, ffn_m_new, ffn_v_new = adam_rows(ffn_w, ffn_sums, ffn_m, ffn_v)
    gd_new, gd_m_new, gd_v_new = adam(gains_d, sum_gd, gd_m, gd_v, GAIN_RATE, 0.0)
    gf_new, gf_m_new, gf_v_new = adam(gains_ff, sum_gf, gf_m, gf_v, GAIN_RATE, 0.0)
    return (
        output,
        grad_tokens,
        attn_unit,
        attn_m_new,
        attn_v_new,
        ffn_unit,
        ffn_m_new,
        ffn_v_new,
        gd_new,
        gd_m_new,
        gd_v_new,
        gf_new,
        gf_m_new,
        gf_v_new,
    )

def solution(mesh):
    return jax.shard_map(
        body,
        mesh=mesh,
        in_specs=(
            P(("rep", "shard"), None),
            P("rep", None),
            P(("rep", "shard"), None),
            P(None, "shard", None),
            P(None, "shard", None),
            P(None, "shard", None),
            P(None, "shard", None),
            P(None, "shard", None),
            P(None, "shard", None),
            P(None, "shard"),
            P(None, "shard"),
            P(None, "shard"),
            P(None, "shard"),
            P(None, "shard"),
            P(None, "shard"),
        ),
        out_specs=(
            P(("rep", "shard"), None),
            P(("rep", "shard"), None),
            P(None, "shard", None),
            P(None, "shard", None),
            P(None, "shard", None),
            P(None, "shard", None),
            P(None, "shard", None),
            P(None, "shard", None),
            P(None, "shard"),
            P(None, "shard"),
            P(None, "shard"),
            P(None, "shard"),
            P(None, "shard"),
            P(None, "shard"),
        ),
        check_vma=False,
    )
```
